32 devices in a mesh: dp: 4 (over x, core), fsdp: 8 (over z, y).
Axes of the slice: x: 2, y: 2, z: 4, core: 2. Of those that a mesh axis runs over, the one named last changes fastest.
Arguments:
- tokens: bfloat16 [8192, 2048], P(('dp', 'fsdp')), may hold values from -6 to 6
- cotangent: bfloat16 [8192, 2048], P(('dp', 'fsdp')), may hold values from -6 to 6
- w_in: bfloat16 [2048, 12288], P(('dp', 'fsdp')), may hold values from -0.125 to 0.125
- w_out: bfloat16 [4096, 2048], P(('dp', 'fsdp')), may hold values from -0.1875 to 0.1875
- w_up: bfloat16 [2048, 4096], P(('dp', 'fsdp')), may hold values from -0.125 to 0.125
- w_down: bfloat16 [4096, 2048], P(('dp', 'fsdp')), may hold values from -0.125 to 0.125
- ln1_gain: bfloat16 [2048], P(('dp', 'fsdp')), may hold values from 0.099609375 to 1.8984375
- ln1_bias: bfloat16 [2048], P(('dp', 'fsdp')), may hold values from -1.5 to 1.5
- group_gain: bfloat16 [4096], P(('dp', 'fsdp')), may hold values from 0.099609375 to 1.8984375
- ln2_gain: bfloat16 [2048], P(('dp', 'fsdp')), may hold values from 0.099609375 to 1.8984375
- ln2_bias: bfloat16 [2048], P(('dp', 'fsdp')), may hold values from -1.5 to 1.5
- seq_lens: int32 [64], replicated, may hold values from 0 to 256, as said below
- seq_owner: int32 [64], replicated, may hold values from 0 to 31, as said below
- seq_offset: int32 [64], replicated, may hold values from 0 to 256, as said below
Outputs:
- output: bfloat16 [8192, 2048], P(('dp', 'fsdp'))
- d_tokens: bfloat16 [8192, 2048], P(('dp', 'fsdp'))
- d_w_in: float32 [2048, 12288], P(('dp', 'fsdp'))
- d_w_out: float32 [4096, 2048], P(('dp', 'fsdp'))
- d_w_up: float32 [2048, 4096], P(('dp', 'fsdp'))
- d_w_down: float32 [4096, 2048], P(('dp', 'fsdp'))
- d_ln1_gain: float32 [2048], P(('dp', 'fsdp'))
- d_ln1_bias: float32 [2048], P(('dp', 'fsdp'))
- d_group_gain: float32 [4096], P(('dp', 'fsdp'))
- d_ln2_gain: float32 [2048], P(('dp', 'fsdp'))
- d_ln2_bias: float32 [2048], P(('dp', 'fsdp'))
The draws below stay inside these ranges and needn't reach their ends.
Inputs may be any that keep to these rules, and one draw needn't show every extreme that they name: `seq_lens`: length 0 marks an unused entry; every other entry is one whole sequence of 128 to 256 tokens, and some sequence has exactly 256. Each device is named by exactly 2 entries, one or both used, and its used sequences lie end to end from position 0 of its buffer. `seq_owner`: the device, as an index over dp+fsdp, whose buffer holds the entry. `seq_offset`: where the entry begins in its device's buffer; an unused entry begins where that device's used positions end.
All inputs are finite; a program needn't handle non-finite values.
Results may differ from the reference program's by a relative error of at most 0.014.
Values may be sent and summed in bfloat16 or wider, within the bound.
A program may use at most 448 MiB of HBM per device.

```python
import jax
import jax.numpy as jnp
from jax import lax

D = 2048
HEADS = 8
QKH = 256
VH = 512
FF = 4096
CAP = 256
MINLEN = 128
SLOTS = 2
DV = 4096
WIN = 12288
TOKENS = 8192
NSEQ = 64


def packing(key):
    device_total = NSEQ // SLOTS
    first_key, longest_key, wanted_key, second_key, shuffle_key = jax.random.split(jax.random.fold_in(key, 11), 5)
    device_ids = jnp.arange(device_total, dtype=jnp.int32)
    first_top = max(CAP - MINLEN, MINLEN)
    first_len = jax.random.randint(first_key, (device_total,), MINLEN, first_top + 1)
    longest = jax.random.randint(longest_key, (), 0, device_total)
    first_len = jnp.where(device_ids == longest, CAP, first_len).astype(jnp.int32)
    spare_room = CAP - first_len
    wanted = jax.random.randint(wanted_key, (device_total,), 0, 4) > 0
    extra_len = jax.random.randint(second_key, (device_total,), 0, CAP + 1) % jnp.maximum(spare_room - MINLEN + 1, 1)
    second_len = jnp.where(wanted & (spare_room >= MINLEN), MINLEN + extra_len, 0).astype(jnp.int32)
    lengths = jnp.stack([first_len, second_len], axis=1).reshape(-1)
    owners = jnp.stack([device_ids, device_ids], axis=1).reshape(-1)
    starts = jnp.stack([jnp.zeros_like(first_len), first_len], axis=1).reshape(-1)
    shuffle = jax.random.permutation(shuffle_key, NSEQ)
    return (lengths[shuffle].astype(jnp.int32), owners[shuffle].astype(jnp.int32), starts[shuffle].astype(jnp.int32))


def draw_seq_lens(key, part):
    return packing(key)[0]


def draw_seq_owner(key, part):
    return packing(key)[1]


def draw_seq_offset(key, part):
    return packing(key)[2]


def block_levels(own_key, shape, cuts, low, largest):
    def one(dim, blocks):
        heights = jax.random.uniform(jax.random.fold_in(jax.random.fold_in(own_key, 6), dim), (blocks,), jnp.float32, low / len(cuts), largest / len(cuts))
        return jnp.repeat(jnp.exp(heights), shape[dim] // blocks).reshape((-1,) + (1,) * (len(shape) - dim - 1))

    factor_of = one(*cuts[0])
    for cut in cuts[1:]:
        factor_of = factor_of * one(*cut)
    return factor_of


def centred(rng, extent, deviation, most, shards=(), kind=jnp.bfloat16):
    array = jax.random.normal(rng, extent, jnp.float32) * deviation
    if len(shards) > 0:
        array = block_levels(rng, extent, shards, -0.22, 0.18) * array
    return jnp.clip(array, min=-most, max=most).astype(kind)


def setup_inputs(seed: int = 0) -> dict:
    key_of = jax.random.split(jax.random.key(seed), 15)
    return {
        "tokens": centred(key_of[0], (TOKENS, D), 1.0, 6.0, ((0, 32),)),
        "cotangent": centred(key_of[1], (TOKENS, D), 1.0, 6.0, ((0, 32),)),
        "w_in": centred(key_of[2], (D, WIN), D ** -0.5, 0.125, ((0, 32),)),
        "w_out": centred(key_of[3], (DV, D), (DV // 4) ** -0.5, 0.1875, ((0, 32),)),
        "w_up": centred(key_of[4], (D, FF), D ** -0.5, 0.125, ((0, 32),)),
        "w_down": centred(key_of[5], (FF, D), (FF // 2) ** -0.5, 0.125, ((0, 32),)),
        "ln1_gain": jnp.clip(1.0 + 0.18 * jax.random.normal(key_of[6], (D,), jnp.float32), 0.099609375, 1.8984375).astype(jnp.bfloat16),
        "ln1_bias": centred(key_of[7], (D,), 0.3, 1.5, ((0, 32),)),
        "group_gain": jnp.clip(1.0 + 0.18 * jax.random.normal(key_of[8], (DV,), jnp.float32), 0.099609375, 1.8984375).astype(jnp.bfloat16),
        "ln2_gain": jnp.clip(1.0 + 0.18 * jax.random.normal(key_of[9], (D,), jnp.float32), 0.099609375, 1.8984375).astype(jnp.bfloat16),
        "ln2_bias": centred(key_of[10], (D,), 0.3, 1.5, ((0, 32),)),
        "seq_lens": draw_seq_lens(jax.random.fold_in(key_of[14], 71), 0),
        "seq_owner": draw_seq_owner(jax.random.fold_in(key_of[14], 71), 0),
        "seq_offset": draw_seq_offset(jax.random.fold_in(key_of[14], 71), 0),
    }


@jax.custom_vjp
def low(v):
    return lax.optimization_barrier(v.astype(jnp.bfloat16)).astype(jnp.float32)

@jax.custom_vjp
def low_back(v):
    return v

def low_keep(v):
    return (low(v), None)

def low_pass(kept, grad):
    return (grad,)

def back_keep(v):
    return (v, None)

def back_low(kept, grad):
    return (low(grad),)
low.defvjp(low_keep, low_pass)
low_back.defvjp(back_keep, back_low)
EPSILON = 1e-05
GROUP_EPSILON = 0.1
HIGHEST_PRECISION = lax.Precision.HIGHEST

def product(left_mat, right_mat):
    return jnp.dot(left_mat, right_mat, preferred_element_type=jnp.float32, precision=HIGHEST_PRECISION)

def layer_norm(values, gain_vec, bias_vec):
    center = values - lax.optimization_barrier(jnp.mean(values, axis=-1, keepdims=True))
    spread = lax.optimization_barrier(jnp.mean(center * center, axis=-1, keepdims=True))
    return center * lax.rsqrt(spread + EPSILON) * gain_vec + bias_vec

def layout(seq_lens, seq_owner, seq_offset, device_id, buffer_len):
    positions = jnp.arange(buffer_len, dtype=jnp.int32)[:, None]
    inside = (seq_owner[None, :] == device_id) & (seq_lens[None, :] > 0) & (positions >= seq_offset[None, :]) & (positions < seq_offset[None, :] + seq_lens[None, :])
    number = jnp.arange(seq_lens.shape[0], dtype=jnp.int32)[None, :] + 1
    seq_ident = lax.optimization_barrier(jnp.sum(jnp.where(inside, number, 0), axis=1)).astype(jnp.int32) - 1
    starts = lax.optimization_barrier(jnp.sum(jnp.where(inside, seq_offset[None, :], 0), axis=1)).astype(jnp.int32)
    places = jnp.where(seq_ident >= 0, positions[:, 0] - starts, 0).astype(jnp.int32)
    return (seq_ident, places)

def rotation(places, head_size):
    half_size = head_size // 2
    pair_index = jnp.arange(half_size, dtype=jnp.float32) / half_size
    inverse_freq = 10000.0 ** (-pair_index)
    zeta_base = (pair_index + 0.4) / 1.4
    offsets = places.astype(jnp.float32)[:, None]
    angles = offsets * inverse_freq[None, :]
    growth = zeta_base[None, :] ** (offsets / 512.0)
    return (jnp.cos(angles), jnp.sin(angles), growth)

def rotate_xpos(vectors, cosine, sine_tab, scaling):
    half_size = vectors.shape[-1] // 2
    first_half = vectors[..., :half_size]
    second_half = vectors[..., half_size:]
    cos_tab = cosine[:, None, :]
    sin_tab = sine_tab[:, None, :]
    scale_tab = scaling[:, None, :]
    return jnp.concatenate([(first_half * cos_tab - second_half * sin_tab) * scale_tab, (second_half * cos_tab + first_half * sin_tab) * scale_tab], axis=-1)

def decay_mask(seq_ident, head_count):
    positions = jnp.arange(seq_ident.shape[0], dtype=jnp.int32)
    distance = positions[:, None] - positions[None, :]
    linked = (distance >= 0) & (seq_ident[:, None] == seq_ident[None, :]) & (seq_ident[:, None] >= 0)
    log_rates = jnp.log1p(-2.0 ** (-5.0 - jnp.arange(head_count, dtype=jnp.float32)))
    powers = jnp.maximum(distance, 0).astype(jnp.float32)
    return jnp.where(linked[None], jnp.exp(log_rates[:, None, None] * powers[None]), 0.0)

def mixer_tail(mixed_out, gate_part, group_vec):
    center = mixed_out - lax.optimization_barrier(jnp.mean(mixed_out, axis=-1, keepdims=True))
    spread = lax.optimization_barrier(jnp.mean(center * center, axis=-1, keepdims=True))
    normal = center * lax.rsqrt(spread + GROUP_EPSILON) * group_vec.reshape(mixed_out.shape[1], mixed_out.shape[2])
    return jax.nn.silu(gate_part) * normal.reshape(mixed_out.shape[0], -1)

def exact_gelu(values):
    return jax.nn.gelu(values, approximate=False)

def block_forward(weights, tok_rows, seq_ident, places):
    w_in, w_out, w_up, w_down, gain_one, bias_one, gain_group, gain_two, bias_two = weights
    row_count = tok_rows.shape[0]
    key_width = HEADS * QKH
    value_width = HEADS * VH
    valid_rows = (seq_ident >= 0).astype(jnp.float32)[:, None]
    normed = low(layer_norm(tok_rows, gain_one, bias_one))
    project = low_back(product(normed, w_in))
    cosine, sine_tab, growth = rotation(places, QKH)
    query_rot = low(rotate_xpos(project[:, :key_width].reshape(row_count, HEADS, QKH), cosine, sine_tab, growth) * QKH ** (-0.5))
    key_rot = low(rotate_xpos(project[:, key_width:2 * key_width].reshape(row_count, HEADS, QKH), cosine, sine_tab, 1.0 / growth))
    value_part = low(project[:, 2 * key_width:2 * key_width + value_width].reshape(row_count, HEADS, VH))
    gate_part = project[:, 2 * key_width + value_width:]
    decay_table = decay_mask(seq_ident, HEADS)
    raw_scores = low_back(jnp.einsum('thd,shd->hts', query_rot, key_rot, precision=HIGHEST_PRECISION))
    masked = low(raw_scores * decay_table)
    mixed_out = low_back(jnp.einsum('hts,shv->thv', masked, value_part, precision=HIGHEST_PRECISION))
    gated_out = low(mixer_tail(mixed_out, gate_part, gain_group))
    branch_out = low_back(product(gated_out, w_out))
    hidden = tok_rows + branch_out
    normed_two = low(layer_norm(hidden, gain_two, bias_two))
    upper_part = low_back(product(normed_two, w_up))
    active = low(exact_gelu(upper_part))
    down_part = low_back(product(active, w_down))
    return (hidden + down_part) * valid_rows

def reference(tokens, cotangent, w_in, w_out, w_up, w_down, ln1_gain, ln1_bias, group_gain, ln2_gain, ln2_bias, seq_lens, seq_owner, seq_offset):
    device_total = NSEQ // SLOTS

    def layout_of(device_id):
        return layout(seq_lens, seq_owner, seq_offset, device_id, CAP)
    seq_ident, places = jax.vmap(layout_of)(jnp.arange(device_total, dtype=jnp.int32))
    tok_blocks = tokens.astype(jnp.float32).reshape(device_total, CAP, D)
    cot_blocks = cotangent.astype(jnp.float32).reshape(device_total, CAP, D)
    weights = (w_in.astype(jnp.float32), w_out.astype(jnp.float32), w_up.astype(jnp.float32), w_down.astype(jnp.float32), ln1_gain.astype(jnp.float32), ln1_bias.astype(jnp.float32), group_gain.astype(jnp.float32), ln2_gain.astype(jnp.float32), ln2_bias.astype(jnp.float32))
    checked = jax.checkpoint(block_forward)

    def whole_layer(weight_set, tok_all):

        def scan_step(carry, item):
            return (carry, checked(weight_set, item[0], item[1], item[2]))
        unused, outs_all = lax.scan(scan_step, jnp.zeros((), jnp.float32), (tok_all, seq_ident, places))
        return outs_all
    result, pullback = jax.vjp(whole_layer, weights, tok_blocks)
    grad_weights, grad_tokens = pullback(cot_blocks)
    return (result.reshape(TOKENS, D).astype(jnp.bfloat16), grad_tokens.reshape(TOKENS, D).astype(jnp.bfloat16), grad_weights[0], grad_weights[1], grad_weights[2], grad_weights[3], grad_weights[4], grad_weights[5], grad_weights[6], grad_weights[7], grad_weights[8])
```

```python
import functools

import jax
import jax.numpy as jnp
from jax import lax
from jax.experimental import pallas as pl
from jax.experimental.pallas import tpu as pltpu
from jax.sharding import PartitionSpec as P

HEADS = 8
QKH = 256
VH = 512
EPSILON = 1e-05
GROUP_EPSILON = 0.1
GROUP = 4
MESH = pl.DeviceIdType.MESH
ANY = pl.ANY
BF16 = jnp.bfloat16
F32 = jnp.float32
MIB = 1 << 20


def ring_place(index, total):
    half = index // 2
    return jnp.where(index % 2 == 0, half, total - 1 - half)


def ring_index(place, total):
    place = lax.rem(place + 2 * total, total)
    return jnp.where(place < total // 2, 2 * place, 2 * (total - 1 - place) + 1)


def flip(group_index, relation):
    low, high = group_index % 2, group_index // 2
    if relation % 2:
        low = 1 - low
    if relation // 2:
        high = 1 - high
    return 2 * high + low


class Place:
    def __init__(self, total):
        self.total = total
        self.group = lax.axis_index("dp")
        self.inner = lax.axis_index("fsdp")
        self.place = ring_place(self.inner, total)
        self.next = (
            ring_index(self.place + 1, total),
            ring_index(self.place - 1, total),
        )

    def peer(self, relation):
        return (flip(self.group, relation), self.inner)

    def neighbour(self, way):
        return (self.group, self.next[way])

    def behind(self, way, steps):
        return ring_index(self.place - steps if way == 0 else self.place + steps, self.total)


def greet(devices):
    barrier = pltpu.get_barrier_semaphore()
    for device in devices:
        pl.semaphore_signal(barrier, inc=1, device_id=device, device_id_type=MESH)
    pl.semaphore_wait(barrier, len(devices))


def remote(src, dst, send_sem, recv_sem, device):
    return pltpu.make_async_remote_copy(
        src_ref=src,
        dst_ref=dst,
        send_sem=send_sem,
        recv_sem=recv_sem,
        device_id=device,
        device_id_type=MESH,
    )


def column_pieces(width_in):
    key = HEADS * QKH
    value = HEADS * VH
    qk, vv = key // GROUP, value // GROUP
    return (
        (0, qk, 0, qk),
        (key, qk, qk, qk),
        (2 * key, vv, 2 * qk, vv),
        (2 * key + value, vv, 2 * qk + vv, vv),
    )


def gather_kernel(
    total,
    w_in,
    w_up,
    w_out,
    w_down,
    tok,
    cot,
    vec,
    full_in,
    full_up,
    full_out,
    full_down,
    full_tok,
    full_cot,
    full_vec,
    a2a_send,
    a2a_recv,
    own_sem,
    ring_send,
    ring_recv,
):
    at = Place(total)
    me, inner = at.group, at.inner
    peers = [at.peer(r) for r in (1, 2, 3)]
    greet(peers + [at.neighbour(0), at.neighbour(1)])
    up_width = full_up.shape[-1]
    half_out = w_out.shape[0] // 2
    pieces = column_pieces(w_in.shape[1])

    def exchange(relation, slot):
        other = flip(me, relation)
        if slot < 4:
            base, stride, off, width = pieces[slot]
            start = pl.multiple_of(base + other * stride, 128)
            src = w_in.at[:, pl.ds(start, width)]
            dst = full_in.at[me, inner, :, pl.ds(off, width)]
        elif slot == 4:
            src = w_up.at[:, pl.ds(pl.multiple_of(other * up_width, 128), up_width)]
            dst = full_up.at[me, inner]
        elif slot == 5:
            src, dst = vec, full_vec.at[inner, me]
        elif slot == 6:
            src, dst = tok, full_tok.at[me]
        else:
            src, dst = cot, full_cot.at[me]
        if relation == 0:
            return pltpu.make_async_copy(src, dst, own_sem.at[slot])
        return remote(
            src,
            dst,
            a2a_send.at[relation - 1, slot],
            a2a_recv.at[relation - 1, slot],
            at.peer(relation),
        )

    def own_block(which):
        src, dst = ((w_out, full_out), (w_down, full_down))[which]
        rows = src.shape[0]
        return pltpu.make_async_copy(src, dst.at[inner], own_sem.at[8 + which])

    for relation in (1, 0, 2, 3):
        for slot in (0, 1, 2, 3):
            exchange(relation, slot).start()
    for relation in (1, 0, 2, 3):
        for slot in (5, 4):
            exchange(relation, slot).start()
    own_block(0).start()
    own_block(1).start()

    ways = ((0, 2), (1, 3))

    def block(item, way, which):
        if item < 2:
            return full_in.at[flip(me, ways[way][item]), which]
        if item < 4:
            return full_up.at[flip(me, ways[way][item - 2]), which]
        if item == 4:
            return full_vec.at[which]
        part = full_out if item == 5 else full_down
        return part.at[which, pl.ds(way * half_out, half_out)]

    def hop(item, way, step):
        which = at.behind(way, step)
        place = block(item, way, which)
        return remote(
            place, place, ring_send.at[item, way, step], ring_recv.at[item, way, step], at.neighbour(way)
        )

    def active(item, way):
        return not (item == 4 and way == 1)

    def first(item, way):
        if item < 4:
            relation = ways[way][item % 2]
            slots = (0, 1, 2, 3) if item < 2 else (4,)
            for slot in slots:
                copy = exchange(relation, slot)
                if relation == 0:
                    copy.wait()
                else:
                    copy.wait_recv()
        elif item == 4:
            for relation in range(4):
                copy = exchange(relation, 5)
                if relation == 0:
                    copy.wait()
                else:
                    copy.wait_recv()
        elif way == 0:
            own_block(item - 5).wait()
        hop(item, way, 0).start()

    groups = ((0, 1), (4, 5, 2, 3, 6))
    for number, group in enumerate(groups):
        for item in group:
            for way in (0, 1):
                if active(item, way):
                    first(item, way)
        if number == 0:
            for relation in (1, 0, 2, 3):
                for slot in (6, 7):
                    exchange(relation, slot).start()

        def onward(step, carry, group=group):
            for item in group:
                for way in (0, 1):
                    if active(item, way):
                        hop(item, way, step - 1).wait_recv()
                        hop(item, way, step).start()
            return carry

        lax.fori_loop(1, total - 1, onward, 0)

    for group in groups:
        for item in group:
            for way in (0, 1):
                if active(item, way):
                    hop(item, way, total - 2).wait_recv()

    def sent(step, carry):
        for group in groups:
            for item in group:
                for way in (0, 1):
                    if active(item, way):
                        hop(item, way, step).wait_send()
        return carry

    lax.fori_loop(0, total - 1, sent, 0)
    for relation in (1, 2, 3):
        for slot in range(8):
            exchange(relation, slot).wait_send()
            if slot >= 6:
                exchange(relation, slot).wait_recv()
    exchange(0, 6).wait()
    exchange(0, 7).wait()


def gather_all(total, w_in, w_up, w_out, w_down, tok, cot, vec):
    width = w_in.shape[1] // GROUP
    up_width = w_up.shape[1] // GROUP
    shapes = (
        ((GROUP, total, w_in.shape[0], width), BF16),
        ((GROUP, total, w_up.shape[0], up_width), BF16),
        ((total,) + w_out.shape, BF16),
        ((total,) + w_down.shape, BF16),
        ((GROUP,) + tok.shape, BF16),
        ((GROUP,) + cot.shape, BF16),
        ((total, GROUP) + vec.shape, F32),
    )
    return pl.pallas_call(
        functools.partial(gather_kernel, total),
        out_shape=[jax.ShapeDtypeStruct(s, d) for s, d in shapes],
        in_specs=[pl.BlockSpec(memory_space=ANY)] * 7,
        out_specs=[pl.BlockSpec(memory_space=ANY)] * 7,
        scratch_shapes=[
            pltpu.SemaphoreType.DMA((3, 8)),
            pltpu.SemaphoreType.DMA((3, 8)),
            pltpu.SemaphoreType.DMA((10,)),
            pltpu.SemaphoreType.DMA((7, 2, total - 1)),
            pltpu.SemaphoreType.DMA((7, 2, total - 1)),
        ],
        compiler_params=pltpu.CompilerParams(collective_id=0, has_side_effects=True),
        name="gather_weights",
    )(w_in, w_up, w_out, w_down, tok, cot, vec)


def norm_parts(values, epsilon):
    center = values - jnp.mean(values, axis=-1, keepdims=True)
    spread = jnp.mean(center * center, axis=-1, keepdims=True)
    scale = lax.rsqrt(spread + epsilon)
    return center * scale, scale


def exchange_kernel(total, chunks, backward, part, extra, hidden_in, gain, bias, *refs):
    if backward:
        (keep, full, sums, core_in, out_x, in_x, low, own_part, sends, recvs, own_sem) = refs
    else:
        (keep, full, core_in, out_x, in_x, low, own_part, sends, recvs, own_sem) = refs
    at = Place(total)
    me = at.group
    core, across = at.peer(1), at.peer(2)
    rows = low.shape[0] // chunks
    greet([core, across])
    mine, far = me, flip(me, 2)

    def rows_of(c):
        return pl.ds(c * rows, rows)

    def copy(kind, c):
        r = rows_of(c)
        if kind == 0:
            src, dst, dev = part.at[flip(me, 3), r], core_in.at[0, r], core
        elif kind == 1:
            src, dst, dev = part.at[flip(me, 1), r], core_in.at[1, r], core
        elif kind == 2:
            src, dst, dev = out_x.at[r], in_x.at[r], across
        elif kind == 3:
            src, dst, dev = low.at[r], full.at[me, r], across
        elif kind == 4:
            src, dst, dev = low.at[r], full.at[me, r], core
        else:
            src, dst, dev = full.at[far, r], full.at[far, r], core
        return remote(src, dst, sends.at[kind, c], recvs.at[kind, c], dev)

    def load(which, c):
        r = rows_of(c)
        source = far if which == 0 else mine
        return pltpu.make_async_copy(part.at[source, r], own_part.at[which, r], own_sem.at[which, c])

    def store(c):
        r = rows_of(c)
        return pltpu.make_async_copy(low.at[r], full.at[me, r], own_sem.at[2, c])

    for c in range(chunks):
        copy(0, c).start()
        load(0, c).start()
    for c in range(chunks):
        copy(1, c).start()
        load(1, c).start()
    for c in range(chunks):
        r = rows_of(c)
        load(0, c).wait()
        copy(0, c).wait_recv()
        out_x[r, :] = (own_part[0, r, :].astype(F32) + core_in[0, r, :].astype(F32)).astype(BF16)
        copy(2, c).start()
    if backward:
        sums[...] = jnp.zeros_like(sums)
    for c in range(chunks):
        r = rows_of(c)
        load(1, c).wait()
        copy(1, c).wait_recv()
        copy(2, c).wait_recv()
        total_rows = (
            own_part[1, r, :].astype(F32) + core_in[1, r, :].astype(F32) + in_x[r, :].astype(F32)
        )
        if backward:
            normal, scale = norm_parts(hidden_in[r, :], EPSILON)
            with_gain = total_rows * gain[...]
            both = with_gain * normal
            sums[0:1, :] += jnp.sum(total_rows * normal, axis=0, keepdims=True)
            sums[1:2, :] += jnp.sum(total_rows, axis=0, keepdims=True)
            result = extra[r, :].astype(F32) + scale * (
                with_gain
                - jnp.mean(with_gain, axis=-1, keepdims=True)
                - normal * jnp.mean(both, axis=-1, keepdims=True)
            )
            keep[r, :] = result
            low[r, :] = result.astype(BF16)
        else:
            hidden = extra[r, :].astype(F32) + total_rows
            keep[r, :] = hidden
            normal, scale = norm_parts(hidden, EPSILON)
            low[r, :] = (normal * gain[...] + bias[...]).astype(BF16)
        copy(3, c).start()
        copy(4, c).start()
        store(c).start()
    for c in range(chunks):
        copy(3, c).wait_recv()
        copy(5, c).start()
    for c in range(chunks):
        copy(4, c).wait_recv()
        copy(5, c).wait_recv()
        store(c).wait()
        for kind in range(6):
            copy(kind, c).wait_send()


def exchange_rows(total, backward, part, extra, hidden, gain, bias):
    rows, width = extra.shape
    chunks = 4
    vmem = pl.BlockSpec(memory_space=pltpu.VMEM)
    shapes = [jax.ShapeDtypeStruct((rows, width), F32), jax.ShapeDtypeStruct((GROUP, rows, width), BF16)]
    specs = [vmem, pl.BlockSpec(memory_space=ANY)]
    if backward:
        shapes.append(jax.ShapeDtypeStruct((8, width), F32))
        specs.append(vmem)
    return pl.pallas_call(
        functools.partial(exchange_kernel, total, chunks, backward),
        out_shape=shapes,
        in_specs=[pl.BlockSpec(memory_space=ANY)] + [vmem] * 4,
        out_specs=specs,
        scratch_shapes=[
            pltpu.VMEM((2, rows, width), BF16),
            pltpu.VMEM((rows, width), BF16),
            pltpu.VMEM((rows, width), BF16),
            pltpu.VMEM((rows, width), BF16),
            pltpu.VMEM((2, rows, width), BF16),
            pltpu.SemaphoreType.DMA((6, chunks)),
            pltpu.SemaphoreType.DMA((6, chunks)),
            pltpu.SemaphoreType.DMA((3, chunks)),
        ],
        compiler_params=pltpu.CompilerParams(
            collective_id=2 if backward else 1, has_side_effects=True, vmem_limit_bytes=40 * MIB
        ),
        name="exchange_backward" if backward else "exchange_forward",
    )(part, extra, hidden, gain, bias)


class Ring:
    def __init__(self, at, way, source, local, arrived, loads, sends, recvs):
        self.at, self.way, self.source = at, way, source
        self.local, self.arrived = local, arrived
        self.loads, self.sends, self.recvs = loads, sends, recvs

    def load(self, which):
        return pltpu.make_async_copy(self.source(which), self.local.at[which], self.loads.at[which])

    def hop(self, step, first=False):
        src = self.local.at[self.at.behind(self.way, 1)] if first else self.arrived.at[step - 1]
        return remote(
            src, self.arrived.at[step], self.sends.at[step], self.recvs.at[step], self.at.neighbour(self.way)
        )

    def begin(self):
        self.load(self.at.behind(self.way, 1)).wait()
        self.hop(0, True).start()

    def onward(self, step):
        which = self.at.behind(self.way, step + 1)
        self.load(which).wait()
        self.hop(step - 1, True).wait_recv()
        self.arrived[step - 1] = (
            self.arrived[step - 1].astype(F32) + self.local[which].astype(F32)
        ).astype(BF16)
        self.hop(step).start()

    def finish(self):
        last = self.at.total - 2
        self.load(self.at.inner).wait()
        self.hop(last, True).wait_recv()
        return self.arrived[last].astype(F32) + self.local[self.at.inner].astype(F32)

    def sent(self, step):
        self.hop(step, True).wait_send()


def run_rings(rings, total, between=()):
    at = rings[0].at
    for ring in rings:
        ring.load(at.behind(ring.way, 1)).start()

    def loads(step, carry):
        for ring in rings:
            ring.load(at.behind(ring.way, step + 1)).start()
        return carry

    lax.fori_loop(1, total, loads, 0)
    for ring in rings:
        ring.begin()
    marks = dict(between)
    last = 1
    for stop in sorted(marks) + [total - 1]:

        def body(step, carry):
            for ring in rings:
                ring.onward(step)
            return carry

        lax.fori_loop(last, stop, body, 0)
        last = stop
        if stop in marks:
            marks[stop]()


def close_rings(rings, total):
    for ring in rings:
        ring.sent(0)

    def body(step, carry):
        for ring in rings:
            ring.sent(step)
        return carry

    lax.fori_loop(1, total - 1, body, 0)


RELATIONS = ((2, 0), (3, 1))


def reduce_rest_kernel(
    total, g_up, g_out, g_down, o_up, o_out, o_down, l_up, r_up, l_od, r_od, stage, landed,
    loads_up, send_up, recv_up, loads_od, send_od, recv_od, a2a_send, a2a_recv,
):
    at = Place(total)
    me = at.group
    greet([at.peer(r) for r in (1, 2, 3)] + [at.neighbour(0), at.neighbour(1)])
    half = g_out.shape[1] // 2
    rings, kinds = [], []
    for order in (0, 1):
        for way in (0, 1):
            relation = RELATIONS[way][order]
            slot = 2 * way + order
            rings.append(
                Ring(
                    at, way,
                    lambda which, relation=relation: g_up.at[flip(me, relation), which],
                    l_up.at[slot], r_up.at[slot], loads_up.at[slot], send_up.at[slot], recv_up.at[slot],
                )
            )
            kinds.append(("up", relation))
    for number, source in enumerate((g_out, g_down)):
        for way in (0, 1):
            slot = 2 * number + way
            rings.append(
                Ring(
                    at, way,
                    lambda which, source=source, way=way: source.at[which, pl.ds(way * half, half)],
                    l_od.at[slot], r_od.at[slot], loads_od.at[slot], send_od.at[slot], recv_od.at[slot],
                )
            )
            kinds.append((number, way))
    run_rings(rings, total)
    width = o_up.shape[1] // GROUP

    def across(relation):
        return remote(
            stage.at[relation - 1], landed.at[relation - 1],
            a2a_send.at[relation - 1], a2a_recv.at[relation - 1], at.peer(relation),
        )

    for ring, (kind, what) in zip(rings, kinds):
        value = ring.finish()
        if kind == "up":
            if what == 0:
                o_up[:, pl.ds(pl.multiple_of(me * width, 128), width)] = value
            else:
                stage[what - 1] = value.astype(BF16)
                across(what).start()
        else:
            out = (o_out, o_down)[kind]
            out[pl.ds(what * half, half), :] = value
    for relation in (1, 2, 3):
        across(relation).wait_recv()
        o_up[:, pl.ds(pl.multiple_of(flip(me, relation) * width, 128), width)] = landed[
            relation - 1
        ].astype(F32)
    for relation in (1, 2, 3):
        across(relation).wait_send()
    close_rings(rings, total)


def reduce_rest(total, g_up, g_out, g_down):
    rows_up, width_up = g_up.shape[2:]
    rows_out, width_out = g_out.shape[1:]
    half = rows_out // 2
    vmem = pl.BlockSpec(memory_space=pltpu.VMEM)
    dma = pltpu.SemaphoreType.DMA
    return pl.pallas_call(
        functools.partial(reduce_rest_kernel, total),
        out_shape=[
            jax.ShapeDtypeStruct((rows_up, width_up * GROUP), F32),
            jax.ShapeDtypeStruct((rows_out, width_out), F32),
            jax.ShapeDtypeStruct((rows_out, width_out), F32),
        ],
        in_specs=[pl.BlockSpec(memory_space=ANY)] * 3,
        out_specs=[vmem] * 3,
        scratch_shapes=[
            pltpu.VMEM((4, total, rows_up, width_up), BF16),
            pltpu.VMEM((4, total - 1, rows_up, width_up), BF16),
            pltpu.VMEM((4, total, half, width_out), BF16),
            pltpu.VMEM((4, total - 1, half, width_out), BF16),
            pltpu.VMEM((3, rows_up, width_up), BF16),
            pltpu.VMEM((3, rows_up, width_up), BF16),
            dma((4, total)), dma((4, total - 1)), dma((4, total - 1)),
            dma((4, total)), dma((4, total - 1)), dma((4, total - 1)),
            dma((3,)), dma((3,)),
        ],
        compiler_params=pltpu.CompilerParams(
            collective_id=3, has_side_effects=True, vmem_limit_bytes=48 * MIB
        ),
        name="reduce_rest",
    )(g_up, g_out, g_down)


def reduce_in_kernel(
    total, g_in, part, o_in, o_part, local, arrived, stage, landed,
    core_in, own_part, out_x, in_x, loads, ring_send, ring_recv, a2a_send, a2a_recv,
    row_send, row_recv, row_own,
):
    at = Place(total)
    me = at.group
    greet([at.peer(r) for r in (1, 2, 3)] + [at.neighbour(0), at.neighbour(1)])
    rings, relations = [], []
    for order in (0, 1):
        for way in (0, 1):
            relation = RELATIONS[way][order]
            slot = 2 * way + order
            rings.append(
                Ring(
                    at, way,
                    lambda which, relation=relation: g_in.at[flip(me, relation), which],
                    local.at[slot], arrived.at[slot], loads.at[slot], ring_send.at[slot], ring_recv.at[slot],
                )
            )
            relations.append(relation)

    count = part.shape[0]

    def row_copy(kind, n):
        if kind == 0:
            src, dst, dev = part.at[n, flip(me, 3)], core_in.at[n, 0], at.peer(1)
        elif kind == 1:
            src, dst, dev = part.at[n, flip(me, 1)], core_in.at[n, 1], at.peer(1)
        else:
            src, dst, dev = out_x.at[n], in_x.at[n], at.peer(2)
        return remote(src, dst, row_send.at[n, kind], row_recv.at[n, kind], dev)

    def row_load(n, which):
        return pltpu.make_async_copy(
            part.at[n, flip(me, 2) if which == 0 else me], own_part.at[n, which], row_own.at[n, which]
        )

    for n in range(count):
        for kind in (0, 1):
            row_copy(kind, n).start()
            row_load(n, kind).start()

    def send_rows():
        for n in range(count):
            row_load(n, 0).wait()
            row_copy(0, n).wait_recv()
            out_x[n] = (own_part[n, 0].astype(F32) + core_in[n, 0].astype(F32)).astype(BF16)
            row_copy(2, n).start()

    def take_rows():
        for n in range(count):
            row_load(n, 1).wait()
            row_copy(1, n).wait_recv()
            row_copy(2, n).wait_recv()
            o_part[n] = (
                own_part[n, 1].astype(F32) + core_in[n, 1].astype(F32) + in_x[n].astype(F32)
            )

    run_rings(rings, total, ((2, send_rows), (total - 2, take_rows)))
    pieces = column_pieces(o_in.shape[1])

    def place(other, value):
        for base, stride, off, width in pieces:
            start = pl.multiple_of(base + other * stride, 128)
            o_in[:, pl.ds(start, width)] = value[:, off : off + width]

    def across(relation):
        return remote(
            stage.at[relation - 1], landed.at[relation - 1],
            a2a_send.at[relation - 1], a2a_recv.at[relation - 1], at.peer(relation),
        )

    for ring, relation in zip(rings, relations):
        value = ring.finish()
        if relation == 0:
            place(me, value)
        else:
            stage[relation - 1] = value.astype(BF16)
            across(relation).start()
    for relation in (1, 2, 3):
        across(relation).wait_recv()
        place(flip(me, relation), landed[relation - 1].astype(F32))
    for relation in (1, 2, 3):
        across(relation).wait_send()
    close_rings(rings, total)
    for n in range(count):
        for kind in (0, 1, 2):
            row_copy(kind, n).wait_send()


def reduce_in(total, g_in, part):
    rows, width = g_in.shape[2:]
    count, _, tokens, features = part.shape
    vmem = pl.BlockSpec(memory_space=pltpu.VMEM)
    dma = pltpu.SemaphoreType.DMA
    return pl.pallas_call(
        functools.partial(reduce_in_kernel, total),
        out_shape=[
            jax.ShapeDtypeStruct((rows, width * GROUP), F32),
            jax.ShapeDtypeStruct((count, tokens, features), F32),
        ],
        in_specs=[pl.BlockSpec(memory_space=ANY)] * 2,
        out_specs=[vmem] * 2,
        scratch_shapes=[
            pltpu.VMEM((4, total, rows, width), BF16),
            pltpu.VMEM((4, total - 1, rows, width), BF16),
            pltpu.VMEM((3, rows, width), BF16),
            pltpu.VMEM((3, rows, width), BF16),
            pltpu.VMEM((count, 2, tokens, features), BF16),
            pltpu.VMEM((count, 2, tokens, features), BF16),
            pltpu.VMEM((count, tokens, features), BF16),
            pltpu.VMEM((count, tokens, features), BF16),
            dma((4, total)), dma((4, total - 1)), dma((4, total - 1)),
            dma((3,)), dma((3,)),
            dma((count, 3)), dma((count, 3)), dma((count, 2)),
        ],
        compiler_params=pltpu.CompilerParams(
            collective_id=4, has_side_effects=True, vmem_limit_bytes=60 * MIB
        ),
        name="reduce_in",
    )(g_in, part)


def reduce_vectors_kernel(total, vec, out, landed, mid, gathered, sends, recvs, far_send, far_recv):
    at = Place(total)
    me, inner = at.group, at.inner
    others = [(me, lax.rem(inner + n, total)) for n in range(1, total)]
    greet([at.peer(r) for r in (1, 2, 3)] + others)

    def near(relation):
        return remote(
            vec.at[flip(me, relation)], landed.at[relation - 1],
            sends.at[relation - 1], recvs.at[relation - 1], at.peer(relation),
        )

    for relation in (1, 2, 3):
        near(relation).start()
    for relation in (1, 2, 3):
        near(relation).wait_recv()
    mid[...] = vec[me] + landed[0] + landed[1] + landed[2]

    def far(n):
        target = lax.rem(inner + n, total)
        return remote(mid.at[target], gathered.at[n - 1], far_send.at[n - 1], far_recv.at[n - 1], (me, target))

    for n in range(1, total):
        far(n).start()
    for n in range(1, total):
        far(n).wait_recv()
    out[...] = mid[inner] + jnp.sum(gathered[...], axis=0)
    for n in range(1, total):
        far(n).wait_send()
    for relation in (1, 2, 3):
        near(relation).wait_send()


def reduce_vectors(total, vec):
    block = vec.shape[2:]
    vmem = pl.BlockSpec(memory_space=pltpu.VMEM)
    dma = pltpu.SemaphoreType.DMA
    return pl.pallas_call(
        functools.partial(reduce_vectors_kernel, total),
        out_shape=jax.ShapeDtypeStruct(block, F32),
        in_specs=[vmem],
        out_specs=vmem,
        scratch_shapes=[
            pltpu.VMEM((3, total) + block, F32),
            pltpu.VMEM((total,) + block, F32),
            pltpu.VMEM((total - 1,) + block, F32),
            dma((3,)), dma((3,)), dma((total - 1,)), dma((total - 1,)),
        ],
        compiler_params=pltpu.CompilerParams(collective_id=5, has_side_effects=True),
        name="reduce_vectors",
    )(vec)


def layout(seq_lens, seq_owner, seq_offset, device_id, buffer_len):
    positions = jnp.arange(buffer_len, dtype=jnp.int32)[:, None]
    inside = (
        (seq_owner[None, :] == device_id)
        & (seq_lens[None, :] > 0)
        & (positions >= seq_offset[None, :])
        & (positions < seq_offset[None, :] + seq_lens[None, :])
    )
    number = jnp.arange(seq_lens.shape[0], dtype=jnp.int32)[None, :] + 1
    seq_ident = jnp.sum(jnp.where(inside, number, 0), axis=1) - 1
    starts = jnp.sum(jnp.where(inside, seq_offset[None, :], 0), axis=1)
    places = jnp.where(seq_ident >= 0, positions[:, 0] - starts, 0)
    return seq_ident, places


def rotation(places):
    half_size = QKH // 2
    pair_index = jnp.arange(half_size, dtype=F32) / half_size
    inverse_freq = 10000.0 ** (-pair_index)
    zeta_base = (pair_index + 0.4) / 1.4
    offsets = places.astype(F32)[..., None]
    angles = offsets * inverse_freq
    growth = zeta_base ** (offsets / 512.0)
    return jnp.cos(angles), jnp.sin(angles), growth


def rotate_xpos(vectors, cosine, sine, scale):
    half = QKH // 2
    first, second = vectors[..., :half], vectors[..., half:]
    cosine, sine, scale = cosine[..., None, :], sine[..., None, :], scale[..., None, :]
    return jnp.concatenate(
        [(first * cosine - second * sine) * scale, (second * cosine + first * sine) * scale], axis=-1
    )


def rotate_back(vectors, cosine, sine, scale):
    return rotate_xpos(vectors, cosine, -sine, scale)


def decay_tables(ident, heads):
    positions = jnp.arange(ident.shape[-1], dtype=jnp.int32)
    distance = positions[:, None] - positions[None, :]
    linked = (distance >= 0) & (ident[:, :, None] == ident[:, None, :]) & (ident[:, :, None] >= 0)
    rates = jnp.log1p(-(2.0 ** (-5.0 - heads.astype(F32))))
    powers = jnp.maximum(distance, 0).astype(F32)
    return jnp.where(linked[:, None], jnp.exp(rates[:, None, None] * powers[None])[None], 0.0)


def dot(left, right):
    return jnp.dot(left, right, preferred_element_type=F32)


def dot_rows(left, right):
    return lax.dot_general(left, right, (((0,), (0,)), ((), ())), preferred_element_type=F32)


def dot_back(left, right):
    return lax.dot_general(left, right, (((1,), (1,)), ((), ())), preferred_element_type=F32)


def mean(values):
    return jnp.mean(values, axis=-1, keepdims=True)


def local(
    total,
    tokens,
    cotangent,
    w_in,
    w_out,
    w_up,
    w_down,
    ln1_gain,
    ln1_bias,
    group_gain,
    ln2_gain,
    ln2_bias,
    seq_lens,
    seq_owner,
    seq_offset,
):
    rows, width = tokens.shape
    heads = HEADS // GROUP
    qk, vv = heads * QKH, heads * VH
    me, inner = lax.axis_index("dp"), lax.axis_index("fsdp")
    small, large = ln1_gain.shape[0], group_gain.shape[0]

    pack = jnp.concatenate([ln1_gain, ln1_bias, ln2_gain, ln2_bias, group_gain]).astype(F32)
    pack = jnp.pad(pack, (0, 1024 - pack.shape[0])).reshape(8, 128)
    full_in, full_up, full_out, full_down, tok, cot, vec = gather_all(
        total, w_in, w_up, w_out, w_down, tokens, cotangent, pack
    )
    full_in = full_in.reshape(width, -1)
    full_up = full_up.reshape(width, -1)
    full_out = full_out.reshape(-1, width)
    full_down = full_down.reshape(-1, width)
    vec = vec.reshape(total, GROUP, 1024)

    def vector(number):
        part = vec[:, :, number * small : (number + 1) * small]
        return jnp.swapaxes(part, 0, 1).reshape(1, width)

    gain_one, bias_one, gain_two, bias_two = (vector(n) for n in range(4))
    gain_group = lax.dynamic_index_in_dim(vec, me, 1, keepdims=False)[:, 4 * small : 4 * small + large]
    gain_group = gain_group.reshape(heads, VH)

    devices = jnp.arange(GROUP, dtype=jnp.int32) * total + inner
    ident, places = jax.vmap(lambda d: layout(seq_lens, seq_owner, seq_offset, d, rows))(devices)
    valid = (ident >= 0).astype(F32)[..., None]
    own_valid = lax.dynamic_index_in_dim(valid, me, 0, keepdims=False)
    count = GROUP * rows

    normal, _ = norm_parts(tok.astype(F32), EPSILON)
    normed = (normal * gain_one + bias_one).astype(BF16).reshape(count, width)
    project = dot(normed, full_in).reshape(GROUP, rows, -1)
    cosine, sine, growth = rotation(places)
    shrink = 1.0 / growth
    query = rotate_xpos(project[..., :qk].reshape(GROUP, rows, heads, QKH), cosine, sine, growth)
    query = (query * QKH ** (-0.5)).astype(BF16)
    keys = rotate_xpos(
        project[..., qk : 2 * qk].reshape(GROUP, rows, heads, QKH), cosine, sine, shrink
    ).astype(BF16)
    values = project[..., 2 * qk : 2 * qk + vv].reshape(GROUP, rows, heads, VH).astype(BF16)
    gate = project[..., 2 * qk + vv :].reshape(GROUP, rows, heads, VH)
    decay = decay_tables(ident, me * heads + jnp.arange(heads))
    raw = jnp.einsum("bthd,bshd->bhts", query, keys, preferred_element_type=F32)
    masked = (raw * decay).astype(BF16)
    mixed = jnp.einsum("bhts,bshv->bthv", masked, values, preferred_element_type=F32)
    group_normal, group_scale = norm_parts(mixed, GROUP_EPSILON)
    sigmoid = jax.nn.sigmoid(gate)
    silu = gate * sigmoid
    gated = (silu * (group_normal * gain_group)).astype(BF16).reshape(count, vv)
    branch = dot(gated, full_out).astype(BF16).reshape(GROUP, rows, width)
    hidden, two = exchange_rows(total, False, branch, tokens, jnp.zeros((8, 128), F32), gain_two, bias_two)
    two = two.reshape(count, width)
    upper = dot(two, full_up)
    cdf = 0.5 * (1.0 + lax.erf(upper * (0.5**0.5)))
    active = (upper * cdf).astype(BF16)
    down = dot(active, full_down).astype(BF16).reshape(GROUP, rows, width)

    seed = (cot.astype(F32) * valid).astype(BF16)
    own_seed = (cotangent.astype(F32) * own_valid).astype(BF16)
    seed = seed.reshape(count, width)
    slope = cdf + upper * jnp.exp(-0.5 * upper * upper) * (2.0 * jnp.pi) ** -0.5
    d_upper = (dot_back(seed, full_down) * slope).astype(BF16)
    d_two = dot_back(d_upper, full_up).astype(BF16).reshape(GROUP, rows, width)
    d_hidden, d_branch, sums_two = exchange_rows(
        total, True, d_two, own_seed, hidden, gain_two, bias_two
    )
    d_branch = d_branch.reshape(count, width)
    g_down = dot_rows(active, seed).astype(BF16).reshape(total, -1, width)
    g_up = dot_rows(two, d_upper).astype(BF16).reshape(GROUP, total, small, -1)
    g_out = dot_rows(gated, d_branch).astype(BF16).reshape(total, -1, width)
    grad_up, grad_out, grad_down = reduce_rest(total, g_up, g_out, g_down)

    d_gated = dot_back(d_branch, full_out).reshape(GROUP, rows, heads, VH)
    d_silu = d_gated * (group_normal * gain_group)
    d_gate = d_silu * (sigmoid + silu * (1.0 - sigmoid))
    d_scaled = d_gated * silu
    d_group = jnp.sum(d_scaled * group_normal, axis=(0, 1))
    d_normal = d_scaled * gain_group
    d_mixed = group_scale * (
        d_normal - mean(d_normal) - group_normal * mean(d_normal * group_normal)
    )
    d_mixed = d_mixed.astype(BF16)
    d_values = jnp.einsum("bhts,bthv->bshv", masked, d_mixed, preferred_element_type=F32)
    d_masked = jnp.einsum("bthv,bshv->bhts", d_mixed, values, preferred_element_type=F32)
    d_raw = (d_masked * decay).astype(BF16)
    d_query = jnp.einsum("bhts,bshd->bthd", d_raw, keys, preferred_element_type=F32)
    d_keys = jnp.einsum("bhts,bthd->bshd", d_raw, query, preferred_element_type=F32)
    d_query = rotate_back(d_query * QKH ** (-0.5), cosine, sine, growth)
    d_keys = rotate_back(d_keys, cosine, sine, shrink)
    d_project = jnp.concatenate(
        [
            d_query.astype(BF16).reshape(count, qk),
            d_keys.astype(BF16).reshape(count, qk),
            d_values.astype(BF16).reshape(count, vv),
            d_gate.astype(BF16).reshape(count, vv),
        ],
        axis=1,
    )
    d_normed = dot_back(d_project, full_in).astype(BF16).reshape(GROUP, rows, width)
    g_in = dot_rows(normed, d_project).astype(BF16).reshape(GROUP, total, small, -1)
    grad_in, own_rows = reduce_in(total, g_in, jnp.stack([d_normed, down]))
    output = ((hidden + own_rows[1]) * own_valid).astype(BF16)
    e_one = own_rows[0]
    normal_one, scale_one = norm_parts(tokens.astype(F32), EPSILON)
    with_gain = e_one * gain_one
    d_tokens = d_hidden + scale_one * (
        with_gain - mean(with_gain) - normal_one * mean(with_gain * normal_one)
    )
    d_tokens = d_tokens.astype(BF16)

    sums = jnp.stack(
        [jnp.sum(e_one * normal_one, axis=0), jnp.sum(e_one, axis=0), sums_two[0], sums_two[1]]
    )
    sums = sums.reshape(4, GROUP, total, small).transpose(1, 2, 0, 3).reshape(GROUP, total, 4 * small)
    mine = (jnp.arange(GROUP) == me).astype(F32)[:, None, None]
    sums = jnp.concatenate([sums, mine * d_group.reshape(1, total, large)], axis=2)
    sums = jnp.pad(sums, ((0, 0), (0, 0), (0, 1024 - sums.shape[2]))).reshape(GROUP, total, 8, 128)
    summed = reduce_vectors(total, sums).reshape(1024)
    grads = [summed[n * small : (n + 1) * small] for n in range(4)]
    grad_group = summed[4 * small : 4 * small + large]
    return (
        output,
        d_tokens,
        grad_in,
        grad_out,
        grad_up,
        grad_down,
        grads[0],
        grads[1],
        grad_group,
        grads[2],
        grads[3],
    )


def solution(mesh):
    flat = ("dp", "fsdp")
    matrix, vector = P(flat, None), P(flat)
    return jax.shard_map(
        functools.partial(local, mesh.shape["fsdp"]),
        mesh=mesh,
        in_specs=(matrix,) * 6 + (vector,) * 5 + (P(),) * 3,
        out_specs=(matrix,) * 6 + (vector,) * 5,
        check_vma=False,
    )
```

```python
import functools

import jax
import jax.numpy as jnp
from jax import lax
from jax.experimental import pallas as pl
from jax.experimental.pallas import tpu as pltpu
from jax.sharding import PartitionSpec as P

HEADS = 8
QKH = 256
VH = 512
EPSILON = 1e-05
GROUP_EPSILON = 0.1
GROUP = 4
MESH = pl.DeviceIdType.MESH
ANY = pl.ANY
BF16 = jnp.bfloat16
F32 = jnp.float32
MIB = 1 << 20


def ring_place(index, total):
    half = index // 2
    return jnp.where(index % 2 == 0, half, total - 1 - half)


def ring_index(place, total):
    place = lax.rem(place + 2 * total, total)
    return jnp.where(place < total // 2, 2 * place, 2 * (total - 1 - place) + 1)


def flip(group_index, relation):
    low, high = group_index % 2, group_index // 2
    if relation % 2:
        low = 1 - low
    if relation // 2:
        high = 1 - high
    return 2 * high + low


class Place:
    def __init__(self, total):
        self.total = total
        self.group = lax.axis_index("dp")
        self.inner = lax.axis_index("fsdp")
        self.place = ring_place(self.inner, total)
        self.next = (
            ring_index(self.place + 1, total),
            ring_index(self.place - 1, total),
        )

    def peer(self, relation):
        return (flip(self.group, relation), self.inner)

    def neighbour(self, way):
        return (self.group, self.next[way])

    def behind(self, way, steps):
        return ring_index(self.place - steps if way == 0 else self.place + steps, self.total)


def greet(devices):
    barrier = pltpu.get_barrier_semaphore()
    for device in devices:
        pl.semaphore_signal(barrier, inc=1, device_id=device, device_id_type=MESH)
    pl.semaphore_wait(barrier, len(devices))


def remote(src, dst, send_sem, recv_sem, device):
    return pltpu.make_async_remote_copy(
        src_ref=src,
        dst_ref=dst,
        send_sem=send_sem,
        recv_sem=recv_sem,
        device_id=device,
        device_id_type=MESH,
    )


def column_pieces(width_in):
    key = HEADS * QKH
    value = HEADS * VH
    qk, vv = key // GROUP, value // GROUP
    return (
        (0, qk, 0, qk),
        (key, qk, qk, qk),
        (2 * key, vv, 2 * qk, vv),
        (2 * key + value, vv, 2 * qk + vv, vv),
    )


def dot(left, right):
    return jnp.dot(left, right, preferred_element_type=F32)


def dot_rows(left, right):
    return lax.dot_general(left, right, (((0,), (0,)), ((), ())), preferred_element_type=F32)


def dot_back(left, right):
    return lax.dot_general(left, right, (((1,), (1,)), ((), ())), preferred_element_type=F32)


def gather_kernel(
    total,
    w_in,
    w_up,
    tok,
    cot,
    vec,
    full_in,
    own_up,
    full_tok,
    full_cot,
    full_vec,
    a2a_send,
    a2a_recv,
    own_sem,
    ring_send,
    ring_recv,
):
    at = Place(total)
    me, inner = at.group, at.inner
    peers = [at.peer(r) for r in (1, 2, 3)]
    greet(peers + [at.neighbour(0), at.neighbour(1)])
    up_width = own_up.shape[-1]
    pieces = column_pieces(w_in.shape[1])

    def exchange(relation, slot):
        other = flip(me, relation)
        if slot < 4:
            base, stride, off, width = pieces[slot]
            start = pl.multiple_of(base + other * stride, 128)
            src = w_in.at[:, pl.ds(start, width)]
            dst = full_in.at[me, inner, :, pl.ds(off, width)]
        elif slot == 4:
            src = w_up.at[:, pl.ds(pl.multiple_of(other * up_width, 128), up_width)]
            dst = own_up.at[me]
        elif slot == 5:
            src, dst = vec, full_vec.at[inner, me]
        elif slot == 6:
            src, dst = tok, full_tok.at[me]
        else:
            src, dst = cot, full_cot.at[me]
        if relation == 0:
            return pltpu.make_async_copy(src, dst, own_sem.at[slot])
        return remote(
            src,
            dst,
            a2a_send.at[relation - 1, slot],
            a2a_recv.at[relation - 1, slot],
            at.peer(relation),
        )

    for relation in (1, 0, 2, 3):
        for slot in (0, 1, 2, 3):
            exchange(relation, slot).start()
    for relation in (1, 0, 2, 3):
        for slot in (5, 4):
            exchange(relation, slot).start()

    ways = ((0, 2), (1, 3))

    def block(item, way, which):
        if item < 2:
            return full_in.at[flip(me, ways[way][item]), which]
        return full_vec.at[which]

    def hop(item, way, step):
        which = at.behind(way, step)
        place = block(item, way, which)
        return remote(
            place, place, ring_send.at[item, way, step], ring_recv.at[item, way, step], at.neighbour(way)
        )

    def active(item, way):
        return not (item == 2 and way == 1)

    def first(item, way):
        relations, slots = ((ways[way][item],), (0, 1, 2, 3)) if item < 2 else (range(4), (5,))
        for relation in relations:
            for slot in slots:
                copy = exchange(relation, slot)
                if relation == 0:
                    copy.wait()
                else:
                    copy.wait_recv()
        hop(item, way, 0).start()

    groups = ((0, 1, 2),)
    for number, group in enumerate(groups):
        for item in group:
            for way in (0, 1):
                if active(item, way):
                    first(item, way)
        if number == 0:
            for relation in (1, 0, 2, 3):
                for slot in (6, 7):
                    exchange(relation, slot).start()

        def onward(step, carry, group=group):
            for item in group:
                for way in (0, 1):
                    if active(item, way):
                        hop(item, way, step - 1).wait_recv()
                        hop(item, way, step).start()
            return carry

        lax.fori_loop(1, total - 1, onward, 0)

    for group in groups:
        for item in group:
            for way in (0, 1):
                if active(item, way):
                    hop(item, way, total - 2).wait_recv()

    def sent(step, carry):
        for group in groups:
            for item in group:
                for way in (0, 1):
                    if active(item, way):
                        hop(item, way, step).wait_send()
        return carry

    lax.fori_loop(0, total - 1, sent, 0)
    for relation in (1, 2, 3):
        for slot in range(8):
            exchange(relation, slot).wait_send()
            if slot in (4, 6, 7):
                exchange(relation, slot).wait_recv()
    exchange(0, 4).wait()
    exchange(0, 6).wait()
    exchange(0, 7).wait()


def gather_all(total, w_in, w_up, tok, cot, vec):
    width = w_in.shape[1] // GROUP
    up_width = w_up.shape[1] // GROUP
    shapes = (
        ((GROUP, total, w_in.shape[0], width), BF16),
        ((GROUP, w_up.shape[0], up_width), BF16),
        ((GROUP,) + tok.shape, BF16),
        ((GROUP,) + cot.shape, BF16),
        ((total, GROUP) + vec.shape, F32),
    )
    return pl.pallas_call(
        functools.partial(gather_kernel, total),
        out_shape=[jax.ShapeDtypeStruct(s, d) for s, d in shapes],
        in_specs=[pl.BlockSpec(memory_space=ANY)] * 5,
        out_specs=[pl.BlockSpec(memory_space=ANY)] * 5,
        scratch_shapes=[
            pltpu.SemaphoreType.DMA((3, 8)),
            pltpu.SemaphoreType.DMA((3, 8)),
            pltpu.SemaphoreType.DMA((8,)),
            pltpu.SemaphoreType.DMA((3, 2, total - 1)),
            pltpu.SemaphoreType.DMA((3, 2, total - 1)),
        ],
        compiler_params=pltpu.CompilerParams(collective_id=0, has_side_effects=True),
        name="gather_weights",
    )(w_in, w_up, tok, cot, vec)


def norm_parts(values, epsilon):
    center = values - jnp.mean(values, axis=-1, keepdims=True)
    spread = jnp.mean(center * center, axis=-1, keepdims=True)
    scale = lax.rsqrt(spread + epsilon)
    return center * scale, scale


def exchange_kernel(total, chunks, backward, part, extra, hidden_in, gain, bias, *refs):
    if backward:
        (keep, full, sums, core_in, out_x, in_x, low, own_part, sends, recvs, own_sem) = refs
    else:
        (keep, full, core_in, out_x, in_x, low, own_part, sends, recvs, own_sem) = refs
    at = Place(total)
    me = at.group
    core, across = at.peer(1), at.peer(2)
    rows = low.shape[0] // chunks
    greet([core, across])
    mine, far = me, flip(me, 2)

    def rows_of(c):
        return pl.ds(c * rows, rows)

    def copy(kind, c):
        r = rows_of(c)
        if kind == 0:
            src, dst, dev = part.at[flip(me, 3), r], core_in.at[0, r], core
        elif kind == 1:
            src, dst, dev = part.at[flip(me, 1), r], core_in.at[1, r], core
        elif kind == 2:
            src, dst, dev = out_x.at[r], in_x.at[r], across
        elif kind == 3:
            src, dst, dev = low.at[r], full.at[me, r], across
        elif kind == 4:
            src, dst, dev = low.at[r], full.at[me, r], core
        else:
            src, dst, dev = full.at[far, r], full.at[far, r], core
        return remote(src, dst, sends.at[kind, c], recvs.at[kind, c], dev)

    def load(which, c):
        r = rows_of(c)
        source = far if which == 0 else mine
        return pltpu.make_async_copy(part.at[source, r], own_part.at[which, r], own_sem.at[which, c])

    def store(c):
        r = rows_of(c)
        return pltpu.make_async_copy(low.at[r], full.at[me, r], own_sem.at[2, c])

    for c in range(chunks):
        copy(0, c).start()
        load(0, c).start()
    for c in range(chunks):
        copy(1, c).start()
        load(1, c).start()
    for c in range(chunks):
        r = rows_of(c)
        load(0, c).wait()
        copy(0, c).wait_recv()
        out_x[r, :] = (own_part[0, r, :].astype(F32) + core_in[0, r, :].astype(F32)).astype(BF16)
        copy(2, c).start()
    if backward:
        sums[...] = jnp.zeros_like(sums)
    for c in range(chunks):
        r = rows_of(c)
        load(1, c).wait()
        copy(1, c).wait_recv()
        copy(2, c).wait_recv()
        total_rows = (
            own_part[1, r, :].astype(F32) + core_in[1, r, :].astype(F32) + in_x[r, :].astype(F32)
        )
        if backward:
            normal, scale = norm_parts(hidden_in[r, :], EPSILON)
            with_gain = total_rows * gain[...]
            both = with_gain * normal
            sums[0:1, :] += jnp.sum(total_rows * normal, axis=0, keepdims=True)
            sums[1:2, :] += jnp.sum(total_rows, axis=0, keepdims=True)
            result = extra[r, :].astype(F32) + scale * (
                with_gain
                - jnp.mean(with_gain, axis=-1, keepdims=True)
                - normal * jnp.mean(both, axis=-1, keepdims=True)
            )
            keep[r, :] = result
            low[r, :] = result.astype(BF16)
        else:
            hidden = extra[r, :].astype(F32) + total_rows
            keep[r, :] = hidden
            normal, scale = norm_parts(hidden, EPSILON)
            low[r, :] = (normal * gain[...] + bias[...]).astype(BF16)
        copy(3, c).start()
        copy(4, c).start()
        store(c).start()
    for c in range(chunks):
        copy(3, c).wait_recv()
        copy(5, c).start()
    for c in range(chunks):
        copy(4, c).wait_recv()
        copy(5, c).wait_recv()
        store(c).wait()
        for kind in range(6):
            copy(kind, c).wait_send()


def exchange_rows(total, backward, part, extra, hidden, gain, bias):
    rows, width = extra.shape
    chunks = 4
    vmem = pl.BlockSpec(memory_space=pltpu.VMEM)
    shapes = [jax.ShapeDtypeStruct((rows, width), F32), jax.ShapeDtypeStruct((GROUP, rows, width), BF16)]
    specs = [vmem, pl.BlockSpec(memory_space=ANY)]
    if backward:
        shapes.append(jax.ShapeDtypeStruct((8, width), F32))
        specs.append(vmem)
    return pl.pallas_call(
        functools.partial(exchange_kernel, total, chunks, backward),
        out_shape=shapes,
        in_specs=[pl.BlockSpec(memory_space=ANY)] + [vmem] * 4,
        out_specs=specs,
        scratch_shapes=[
            pltpu.VMEM((2, rows, width), BF16),
            pltpu.VMEM((rows, width), BF16),
            pltpu.VMEM((rows, width), BF16),
            pltpu.VMEM((rows, width), BF16),
            pltpu.VMEM((2, rows, width), BF16),
            pltpu.SemaphoreType.DMA((6, chunks)),
            pltpu.SemaphoreType.DMA((6, chunks)),
            pltpu.SemaphoreType.DMA((3, chunks)),
        ],
        compiler_params=pltpu.CompilerParams(
            collective_id=2 if backward else 1, has_side_effects=True, vmem_limit_bytes=40 * MIB
        ),
        name="exchange_backward" if backward else "exchange_forward",
    )(part, extra, hidden, gain, bias)


RELATIONS = ((2, 0), (3, 1))


class Passing:
    def __init__(self, at, way, own, place, sends, recvs):
        self.at, self.way, self.own, self.place = at, way, own, place
        self.sends, self.recvs = sends, recvs

    def hop(self, step, first=False):
        which = self.at.inner if first else self.at.behind(self.way, step)
        dst = self.place(which)
        return remote(
            self.own if first else dst, dst, self.sends.at[step], self.recvs.at[step],
            self.at.neighbour(self.way),
        )

    def begin(self):
        self.hop(0, True).start()

    def onward(self, step):
        self.hop(step - 1).wait_recv()
        self.hop(step).start()

    def finish(self):
        self.hop(self.at.total - 2).wait_recv()


def wait_sent(rings, total):
    def body(step, carry):
        for ring in rings:
            ring.hop(step).wait_send()
        return carry

    lax.fori_loop(0, total - 1, body, 0)


def tick_plan(total, places):
    steps = total - 2
    cuts = [1 + (steps * n) // places for n in range(places + 1)]
    return list(zip(cuts[:-1], cuts[1:]))


def run_steps(rings, start, stop):
    def body(step, carry):
        for ring in rings:
            ring.onward(step)
        return carry

    lax.fori_loop(start, stop, body, 0)


def weight_rings(at, own_up, w_out, w_down, full_up, full_out, full_down, sends, recvs):
    me = at.group
    half = w_out.shape[0] // 2
    side = w_out.shape[1] // 2

    def halves(own, full, slot):
        return [
            Passing(
                at, way,
                own.at[pl.ds(way * half, half), pl.ds(c * side, side)],
                lambda which, way=way, c=c: full.at[which, pl.ds(way * half, half), pl.ds(c * side, side)],
                sends.at[slot + 2 * c + way], recvs.at[slot + 2 * c + way],
            )
            for c in (0, 1)
            for way in (0, 1)
        ]

    ups = []
    for order in (0, 1):
        for way in (0, 1):
            relation = RELATIONS[way][order]
            slot = 8 + 2 * order + way
            ups.append(
                Passing(
                    at, way, own_up.at[flip(me, relation)],
                    lambda which, relation=relation: full_up.at[flip(me, relation), which],
                    sends.at[slot], recvs.at[slot],
                )
            )
    return halves(w_out, full_out, 0), ups, halves(w_down, full_down, 4)


def rotated(value, cosine, sine, scale):
    half = QKH // 2
    first, second = value[:, :half], value[:, half:]
    return jnp.concatenate(
        [(first * cosine - second * sine) * scale, (second * cosine + first * sine) * scale], axis=1
    )


def forward_kernel(
    total, own_up, w_out, w_down, full_in, tok, gain_one, bias_one, gain_group, cosine, sine, growth, shrink,
    powers, ident_col, ident_row, own_tok, gain_two, bias_two,
    full_up, full_out, full_down, o_normed, o_query, o_keys, o_values, o_gate, o_mixed, o_gated, hidden, full_two,
    win, part, x, query, keys, values, gate, mixed, gated, wo, core_in, out_x, in_x, low,
    ring_send, ring_recv, own_sem, load_sem, win_sem, store_sem, row_send, row_recv, row_own,
):
    at = Place(total)
    me, inner = at.group, at.inner
    core, across = at.peer(1), at.peer(2)
    greet([core, across, at.neighbour(0), at.neighbour(1)])
    rows, width = own_tok.shape
    count = GROUP * rows
    heads = HEADS // GROUP
    outs, ups, downs = weight_rings(
        at, own_up, w_out, w_down, full_up, full_out, full_down, ring_send, ring_recv
    )
    for ring in outs:
        ring.begin()
    own_copies = [
        pltpu.make_async_copy(w_out, full_out.at[inner], own_sem.at[0]),
        pltpu.make_async_copy(w_down, full_down.at[inner], own_sem.at[1]),
        pltpu.make_async_copy(own_up, full_up.at[:, inner], own_sem.at[2]),
    ]
    for b in range(GROUP):
        pltpu.make_async_copy(tok.at[b], part.at[b], load_sem.at[b]).start()

    def win_copies(h):
        qk, vv = heads * QKH, heads * VH
        table = (
            (h * QKH, 0, QKH),
            (qk + h * QKH, QKH, QKH),
            (2 * qk + h * VH, 2 * QKH, VH),
            (2 * qk + vv + h * VH, 2 * QKH + VH, VH),
        )
        return [
            pltpu.make_async_copy(
                full_in.at[:, pl.ds(pl.multiple_of(start, 128), size)],
                win.at[h, :, pl.ds(off, size)],
                win_sem.at[h, n],
            )
            for n, (start, off, size) in enumerate(table)
        ]

    for h in range(heads):
        for copy in win_copies(h):
            copy.start()
    for copy in own_copies:
        copy.start()

    step_rows = 32

    def norm_buffer(b, carry):
        pltpu.make_async_copy(tok.at[b], part.at[b], load_sem.at[b]).wait()

        def norm_rows(n, carry):
            r = pl.multiple_of(n * step_rows, step_rows)
            normal, _ = norm_parts(part[b, pl.ds(r, step_rows), :].astype(F32), EPSILON)
            at_rows = pl.ds(pl.multiple_of(b * rows + r, step_rows), step_rows)
            x[at_rows, :] = (normal * gain_one[...] + bias_one[...]).astype(BF16)
            return carry

        lax.fori_loop(0, rows // step_rows, norm_rows, 0)
        return carry

    lax.fori_loop(0, GROUP, norm_buffer, 0)
    pltpu.make_async_copy(x, o_normed, store_sem.at[0]).start()

    tile = 512
    spots = 6
    plan = tick_plan(total, spots)
    span = [stop - start for start, stop in plan]

    def spot(h, number):
        lows = [plan[k * (spots // heads) + number][0] for k in range(heads)]
        highs = [plan[k * (spots // heads) + number][1] for k in range(heads)]
        low_step = lows[0] + h * (lows[1] - lows[0])
        high_step = highs[0] + h * (highs[1] - highs[0])
        run_steps(outs, low_step, high_step)

    def project(h, off):
        def at_tile(m, use):
            r = pl.ds(pl.multiple_of(m * tile, tile), tile)
            use(r, dot(x[r, :], win[h, :, off : off + QKH]))

        return at_tile

    def head(h, carry):
        for copy in win_copies(h):
            copy.wait()

        def rotate_tiles(m, carry):
            def put_query(r, value):
                turned = rotated(value, cosine[r, :], sine[r, :], growth[r, :])
                query[h, r, :] = (turned * QKH ** (-0.5)).astype(BF16)

            def put_keys(r, value):
                keys[h, r, :] = rotated(value, cosine[r, :], sine[r, :], shrink[r, :]).astype(BF16)

            project(h, 0)(m, put_query)
            project(h, QKH)(m, put_keys)
            return carry

        lax.fori_loop(0, count // tile, rotate_tiles, 0)
        spot(h, 0)

        def plain_tiles(m, carry):
            for c in range(VH // QKH):
                off = c * QKH

                def put_values(r, value, off=off):
                    values[h, r, off : off + QKH] = value.astype(BF16)

                def put_gate(r, value, off=off):
                    gate[h, r, off : off + QKH] = value

                project(h, 2 * QKH + off)(m, put_values)
                project(h, 2 * QKH + VH + off)(m, put_gate)
            return carry

        lax.fori_loop(0, count // tile, plain_tiles, 0)
        spot(h, 1)

        def buffer(b, carry):
            r = pl.ds(pl.multiple_of(b * rows, rows), rows)
            raw = dot_back(query[h, r, :], keys[h, r, :])
            linked = (ident_col[b] == ident_row[b]) & (ident_col[b] >= 0)
            masked = (raw * jnp.where(linked, powers[h], 0.0)).astype(BF16)
            value = dot(masked, values[h, r, :])
            mixed[h, r, :] = value
            normal, _ = norm_parts(value, GROUP_EPSILON)
            z = gate[h, r, :]
            result = z / (1.0 + jnp.exp(-z)) * (normal * gain_group[h])
            gated[r, pl.ds(pl.multiple_of(h * VH, VH), VH)] = result.astype(BF16)
            return carry

        lax.fori_loop(0, GROUP, buffer, 0)
        spot(h, 2)
        return carry

    lax.fori_loop(0, heads, head, 0)
    for ring in outs:
        ring.finish()
    for ring in ups + downs:
        ring.begin()
    stores = [
        pltpu.make_async_copy(src, dst, store_sem.at[1 + n])
        for n, (src, dst) in enumerate(
            ((query, o_query), (keys, o_keys), (values, o_values), (gate, o_gate), (mixed, o_mixed), (gated, o_gated))
        )
    ]
    for copy in stores:
        copy.start()
    own_copies[0].wait()
    block = w_out.shape[0]
    fetch = pltpu.make_async_copy(full_out, wo, load_sem.at[GROUP])
    fetch.start()
    fetch.wait()

    chunks = 4
    size = rows // chunks
    rest = ups + downs
    later = tick_plan(total, 6)

    def branch(relation):
        b = flip(me, relation)

        def column(n, carry):
            wide = 512
            c = pl.ds(pl.multiple_of(n * wide, wide), wide)
            r = pl.ds(pl.multiple_of(b * rows, rows), rows)
            acc = jnp.zeros((rows, wide), F32)
            piece = gated[r, :]
            acc = dot(piece, wo[:, :, c].reshape(total * block, wide))
            part[b, :, c] = acc.astype(BF16)
            return carry

        lax.fori_loop(0, width // 512, column, 0)

    def rows_of(c):
        return pl.ds(c * size, size)

    far = flip(me, 2)

    def copy(kind, c):
        r = rows_of(c)
        if kind == 0:
            src, dst, dev = part.at[flip(me, 3), r], core_in.at[0, r], core
        elif kind == 1:
            src, dst, dev = part.at[flip(me, 1), r], core_in.at[1, r], core
        elif kind == 2:
            src, dst, dev = out_x.at[r], in_x.at[r], across
        elif kind == 3:
            src, dst, dev = low.at[r], full_two.at[me, r], across
        elif kind == 4:
            src, dst, dev = low.at[r], full_two.at[me, r], core
        else:
            src, dst, dev = full_two.at[far, r], full_two.at[far, r], core
        return remote(src, dst, row_send.at[kind, c], row_recv.at[kind, c], dev)

    def store(c):
        r = rows_of(c)
        return pltpu.make_async_copy(low.at[r], full_two.at[me, r], row_own.at[c])

    branch(3)
    for c in range(chunks):
        copy(0, c).start()
    branch(2)
    for c in range(chunks):
        r = rows_of(c)
        copy(0, c).wait_recv()
        out_x[r, :] = (part[far, r, :].astype(F32) + core_in[0, r, :].astype(F32)).astype(BF16)
        copy(2, c).start()
    branch(1)
    for c in range(chunks):
        copy(1, c).start()
    branch(0)
    run_steps(rest, *later[0])
    for c in range(chunks):
        r = rows_of(c)
        copy(1, c).wait_recv()
        copy(2, c).wait_recv()

        def finish_rows(n, carry, c=c):
            s = pl.ds(pl.multiple_of(c * size + n * step_rows, step_rows), step_rows)
            value = own_tok[s, :].astype(F32) + (
                part[me, s, :].astype(F32) + core_in[1, s, :].astype(F32) + in_x[s, :].astype(F32)
            )
            hidden[s, :] = value
            normal, _ = norm_parts(value, EPSILON)
            low[s, :] = (normal * gain_two[...] + bias_two[...]).astype(BF16)
            return carry

        lax.fori_loop(0, size // step_rows, finish_rows, 0)
        copy(3, c).start()
        copy(4, c).start()
        store(c).start()
        if c % 2:
            run_steps(rest, *later[1 + c // 2])
    for c in range(chunks):
        copy(3, c).wait_recv()
        copy(5, c).start()
        if c % 2:
            run_steps(rest, *later[3 + c // 2])
    for c in range(chunks):
        copy(4, c).wait_recv()
        copy(5, c).wait_recv()
        store(c).wait()
        for kind in range(6):
            copy(kind, c).wait_send()
    run_steps(rest, *later[5])
    for ring in rest:
        ring.finish()
    wait_sent(outs + rest, total)
    own_copies[1].wait()
    own_copies[2].wait()
    pltpu.make_async_copy(x, o_normed, store_sem.at[0]).wait()
    for c in stores:
        c.wait()


def forward(
    total, own_up, w_out, w_down, full_in, tok, gain_one, bias_one, gain_group, tables, powers, ident_col, ident_row,
    own_tok, gain_two, bias_two,
):
    rows, width = own_tok.shape
    count = GROUP * rows
    heads = HEADS // GROUP
    vmem, hbm = pl.BlockSpec(memory_space=pltpu.VMEM), pl.BlockSpec(memory_space=ANY)
    dma = pltpu.SemaphoreType.DMA
    kept = (
        ((count, width), BF16),
        ((heads, count, QKH), BF16),
        ((heads, count, QKH), BF16),
        ((heads, count, VH), BF16),
        ((heads, count, VH), F32),
        ((heads, count, VH), F32),
        ((count, heads * VH), BF16),
    )
    shapes = (
        ((GROUP, total) + own_up.shape[1:], BF16),
        ((total,) + w_out.shape, BF16),
        ((total,) + w_down.shape, BF16),
        *kept,
        ((rows, width), F32),
        ((GROUP, rows, width), BF16),
    )
    return pl.pallas_call(
        functools.partial(forward_kernel, total),
        out_shape=[jax.ShapeDtypeStruct(s, d) for s, d in shapes],
        in_specs=[hbm] * 5 + [vmem] * 13,
        out_specs=[hbm] * 10 + [vmem, hbm],
        scratch_shapes=[
            pltpu.VMEM((heads, width, 2 * QKH + 2 * VH), BF16),
            pltpu.VMEM((GROUP, rows, width), BF16),
            *[pltpu.VMEM(s, d) for s, d in kept],
            pltpu.VMEM((total,) + w_out.shape, BF16),
            pltpu.VMEM((2, rows, width), BF16),
            pltpu.VMEM((rows, width), BF16),
            pltpu.VMEM((rows, width), BF16),
            pltpu.VMEM((rows, width), BF16),
            dma((12, total - 1)), dma((12, total - 1)), dma((3,)), dma((GROUP + 1,)), dma((heads, 4)),
            dma((7,)), dma((6, 4)), dma((6, 4)), dma((4,)),
        ],
        compiler_params=pltpu.CompilerParams(
            collective_id=1, has_side_effects=True, vmem_limit_bytes=63 * MIB
        ),
        name="forward_retention",
    )(
        own_up, w_out, w_down, full_in, tok, gain_one, bias_one, gain_group, *tables, powers, ident_col,
        ident_row, own_tok, gain_two, bias_two,
    )


class Ring:
    def __init__(self, at, way, source, local, arrived, loads, sends, recvs):
        self.at, self.way, self.source = at, way, source
        self.local, self.arrived = local, arrived
        self.loads, self.sends, self.recvs = loads, sends, recvs

    def load(self, which):
        return pltpu.make_async_copy(self.source(which), self.local.at[which], self.loads.at[which])

    def hop(self, step, first=False):
        src = self.local.at[self.at.behind(self.way, 1)] if first else self.arrived.at[step - 1]
        return remote(
            src, self.arrived.at[step], self.sends.at[step], self.recvs.at[step], self.at.neighbour(self.way)
        )

    def begin(self):
        self.load(self.at.behind(self.way, 1)).wait()
        self.hop(0, True).start()

    def onward(self, step):
        which = self.at.behind(self.way, step + 1)
        self.load(which).wait()
        self.hop(step - 1, True).wait_recv()
        self.arrived[step - 1] = (
            self.arrived[step - 1].astype(F32) + self.local[which].astype(F32)
        ).astype(BF16)
        self.hop(step).start()

    def finish(self):
        last = self.at.total - 2
        self.load(self.at.inner).wait()
        self.hop(last, True).wait_recv()
        return self.arrived[last].astype(F32) + self.local[self.at.inner].astype(F32)

    def sent(self, step):
        self.hop(step, True).wait_send()


def run_rings(rings, total, between=()):
    at = rings[0].at
    for ring in rings:
        ring.load(at.behind(ring.way, 1)).start()

    def loads(step, carry):
        for ring in rings:
            ring.load(at.behind(ring.way, step + 1)).start()
        return carry

    lax.fori_loop(1, total, loads, 0)
    for ring in rings:
        ring.begin()
    marks = dict(between)
    last = 1
    for stop in sorted(marks) + [total - 1]:

        def body(step, carry):
            for ring in rings:
                ring.onward(step)
            return carry

        lax.fori_loop(last, stop, body, 0)
        last = stop
        if stop in marks:
            marks[stop]()


def close_rings(rings, total):
    for ring in rings:
        ring.sent(0)

    def body(step, carry):
        for ring in rings:
            ring.sent(step)
        return carry

    lax.fori_loop(1, total - 1, body, 0)


def reduce_in_kernel(
    total, g_in, part, up, o_in, o_part, o_up, up_in, local, arrived, stage, landed,
    core_in, own_part, out_x, in_x, loads, ring_send, ring_recv, a2a_send, a2a_recv,
    row_send, row_recv, row_own, up_send, up_recv,
):
    at = Place(total)
    me = at.group
    greet([at.peer(r) for r in (1, 2, 3)] + [at.neighbour(0), at.neighbour(1)])
    rings, relations = [], []
    for order in (0, 1):
        for way in (0, 1):
            relation = RELATIONS[way][order]
            slot = 2 * way + order
            rings.append(
                Ring(
                    at, way,
                    lambda which, relation=relation: g_in.at[flip(me, relation), which],
                    local.at[slot], arrived.at[slot], loads.at[slot], ring_send.at[slot], ring_recv.at[slot],
                )
            )
            relations.append(relation)

    count = part.shape[0]
    up_width = up.shape[-1]

    def up_copy(relation):
        return remote(
            up.at[flip(me, relation)], up_in.at[relation - 1],
            up_send.at[relation - 1], up_recv.at[relation - 1], at.peer(relation),
        )

    def row_copy(kind, n):
        if kind == 0:
            src, dst, dev = part.at[n, flip(me, 3)], core_in.at[n, 0], at.peer(1)
        elif kind == 1:
            src, dst, dev = part.at[n, flip(me, 1)], core_in.at[n, 1], at.peer(1)
        else:
            src, dst, dev = out_x.at[n], in_x.at[n], at.peer(2)
        return remote(src, dst, row_send.at[n, kind], row_recv.at[n, kind], dev)

    def row_load(n, which):
        return pltpu.make_async_copy(
            part.at[n, flip(me, 2) if which == 0 else me], own_part.at[n, which], row_own.at[n, which]
        )

    for n in range(count):
        for kind in (0, 1):
            row_copy(kind, n).start()
            row_load(n, kind).start()
    for relation in (1, 2, 3):
        up_copy(relation).start()

    def send_rows():
        for n in range(count):
            row_load(n, 0).wait()
            row_copy(0, n).wait_recv()
            out_x[n] = (own_part[n, 0].astype(F32) + core_in[n, 0].astype(F32)).astype(BF16)
            row_copy(2, n).start()

    def take_rows():
        for n in range(count):
            row_load(n, 1).wait()
            row_copy(1, n).wait_recv()
            row_copy(2, n).wait_recv()
            o_part[n] = (
                own_part[n, 1].astype(F32) + core_in[n, 1].astype(F32) + in_x[n].astype(F32)
            )
        for relation in range(4):
            if relation:
                up_copy(relation).wait_recv()
            value = up_in[relation - 1] if relation else up[me]
            start = pl.multiple_of(flip(me, relation) * up_width, 128)
            o_up[:, pl.ds(start, up_width)] = value.astype(F32)
        for relation in (1, 2, 3):
            up_copy(relation).wait_send()

    run_rings(rings, total, ((2, send_rows), (total - 2, take_rows)))
    pieces = column_pieces(o_in.shape[1])

    def place(other, value):
        for base, stride, off, width in pieces:
            start = pl.multiple_of(base + other * stride, 128)
            o_in[:, pl.ds(start, width)] = value[:, off : off + width]

    def across(relation):
        return remote(
            stage.at[relation - 1], landed.at[relation - 1],
            a2a_send.at[relation - 1], a2a_recv.at[relation - 1], at.peer(relation),
        )

    for ring, relation in zip(rings, relations):
        value = ring.finish()
        if relation == 0:
            place(me, value)
        else:
            stage[relation - 1] = value.astype(BF16)
            across(relation).start()
    for relation in (1, 2, 3):
        across(relation).wait_recv()
        place(flip(me, relation), landed[relation - 1].astype(F32))
    for relation in (1, 2, 3):
        across(relation).wait_send()
    close_rings(rings, total)
    for n in range(count):
        for kind in (0, 1, 2):
            row_copy(kind, n).wait_send()


def reduce_in(total, g_in, part, up):
    rows, width = g_in.shape[2:]
    count, _, tokens, features = part.shape
    vmem = pl.BlockSpec(memory_space=pltpu.VMEM)
    dma = pltpu.SemaphoreType.DMA
    return pl.pallas_call(
        functools.partial(reduce_in_kernel, total),
        out_shape=[
            jax.ShapeDtypeStruct((rows, width * GROUP), F32),
            jax.ShapeDtypeStruct((count, tokens, features), F32),
            jax.ShapeDtypeStruct((up.shape[1], up.shape[2] * GROUP), F32),
        ],
        in_specs=[pl.BlockSpec(memory_space=ANY)] * 2 + [vmem],
        out_specs=[vmem] * 3,
        scratch_shapes=[
            pltpu.VMEM((3,) + up.shape[1:], BF16),
            pltpu.VMEM((4, total, rows, width), BF16),
            pltpu.VMEM((4, total - 1, rows, width), BF16),
            pltpu.VMEM((3, rows, width), BF16),
            pltpu.VMEM((3, rows, width), BF16),
            pltpu.VMEM((count, 2, tokens, features), BF16),
            pltpu.VMEM((count, 2, tokens, features), BF16),
            pltpu.VMEM((count, tokens, features), BF16),
            pltpu.VMEM((count, tokens, features), BF16),
            dma((4, total)), dma((4, total - 1)), dma((4, total - 1)),
            dma((3,)), dma((3,)),
            dma((count, 3)), dma((count, 3)), dma((count, 2)), dma((3,)), dma((3,)),
        ],
        compiler_params=pltpu.CompilerParams(
            collective_id=4, has_side_effects=True, vmem_limit_bytes=60 * MIB
        ),
        name="reduce_in",
    )(g_in, part, up)


def reduce_vectors_kernel(total, vec, out, landed, mid, gathered, sends, recvs, far_send, far_recv):
    at = Place(total)
    me, inner = at.group, at.inner
    others = [(me, lax.rem(inner + n, total)) for n in range(1, total)]
    greet([at.peer(r) for r in (1, 2, 3)] + others)

    def near(relation):
        return remote(
            vec.at[flip(me, relation)], landed.at[relation - 1],
            sends.at[relation - 1], recvs.at[relation - 1], at.peer(relation),
        )

    for relation in (1, 2, 3):
        near(relation).start()
    for relation in (1, 2, 3):
        near(relation).wait_recv()
    mid[...] = vec[me] + landed[0] + landed[1] + landed[2]

    def far(n):
        target = lax.rem(inner + n, total)
        return remote(mid.at[target], gathered.at[n - 1], far_send.at[n - 1], far_recv.at[n - 1], (me, target))

    for n in range(1, total):
        far(n).start()
    for n in range(1, total):
        far(n).wait_recv()
    out[...] = mid[inner] + jnp.sum(gathered[...], axis=0)
    for n in range(1, total):
        far(n).wait_send()
    for relation in (1, 2, 3):
        near(relation).wait_send()


def reduce_vectors(total, vec):
    block = vec.shape[2:]
    vmem = pl.BlockSpec(memory_space=pltpu.VMEM)
    dma = pltpu.SemaphoreType.DMA
    return pl.pallas_call(
        functools.partial(reduce_vectors_kernel, total),
        out_shape=jax.ShapeDtypeStruct(block, F32),
        in_specs=[vmem],
        out_specs=vmem,
        scratch_shapes=[
            pltpu.VMEM((3, total) + block, F32),
            pltpu.VMEM((total,) + block, F32),
            pltpu.VMEM((total - 1,) + block, F32),
            dma((3,)), dma((3,)), dma((total - 1,)), dma((total - 1,)),
        ],
        compiler_params=pltpu.CompilerParams(collective_id=5, has_side_effects=True),
        name="reduce_vectors",
    )(vec)


def layout(seq_lens, seq_owner, seq_offset, device_id, buffer_len):
    positions = jnp.arange(buffer_len, dtype=jnp.int32)[:, None]
    inside = (
        (seq_owner[None, :] == device_id)
        & (seq_lens[None, :] > 0)
        & (positions >= seq_offset[None, :])
        & (positions < seq_offset[None, :] + seq_lens[None, :])
    )
    number = jnp.arange(seq_lens.shape[0], dtype=jnp.int32)[None, :] + 1
    seq_ident = jnp.sum(jnp.where(inside, number, 0), axis=1) - 1
    starts = jnp.sum(jnp.where(inside, seq_offset[None, :], 0), axis=1)
    places = jnp.where(seq_ident >= 0, positions[:, 0] - starts, 0)
    return seq_ident, places


def rotation(places):
    half_size = QKH // 2
    pair_index = jnp.arange(half_size, dtype=F32) / half_size
    inverse_freq = 10000.0 ** (-pair_index)
    zeta_base = (pair_index + 0.4) / 1.4
    offsets = places.astype(F32)[..., None]
    angles = offsets * inverse_freq
    growth = zeta_base ** (offsets / 512.0)
    return jnp.cos(angles), jnp.sin(angles), growth


def rotate_xpos(vectors, cosine, sine, scale):
    half = QKH // 2
    first, second = vectors[..., :half], vectors[..., half:]
    cosine, sine, scale = cosine[..., None, :], sine[..., None, :], scale[..., None, :]
    return jnp.concatenate(
        [(first * cosine - second * sine) * scale, (second * cosine + first * sine) * scale], axis=-1
    )


def rotate_back(vectors, cosine, sine, scale):
    return rotate_xpos(vectors, cosine, -sine, scale)


def decay_tables(ident, heads):
    positions = jnp.arange(ident.shape[-1], dtype=jnp.int32)
    distance = positions[:, None] - positions[None, :]
    linked = (distance >= 0) & (ident[:, :, None] == ident[:, None, :]) & (ident[:, :, None] >= 0)
    rates = jnp.log1p(-(2.0 ** (-5.0 - heads.astype(F32))))
    powers = jnp.maximum(distance, 0).astype(F32)
    return jnp.where(linked[:, None], jnp.exp(rates[:, None, None] * powers[None])[None], 0.0)


def mean(values):
    return jnp.mean(values, axis=-1, keepdims=True)


def local(
    total,
    tokens,
    cotangent,
    w_in,
    w_out,
    w_up,
    w_down,
    ln1_gain,
    ln1_bias,
    group_gain,
    ln2_gain,
    ln2_bias,
    seq_lens,
    seq_owner,
    seq_offset,
):
    rows, width = tokens.shape
    heads = HEADS // GROUP
    qk, vv = heads * QKH, heads * VH
    me, inner = lax.axis_index("dp"), lax.axis_index("fsdp")
    small, large = ln1_gain.shape[0], group_gain.shape[0]

    pack = jnp.concatenate([ln1_gain, ln1_bias, ln2_gain, ln2_bias, group_gain]).astype(F32)
    pack = jnp.pad(pack, (0, 1024 - pack.shape[0])).reshape(8, 128)
    full_in, own_up, tok, cot, vec = gather_all(total, w_in, w_up, tokens, cotangent, pack)
    full_in = full_in.reshape(width, -1)
    vec = vec.reshape(total, GROUP, 1024)

    def vector(number):
        part = vec[:, :, number * small : (number + 1) * small]
        return jnp.swapaxes(part, 0, 1).reshape(1, width)

    gain_one, bias_one, gain_two, bias_two = (vector(n) for n in range(4))
    gain_group = lax.dynamic_index_in_dim(vec, me, 1, keepdims=False)[:, 4 * small : 4 * small + large]
    gain_group = gain_group.reshape(heads, 1, VH)

    devices = jnp.arange(GROUP, dtype=jnp.int32) * total + inner
    ident, places = jax.vmap(lambda d: layout(seq_lens, seq_owner, seq_offset, d, rows))(devices)
    valid = (ident >= 0).astype(F32)[..., None]
    own_valid = lax.dynamic_index_in_dim(valid, me, 0, keepdims=False)
    count = GROUP * rows

    tables = rotation(places.reshape(count))
    tables = (*tables, 1.0 / tables[2])
    distance = jnp.arange(rows)[:, None] - jnp.arange(rows)[None, :]
    rates = jnp.log1p(-(2.0 ** (-5.0 - (me * heads + jnp.arange(heads)).astype(F32))))
    powers = jnp.exp(rates[:, None, None] * jnp.maximum(distance, 0).astype(F32)[None])
    powers = jnp.where(distance[None] >= 0, powers, 0.0)
    (
        full_up, full_out, full_down, normed, query, keys, values, gate, mixed, gated, hidden, two,
    ) = forward(
        total, own_up, w_out, w_down, full_in, tok, gain_one, bias_one, gain_group, tables, powers,
        ident[:, :, None], ident[:, None, :], tokens, gain_two, bias_two,
    )
    full_up = full_up.reshape(width, -1)
    full_out = full_out.reshape(-1, width)
    full_down = full_down.reshape(-1, width)
    two = two.reshape(count, width)
    upper = dot(two, full_up)
    cdf = 0.5 * (1.0 + lax.erf(upper * (0.5**0.5)))
    active = (upper * cdf).astype(BF16)
    down = dot(active, full_down).astype(BF16).reshape(GROUP, rows, width)

    seed = (cot.astype(F32) * valid).astype(BF16)
    own_seed = (cotangent.astype(F32) * own_valid).astype(BF16)
    seed = seed.reshape(count, width)
    slope = cdf + upper * jnp.exp(-0.5 * upper * upper) * (2.0 * jnp.pi) ** -0.5
    d_upper = (dot_back(seed, full_down) * slope).astype(BF16)
    d_two = dot_back(d_upper, full_up).astype(BF16).reshape(GROUP, rows, width)
    d_hidden, d_branch, sums_two = exchange_rows(
        total, True, d_two, own_seed, hidden, gain_two, bias_two
    )
    d_branch = d_branch.reshape(count, width)
    def summed_over(value, dim):
        return lax.psum_scatter(value, "fsdp", scatter_dimension=dim, tiled=True)

    grad_down = summed_over(dot_rows(active, seed).astype(BF16), 0).astype(F32)
    g_up = summed_over(dot_rows(two, d_upper).astype(BF16).reshape(GROUP, total * small, -1), 1)
    grad_out = summed_over(dot_rows(gated, d_branch).astype(BF16), 0).astype(F32)

    split = (heads, GROUP, rows)
    query, keys, values = (v.reshape(split + v.shape[2:]) for v in (query, keys, values))
    gate, mixed = gate.reshape(split + (VH,)), mixed.reshape(split + (VH,))
    gains = gain_group[:, None]
    linked = (ident[:, :, None] == ident[:, None, :]) & (ident[:, :, None] >= 0)
    decay = jnp.where(linked[None], powers[:, None], 0.0)
    masked = (jnp.einsum("hbtd,hbsd->hbts", query, keys, preferred_element_type=F32) * decay).astype(BF16)
    d_gated = jnp.stack(
        [dot_back(d_branch, full_out[h * VH : (h + 1) * VH]) for h in range(heads)]
    ).reshape(split + (VH,))
    group_normal, group_scale = norm_parts(mixed, GROUP_EPSILON)
    sigmoid = jax.nn.sigmoid(gate)
    silu = gate * sigmoid
    d_silu = d_gated * (group_normal * gains)
    d_gate = d_silu * (sigmoid + silu * (1.0 - sigmoid))
    d_scaled = d_gated * silu
    d_group = jnp.sum(d_scaled * group_normal, axis=(1, 2))
    d_normal = d_scaled * gains
    d_mixed = group_scale * (
        d_normal - mean(d_normal) - group_normal * mean(d_normal * group_normal)
    )
    d_mixed = d_mixed.astype(BF16)
    d_values = jnp.einsum("hbts,hbtv->hbsv", masked, d_mixed, preferred_element_type=F32)
    d_masked = jnp.einsum("hbtv,hbsv->hbts", d_mixed, values, preferred_element_type=F32)
    d_raw = (d_masked * decay).astype(BF16)
    d_query = jnp.einsum("hbts,hbsd->hbtd", d_raw, keys, preferred_element_type=F32)
    d_keys = jnp.einsum("hbts,hbtd->hbsd", d_raw, query, preferred_element_type=F32)
    cosine, sine, growth, shrink = (t.reshape(GROUP, rows, -1) for t in tables)

    def back(value, scale):
        half = QKH // 2
        first, second = value[..., :half], value[..., half:]
        return jnp.concatenate(
            [(first * cosine + second * sine) * scale, (second * cosine - first * sine) * scale], axis=-1
        )

    d_query = back(d_query * QKH ** (-0.5), growth).astype(BF16)
    d_keys = back(d_keys, shrink).astype(BF16)
    parts = [
        value[h].reshape(count, -1).astype(BF16)
        for value in (d_query, d_keys, d_values, d_gate)
        for h in range(heads)
    ]
    d_project = jnp.concatenate(parts, axis=1)
    d_normed = dot_back(d_project, full_in).astype(BF16).reshape(GROUP, rows, width)
    g_in = dot_rows(normed, d_project).astype(BF16).reshape(GROUP, total, small, -1)
    grad_in, own_rows, grad_up = reduce_in(total, g_in, jnp.stack([d_normed, down]), g_up)
    output = ((hidden + own_rows[1]) * own_valid).astype(BF16)
    e_one = own_rows[0]
    normal_one, scale_one = norm_parts(tokens.astype(F32), EPSILON)
    with_gain = e_one * gain_one
    d_tokens = d_hidden + scale_one * (
        with_gain - mean(with_gain) - normal_one * mean(with_gain * normal_one)
    )
    d_tokens = d_tokens.astype(BF16)

    sums = jnp.stack(
        [jnp.sum(e_one * normal_one, axis=0), jnp.sum(e_one, axis=0), sums_two[0], sums_two[1]]
    )
    sums = sums.reshape(4, GROUP, total, small).transpose(1, 2, 0, 3).reshape(GROUP, total, 4 * small)
    mine = (jnp.arange(GROUP) == me).astype(F32)[:, None, None]
    sums = jnp.concatenate([sums, mine * d_group.reshape(1, total, large)], axis=2)
    sums = jnp.pad(sums, ((0, 0), (0, 0), (0, 1024 - sums.shape[2]))).reshape(GROUP, total, 8, 128)
    summed = reduce_vectors(total, sums).reshape(1024)
    grads = [summed[n * small : (n + 1) * small] for n in range(4)]
    grad_group = summed[4 * small : 4 * small + large]
    return (
        output,
        d_tokens,
        grad_in,
        grad_out,
        grad_up,
        grad_down,
        grads[0],
        grads[1],
        grad_group,
        grads[2],
        grads[3],
    )


def solution(mesh):
    flat = ("dp", "fsdp")
    matrix, vector = P(flat, None), P(flat)
    return jax.shard_map(
        functools.partial(local, mesh.shape["fsdp"]),
        mesh=mesh,
        in_specs=(matrix,) * 6 + (vector,) * 5 + (P(),) * 3,
        out_specs=(matrix,) * 6 + (vector,) * 5,
        check_vma=False,
    )
```

```python
import functools

import jax
import jax.numpy as jnp
from jax import lax
from jax.experimental import pallas as pl
from jax.experimental.pallas import tpu as pltpu
from jax.sharding import PartitionSpec as P

HEADS = 8
QKH = 256
VH = 512
EPSILON = 1e-05
GROUP_EPSILON = 0.1
GROUP = 4
MESH = pl.DeviceIdType.MESH
ANY = pl.ANY
BF16 = jnp.bfloat16
F32 = jnp.float32
MIB = 1 << 20


def ring_place(index, total):
    half = index // 2
    return jnp.where(index % 2 == 0, half, total - 1 - half)


def ring_index(place, total):
    place = lax.rem(place + 2 * total, total)
    return jnp.where(place < total // 2, 2 * place, 2 * (total - 1 - place) + 1)


def flip(group_index, relation):
    low, high = group_index % 2, group_index // 2
    if relation % 2:
        low = 1 - low
    if relation // 2:
        high = 1 - high
    return 2 * high + low


class Place:
    def __init__(self, total):
        self.total = total
        self.group = lax.axis_index("dp")
        self.inner = lax.axis_index("fsdp")
        self.place = ring_place(self.inner, total)
        self.next = (
            ring_index(self.place + 1, total),
            ring_index(self.place - 1, total),
        )

    def peer(self, relation):
        return (flip(self.group, relation), self.inner)

    def neighbour(self, way):
        return (self.group, self.next[way])

    def behind(self, way, steps):
        return ring_index(self.place - steps if way == 0 else self.place + steps, self.total)


def greet(devices):
    barrier = pltpu.get_barrier_semaphore()
    for device in devices:
        pl.semaphore_signal(barrier, inc=1, device_id=device, device_id_type=MESH)
    pl.semaphore_wait(barrier, len(devices))


def remote(src, dst, send_sem, recv_sem, device):
    return pltpu.make_async_remote_copy(
        src_ref=src,
        dst_ref=dst,
        send_sem=send_sem,
        recv_sem=recv_sem,
        device_id=device,
        device_id_type=MESH,
    )


def column_pieces(width_in):
    key = HEADS * QKH
    value = HEADS * VH
    qk, vv = key // GROUP, value // GROUP
    return (
        (0, qk, 0, qk),
        (key, qk, qk, qk),
        (2 * key, vv, 2 * qk, vv),
        (2 * key + value, vv, 2 * qk + vv, vv),
    )


def dot(left, right):
    return jnp.dot(left, right, preferred_element_type=F32)


def dot_rows(left, right):
    return lax.dot_general(left, right, (((0,), (0,)), ((), ())), preferred_element_type=F32)


def dot_back(left, right):
    return lax.dot_general(left, right, (((1,), (1,)), ((), ())), preferred_element_type=F32)


def gather_kernel(
    total,
    w_in,
    w_up,
    tok,
    cot,
    vec,
    full_in,
    own_up,
    full_tok,
    full_cot,
    full_vec,
    a2a_send,
    a2a_recv,
    own_sem,
    ring_send,
    ring_recv,
):
    at = Place(total)
    me, inner = at.group, at.inner
    peers = [at.peer(r) for r in (1, 2, 3)]
    greet(peers + [at.neighbour(0), at.neighbour(1)])
    up_width = own_up.shape[-1]
    pieces = column_pieces(w_in.shape[1])

    def exchange(relation, slot):
        other = flip(me, relation)
        if slot < 4:
            base, stride, off, width = pieces[slot]
            start = pl.multiple_of(base + other * stride, 128)
            src = w_in.at[:, pl.ds(start, width)]
            dst = full_in.at[me, inner, :, pl.ds(off, width)]
        elif slot == 4:
            src = w_up.at[:, pl.ds(pl.multiple_of(other * up_width, 128), up_width)]
            dst = own_up.at[me]
        elif slot == 5:
            src, dst = vec, full_vec.at[inner, me]
        elif slot == 6:
            src, dst = tok, full_tok.at[me]
        else:
            src, dst = cot, full_cot.at[me]
        if relation == 0:
            return pltpu.make_async_copy(src, dst, own_sem.at[slot])
        return remote(
            src,
            dst,
            a2a_send.at[relation - 1, slot],
            a2a_recv.at[relation - 1, slot],
            at.peer(relation),
        )

    for relation in (1, 0, 2, 3):
        for slot in (0, 1, 2, 3):
            exchange(relation, slot).start()
    for relation in (1, 0, 2, 3):
        for slot in (5, 4):
            exchange(relation, slot).start()

    ways = ((0, 2), (1, 3))

    def block(item, way, which):
        if item < 2:
            return full_in.at[flip(me, ways[way][item]), which]
        return full_vec.at[which]

    def hop(item, way, step):
        which = at.behind(way, step)
        place = block(item, way, which)
        return remote(
            place, place, ring_send.at[item, way, step], ring_recv.at[item, way, step], at.neighbour(way)
        )

    def active(item, way):
        return not (item == 2 and way == 1)

    def first(item, way):
        relations, slots = ((ways[way][item],), (0, 1, 2, 3)) if item < 2 else (range(4), (5,))
        for relation in relations:
            for slot in slots:
                copy = exchange(relation, slot)
                if relation == 0:
                    copy.wait()
                else:
                    copy.wait_recv()
        hop(item, way, 0).start()

    groups = ((0, 1, 2),)
    for number, group in enumerate(groups):
        for item in group:
            for way in (0, 1):
                if active(item, way):
                    first(item, way)
        if number == 0:
            for relation in (1, 0, 2, 3):
                for slot in (6, 7):
                    exchange(relation, slot).start()

        def onward(step, carry, group=group):
            for item in group:
                for way in (0, 1):
                    if active(item, way):
                        hop(item, way, step - 1).wait_recv()
                        hop(item, way, step).start()
            return carry

        lax.fori_loop(1, total - 1, onward, 0)

    for group in groups:
        for item in group:
            for way in (0, 1):
                if active(item, way):
                    hop(item, way, total - 2).wait_recv()

    def sent(step, carry):
        for group in groups:
            for item in group:
                for way in (0, 1):
                    if active(item, way):
                        hop(item, way, step).wait_send()
        return carry

    lax.fori_loop(0, total - 1, sent, 0)
    for relation in (1, 2, 3):
        for slot in range(8):
            exchange(relation, slot).wait_send()
            if slot in (4, 6, 7):
                exchange(relation, slot).wait_recv()
    exchange(0, 4).wait()
    exchange(0, 6).wait()
    exchange(0, 7).wait()


def gather_all(total, w_in, w_up, tok, cot, vec):
    width = w_in.shape[1] // GROUP
    up_width = w_up.shape[1] // GROUP
    shapes = (
        ((GROUP, total, w_in.shape[0], width), BF16),
        ((GROUP, w_up.shape[0], up_width), BF16),
        ((GROUP,) + tok.shape, BF16),
        ((GROUP,) + cot.shape, BF16),
        ((total, GROUP) + vec.shape, F32),
    )
    return pl.pallas_call(
        functools.partial(gather_kernel, total),
        out_shape=[jax.ShapeDtypeStruct(s, d) for s, d in shapes],
        in_specs=[pl.BlockSpec(memory_space=ANY)] * 5,
        out_specs=[pl.BlockSpec(memory_space=ANY)] * 5,
        scratch_shapes=[
            pltpu.SemaphoreType.DMA((3, 8)),
            pltpu.SemaphoreType.DMA((3, 8)),
            pltpu.SemaphoreType.DMA((8,)),
            pltpu.SemaphoreType.DMA((3, 2, total - 1)),
            pltpu.SemaphoreType.DMA((3, 2, total - 1)),
        ],
        compiler_params=pltpu.CompilerParams(collective_id=0, has_side_effects=True),
        name="gather_weights",
    )(w_in, w_up, tok, cot, vec)


def norm_parts(values, epsilon):
    center = values - jnp.mean(values, axis=-1, keepdims=True)
    spread = jnp.mean(center * center, axis=-1, keepdims=True)
    scale = lax.rsqrt(spread + epsilon)
    return center * scale, scale


RELATIONS = ((2, 0), (3, 1))


class Passing:
    def __init__(self, at, way, own, place, sends, recvs):
        self.at, self.way, self.own, self.place = at, way, own, place
        self.sends, self.recvs = sends, recvs

    def hop(self, step, first=False):
        which = self.at.inner if first else self.at.behind(self.way, step)
        dst = self.place(which)
        return remote(
            self.own if first else dst, dst, self.sends.at[step], self.recvs.at[step],
            self.at.neighbour(self.way),
        )

    def begin(self):
        self.hop(0, True).start()

    def onward(self, step):
        self.hop(step - 1).wait_recv()
        self.hop(step).start()

    def finish(self):
        self.hop(self.at.total - 2).wait_recv()


def wait_sent(rings, total):
    def body(step, carry):
        for ring in rings:
            ring.hop(step).wait_send()
        return carry

    lax.fori_loop(0, total - 1, body, 0)


def tick_plan(total, places):
    steps = total - 2
    cuts = [1 + (steps * n) // places for n in range(places + 1)]
    return list(zip(cuts[:-1], cuts[1:]))


def run_steps(rings, start, stop):
    def body(step, carry):
        for ring in rings:
            ring.onward(step)
        return carry

    lax.fori_loop(start, stop, body, 0)


def weight_rings(at, own_up, w_out, w_down, full_up, full_out, full_down, sends, recvs):
    me = at.group
    half = w_out.shape[0] // 2
    side = w_out.shape[1] // 2

    def halves(own, full, slot):
        return [
            Passing(
                at, way,
                own.at[pl.ds(way * half, half), pl.ds(c * side, side)],
                lambda which, way=way, c=c: full.at[which, pl.ds(way * half, half), pl.ds(c * side, side)],
                sends.at[slot + 2 * c + way], recvs.at[slot + 2 * c + way],
            )
            for c in (0, 1)
            for way in (0, 1)
        ]

    ups = []
    for order in (0, 1):
        for way in (0, 1):
            relation = RELATIONS[way][order]
            slot = 8 + 2 * order + way
            ups.append(
                Passing(
                    at, way, own_up.at[flip(me, relation)],
                    lambda which, relation=relation: full_up.at[flip(me, relation), which],
                    sends.at[slot], recvs.at[slot],
                )
            )
    return halves(w_out, full_out, 0), ups, halves(w_down, full_down, 4)


def rotated(value, cosine, sine, scale):
    half = QKH // 2
    first, second = value[:, :half], value[:, half:]
    return jnp.concatenate(
        [(first * cosine - second * sine) * scale, (second * cosine + first * sine) * scale], axis=1
    )


def forward_kernel(
    total, own_up, w_out, w_down, full_in, tok, gain_one, bias_one, gain_group, cosine, sine, growth, shrink,
    powers, ident_col, ident_row, own_tok, gain_two, bias_two,
    full_up, full_out, full_down, o_turned, o_query, o_keys, o_values, o_gate, o_mixed, o_gated, hidden, full_two,
    win, part, x, query, keys, values, gate, mixed, gated, wo, core_in, out_x, in_x, low,
    ring_send, ring_recv, own_sem, load_sem, win_sem, store_sem, row_send, row_recv, row_own,
):
    at = Place(total)
    me, inner = at.group, at.inner
    core, across = at.peer(1), at.peer(2)
    greet([core, across, at.neighbour(0), at.neighbour(1)])
    rows, width = own_tok.shape
    count = GROUP * rows
    heads = HEADS // GROUP
    outs, ups, downs = weight_rings(
        at, own_up, w_out, w_down, full_up, full_out, full_down, ring_send, ring_recv
    )
    for ring in outs:
        ring.begin()
    own_copies = [
        pltpu.make_async_copy(w_out, full_out.at[inner], own_sem.at[0]),
        pltpu.make_async_copy(w_down, full_down.at[inner], own_sem.at[1]),
        pltpu.make_async_copy(own_up, full_up.at[:, inner], own_sem.at[2]),
    ]
    for b in range(GROUP):
        pltpu.make_async_copy(tok.at[b], part.at[b], load_sem.at[b]).start()

    def win_copies(h):
        qk, vv = heads * QKH, heads * VH
        table = (
            (h * QKH, 0, QKH),
            (qk + h * QKH, QKH, QKH),
            (2 * qk + h * VH, 2 * QKH, VH),
            (2 * qk + vv + h * VH, 2 * QKH + VH, VH),
        )
        return [
            pltpu.make_async_copy(
                full_in.at[:, pl.ds(pl.multiple_of(start, 128), size)],
                win.at[h, :, pl.ds(off, size)],
                win_sem.at[h, n],
            )
            for n, (start, off, size) in enumerate(table)
        ]

    for h in range(heads):
        for copy in win_copies(h):
            copy.start()
    for copy in own_copies:
        copy.start()

    step_rows = 32

    def norm_buffer(b, carry):
        pltpu.make_async_copy(tok.at[b], part.at[b], load_sem.at[b]).wait()

        def norm_rows(n, carry):
            r = pl.multiple_of(n * step_rows, step_rows)
            normal, _ = norm_parts(part[b, pl.ds(r, step_rows), :].astype(F32), EPSILON)
            at_rows = pl.ds(pl.multiple_of(b * rows + r, step_rows), step_rows)
            x[at_rows, :] = (normal * gain_one[...] + bias_one[...]).astype(BF16)
            return carry

        lax.fori_loop(0, rows // step_rows, norm_rows, 0)
        return carry

    lax.fori_loop(0, GROUP, norm_buffer, 0)
    tile = 512
    spots = 6
    plan = tick_plan(total, spots)
    span = [stop - start for start, stop in plan]

    def spot(h, number):
        lows = [plan[k * (spots // heads) + number][0] for k in range(heads)]
        highs = [plan[k * (spots // heads) + number][1] for k in range(heads)]
        low_step = lows[0] + h * (lows[1] - lows[0])
        high_step = highs[0] + h * (highs[1] - highs[0])
        run_steps(outs, low_step, high_step)

    def project(h, off):
        def at_tile(m, use):
            r = pl.ds(pl.multiple_of(m * tile, tile), tile)
            use(r, dot(x[r, :], win[h, :, off : off + QKH]))

        return at_tile

    def head(h, carry):
        for copy in win_copies(h):
            copy.wait()

        def rotate_tiles(m, carry):
            def put_query(r, value):
                turned = rotated(value, cosine[r, :], sine[r, :], growth[r, :])
                query[h, r, :] = (turned * QKH ** (-0.5)).astype(BF16)

            def put_keys(r, value):
                keys[h, r, :] = rotated(value, cosine[r, :], sine[r, :], shrink[r, :]).astype(BF16)

            project(h, 0)(m, put_query)
            project(h, QKH)(m, put_keys)
            return carry

        lax.fori_loop(0, count // tile, rotate_tiles, 0)
        spot(h, 0)

        def plain_tiles(m, carry):
            for c in range(VH // QKH):
                off = c * QKH

                def put_values(r, value, off=off):
                    values[h, r, off : off + QKH] = value.astype(BF16)

                def put_gate(r, value, off=off):
                    gate[h, r, off : off + QKH] = value

                project(h, 2 * QKH + off)(m, put_values)
                project(h, 2 * QKH + VH + off)(m, put_gate)
            return carry

        lax.fori_loop(0, count // tile, plain_tiles, 0)
        spot(h, 1)

        def buffer(b, carry):
            r = pl.ds(pl.multiple_of(b * rows, rows), rows)
            raw = dot_back(query[h, r, :], keys[h, r, :])
            linked = (ident_col[b] == ident_row[b]) & (ident_col[b] >= 0)
            masked = (raw * jnp.where(linked, powers[h], 0.0)).astype(BF16)
            value = dot(masked, values[h, r, :])
            mixed[h, r, :] = value
            normal, _ = norm_parts(value, GROUP_EPSILON)
            z = gate[h, r, :]
            result = z / (1.0 + jnp.exp(-z)) * (normal * gain_group[h])
            gated[r, pl.ds(pl.multiple_of(h * VH, VH), VH)] = result.astype(BF16)
            return carry

        lax.fori_loop(0, GROUP, buffer, 0)
        spot(h, 2)
        return carry

    lax.fori_loop(0, heads, head, 0)
    for ring in outs:
        ring.finish()
    for ring in ups + downs:
        ring.begin()
    stores = [
        pltpu.make_async_copy(src, dst, store_sem.at[1 + n])
        for n, (src, dst) in enumerate(
            ((query, o_query), (keys, o_keys), (values, o_values), (gate, o_gate), (mixed, o_mixed), (gated, o_gated))
        )
    ]
    for copy in stores:
        copy.start()
    own_copies[0].wait()
    block = w_out.shape[0]
    fetch = pltpu.make_async_copy(full_out, wo, load_sem.at[GROUP])
    fetch.start()
    fetch.wait()

    chunks = 4
    size = rows // chunks
    rest = ups + downs
    later = tick_plan(total, 6)

    def branch(relation):
        b = flip(me, relation)

        def column(n, carry):
            wide = 512
            c = pl.ds(pl.multiple_of(n * wide, wide), wide)
            r = pl.ds(pl.multiple_of(b * rows, rows), rows)
            acc = jnp.zeros((rows, wide), F32)
            piece = gated[r, :]
            acc = dot(piece, wo[:, :, c].reshape(total * block, wide))
            part[b, :, c] = acc.astype(BF16)
            return carry

        lax.fori_loop(0, width // 512, column, 0)

    def rows_of(c):
        return pl.ds(c * size, size)

    far = flip(me, 2)

    def copy(kind, c):
        r = rows_of(c)
        if kind == 0:
            src, dst, dev = part.at[flip(me, 3), r], core_in.at[0, r], core
        elif kind == 1:
            src, dst, dev = part.at[flip(me, 1), r], core_in.at[1, r], core
        elif kind == 2:
            src, dst, dev = out_x.at[r], in_x.at[r], across
        elif kind == 3:
            src, dst, dev = low.at[r], full_two.at[me, r], across
        elif kind == 4:
            src, dst, dev = low.at[r], full_two.at[me, r], core
        else:
            src, dst, dev = full_two.at[far, r], full_two.at[far, r], core
        return remote(src, dst, row_send.at[kind, c], row_recv.at[kind, c], dev)

    def store(c):
        r = rows_of(c)
        return pltpu.make_async_copy(low.at[r], full_two.at[me, r], row_own.at[c])

    branch(3)
    for c in range(chunks):
        copy(0, c).start()
    branch(2)
    for c in range(chunks):
        r = rows_of(c)
        copy(0, c).wait_recv()
        out_x[r, :] = (part[far, r, :].astype(F32) + core_in[0, r, :].astype(F32)).astype(BF16)
        copy(2, c).start()
    branch(1)
    for c in range(chunks):
        copy(1, c).start()
    branch(0)
    run_steps(rest, *later[0])

    def turn(n, carry):
        i, j = n // (count // 256), lax.rem(n, count // 256)
        i, j = (pl.ds(pl.multiple_of(k * 256, 256), 256) for k in (i, j))
        win[0, i, j] = x[j, i].T
        return carry

    lax.fori_loop(0, (width // 256) * (count // 256), turn, 0)
    store_turned = pltpu.make_async_copy(win.at[0, :, pl.ds(0, count)], o_turned, store_sem.at[0])
    store_turned.start()
    for c in range(chunks):
        r = rows_of(c)
        copy(1, c).wait_recv()
        copy(2, c).wait_recv()

        def finish_rows(n, carry, c=c):
            s = pl.ds(pl.multiple_of(c * size + n * step_rows, step_rows), step_rows)
            value = own_tok[s, :].astype(F32) + (
                part[me, s, :].astype(F32) + core_in[1, s, :].astype(F32) + in_x[s, :].astype(F32)
            )
            hidden[s, :] = value
            normal, _ = norm_parts(value, EPSILON)
            low[s, :] = (normal * gain_two[...] + bias_two[...]).astype(BF16)
            return carry

        lax.fori_loop(0, size // step_rows, finish_rows, 0)
        copy(3, c).start()
        copy(4, c).start()
        store(c).start()
        if c % 2:
            run_steps(rest, *later[1 + c // 2])
    for c in range(chunks):
        copy(3, c).wait_recv()
        copy(5, c).start()
        if c % 2:
            run_steps(rest, *later[3 + c // 2])
    for c in range(chunks):
        copy(4, c).wait_recv()
        copy(5, c).wait_recv()
        store(c).wait()
        for kind in range(6):
            copy(kind, c).wait_send()
    run_steps(rest, *later[5])
    for ring in rest:
        ring.finish()
    wait_sent(outs + rest, total)
    own_copies[1].wait()
    own_copies[2].wait()
    store_turned.wait()
    for c in stores:
        c.wait()


def forward(
    total, own_up, w_out, w_down, full_in, tok, gain_one, bias_one, gain_group, tables, powers, ident_col, ident_row,
    own_tok, gain_two, bias_two,
):
    rows, width = own_tok.shape
    count = GROUP * rows
    heads = HEADS // GROUP
    vmem, hbm = pl.BlockSpec(memory_space=pltpu.VMEM), pl.BlockSpec(memory_space=ANY)
    dma = pltpu.SemaphoreType.DMA
    kept = (
        ((heads, count, QKH), BF16),
        ((heads, count, QKH), BF16),
        ((heads, count, VH), BF16),
        ((heads, count, VH), F32),
        ((heads, count, VH), F32),
        ((count, heads * VH), BF16),
    )
    shapes = (
        ((GROUP, total) + own_up.shape[1:], BF16),
        ((total,) + w_out.shape, BF16),
        ((total,) + w_down.shape, BF16),
        ((width, count), BF16),
        *kept,
        ((rows, width), F32),
        ((GROUP, rows, width), BF16),
    )
    return pl.pallas_call(
        functools.partial(forward_kernel, total),
        out_shape=[jax.ShapeDtypeStruct(s, d) for s, d in shapes],
        in_specs=[hbm] * 5 + [vmem] * 13,
        out_specs=[hbm] * 10 + [vmem, hbm],
        scratch_shapes=[
            pltpu.VMEM((heads, width, 2 * QKH + 2 * VH), BF16),
            pltpu.VMEM((GROUP, rows, width), BF16),
            pltpu.VMEM((count, width), BF16),
            *[pltpu.VMEM(s, d) for s, d in kept],
            pltpu.VMEM((total,) + w_out.shape, BF16),
            pltpu.VMEM((2, rows, width), BF16),
            pltpu.VMEM((rows, width), BF16),
            pltpu.VMEM((rows, width), BF16),
            pltpu.VMEM((rows, width), BF16),
            dma((12, total - 1)), dma((12, total - 1)), dma((3,)), dma((GROUP + 1,)), dma((heads, 4)),
            dma((7,)), dma((6, 4)), dma((6, 4)), dma((4,)),
        ],
        compiler_params=pltpu.CompilerParams(
            collective_id=1, has_side_effects=True, vmem_limit_bytes=63 * MIB
        ),
        name="forward_retention",
    )(
        own_up, w_out, w_down, full_in, tok, gain_one, bias_one, gain_group, *tables, powers, ident_col,
        ident_row, own_tok, gain_two, bias_two,
    )


class Adding:
    def __init__(self, at, way, term, arrived, sends, recvs):
        self.at, self.way, self.term, self.arrived = at, way, term, arrived
        self.sends, self.recvs = sends, recvs

    def hop(self, step, first=False):
        src = self.term(self.at.behind(self.way, 1)) if first else self.arrived.at[step - 1]
        return remote(
            src, self.arrived.at[step], self.sends.at[step], self.recvs.at[step], self.at.neighbour(self.way)
        )

    def begin(self):
        self.hop(0, True).start()

    def sum_at(self, step, which):
        self.hop(step, True).wait_recv()
        return self.arrived[step].astype(F32) + self.term(which)[...].astype(F32)

    def onward(self, step):
        self.arrived[step - 1] = self.sum_at(step - 1, self.at.behind(self.way, step + 1)).astype(BF16)
        self.hop(step).start()

    def finish(self):
        return self.sum_at(self.at.total - 2, self.at.inner)


def wait_added(rings, total):
    def body(step, carry):
        for ring in rings:
            ring.hop(step, True).wait_send()
        return carry

    lax.fori_loop(0, total - 1, body, 0)


def backward_kernel(
    total, g_down, two, d_upper, part, seed, hidden, gain_two, h_gated, h_out, h_query, h_keys, h_values, h_gate,
    h_mixed, cosine, sine, growth, shrink, powers, ident_col, ident_row, gain_group,
    o_down, o_up, o_out, d_hidden, full_branch, sums, o_group, o_project,
    g_up, g_out, arrived, wide_buf, narrow_buf, wo, own_part, core_in, out_x, in_x, low,
    query, keys, values, gate, mixed, back, d_mixed, staged, stage, landed,
    ring_send, ring_recv, row_send, row_recv, row_own, load_sem, unit_sem, out_sem, a2a_send, a2a_recv,
):
    at = Place(total)
    me = at.group
    core, across = at.peer(1), at.peer(2)
    greet([core, across, at.peer(3), at.neighbour(0), at.neighbour(1)])
    rows, width = seed.shape
    count = GROUP * rows
    heads = HEADS // GROUP
    r_up, r_out = o_up.shape[0], o_out.shape[0]
    up_width = o_up.shape[1] // GROUP
    half, side = r_out // 2, width // 2

    def halves(source, base):
        return [
            Adding(
                at, way,
                lambda which, way=way, c=c: source.at[
                    pl.ds(pl.multiple_of(which * r_out + way * half, half), half), pl.ds(c * side, side)
                ],
                arrived.at[base + 2 * c + way], ring_send.at[base + 2 * c + way], ring_recv.at[base + 2 * c + way],
            )
            for c in (0, 1)
            for way in (0, 1)
        ]

    downs, outs, ups = halves(g_down, 0), halves(g_out, 8), []
    for order in (0, 1):
        for way in (0, 1):
            relation = RELATIONS[way][order]
            slot = 4 + 2 * order + way
            ups.append(
                Adding(
                    at, way,
                    lambda which, relation=relation: g_up.at[
                        pl.ds(pl.multiple_of((flip(me, relation) * total + which) * r_up, r_up), r_up), :
                    ],
                    arrived.at[slot], ring_send.at[slot], ring_recv.at[slot],
                )
            )

    chunks = 4
    size = rows // chunks
    step_rows = 32
    far = flip(me, 2)

    def rows_of(c):
        return pl.ds(c * size, size)

    def copy(kind, c):
        r = rows_of(c)
        if kind == 0:
            src, dst, dev = part.at[flip(me, 3), r], core_in.at[0, r], core
        elif kind == 1:
            src, dst, dev = part.at[flip(me, 1), r], core_in.at[1, r], core
        elif kind == 2:
            src, dst, dev = out_x.at[r], in_x.at[r], across
        elif kind == 3:
            src, dst, dev = low.at[r], full_branch.at[me, r], across
        elif kind == 4:
            src, dst, dev = low.at[r], full_branch.at[me, r], core
        else:
            src, dst, dev = full_branch.at[far, r], full_branch.at[far, r], core
        return remote(src, dst, row_send.at[kind, c], row_recv.at[kind, c], dev)

    def load(which, c):
        r = rows_of(c)
        source = far if which == 0 else me
        return pltpu.make_async_copy(part.at[source, r], own_part.at[which, r], row_own.at[which, c])

    def store(c):
        r = rows_of(c)
        return pltpu.make_async_copy(low.at[r], full_branch.at[me, r], row_own.at[2, c])

    for which in (0, 1):
        for c in range(chunks):
            copy(which, c).start()
            load(which, c).start()
    for ring in downs:
        ring.begin()
    fetch_two = pltpu.make_async_copy(two, wide_buf, load_sem.at[0])
    fetch_upper = pltpu.make_async_copy(d_upper, narrow_buf, load_sem.at[1])
    fetch_out = pltpu.make_async_copy(h_out, wo, load_sem.at[2])
    for fetch in (fetch_two, fetch_upper, fetch_out):
        fetch.start()

    def unit_loads(unit, slot):
        h, b = unit // GROUP, lax.rem(unit, GROUP)
        r = pl.ds(pl.multiple_of(b * rows, rows), rows)
        pairs = ((h_query, query), (h_keys, keys), (h_values, values), (h_gate, gate), (h_mixed, mixed))
        return [
            pltpu.make_async_copy(src.at[h, r], dst.at[slot], unit_sem.at[slot, n])
            for n, (src, dst) in enumerate(pairs)
        ]

    for unit in (0, 1):
        for fetch in unit_loads(jnp.int32(unit), unit):
            fetch.start()

    def send_sums(c):
        r = rows_of(c)
        load(0, c).wait()
        copy(0, c).wait_recv()
        out_x[r, :] = (own_part[0, r, :].astype(F32) + core_in[0, r, :].astype(F32)).astype(BF16)
        copy(2, c).start()

    def norm_back(c):
        load(1, c).wait()
        copy(1, c).wait_recv()
        copy(2, c).wait_recv()

        def some_rows(n, carry):
            s = pl.ds(pl.multiple_of(c * size + n * step_rows, step_rows), step_rows)
            e = own_part[1, s, :].astype(F32) + core_in[1, s, :].astype(F32) + in_x[s, :].astype(F32)
            normal, scale = norm_parts(hidden[s, :], EPSILON)
            with_gain = e * gain_two[...]
            sums[0:1, :] += jnp.sum(e * normal, axis=0, keepdims=True)
            sums[1:2, :] += jnp.sum(e, axis=0, keepdims=True)
            value = seed[s, :].astype(F32) + scale * (
                with_gain
                - jnp.mean(with_gain, axis=-1, keepdims=True)
                - normal * jnp.mean(with_gain * normal, axis=-1, keepdims=True)
            )
            d_hidden[s, :] = value
            low[s, :] = value.astype(BF16)
            return carry

        lax.fori_loop(0, size // step_rows, some_rows, 0)
        copy(3, c).start()
        copy(4, c).start()
        store(c).start()

    sums[...] = jnp.zeros_like(sums)
    o_group[...] = jnp.zeros_like(o_group)
    for c in range(chunks):
        send_sums(c)
    plan = tick_plan(total, 6)
    add_steps(downs, *plan[0])
    fetch_two.wait()
    fetch_upper.wait()

    def grad_tiles(left, right, out, start, stop):
        wide = 512

        def tile(n, carry):
            rows_n = right.shape[1] // wide
            i, j = n // rows_n, lax.rem(n, rows_n)
            a = pl.ds(pl.multiple_of(i * 256, 256), 256)
            c = pl.ds(pl.multiple_of(j * wide, wide), wide)
            out[a, c] = dot_rows(left[:, a], right[:, c]).astype(BF16)
            return carry

        lax.fori_loop(start, stop, tile, 0)

    tiles = (width // 256) * (up_width // 512)
    for quarter in range(4):
        grad_tiles(wide_buf, narrow_buf, g_up, tiles * quarter // 4, tiles * (quarter + 1) // 4)
        if quarter:
            norm_back(quarter - 1)
        add_steps(downs, *plan[1 + quarter])
    norm_back(3)
    add_steps(downs, *plan[5])
    for ring in ups:
        ring.begin()
    fetch_gated = pltpu.make_async_copy(h_gated, narrow_buf, load_sem.at[1])
    fetch_gated.start()
    for n, ring in enumerate(downs):
        c, way = n // 2, n % 2
        o_down[pl.ds(way * half, half), pl.ds(c * side, side)] = ring.finish()
    for c in range(chunks):
        copy(3, c).wait_recv()
        copy(5, c).start()
        if c % 2:
            add_steps(ups, *plan[c // 2])
    for c in range(chunks):
        copy(4, c).wait_recv()
        copy(5, c).wait_recv()
        store(c).wait()
    branch = wide_buf
    fetch_branch = [
        pltpu.make_async_copy(full_branch.at[b], branch.at[pl.ds(b * rows, rows)], load_sem.at[3 + b])
        for b in range(GROUP)
    ]
    for fetch in fetch_branch:
        fetch.start()
    for fetch in fetch_branch:
        fetch.wait()
    fetch_gated.wait()
    fetch_out.wait()
    tiles = (narrow_buf.shape[1] // 256) * (width // 512)
    for quarter in range(4):
        grad_tiles(narrow_buf, branch, g_out, tiles * quarter // 4, tiles * (quarter + 1) // 4)
        add_steps(ups, *plan[2 + quarter])
    for ring in outs:
        ring.begin()

    def sent_across(relation):
        return remote(
            stage.at[relation - 1], landed.at[relation - 1],
            a2a_send.at[relation - 1], a2a_recv.at[relation - 1], at.peer(relation),
        )

    for n, ring in enumerate(ups):
        relation = RELATIONS[n % 2][n // 2]
        value = ring.finish()
        if relation == 0:
            o_up[:, pl.ds(pl.multiple_of(me * up_width, 128), up_width)] = value
        else:
            stage[relation - 1] = value.astype(BF16)
            sent_across(relation).start()

    units = heads * GROUP
    qk, vv = heads * QKH, heads * VH

    def unit_stores(unit, slot):
        h, b = unit // GROUP, lax.rem(unit, GROUP)
        r = pl.ds(pl.multiple_of(b * rows, rows), rows)
        table = (
            (h * QKH, 0, QKH),
            (qk + h * QKH, QKH, QKH),
            (2 * qk + h * VH, 2 * QKH, VH),
            (2 * qk + vv + h * VH, 2 * QKH + VH, VH),
        )
        return [
            pltpu.make_async_copy(
                staged.at[slot, :, pl.ds(off, size)],
                o_project.at[r, pl.ds(pl.multiple_of(start, 128), size)],
                out_sem.at[slot, n],
            )
            for n, (start, off, size) in enumerate(table)
        ]

    def unrotated(value, r, scale):
        mid = QKH // 2
        first, second = value[:, :mid], value[:, mid:]
        c, s = cosine[r, :], sine[r, :]
        return jnp.concatenate(
            [(first * c + second * s) * scale, (second * c - first * s) * scale], axis=1
        )

    def unit_body(unit, carry):
        slot = lax.rem(unit, 2)
        h, b = unit // GROUP, lax.rem(unit, GROUP)
        r = pl.ds(pl.multiple_of(b * rows, rows), rows)
        back[...] = dot_back(branch[r, :], wo[pl.ds(pl.multiple_of(h * VH, VH), VH), :])
        for fetch in unit_loads(unit, slot):
            fetch.wait()

        @pl.when(unit >= 2)
        def _():
            for done in unit_stores(unit - 2, slot):
                done.wait()

        gains = gain_group[h]

        def some_rows(n, carry):
            s = pl.ds(pl.multiple_of(n * step_rows, step_rows), step_rows)
            normal, scale = norm_parts(mixed[slot, s, :], GROUP_EPSILON)
            z = gate[slot, s, :]
            f = back[s, :]
            sigmoid = 1.0 / (1.0 + jnp.exp(-z))
            silu = z * sigmoid
            d_silu = f * (normal * gains)
            staged[slot, s, 2 * QKH + VH :] = (d_silu * (sigmoid + silu * (1.0 - sigmoid))).astype(BF16)
            d_scaled = f * silu
            o_group[h] += jnp.sum(d_scaled * normal, axis=0, keepdims=True)
            d_normal = d_scaled * gains
            d_mixed[s, :] = (
                scale
                * (
                    d_normal
                    - jnp.mean(d_normal, axis=-1, keepdims=True)
                    - normal * jnp.mean(d_normal * normal, axis=-1, keepdims=True)
                )
            ).astype(BF16)
            return carry

        lax.fori_loop(0, rows // step_rows, some_rows, 0)
        linked = (ident_col[b] == ident_row[b]) & (ident_col[b] >= 0)
        decay = jnp.where(linked, powers[h], 0.0)
        masked = (dot_back(query[slot], keys[slot]) * decay).astype(BF16)
        staged[slot, :, 2 * QKH : 2 * QKH + VH] = dot_rows(masked, d_mixed[...]).astype(BF16)
        d_raw = (dot_back(d_mixed[...], values[slot]) * decay).astype(BF16)
        d_query = dot(d_raw, keys[slot]) * QKH ** (-0.5)
        staged[slot, :, :QKH] = unrotated(d_query, r, growth[r, :]).astype(BF16)
        d_keys = dot_rows(d_raw, query[slot])
        staged[slot, :, QKH : 2 * QKH] = unrotated(d_keys, r, shrink[r, :]).astype(BF16)
        for done in unit_stores(unit, slot):
            done.start()

        @pl.when(unit + 2 < units)
        def _():
            for fetch in unit_loads(unit + 2, slot):
                fetch.start()

        steps = total - 2
        add_steps(outs, 1 + (steps * unit) // units, 1 + (steps * (unit + 1)) // units)
        return carry

    lax.fori_loop(0, units, unit_body, 0)
    for relation in (1, 2, 3):
        sent_across(relation).wait_recv()
        o_up[:, pl.ds(pl.multiple_of(flip(me, relation) * up_width, 128), up_width)] = landed[
            relation - 1
        ].astype(F32)
        sent_across(relation).wait_send()
    for slot in (0, 1):
        for done in unit_stores(jnp.int32(units - 2 + slot), slot):
            done.wait()
    for n, ring in enumerate(outs):
        c, way = n // 2, n % 2
        o_out[pl.ds(way * half, half), pl.ds(c * side, side)] = ring.finish()
    for c in range(chunks):
        for kind in range(6):
            copy(kind, c).wait_send()
    wait_added(downs + ups + outs, total)


def add_steps(rings, start, stop):
    def body(step, carry):
        for ring in rings:
            ring.onward(step)
        return carry

    lax.fori_loop(start, stop, body, 0)


def backward(
    total, g_down, two, d_upper, part, seed, hidden, gain_two, gated, full_out, query, keys, values, gate, mixed,
    tables, powers, ident_col, ident_row, gain_group,
):
    rows, width = seed.shape
    count = GROUP * rows
    heads = HEADS // GROUP
    up_width = d_upper.shape[1]
    r_out, r_up = g_down.shape[0] // total, width // GROUP // total
    half, side = r_out // 2, width // 2
    vmem, hbm = pl.BlockSpec(memory_space=pltpu.VMEM), pl.BlockSpec(memory_space=ANY)
    dma = pltpu.SemaphoreType.DMA
    shapes = (
        ((r_out, width), F32),
        ((r_up, up_width * GROUP), F32),
        ((r_out, width), F32),
        ((rows, width), F32),
        ((GROUP, rows, width), BF16),
        ((8, width), F32),
        ((heads, 1, VH), F32),
        ((count, 2 * heads * (QKH + VH)), BF16),
    )
    return pl.pallas_call(
        functools.partial(backward_kernel, total),
        out_shape=[jax.ShapeDtypeStruct(s, d) for s, d in shapes],
        in_specs=[vmem, hbm, hbm, hbm, vmem, vmem, vmem] + [hbm] * 7 + [vmem] * 8,
        out_specs=[vmem] * 4 + [hbm, vmem, vmem, hbm],
        scratch_shapes=[
            pltpu.VMEM((width, up_width), BF16),
            pltpu.VMEM(g_down.shape, BF16),
            pltpu.VMEM((12, total - 1, half, side), BF16),
            pltpu.VMEM((count, width), BF16),
            pltpu.VMEM((count, up_width), BF16),
            pltpu.VMEM(full_out.shape, BF16),
            pltpu.VMEM((2, rows, width), BF16),
            pltpu.VMEM((2, rows, width), BF16),
            pltpu.VMEM((rows, width), BF16),
            pltpu.VMEM((rows, width), BF16),
            pltpu.VMEM((rows, width), BF16),
            pltpu.VMEM((2, rows, QKH), BF16),
            pltpu.VMEM((2, rows, QKH), BF16),
            pltpu.VMEM((2, rows, VH), BF16),
            pltpu.VMEM((2, rows, VH), F32),
            pltpu.VMEM((2, rows, VH), F32),
            pltpu.VMEM((rows, VH), F32),
            pltpu.VMEM((rows, VH), BF16),
            pltpu.VMEM((2, rows, 2 * (QKH + VH)), BF16),
            pltpu.VMEM((3, r_up, up_width), BF16),
            pltpu.VMEM((3, r_up, up_width), BF16),
            dma((12, total - 1)), dma((12, total - 1)), dma((6, 4)), dma((6, 4)), dma((3, 4)), dma((7,)),
            dma((2, 5)), dma((2, 4)), dma((3,)), dma((3,)),
        ],
        compiler_params=pltpu.CompilerParams(
            collective_id=2, has_side_effects=True, vmem_limit_bytes=63 * MIB
        ),
        name="backward_retention",
    )(
        g_down, two, d_upper, part, seed, hidden, gain_two, gated, full_out, query, keys, values, gate, mixed,
        *tables, powers, ident_col, ident_row, gain_group,
    )


def final_kernel(
    total, h_project, h_in, h_turned, part_down, hidden, d_hidden, tok, gain_one, valid, sums_two, d_group,
    o_in, output, d_tokens, o_vec, o_grp,
    project, turned, first_term, term, arrived, win, part, own_part, core_in, out_x, in_x, stage, landed,
    vec, grp, near_in, mid, far_in, far_grp,
    load_sem, win_sem, ring_send, ring_recv, a2a_send, a2a_recv, row_send, row_recv, row_own,
    near_send, near_recv, far_send, far_recv,
):
    at = Place(total)
    me, inner = at.group, at.inner
    others = [(me, lax.rem(inner + n, total)) for n in range(1, total)]
    greet([at.peer(r) for r in (1, 2, 3)] + others)
    rows, width = tok.shape
    count = GROUP * rows
    block = o_in.shape[0]
    step_rows = 32

    fetch_turned = pltpu.make_async_copy(h_turned, turned, load_sem.at[0])
    fetch_project = pltpu.make_async_copy(h_project, project, load_sem.at[1])
    fetch_turned.start()
    fetch_project.start()

    def source(n, b):
        if n == 0:
            return part_down.at[b]
        return part.at[pl.ds(pl.multiple_of(b * rows, rows), rows), :]

    def row_copy(kind, n):
        if kind < 2:
            return remote(
                source(n, flip(me, 3 - 2 * kind)), core_in.at[n, kind], row_send.at[n, kind], row_recv.at[n, kind],
                at.peer(1),
            )
        return remote(out_x.at[n], in_x.at[n], row_send.at[n, 2], row_recv.at[n, 2], at.peer(2))

    def row_load(which):
        return pltpu.make_async_copy(
            source(0, flip(me, 2) if which == 0 else me), own_part.at[which], row_own.at[which]
        )

    def own_rows(n, which, r):
        if n == 0:
            return own_part[which, pl.ds(r, step_rows), :]
        b = flip(me, 2) if which == 0 else me
        return part[pl.ds(pl.multiple_of(b * rows + r, step_rows), step_rows), :]

    def by_rows(body):
        def some(k, carry):
            body(pl.multiple_of(k * step_rows, step_rows))
            return carry

        lax.fori_loop(0, rows // step_rows, some, 0)

    def send_rows(n):
        row_copy(0, n).wait_recv()

        def some(r):
            s = pl.ds(r, step_rows)
            out_x[n, s, :] = (own_rows(n, 0, r).astype(F32) + core_in[n, 0, s, :].astype(F32)).astype(BF16)

        by_rows(some)
        row_copy(2, n).start()

    def summed_rows(n, r):
        s = pl.ds(r, step_rows)
        return own_rows(n, 1, r).astype(F32) + core_in[n, 1, s, :].astype(F32) + in_x[n, s, :].astype(F32)

    def take_down():
        row_copy(1, 0).wait_recv()
        row_copy(2, 0).wait_recv()

        def some(r):
            s = pl.ds(r, step_rows)
            output[s, :] = ((hidden[s, :] + summed_rows(0, r)) * valid[s, :]).astype(BF16)

        by_rows(some)

    def take_rows():
        row_copy(1, 1).wait_recv()
        row_copy(2, 1).wait_recv()
        vec[...] = jnp.zeros_like(vec)
        vec[2:4, :] = sums_two[0:2, :]

        def some(r):
            s = pl.ds(r, step_rows)
            e = summed_rows(1, r)
            normal, scale = norm_parts(tok[s, :].astype(F32), EPSILON)
            with_gain = e * gain_one[...]
            vec[0:1, :] += jnp.sum(e * normal, axis=0, keepdims=True)
            vec[1:2, :] += jnp.sum(e, axis=0, keepdims=True)
            value = d_hidden[s, :] + scale * (
                with_gain
                - jnp.mean(with_gain, axis=-1, keepdims=True)
                - normal * jnp.mean(with_gain * normal, axis=-1, keepdims=True)
            )
            d_tokens[s, :] = value.astype(BF16)

        by_rows(some)

    quarter = width // GROUP
    small = quarter // total
    large = grp.shape[1] // total

    def near(relation):
        start = pl.multiple_of(flip(me, relation) * quarter, 128)
        return remote(
            vec.at[:, pl.ds(start, quarter)], near_in.at[relation - 1], near_send.at[relation - 1],
            near_recv.at[relation - 1], at.peer(relation),
        )

    def tile_of(index, size):
        return pl.ds(pl.multiple_of((index * size) // 128 * 128, 128), 128)

    def distant(kind, n):
        target = lax.rem(inner + n, total)
        src = mid.at[:, tile_of(target, small)] if kind == 0 else grp.at[:, tile_of(target, large)]
        dst = far_in if kind == 0 else far_grp
        return remote(
            src, dst.at[n - 1], far_send.at[kind, n - 1], far_recv.at[kind, n - 1], (me, target)
        )

    def vectors_near():
        for relation in (1, 2, 3):
            near(relation).start()
        grp[...] = jnp.zeros_like(grp)
        for h in range(d_group.shape[0]):
            grp[0:1, h * VH : (h + 1) * VH] = d_group[h]

    def vectors_far():
        for relation in (1, 2, 3):
            near(relation).wait_recv()
        mid[...] = (
            vec[:, pl.ds(pl.multiple_of(me * quarter, 128), quarter)] + near_in[0] + near_in[1] + near_in[2]
        )
        for n in range(1, total):
            for kind in (0, 1):
                distant(kind, n).start()

    def vectors_end():
        for n in range(1, total):
            for kind in (0, 1):
                distant(kind, n).wait_recv()
        o_vec[...] = mid[:, tile_of(inner, small)] + jnp.sum(far_in[...], axis=0)
        o_grp[...] = grp[:, tile_of(inner, large)] + jnp.sum(far_grp[...], axis=0)

    wide = 512

    def terms(step, out):
        for way in (0, 1):
            which = at.behind(way, step + 1)
            left = jnp.concatenate(
                [
                    turned[
                        pl.ds(pl.multiple_of((flip(me, relation) * total + which) * block, block), block), :
                    ]
                    for relation in RELATIONS[way]
                ],
                axis=0,
            )

            def tile(n, carry, left=left, way=way):
                c = pl.ds(pl.multiple_of(n * wide, wide), wide)
                value = dot(left, project[:, c]).astype(BF16)
                out[2 * way, :, c] = value[:block]
                out[2 * way + 1, :, c] = value[block:]
                return carry

            lax.fori_loop(0, project.shape[1] // wide, tile, 0)

    def hop(slot, step, first=False):
        src = first_term.at[slot] if first else arrived.at[slot, step - 1]
        return remote(
            src, arrived.at[slot, step], ring_send.at[slot, step], ring_recv.at[slot, step],
            at.neighbour(slot // 2),
        )

    order = (0, 2, 1, 3)

    def onward(step, carry):
        terms(step, term)
        for slot in order:
            hop(slot, step - 1, True).wait_recv()
            arrived[slot, step - 1] = (
                arrived[slot, step - 1].astype(F32) + term[slot].astype(F32)
            ).astype(BF16)
            hop(slot, step).start()
        return carry

    def fetch_win(n):
        return pltpu.make_async_copy(
            h_in.at[pl.ds(n * 256, 256), :], win.at[n % 2], win_sem.at[n % 2]
        )

    columns = width // 256

    def row_tiles(n):
        fetch_win(n).wait()

        def tile(m, carry):
            r = pl.ds(pl.multiple_of(m * 512, 512), 512)
            part[r, n * 256 : (n + 1) * 256] = dot_back(project[r, :], win[n % 2]).astype(BF16)
            return carry

        lax.fori_loop(0, count // 512, tile, 0)
        if n + 2 < columns:
            fetch_win(n + 2).start()

    row_copy(0, 0).start()
    row_copy(1, 0).start()
    row_load(0).start()
    row_load(1).start()
    fetch_win(0).start()
    fetch_win(1).start()
    fetch_turned.wait()
    fetch_project.wait()
    terms(0, first_term)
    for slot in order:
        hop(slot, 0, True).start()
    row_load(0).wait()
    send_rows(0)
    plan = tick_plan(total, 6)

    def extra(number):
        if number < 4:
            for n in range(columns * number // 4, columns * (number + 1) // 4):
                row_tiles(n)
            if number == 3:
                row_copy(0, 1).start()
                row_copy(1, 1).start()
        elif number == 4:
            send_rows(1)
            row_load(1).wait()
            take_down()
        else:
            take_rows()
            vectors_near()

    for number in range(6):
        extra(number)
        lax.fori_loop(*plan[number], onward, 0)
    vectors_far()
    terms(total - 1, term)
    pieces = column_pieces(o_in.shape[1])

    def place(other, value):
        for base, stride, off, size in pieces:
            start = pl.multiple_of(base + other * stride, 128)
            o_in[:, pl.ds(start, size)] = value[:, off : off + size]

    def sent_across(relation):
        return remote(
            stage.at[relation - 1], landed.at[relation - 1],
            a2a_send.at[relation - 1], a2a_recv.at[relation - 1], at.peer(relation),
        )

    for slot in order:
        relation = RELATIONS[slot // 2][slot % 2]
        hop(slot, total - 2, True).wait_recv()
        value = arrived[slot, total - 2].astype(F32) + term[slot].astype(F32)
        if relation == 0:
            place(me, value)
        else:
            stage[relation - 1] = value.astype(BF16)
            sent_across(relation).start()
    vectors_end()
    for relation in (1, 2, 3):
        sent_across(relation).wait_recv()
        place(flip(me, relation), landed[relation - 1].astype(F32))
    for relation in (1, 2, 3):
        sent_across(relation).wait_send()
        near(relation).wait_send()
    for n in range(1, total):
        for kind in (0, 1):
            distant(kind, n).wait_send()
    for n in (0, 1):
        for kind in (0, 1, 2):
            row_copy(kind, n).wait_send()

    def sent(step, carry):
        for slot in order:
            hop(slot, step, True).wait_send()
        return carry

    lax.fori_loop(0, total - 1, sent, 0)


def final(
    total, d_project, full_in, turned, down, hidden, d_hidden, tok, gain_one, valid, sums_two, d_group
):
    rows, width = tok.shape
    count, wide = d_project.shape
    block = width // GROUP // total
    vmem, hbm = pl.BlockSpec(memory_space=pltpu.VMEM), pl.BlockSpec(memory_space=ANY)
    dma = pltpu.SemaphoreType.DMA
    group_width = d_group.shape[0] * d_group.shape[2]
    shapes = (
        ((block, wide * GROUP), F32),
        ((rows, width), BF16),
        ((rows, width), BF16),
        ((8, 128), F32),
        ((8, 128), F32),
    )
    return pl.pallas_call(
        functools.partial(final_kernel, total),
        out_shape=[jax.ShapeDtypeStruct(s, d) for s, d in shapes],
        in_specs=[hbm] * 4 + [vmem] * 7,
        out_specs=[vmem] * 5,
        scratch_shapes=[
            pltpu.VMEM((count, wide), BF16),
            pltpu.VMEM(turned.shape, BF16),
            pltpu.VMEM((4, block, wide), BF16),
            pltpu.VMEM((4, block, wide), BF16),
            pltpu.VMEM((4, total - 1, block, wide), BF16),
            pltpu.VMEM((2, 256, wide), BF16),
            pltpu.VMEM((count, width), BF16),
            pltpu.VMEM((2, rows, width), BF16),
            pltpu.VMEM((2, 2, rows, width), BF16),
            pltpu.VMEM((2, rows, width), BF16),
            pltpu.VMEM((2, rows, width), BF16),
            pltpu.VMEM((3, block, wide), BF16),
            pltpu.VMEM((3, block, wide), BF16),
            pltpu.VMEM((8, width), F32),
            pltpu.VMEM((8, group_width), F32),
            pltpu.VMEM((3, 8, width // GROUP), F32),
            pltpu.VMEM((8, width // GROUP), F32),
            pltpu.VMEM((total - 1, 8, 128), F32),
            pltpu.VMEM((total - 1, 8, 128), F32),
            dma((2,)), dma((2,)), dma((4, total - 1)), dma((4, total - 1)), dma((3,)), dma((3,)),
            dma((2, 3)), dma((2, 3)), dma((2,)), dma((3,)), dma((3,)), dma((2, total - 1)), dma((2, total - 1)),
        ],
        compiler_params=pltpu.CompilerParams(
            collective_id=3, has_side_effects=True, vmem_limit_bytes=63 * MIB
        ),
        name="final_sums",
    )(d_project, full_in, turned, down, hidden, d_hidden, tok, gain_one, valid, sums_two, d_group)


def layout(seq_lens, seq_owner, seq_offset, device_id, buffer_len):
    positions = jnp.arange(buffer_len, dtype=jnp.int32)[:, None]
    inside = (
        (seq_owner[None, :] == device_id)
        & (seq_lens[None, :] > 0)
        & (positions >= seq_offset[None, :])
        & (positions < seq_offset[None, :] + seq_lens[None, :])
    )
    number = jnp.arange(seq_lens.shape[0], dtype=jnp.int32)[None, :] + 1
    seq_ident = jnp.sum(jnp.where(inside, number, 0), axis=1) - 1
    starts = jnp.sum(jnp.where(inside, seq_offset[None, :], 0), axis=1)
    places = jnp.where(seq_ident >= 0, positions[:, 0] - starts, 0)
    return seq_ident, places


def rotation(places):
    half_size = QKH // 2
    pair_index = jnp.arange(half_size, dtype=F32) / half_size
    inverse_freq = 10000.0 ** (-pair_index)
    zeta_base = (pair_index + 0.4) / 1.4
    offsets = places.astype(F32)[..., None]
    angles = offsets * inverse_freq
    growth = zeta_base ** (offsets / 512.0)
    return jnp.cos(angles), jnp.sin(angles), growth


def rotate_xpos(vectors, cosine, sine, scale):
    half = QKH // 2
    first, second = vectors[..., :half], vectors[..., half:]
    cosine, sine, scale = cosine[..., None, :], sine[..., None, :], scale[..., None, :]
    return jnp.concatenate(
        [(first * cosine - second * sine) * scale, (second * cosine + first * sine) * scale], axis=-1
    )


def rotate_back(vectors, cosine, sine, scale):
    return rotate_xpos(vectors, cosine, -sine, scale)


def decay_tables(ident, heads):
    positions = jnp.arange(ident.shape[-1], dtype=jnp.int32)
    distance = positions[:, None] - positions[None, :]
    linked = (distance >= 0) & (ident[:, :, None] == ident[:, None, :]) & (ident[:, :, None] >= 0)
    rates = jnp.log1p(-(2.0 ** (-5.0 - heads.astype(F32))))
    powers = jnp.maximum(distance, 0).astype(F32)
    return jnp.where(linked[:, None], jnp.exp(rates[:, None, None] * powers[None])[None], 0.0)


def mean(values):
    return jnp.mean(values, axis=-1, keepdims=True)


def local(
    total,
    tokens,
    cotangent,
    w_in,
    w_out,
    w_up,
    w_down,
    ln1_gain,
    ln1_bias,
    group_gain,
    ln2_gain,
    ln2_bias,
    seq_lens,
    seq_owner,
    seq_offset,
):
    rows, width = tokens.shape
    heads = HEADS // GROUP
    qk, vv = heads * QKH, heads * VH
    me, inner = lax.axis_index("dp"), lax.axis_index("fsdp")
    small, large = ln1_gain.shape[0], group_gain.shape[0]

    pack = jnp.concatenate([ln1_gain, ln1_bias, ln2_gain, ln2_bias, group_gain]).astype(F32)
    pack = jnp.pad(pack, (0, 1024 - pack.shape[0])).reshape(8, 128)
    full_in, own_up, tok, cot, vec = gather_all(total, w_in, w_up, tokens, cotangent, pack)
    full_in = full_in.reshape(width, -1)
    vec = vec.reshape(total, GROUP, 1024)

    def vector(number):
        part = vec[:, :, number * small : (number + 1) * small]
        return jnp.swapaxes(part, 0, 1).reshape(1, width)

    gain_one, bias_one, gain_two, bias_two = (vector(n) for n in range(4))
    gain_group = lax.dynamic_index_in_dim(vec, me, 1, keepdims=False)[:, 4 * small : 4 * small + large]
    gain_group = gain_group.reshape(heads, 1, VH)

    devices = jnp.arange(GROUP, dtype=jnp.int32) * total + inner
    ident, places = jax.vmap(lambda d: layout(seq_lens, seq_owner, seq_offset, d, rows))(devices)
    valid = (ident >= 0).astype(F32)[..., None]
    own_valid = lax.dynamic_index_in_dim(valid, me, 0, keepdims=False)
    count = GROUP * rows

    tables = rotation(places.reshape(count))
    tables = (*tables, 1.0 / tables[2])
    distance = jnp.arange(rows)[:, None] - jnp.arange(rows)[None, :]
    rates = jnp.log1p(-(2.0 ** (-5.0 - (me * heads + jnp.arange(heads)).astype(F32))))
    powers = jnp.exp(rates[:, None, None] * jnp.maximum(distance, 0).astype(F32)[None])
    powers = jnp.where(distance[None] >= 0, powers, 0.0)
    (
        full_up, full_out, full_down, turned, query, keys, values, gate, mixed, gated, hidden, two,
    ) = forward(
        total, own_up, w_out, w_down, full_in, tok, gain_one, bias_one, gain_group, tables, powers,
        ident[:, :, None], ident[:, None, :], tokens, gain_two, bias_two,
    )
    full_up = full_up.reshape(width, -1)
    full_out = full_out.reshape(-1, width)
    full_down = full_down.reshape(-1, width)
    two = two.reshape(count, width)
    upper = dot(two, full_up)
    cdf = 0.5 * (1.0 + lax.erf(upper * (0.5**0.5)))
    active = (upper * cdf).astype(BF16)
    down = dot(active, full_down).astype(BF16).reshape(GROUP, rows, width)

    seed = (cot.astype(F32) * valid).astype(BF16)
    own_seed = (cotangent.astype(F32) * own_valid).astype(BF16)
    seed = seed.reshape(count, width)
    slope = cdf + upper * jnp.exp(-0.5 * upper * upper) * (2.0 * jnp.pi) ** -0.5
    d_upper = (dot_back(seed, full_down) * slope).astype(BF16)
    d_two = dot_back(d_upper, full_up).astype(BF16).reshape(GROUP, rows, width)
    g_down = dot_rows(active, seed).astype(BF16)
    grad_down, grad_up, grad_out, d_hidden, _, sums_two, d_group, d_project = backward(
        total, g_down, two, d_upper, d_two, own_seed, hidden, gain_two, gated, full_out, query, keys, values,
        gate, mixed, tables, powers, ident[:, :, None], ident[:, None, :], gain_group,
    )
    grad_in, output, d_tokens, vec_one, vec_two = final(
        total, d_project, full_in, turned, down, hidden, d_hidden, tokens, gain_one, own_valid, sums_two, d_group
    )
    grads = lax.dynamic_slice(vec_one, (0, lax.rem(inner * small, 128)), (4, small))
    grad_group = lax.dynamic_slice(vec_two, (0, lax.rem(inner * large, 128)), (1, large))[0]
    return (
        output,
        d_tokens,
        grad_in,
        grad_out,
        grad_up,
        grad_down,
        grads[0],
        grads[1],
        grad_group,
        grads[2],
        grads[3],
    )


def solution(mesh):
    flat = ("dp", "fsdp")
    matrix, vector = P(flat, None), P(flat)
    return jax.shard_map(
        functools.partial(local, mesh.shape["fsdp"]),
        mesh=mesh,
        in_specs=(matrix,) * 6 + (vector,) * 5 + (P(),) * 3,
        out_specs=(matrix,) * 6 + (vector,) * 5,
        check_vma=False,
    )
```

```python
import functools

import jax
import jax.numpy as jnp
import numpy as np
from jax import lax
from jax.experimental import pallas as pl
from jax.experimental.pallas import tpu as pltpu
from jax.sharding import PartitionSpec as P

HEADS = 8
QKH = 256
VH = 512
EPSILON = 1e-05
GROUP_EPSILON = 0.1
GROUP = 4
MESH = pl.DeviceIdType.MESH
ANY = pl.ANY
BF16 = jnp.bfloat16
F32 = jnp.float32
MIB = 1 << 20


def ring_place(index, total):
    half = index // 2
    return jnp.where(index % 2 == 0, half, total - 1 - half)


def ring_index(place, total):
    place = lax.rem(place + 2 * total, total)
    return jnp.where(place < total // 2, 2 * place, 2 * (total - 1 - place) + 1)


def flip(group_index, relation):
    low, high = group_index % 2, group_index // 2
    if relation % 2:
        low = 1 - low
    if relation // 2:
        high = 1 - high
    return 2 * high + low


class Place:
    def __init__(self, total):
        self.total = total
        self.group = lax.axis_index("dp")
        self.inner = lax.axis_index("fsdp")
        self.place = ring_place(self.inner, total)
        self.next = (
            ring_index(self.place + 1, total),
            ring_index(self.place - 1, total),
        )

    def peer(self, relation):
        return (flip(self.group, relation), self.inner)

    def neighbour(self, way):
        return (self.group, self.next[way])

    def behind(self, way, steps):
        return ring_index(self.place - steps if way == 0 else self.place + steps, self.total)


def greet(devices):
    barrier = pltpu.get_barrier_semaphore()
    for device in devices:
        pl.semaphore_signal(barrier, inc=1, device_id=device, device_id_type=MESH)
    pl.semaphore_wait(barrier, len(devices))


def remote(src, dst, send_sem, recv_sem, device):
    return pltpu.make_async_remote_copy(
        src_ref=src,
        dst_ref=dst,
        send_sem=send_sem,
        recv_sem=recv_sem,
        device_id=device,
        device_id_type=MESH,
    )


def column_pieces():
    heads = HEADS // GROUP
    table = []
    base, off = 0, 0
    for size in (QKH, QKH, VH, VH):
        for h in range(heads):
            table.append((base + h * size, heads * size, h, off, size))
        base += HEADS * size
        off += size
    return table


def dot(left, right):
    return jnp.dot(left, right, preferred_element_type=F32)


def dot_rows(left, right):
    return lax.dot_general(left, right, (((0,), (0,)), ((), ())), preferred_element_type=F32)


def dot_back(left, right):
    return lax.dot_general(left, right, (((1,), (1,)), ((), ())), preferred_element_type=F32)


def norm_parts(values, epsilon):
    center = values - jnp.mean(values, axis=-1, keepdims=True)
    spread = jnp.mean(center * center, axis=-1, keepdims=True)
    scale = lax.rsqrt(spread + epsilon)
    return center * scale, scale


RELATIONS = ((2, 0), (3, 1))


class Passing:
    def __init__(self, at, way, own, place, sends, recvs):
        self.at, self.way, self.own, self.place = at, way, own, place
        self.sends, self.recvs = sends, recvs

    def hop(self, step, first=False):
        which = self.at.inner if first else self.at.behind(self.way, step)
        dst = self.place(which)
        return remote(
            self.own if first else dst, dst, self.sends.at[step], self.recvs.at[step],
            self.at.neighbour(self.way),
        )

    def begin(self):
        self.hop(0, True).start()

    def onward(self, step):
        self.hop(step - 1).wait_recv()
        self.hop(step).start()

    def finish(self):
        self.hop(self.at.total - 2).wait_recv()


def wait_sent(rings, total):
    def body(step, carry):
        for ring in rings:
            ring.hop(step).wait_send()
        return carry

    lax.fori_loop(0, total - 1, body, 0)


def tick_plan(total, places):
    steps = total - 2
    cuts = [1 + (steps * n) // places for n in range(places + 1)]
    return list(zip(cuts[:-1], cuts[1:]))


def run_steps(rings, start, stop):
    def body(step, carry):
        for ring in rings:
            ring.onward(step)
        return carry

    lax.fori_loop(start, stop, body, 0)


def weight_rings(at, w_out, w_down, full_up, full_out, full_down, sends, recvs):
    me = at.group
    half = w_out.shape[0] // 2
    side = w_out.shape[1] // 2

    def halves(own, full, slot):
        return [
            Passing(
                at, way,
                own.at[pl.ds(way * half, half), pl.ds(c * side, side)],
                lambda which, way=way, c=c: full.at[which, pl.ds(way * half, half), pl.ds(c * side, side)],
                sends.at[slot + 2 * c + way], recvs.at[slot + 2 * c + way],
            )
            for c in (0, 1)
            for way in (0, 1)
        ]

    ups = []
    for order in (0, 1):
        for way in (0, 1):
            relation = RELATIONS[way][order]
            slot = 8 + 2 * order + way
            ups.append(
                Passing(
                    at, way, full_up.at[flip(me, relation), at.inner],
                    lambda which, relation=relation: full_up.at[flip(me, relation), which],
                    sends.at[slot], recvs.at[slot],
                )
            )
    return halves(w_out, full_out, 0), ups, halves(w_down, full_down, 4)


def rotated(value, cosine, sine, scale):
    half = QKH // 2
    first, second = value[:, :half], value[:, half:]
    return jnp.concatenate(
        [(first * cosine - second * sine) * scale, (second * cosine + first * sine) * scale], axis=1
    )


def forward_kernel(
    total, w_in, w_up, w_out, w_down, tok, cot, pack, rates, seq_cols, seq_rows, curves,
    full_in, full_up, full_out, full_down, full_seed, o_turned, o_query, o_keys, o_values, o_gate, o_mixed,
    o_gated, hidden, full_two, own_seed, cosine, sine, growth, shrink, powers, ident_col, ident_row, gains,
    gain_group,
    win, part, x, query, keys, values, gate, mixed, gated, wo, core_in, out_x, in_x, low, full_vec,
    ring_send, ring_recv, own_sem, load_sem, store_sem, row_send, row_recv, row_own,
    swap_send, swap_recv, swap_own, vec_send, vec_recv,
):
    at = Place(total)
    me, inner = at.group, at.inner
    core, across = at.peer(1), at.peer(2)
    others = [(me, lax.rem(inner + n, total)) for n in range(1, total)]
    greet([core, across, at.peer(3)] + others)
    rows, width = tok.shape
    count = GROUP * rows
    heads = HEADS // GROUP
    r_in = w_in.shape[0]
    up_width = full_up.shape[-1]
    pieces = column_pieces()
    step_rows = 32

    def rows_in(group_index, which):
        return pl.ds(pl.multiple_of((group_index * total + which) * r_in, r_in), r_in)

    last = len(pieces)

    def swap(relation, slot):
        other = flip(me, relation)
        if slot < last:
            base, stride, h, off, size = pieces[slot]
            src = w_in.at[:, pl.ds(pl.multiple_of(base + other * stride, 128), size)]
            dst = win.at[h, rows_in(me, inner), pl.ds(off, size)]
        elif slot == last:
            src = w_up.at[:, pl.ds(pl.multiple_of(other * up_width, 128), up_width)]
            dst = full_up.at[me, inner]
        elif slot == last + 1:
            src, dst = pack, full_vec.at[inner, me]
        elif slot == last + 2:
            src, dst = tok, part.at[me]
        else:
            src, dst = own_seed, full_seed.at[me]
        if relation == 0:
            return pltpu.make_async_copy(src, dst, swap_own.at[slot])
        return remote(
            src, dst, swap_send.at[relation - 1, slot], swap_recv.at[relation - 1, slot], at.peer(relation)
        )

    def arrived(relation, slot):
        if relation == 0:
            swap(0, slot).wait()
        else:
            swap(relation, slot).wait_recv()

    for relation in (1, 0, 2, 3):
        for slot in range(last):
            swap(relation, slot).start()
    for relation in range(4):
        swap(relation, last + 1).start()
    for slot in (last + 2, last):
        for relation in (1, 0, 2, 3):
            swap(relation, slot).start()

    def in_ring(relation, way, slot):
        def place(which):
            return win.at[:, rows_in(flip(me, relation), which), :]

        return Passing(at, way, place(inner), place, ring_send.at[slot], ring_recv.at[slot])

    near = [in_ring(0, 0, 12), in_ring(1, 1, 13)]
    far_in = [in_ring(2, 0, 14), in_ring(3, 1, 15)]
    for relation in (0, 1):
        for slot in range(last):
            arrived(relation, slot)
        near[relation].begin()

    def layout_of(b, down):
        shape = (rows, 1) if down else (1, rows)
        source = seq_rows if down else seq_cols
        lens, owner, offset = source[0], source[1], source[2]
        positions = lax.broadcasted_iota(jnp.int32, shape, 0 if down else 1)
        inside = (
            (owner == b * total + inner)
            & (lens > 0)
            & (positions >= offset)
            & (positions < offset + lens)
        )
        axis = 1 if down else 0
        number = lax.broadcasted_iota(jnp.int32, lens.shape, axis).astype(F32) + 1.0
        ident = jnp.sum(jnp.where(inside, number, 0.0), axis=axis, keepdims=True) - 1.0
        starts = jnp.sum(jnp.where(inside, offset.astype(F32), 0.0), axis=axis, keepdims=True)
        places = jnp.where(ident >= 0.0, positions.astype(F32) - starts, 0.0)
        return ident, places

    for b in range(GROUP):
        ident_col[b] = layout_of(b, True)[0]
        ident_row[b] = layout_of(b, False)[0]

    def seed_rows(n, carry):
        s = pl.ds(pl.multiple_of(n * step_rows, step_rows), step_rows)
        valid = jnp.where(ident_col[me, s, :] >= 0.0, 1.0, 0.0)
        own_seed[s, :] = (cot[s, :].astype(F32) * valid).astype(BF16)
        return carry

    lax.fori_loop(0, rows // step_rows, seed_rows, 0)

    for relation in range(4):
        arrived(relation, last + 1)

    def spread(n):
        target = lax.rem(inner + n, total)
        return remote(
            full_vec.at[inner], full_vec.at[inner], vec_send.at[n - 1], vec_recv.at[n - 1], (me, target)
        )

    for n in range(1, total):
        spread(n).start()
    for ring in near:
        ring.onward(1)
    for relation in (2, 3):
        for slot in range(last):
            arrived(relation, slot)
        far_in[relation - 2].begin()
    for relation in (1, 0, 2, 3):
        swap(relation, last + 3).start()

    def both_in(step, carry):
        for ring in near:
            ring.onward(step)
        for ring in far_in:
            ring.onward(step - 1)
        return carry

    def take_vectors():
        for n in range(1, total):
            spread(n).wait_recv()
        quarter = width // GROUP
        small = quarter // total
        large = heads * VH // total
        for d in range(GROUP):
            tiles = {}
            for f in range(total):
                t = f * small // 128
                value = full_vec[f, d]
                tiles[t] = tiles[t] + value if t in tiles else value
            for t, value in tiles.items():
                gains[:, d * quarter + t * 128 : d * quarter + (t + 1) * 128] = value
        tiles = {}
        for f in range(total):
            t = f * large // 128
            value = full_vec[f, me, 4:5, :]
            tiles[t] = tiles[t] + value if t in tiles else value
        for t, value in tiles.items():
            h, off = t * 128 // VH, t * 128 % VH
            gain_group[h, :, off : off + 128] = value

    def make_tables():
        distance = lax.broadcasted_iota(jnp.int32, (rows, rows), 0) - lax.broadcasted_iota(
            jnp.int32, (rows, rows), 1
        )
        away = jnp.maximum(distance, 0).astype(F32)
        for h in range(heads):
            powers[h] = jnp.where(distance >= 0, jnp.exp(rates[h] * away), 0.0)
        for b in range(GROUP):
            places = layout_of(b, True)[1]
            angles = places * curves[0:1, :]
            r = slice(b * rows, (b + 1) * rows)
            cosine[r, :] = jnp.cos(angles)
            sine[r, :] = jnp.sin(angles)
            lift = places * (1.0 / 512.0) * curves[1:2, :]
            growth[r, :] = jnp.exp(lift)
            shrink[r, :] = jnp.exp(-lift)

    def norm_buffer(relation):
        b = flip(me, relation)
        arrived(relation, last + 2)

        def norm_rows(n, carry):
            r = pl.multiple_of(n * step_rows, step_rows)
            normal, _ = norm_parts(part[b, pl.ds(r, step_rows), :].astype(F32), EPSILON)
            at_rows = pl.ds(pl.multiple_of(b * rows + r, step_rows), step_rows)
            x[at_rows, :] = (normal * gains[0:1, :] + gains[1:2, :]).astype(BF16)
            return carry

        lax.fori_loop(0, rows // step_rows, norm_rows, 0)

    beside = [
        make_tables,
        take_vectors,
        lambda: (norm_buffer(0), norm_buffer(1)),
        lambda: norm_buffer(2),
        lambda: norm_buffer(3),
    ]
    cuts = [2 + (total - 3) * n // 5 for n in range(6)]
    for n in range(5):
        lax.fori_loop(cuts[n], cuts[n + 1], both_in, 0)
        beside[n]()
    for ring in far_in:
        ring.onward(total - 2)
    outs, ups, downs = weight_rings(
        at, w_out, w_down, full_up, full_out, full_down, ring_send, ring_recv
    )
    for ring in outs:
        ring.begin()
    own_copies = [
        pltpu.make_async_copy(w_out, full_out.at[inner], own_sem.at[0]),
        pltpu.make_async_copy(w_down, full_down.at[inner], own_sem.at[1]),
    ]
    for copy in own_copies:
        copy.start()
    for ring in near + far_in:
        ring.finish()
    store_win = pltpu.make_async_copy(win, full_in, load_sem.at[1])
    store_win.start()

    tile = 512
    spots = 6
    plan = tick_plan(total, spots)
    span = [stop - start for start, stop in plan]

    def spot(h, number):
        lows = [plan[k * (spots // heads) + number][0] for k in range(heads)]
        highs = [plan[k * (spots // heads) + number][1] for k in range(heads)]
        low_step = lows[0] + h * (lows[1] - lows[0])
        high_step = highs[0] + h * (highs[1] - highs[0])
        run_steps(outs, low_step, high_step)

    def project(h, off):
        def at_tile(m, use):
            r = pl.ds(pl.multiple_of(m * tile, tile), tile)
            use(r, dot(x[r, :], win[h, :, off : off + QKH]))

        return at_tile

    def head(h, carry):
        def rotate_tiles(m, carry):
            def put_query(r, value):
                turned = rotated(value, cosine[r, :], sine[r, :], growth[r, :])
                query[h, r, :] = (turned * QKH ** (-0.5)).astype(BF16)

            def put_keys(r, value):
                keys[h, r, :] = rotated(value, cosine[r, :], sine[r, :], shrink[r, :]).astype(BF16)

            project(h, 0)(m, put_query)
            project(h, QKH)(m, put_keys)
            return carry

        lax.fori_loop(0, count // tile, rotate_tiles, 0)
        spot(h, 0)

        def plain_tiles(m, carry):
            for c in range(VH // QKH):
                off = c * QKH

                def put_values(r, value, off=off):
                    values[h, r, off : off + QKH] = value.astype(BF16)

                def put_gate(r, value, off=off):
                    gate[h, r, off : off + QKH] = value

                project(h, 2 * QKH + off)(m, put_values)
                project(h, 2 * QKH + VH + off)(m, put_gate)
            return carry

        lax.fori_loop(0, count // tile, plain_tiles, 0)
        spot(h, 1)

        def buffer(b, carry):
            r = pl.ds(pl.multiple_of(b * rows, rows), rows)
            raw = dot_back(query[h, r, :], keys[h, r, :])
            linked = (ident_col[b] == ident_row[b]) & (ident_col[b] >= 0.0)
            masked = (raw * jnp.where(linked, powers[h], 0.0)).astype(BF16)
            value = dot(masked, values[h, r, :])
            mixed[h, r, :] = value
            normal, _ = norm_parts(value, GROUP_EPSILON)
            z = gate[h, r, :]
            result = z / (1.0 + jnp.exp(-z)) * (normal * gain_group[h])
            gated[r, pl.ds(pl.multiple_of(h * VH, VH), VH)] = result.astype(BF16)
            return carry

        lax.fori_loop(0, GROUP, buffer, 0)
        spot(h, 2)
        return carry

    lax.fori_loop(0, heads, head, 0)
    for relation in range(4):
        arrived(relation, last)
    for ring in ups + downs:
        ring.begin()
    for ring in outs:
        ring.finish()
    stores = [
        pltpu.make_async_copy(src, dst, store_sem.at[1 + n])
        for n, (src, dst) in enumerate(
            ((query, o_query), (keys, o_keys), (values, o_values), (gate, o_gate), (mixed, o_mixed), (gated, o_gated))
        )
    ]
    for copy in stores:
        copy.start()
    own_copies[0].wait()
    block = w_out.shape[0]
    fetch = pltpu.make_async_copy(full_out, wo, load_sem.at[0])
    fetch.start()
    fetch.wait()

    chunks = 4
    size = rows // chunks
    rest = ups + downs
    later = tick_plan(total, 6)

    def branch(relation):
        b = flip(me, relation)

        def column(n, carry):
            wide = 512
            c = pl.ds(pl.multiple_of(n * wide, wide), wide)
            r = pl.ds(pl.multiple_of(b * rows, rows), rows)
            acc = jnp.zeros((rows, wide), F32)
            piece = gated[r, :]
            acc = dot(piece, wo[:, :, c].reshape(total * block, wide))
            part[b, :, c] = acc.astype(BF16)
            return carry

        lax.fori_loop(0, width // 512, column, 0)

    def rows_of(c):
        return pl.ds(c * size, size)

    far = flip(me, 2)

    def copy(kind, c):
        r = rows_of(c)
        if kind == 0:
            src, dst, dev = part.at[flip(me, 3), r], core_in.at[0, r], core
        elif kind == 1:
            src, dst, dev = part.at[flip(me, 1), r], core_in.at[1, r], core
        elif kind == 2:
            src, dst, dev = out_x.at[r], in_x.at[r], across
        elif kind == 3:
            src, dst, dev = low.at[r], full_two.at[me, r], across
        elif kind == 4:
            src, dst, dev = low.at[r], full_two.at[me, r], core
        else:
            src, dst, dev = full_two.at[far, r], full_two.at[far, r], core
        return remote(src, dst, row_send.at[kind, c], row_recv.at[kind, c], dev)

    def store(c):
        r = rows_of(c)
        return pltpu.make_async_copy(low.at[r], full_two.at[me, r], row_own.at[c])

    branch(3)
    for c in range(chunks):
        copy(0, c).start()
    branch(2)
    for c in range(chunks):
        r = rows_of(c)
        copy(0, c).wait_recv()
        out_x[r, :] = (part[far, r, :].astype(F32) + core_in[0, r, :].astype(F32)).astype(BF16)
        copy(2, c).start()
    branch(1)
    for c in range(chunks):
        copy(1, c).start()
    branch(0)
    run_steps(rest, *later[0])

    def turn(n, carry):
        i, j = n // (count // 256), lax.rem(n, count // 256)
        i, j = (pl.ds(pl.multiple_of(k * 256, 256), 256) for k in (i, j))
        win[0, i, j] = x[j, i].T
        return carry

    store_win.wait()
    wait_sent(near + far_in, total)
    lax.fori_loop(0, (width // 256) * (count // 256), turn, 0)
    store_turned = pltpu.make_async_copy(win.at[0, :, pl.ds(0, count)], o_turned, store_sem.at[0])
    store_turned.start()
    for c in range(chunks):
        r = rows_of(c)
        copy(1, c).wait_recv()
        copy(2, c).wait_recv()

        def finish_rows(n, carry, c=c):
            s = pl.ds(pl.multiple_of(c * size + n * step_rows, step_rows), step_rows)
            value = tok[s, :].astype(F32) + (
                part[me, s, :].astype(F32) + core_in[1, s, :].astype(F32) + in_x[s, :].astype(F32)
            )
            hidden[s, :] = value
            normal, _ = norm_parts(value, EPSILON)
            low[s, :] = (normal * gains[2:3, :] + gains[3:4, :]).astype(BF16)
            return carry

        lax.fori_loop(0, size // step_rows, finish_rows, 0)
        copy(3, c).start()
        copy(4, c).start()
        store(c).start()
        if c % 2:
            run_steps(rest, *later[1 + c // 2])
    for c in range(chunks):
        copy(3, c).wait_recv()
        copy(5, c).start()
        if c % 2:
            run_steps(rest, *later[3 + c // 2])
    for c in range(chunks):
        copy(4, c).wait_recv()
        copy(5, c).wait_recv()
        store(c).wait()
        for kind in range(6):
            copy(kind, c).wait_send()
    run_steps(rest, *later[5])
    for ring in rest:
        ring.finish()
    wait_sent(outs + rest, total)
    own_copies[1].wait()
    arrived(0, last + 3)
    for relation in (1, 2, 3):
        arrived(relation, last + 3)
        for slot in range(last + 4):
            swap(relation, slot).wait_send()
    for n in range(1, total):
        spread(n).wait_send()
    store_turned.wait()
    for c in stores:
        c.wait()


def forward(total, w_in, w_up, w_out, w_down, tok, cot, pack, rates, seq_cols, seq_rows):
    rows, width = tok.shape
    count = GROUP * rows
    heads = HEADS // GROUP
    head_width = 2 * (QKH + VH)
    vmem, hbm = pl.BlockSpec(memory_space=pltpu.VMEM), pl.BlockSpec(memory_space=ANY)
    dma = pltpu.SemaphoreType.DMA
    pair = np.arange(QKH // 2) / (QKH // 2)
    curves = np.zeros((8, QKH // 2), np.float32)
    curves[0] = 10000.0**-pair
    curves[1] = np.log((pair + 0.4) / 1.4)
    kept = (
        ((heads, count, QKH), BF16),
        ((heads, count, QKH), BF16),
        ((heads, count, VH), BF16),
        ((heads, count, VH), F32),
        ((heads, count, VH), F32),
        ((count, heads * VH), BF16),
    )
    in_hbm = (
        ((heads, width, head_width), BF16),
        ((GROUP, total, w_up.shape[0], w_up.shape[1] // GROUP), BF16),
        ((total,) + w_out.shape, BF16),
        ((total,) + w_down.shape, BF16),
        ((GROUP, rows, width), BF16),
        ((width, count), BF16),
        *kept,
    )
    in_vmem = (
        ((rows, width), BF16),
        ((count, QKH // 2), F32),
        ((count, QKH // 2), F32),
        ((count, QKH // 2), F32),
        ((count, QKH // 2), F32),
        ((heads, rows, rows), F32),
        ((GROUP, rows, 1), F32),
        ((GROUP, 1, rows), F32),
        ((8, width), F32),
        ((heads, 1, VH), F32),
    )
    shapes = (*in_hbm, ((rows, width), F32), ((GROUP, rows, width), BF16), *in_vmem)
    return pl.pallas_call(
        functools.partial(forward_kernel, total),
        out_shape=[jax.ShapeDtypeStruct(s, d) for s, d in shapes],
        in_specs=[hbm] * 4 + [vmem] * 7,
        out_specs=[hbm] * len(in_hbm) + [vmem, hbm] + [vmem] * len(in_vmem),
        scratch_shapes=[
            pltpu.VMEM((heads, width, head_width), BF16),
            pltpu.VMEM((GROUP, rows, width), BF16),
            pltpu.VMEM((count, width), BF16),
            *[pltpu.VMEM(s, d) for s, d in kept],
            pltpu.VMEM((total,) + w_out.shape, BF16),
            pltpu.VMEM((2, rows, width), BF16),
            pltpu.VMEM((rows, width), BF16),
            pltpu.VMEM((rows, width), BF16),
            pltpu.VMEM((rows, width), BF16),
            pltpu.VMEM((total, GROUP, 8, 128), F32),
            dma((16, total - 1)), dma((16, total - 1)), dma((2,)), dma((2,)),
            dma((7,)), dma((6, 4)), dma((6, 4)), dma((4,)),
            dma((3, 12)), dma((3, 12)), dma((12,)), dma((total - 1,)), dma((total - 1,)),
        ],
        compiler_params=pltpu.CompilerParams(
            collective_id=1, has_side_effects=True, vmem_limit_bytes=63 * MIB
        ),
        name="forward_retention",
    )(w_in, w_up, w_out, w_down, tok, cot, pack, rates, seq_cols, seq_rows, jnp.asarray(curves))


class Adding:
    def __init__(self, at, way, term, arrived, sends, recvs):
        self.at, self.way, self.term, self.arrived = at, way, term, arrived
        self.sends, self.recvs = sends, recvs

    def hop(self, step, first=False):
        src = self.term(self.at.behind(self.way, 1)) if first else self.arrived.at[step - 1]
        return remote(
            src, self.arrived.at[step], self.sends.at[step], self.recvs.at[step], self.at.neighbour(self.way)
        )

    def begin(self):
        self.hop(0, True).start()

    def sum_at(self, step, which):
        self.hop(step, True).wait_recv()
        return self.arrived[step].astype(F32) + self.term(which)[...].astype(F32)

    def onward(self, step):
        self.arrived[step - 1] = self.sum_at(step - 1, self.at.behind(self.way, step + 1)).astype(BF16)
        self.hop(step).start()

    def finish(self):
        return self.sum_at(self.at.total - 2, self.at.inner)


def wait_added(rings, total):
    def body(step, carry):
        for ring in rings:
            ring.hop(step, True).wait_send()
        return carry

    lax.fori_loop(0, total - 1, body, 0)


def backward_kernel(
    total, g_down, two, d_upper, part, seed, hidden, gains_all, h_gated, h_out, h_query, h_keys, h_values, h_gate,
    h_mixed, cosine, sine, growth, shrink, powers, ident_col, ident_row, gain_group,
    o_down, o_up, o_out, d_hidden, full_branch, sums, o_group, o_project,
    g_up, g_out, arrived, wide_buf, narrow_buf, wo, own_part, core_in, out_x, in_x, low,
    query, keys, values, gate, mixed, back, d_mixed, staged, stage, landed,
    ring_send, ring_recv, row_send, row_recv, row_own, load_sem, unit_sem, out_sem, a2a_send, a2a_recv,
):
    at = Place(total)
    me = at.group
    core, across = at.peer(1), at.peer(2)
    greet([core, across, at.peer(3), at.neighbour(0), at.neighbour(1)])
    rows, width = seed.shape
    count = GROUP * rows
    heads = HEADS // GROUP
    r_up, r_out = o_up.shape[0], o_out.shape[0]
    up_width = o_up.shape[1] // GROUP
    half, side = r_out // 2, width // 2

    def halves(source, base):
        return [
            Adding(
                at, way,
                lambda which, way=way, c=c: source.at[
                    pl.ds(pl.multiple_of(which * r_out + way * half, half), half), pl.ds(c * side, side)
                ],
                arrived.at[base + 2 * c + way], ring_send.at[base + 2 * c + way], ring_recv.at[base + 2 * c + way],
            )
            for c in (0, 1)
            for way in (0, 1)
        ]

    downs, outs, ups = halves(g_down, 0), halves(g_out, 8), []
    for order in (0, 1):
        for way in (0, 1):
            relation = RELATIONS[way][order]
            slot = 4 + 2 * order + way
            ups.append(
                Adding(
                    at, way,
                    lambda which, relation=relation: g_up.at[
                        pl.ds(pl.multiple_of((flip(me, relation) * total + which) * r_up, r_up), r_up), :
                    ],
                    arrived.at[slot], ring_send.at[slot], ring_recv.at[slot],
                )
            )

    chunks = 4
    size = rows // chunks
    step_rows = 32
    far = flip(me, 2)

    def rows_of(c):
        return pl.ds(c * size, size)

    def copy(kind, c):
        r = rows_of(c)
        if kind == 0:
            src, dst, dev = part.at[flip(me, 3), r], core_in.at[0, r], core
        elif kind == 1:
            src, dst, dev = part.at[flip(me, 1), r], core_in.at[1, r], core
        elif kind == 2:
            src, dst, dev = out_x.at[r], in_x.at[r], across
        elif kind == 3:
            src, dst, dev = low.at[r], full_branch.at[me, r], across
        elif kind == 4:
            src, dst, dev = low.at[r], full_branch.at[me, r], core
        else:
            src, dst, dev = full_branch.at[far, r], full_branch.at[far, r], core
        return remote(src, dst, row_send.at[kind, c], row_recv.at[kind, c], dev)

    def load(which, c):
        r = rows_of(c)
        source = far if which == 0 else me
        return pltpu.make_async_copy(part.at[source, r], own_part.at[which, r], row_own.at[which, c])

    def store(c):
        r = rows_of(c)
        return pltpu.make_async_copy(low.at[r], full_branch.at[me, r], row_own.at[2, c])

    for which in (0, 1):
        for c in range(chunks):
            copy(which, c).start()
            load(which, c).start()
    for ring in downs:
        ring.begin()
    fetch_two = pltpu.make_async_copy(two, wide_buf, load_sem.at[0])
    fetch_upper = pltpu.make_async_copy(d_upper, narrow_buf, load_sem.at[1])
    fetch_out = pltpu.make_async_copy(h_out, wo, load_sem.at[2])
    for fetch in (fetch_two, fetch_upper, fetch_out):
        fetch.start()

    def unit_loads(unit, slot):
        h, b = unit // GROUP, lax.rem(unit, GROUP)
        r = pl.ds(pl.multiple_of(b * rows, rows), rows)
        pairs = ((h_query, query), (h_keys, keys), (h_values, values), (h_gate, gate), (h_mixed, mixed))
        return [
            pltpu.make_async_copy(src.at[h, r], dst.at[slot], unit_sem.at[slot, n])
            for n, (src, dst) in enumerate(pairs)
        ]

    for unit in (0, 1):
        for fetch in unit_loads(jnp.int32(unit), unit):
            fetch.start()

    def send_sums(c):
        r = rows_of(c)
        load(0, c).wait()
        copy(0, c).wait_recv()
        out_x[r, :] = (own_part[0, r, :].astype(F32) + core_in[0, r, :].astype(F32)).astype(BF16)
        copy(2, c).start()

    def norm_back(c):
        load(1, c).wait()
        copy(1, c).wait_recv()
        copy(2, c).wait_recv()

        def some_rows(n, carry):
            s = pl.ds(pl.multiple_of(c * size + n * step_rows, step_rows), step_rows)
            e = own_part[1, s, :].astype(F32) + core_in[1, s, :].astype(F32) + in_x[s, :].astype(F32)
            normal, scale = norm_parts(hidden[s, :], EPSILON)
            with_gain = e * gains_all[2:3, :]
            sums[0:1, :] += jnp.sum(e * normal, axis=0, keepdims=True)
            sums[1:2, :] += jnp.sum(e, axis=0, keepdims=True)
            value = seed[s, :].astype(F32) + scale * (
                with_gain
                - jnp.mean(with_gain, axis=-1, keepdims=True)
                - normal * jnp.mean(with_gain * normal, axis=-1, keepdims=True)
            )
            d_hidden[s, :] = value
            low[s, :] = value.astype(BF16)
            return carry

        lax.fori_loop(0, size // step_rows, some_rows, 0)
        copy(3, c).start()
        copy(4, c).start()
        store(c).start()

    sums[...] = jnp.zeros_like(sums)
    o_group[...] = jnp.zeros_like(o_group)
    for c in range(chunks):
        send_sums(c)
    plan = tick_plan(total, 6)
    add_steps(downs, *plan[0])
    fetch_two.wait()
    fetch_upper.wait()

    def grad_tiles(left, right, out, start, stop):
        wide = 512

        def tile(n, carry):
            rows_n = right.shape[1] // wide
            i, j = n // rows_n, lax.rem(n, rows_n)
            a = pl.ds(pl.multiple_of(i * 256, 256), 256)
            c = pl.ds(pl.multiple_of(j * wide, wide), wide)
            out[a, c] = dot_rows(left[:, a], right[:, c]).astype(BF16)
            return carry

        lax.fori_loop(start, stop, tile, 0)

    tiles = (width // 256) * (up_width // 512)
    for quarter in range(4):
        grad_tiles(wide_buf, narrow_buf, g_up, tiles * quarter // 4, tiles * (quarter + 1) // 4)
        if quarter:
            norm_back(quarter - 1)
        add_steps(downs, *plan[1 + quarter])
    norm_back(3)
    add_steps(downs, *plan[5])
    for ring in ups:
        ring.begin()
    fetch_gated = pltpu.make_async_copy(h_gated, narrow_buf, load_sem.at[1])
    fetch_gated.start()
    for n, ring in enumerate(downs):
        c, way = n // 2, n % 2
        o_down[pl.ds(way * half, half), pl.ds(c * side, side)] = ring.finish()
    for c in range(chunks):
        copy(3, c).wait_recv()
        copy(5, c).start()
        if c % 2:
            add_steps(ups, *plan[c // 2])
    for c in range(chunks):
        copy(4, c).wait_recv()
        copy(5, c).wait_recv()
        store(c).wait()
    branch = wide_buf
    fetch_branch = [
        pltpu.make_async_copy(full_branch.at[b], branch.at[pl.ds(b * rows, rows)], load_sem.at[3 + b])
        for b in range(GROUP)
    ]
    for fetch in fetch_branch:
        fetch.start()
    for fetch in fetch_branch:
        fetch.wait()
    fetch_gated.wait()
    fetch_out.wait()
    tiles = (narrow_buf.shape[1] // 256) * (width // 512)
    for quarter in range(4):
        grad_tiles(narrow_buf, branch, g_out, tiles * quarter // 4, tiles * (quarter + 1) // 4)
        add_steps(ups, *plan[2 + quarter])
    for ring in outs:
        ring.begin()

    def sent_across(relation):
        return remote(
            stage.at[relation - 1], landed.at[relation - 1],
            a2a_send.at[relation - 1], a2a_recv.at[relation - 1], at.peer(relation),
        )

    for n, ring in enumerate(ups):
        relation = RELATIONS[n % 2][n // 2]
        value = ring.finish()
        if relation == 0:
            o_up[:, pl.ds(pl.multiple_of(me * up_width, 128), up_width)] = value
        else:
            stage[relation - 1] = value.astype(BF16)
            sent_across(relation).start()

    units = heads * GROUP

    def unit_stores(unit, slot):
        h, b = unit // GROUP, lax.rem(unit, GROUP)
        r = pl.ds(pl.multiple_of(b * rows, rows), rows)
        start = pl.multiple_of(h * staged.shape[2], 128)
        return pltpu.make_async_copy(
            staged.at[slot], o_project.at[r, pl.ds(start, staged.shape[2])], out_sem.at[slot]
        )

    def unrotated(value, r, scale):
        mid = QKH // 2
        first, second = value[:, :mid], value[:, mid:]
        c, s = cosine[r, :], sine[r, :]
        return jnp.concatenate(
            [(first * c + second * s) * scale, (second * c - first * s) * scale], axis=1
        )

    def unit_body(unit, carry):
        slot = lax.rem(unit, 2)
        h, b = unit // GROUP, lax.rem(unit, GROUP)
        r = pl.ds(pl.multiple_of(b * rows, rows), rows)
        back[...] = dot_back(branch[r, :], wo[pl.ds(pl.multiple_of(h * VH, VH), VH), :])
        for fetch in unit_loads(unit, slot):
            fetch.wait()

        @pl.when(unit >= 2)
        def _():
            unit_stores(unit - 2, slot).wait()

        gains = gain_group[h]

        def some_rows(n, carry):
            s = pl.ds(pl.multiple_of(n * step_rows, step_rows), step_rows)
            normal, scale = norm_parts(mixed[slot, s, :], GROUP_EPSILON)
            z = gate[slot, s, :]
            f = back[s, :]
            sigmoid = 1.0 / (1.0 + jnp.exp(-z))
            silu = z * sigmoid
            d_silu = f * (normal * gains)
            staged[slot, s, 2 * QKH + VH :] = (d_silu * (sigmoid + silu * (1.0 - sigmoid))).astype(BF16)
            d_scaled = f * silu
            o_group[h] += jnp.sum(d_scaled * normal, axis=0, keepdims=True)
            d_normal = d_scaled * gains
            d_mixed[s, :] = (
                scale
                * (
                    d_normal
                    - jnp.mean(d_normal, axis=-1, keepdims=True)
                    - normal * jnp.mean(d_normal * normal, axis=-1, keepdims=True)
                )
            ).astype(BF16)
            return carry

        lax.fori_loop(0, rows // step_rows, some_rows, 0)
        linked = (ident_col[b] == ident_row[b]) & (ident_col[b] >= 0.0)
        decay = jnp.where(linked, powers[h], 0.0)
        masked = (dot_back(query[slot], keys[slot]) * decay).astype(BF16)
        staged[slot, :, 2 * QKH : 2 * QKH + VH] = dot_rows(masked, d_mixed[...]).astype(BF16)
        d_raw = (dot_back(d_mixed[...], values[slot]) * decay).astype(BF16)
        d_query = dot(d_raw, keys[slot]) * QKH ** (-0.5)
        staged[slot, :, :QKH] = unrotated(d_query, r, growth[r, :]).astype(BF16)
        d_keys = dot_rows(d_raw, query[slot])
        staged[slot, :, QKH : 2 * QKH] = unrotated(d_keys, r, shrink[r, :]).astype(BF16)
        unit_stores(unit, slot).start()

        @pl.when(unit + 2 < units)
        def _():
            for fetch in unit_loads(unit + 2, slot):
                fetch.start()

        steps = total - 2
        add_steps(outs, 1 + (steps * unit) // units, 1 + (steps * (unit + 1)) // units)
        return carry

    lax.fori_loop(0, units, unit_body, 0)
    for relation in (1, 2, 3):
        sent_across(relation).wait_recv()
        o_up[:, pl.ds(pl.multiple_of(flip(me, relation) * up_width, 128), up_width)] = landed[
            relation - 1
        ].astype(F32)
        sent_across(relation).wait_send()
    for slot in (0, 1):
        unit_stores(jnp.int32(units - 2 + slot), slot).wait()
    for n, ring in enumerate(outs):
        c, way = n // 2, n % 2
        o_out[pl.ds(way * half, half), pl.ds(c * side, side)] = ring.finish()
    for c in range(chunks):
        for kind in range(6):
            copy(kind, c).wait_send()
    wait_added(downs + ups + outs, total)


def add_steps(rings, start, stop):
    def body(step, carry):
        for ring in rings:
            ring.onward(step)
        return carry

    lax.fori_loop(start, stop, body, 0)


def backward(
    total, g_down, two, d_upper, part, seed, hidden, gain_two, gated, full_out, query, keys, values, gate, mixed,
    tables, powers, ident_col, ident_row, gain_group,
):
    rows, width = seed.shape
    count = GROUP * rows
    heads = HEADS // GROUP
    up_width = d_upper.shape[1]
    r_out, r_up = g_down.shape[0] // total, width // GROUP // total
    half, side = r_out // 2, width // 2
    vmem, hbm = pl.BlockSpec(memory_space=pltpu.VMEM), pl.BlockSpec(memory_space=ANY)
    dma = pltpu.SemaphoreType.DMA
    shapes = (
        ((r_out, width), F32),
        ((r_up, up_width * GROUP), F32),
        ((r_out, width), F32),
        ((rows, width), F32),
        ((GROUP, rows, width), BF16),
        ((8, width), F32),
        ((heads, 1, VH), F32),
        ((count, 2 * heads * (QKH + VH)), BF16),
    )
    return pl.pallas_call(
        functools.partial(backward_kernel, total),
        out_shape=[jax.ShapeDtypeStruct(s, d) for s, d in shapes],
        in_specs=[vmem, hbm, hbm, hbm, vmem, vmem, vmem] + [hbm] * 7 + [vmem] * 8,
        out_specs=[vmem] * 4 + [hbm, vmem, vmem, hbm],
        scratch_shapes=[
            pltpu.VMEM((width, up_width), BF16),
            pltpu.VMEM(g_down.shape, BF16),
            pltpu.VMEM((12, total - 1, half, side), BF16),
            pltpu.VMEM((count, width), BF16),
            pltpu.VMEM((count, up_width), BF16),
            pltpu.VMEM(full_out.shape, BF16),
            pltpu.VMEM((2, rows, width), BF16),
            pltpu.VMEM((2, rows, width), BF16),
            pltpu.VMEM((rows, width), BF16),
            pltpu.VMEM((rows, width), BF16),
            pltpu.VMEM((rows, width), BF16),
            pltpu.VMEM((2, rows, QKH), BF16),
            pltpu.VMEM((2, rows, QKH), BF16),
            pltpu.VMEM((2, rows, VH), BF16),
            pltpu.VMEM((2, rows, VH), F32),
            pltpu.VMEM((2, rows, VH), F32),
            pltpu.VMEM((rows, VH), F32),
            pltpu.VMEM((rows, VH), BF16),
            pltpu.VMEM((2, rows, 2 * (QKH + VH)), BF16),
            pltpu.VMEM((3, r_up, up_width), BF16),
            pltpu.VMEM((3, r_up, up_width), BF16),
            dma((12, total - 1)), dma((12, total - 1)), dma((6, 4)), dma((6, 4)), dma((3, 4)), dma((7,)),
            dma((2, 5)), dma((2,)), dma((3,)), dma((3,)),
        ],
        compiler_params=pltpu.CompilerParams(
            collective_id=2, has_side_effects=True, vmem_limit_bytes=63 * MIB
        ),
        name="backward_retention",
    )(
        g_down, two, d_upper, part, seed, hidden, gain_two, gated, full_out, query, keys, values, gate, mixed,
        *tables, powers, ident_col, ident_row, gain_group,
    )


def final_kernel(
    total, h_project, h_in, h_turned, part_down, hidden, d_hidden, tok, gains_all, ident_col, sums_two, d_group,
    o_in, output, d_tokens, o_vec, o_grp,
    project, turned, first_term, term, arrived, win, part, own_part, core_in, out_x, in_x, stage, landed,
    vec, grp, near_in, mid, far_in, far_grp,
    load_sem, win_sem, ring_send, ring_recv, a2a_send, a2a_recv, row_send, row_recv, row_own,
    near_send, near_recv, far_send, far_recv,
):
    at = Place(total)
    me, inner = at.group, at.inner
    others = [(me, lax.rem(inner + n, total)) for n in range(1, total)]
    greet([at.peer(r) for r in (1, 2, 3)] + others)
    rows, width = tok.shape
    count = GROUP * rows
    block = o_in.shape[0]
    step_rows = 32

    fetch_turned = pltpu.make_async_copy(h_turned, turned, load_sem.at[0])
    fetch_project = pltpu.make_async_copy(h_project, project, load_sem.at[1])
    fetch_turned.start()
    fetch_project.start()

    def source(n, b):
        if n == 0:
            return part_down.at[b]
        return part.at[pl.ds(pl.multiple_of(b * rows, rows), rows), :]

    def row_copy(kind, n):
        if kind < 2:
            return remote(
                source(n, flip(me, 3 - 2 * kind)), core_in.at[n, kind], row_send.at[n, kind], row_recv.at[n, kind],
                at.peer(1),
            )
        return remote(out_x.at[n], in_x.at[n], row_send.at[n, 2], row_recv.at[n, 2], at.peer(2))

    def row_load(which):
        return pltpu.make_async_copy(
            source(0, flip(me, 2) if which == 0 else me), own_part.at[which], row_own.at[which]
        )

    def own_rows(n, which, r):
        if n == 0:
            return own_part[which, pl.ds(r, step_rows), :]
        b = flip(me, 2) if which == 0 else me
        return part[pl.ds(pl.multiple_of(b * rows + r, step_rows), step_rows), :]

    def by_rows(body):
        def some(k, carry):
            body(pl.multiple_of(k * step_rows, step_rows))
            return carry

        lax.fori_loop(0, rows // step_rows, some, 0)

    def send_rows(n):
        row_copy(0, n).wait_recv()

        def some(r):
            s = pl.ds(r, step_rows)
            out_x[n, s, :] = (own_rows(n, 0, r).astype(F32) + core_in[n, 0, s, :].astype(F32)).astype(BF16)

        by_rows(some)
        row_copy(2, n).start()

    def summed_rows(n, r):
        s = pl.ds(r, step_rows)
        return own_rows(n, 1, r).astype(F32) + core_in[n, 1, s, :].astype(F32) + in_x[n, s, :].astype(F32)

    def take_down():
        row_copy(1, 0).wait_recv()
        row_copy(2, 0).wait_recv()

        def some(r):
            s = pl.ds(r, step_rows)
            valid = jnp.where(ident_col[me, s, :] >= 0.0, 1.0, 0.0)
            output[s, :] = ((hidden[s, :] + summed_rows(0, r)) * valid).astype(BF16)

        by_rows(some)

    def take_rows():
        row_copy(1, 1).wait_recv()
        row_copy(2, 1).wait_recv()
        vec[...] = jnp.zeros_like(vec)
        vec[2:4, :] = sums_two[0:2, :]

        def some(r):
            s = pl.ds(r, step_rows)
            e = summed_rows(1, r)
            normal, scale = norm_parts(tok[s, :].astype(F32), EPSILON)
            with_gain = e * gains_all[0:1, :]
            vec[0:1, :] += jnp.sum(e * normal, axis=0, keepdims=True)
            vec[1:2, :] += jnp.sum(e, axis=0, keepdims=True)
            value = d_hidden[s, :] + scale * (
                with_gain
                - jnp.mean(with_gain, axis=-1, keepdims=True)
                - normal * jnp.mean(with_gain * normal, axis=-1, keepdims=True)
            )
            d_tokens[s, :] = value.astype(BF16)

        by_rows(some)

    quarter = width // GROUP
    small = quarter // total
    large = grp.shape[1] // total

    def near(relation):
        start = pl.multiple_of(flip(me, relation) * quarter, 128)
        return remote(
            vec.at[:, pl.ds(start, quarter)], near_in.at[relation - 1], near_send.at[relation - 1],
            near_recv.at[relation - 1], at.peer(relation),
        )

    def tile_of(index, size):
        return pl.ds(pl.multiple_of((index * size) // 128 * 128, 128), 128)

    def distant(kind, n):
        target = lax.rem(inner + n, total)
        src = mid.at[:, tile_of(target, small)] if kind == 0 else grp.at[:, tile_of(target, large)]
        dst = far_in if kind == 0 else far_grp
        return remote(
            src, dst.at[n - 1], far_send.at[kind, n - 1], far_recv.at[kind, n - 1], (me, target)
        )

    def vectors_near():
        for relation in (1, 2, 3):
            near(relation).start()
        grp[...] = jnp.zeros_like(grp)
        for h in range(d_group.shape[0]):
            grp[0:1, h * VH : (h + 1) * VH] = d_group[h]

    def vectors_far():
        for relation in (1, 2, 3):
            near(relation).wait_recv()
        mid[...] = (
            vec[:, pl.ds(pl.multiple_of(me * quarter, 128), quarter)] + near_in[0] + near_in[1] + near_in[2]
        )
        for n in range(1, total):
            for kind in (0, 1):
                distant(kind, n).start()

    def vectors_end():
        for n in range(1, total):
            for kind in (0, 1):
                distant(kind, n).wait_recv()
        o_vec[...] = mid[:, tile_of(inner, small)] + jnp.sum(far_in[...], axis=0)
        o_grp[...] = grp[:, tile_of(inner, large)] + jnp.sum(far_grp[...], axis=0)

    wide = 512

    def terms(step, out):
        for way in (0, 1):
            which = at.behind(way, step + 1)
            left = jnp.concatenate(
                [
                    turned[
                        pl.ds(pl.multiple_of((flip(me, relation) * total + which) * block, block), block), :
                    ]
                    for relation in RELATIONS[way]
                ],
                axis=0,
            )

            def tile(n, carry, left=left, way=way):
                c = pl.ds(pl.multiple_of(n * wide, wide), wide)
                value = dot(left, project[:, c]).astype(BF16)
                out[2 * way, :, c] = value[:block]
                out[2 * way + 1, :, c] = value[block:]
                return carry

            lax.fori_loop(0, project.shape[1] // wide, tile, 0)

    def hop(slot, step, first=False):
        src = first_term.at[slot] if first else arrived.at[slot, step - 1]
        return remote(
            src, arrived.at[slot, step], ring_send.at[slot, step], ring_recv.at[slot, step],
            at.neighbour(slot // 2),
        )

    order = (0, 2, 1, 3)

    def onward(step, carry):
        terms(step, term)
        for slot in order:
            hop(slot, step - 1, True).wait_recv()
            arrived[slot, step - 1] = (
                arrived[slot, step - 1].astype(F32) + term[slot].astype(F32)
            ).astype(BF16)
            hop(slot, step).start()
        return carry

    parts = h_in.shape[0]
    part_width = h_in.shape[2]

    class fetch_win:
        def __init__(self, n):
            self.copies = [
                pltpu.make_async_copy(
                    h_in.at[h, pl.ds(n * 256, 256), :],
                    win.at[n % 2, :, pl.ds(h * part_width, part_width)],
                    win_sem.at[n % 2, h],
                )
                for h in range(parts)
            ]

        def start(self):
            for copy in self.copies:
                copy.start()

        def wait(self):
            for copy in self.copies:
                copy.wait()

    columns = width // 256

    def row_tiles(n):
        fetch_win(n).wait()

        def tile(m, carry):
            r = pl.ds(pl.multiple_of(m * 512, 512), 512)
            part[r, n * 256 : (n + 1) * 256] = dot_back(project[r, :], win[n % 2]).astype(BF16)
            return carry

        lax.fori_loop(0, count // 512, tile, 0)
        if n + 2 < columns:
            fetch_win(n + 2).start()

    row_copy(0, 0).start()
    row_copy(1, 0).start()
    row_load(0).start()
    row_load(1).start()
    fetch_win(0).start()
    fetch_win(1).start()
    fetch_turned.wait()
    fetch_project.wait()
    terms(0, first_term)
    for slot in order:
        hop(slot, 0, True).start()
    row_load(0).wait()
    send_rows(0)
    plan = tick_plan(total, 6)

    def extra(number):
        if number < 4:
            for n in range(columns * number // 4, columns * (number + 1) // 4):
                row_tiles(n)
            if number == 3:
                row_copy(0, 1).start()
                row_copy(1, 1).start()
        elif number == 4:
            send_rows(1)
            row_load(1).wait()
            take_down()
        else:
            take_rows()
            vectors_near()

    for number in range(6):
        extra(number)
        lax.fori_loop(*plan[number], onward, 0)
    vectors_far()
    terms(total - 1, term)
    pieces = column_pieces()

    def place(other, value):
        for base, stride, h, off, size in pieces:
            start = pl.multiple_of(base + other * stride, 128)
            off = h * part_width + off
            o_in[:, pl.ds(start, size)] = value[:, off : off + size]

    def sent_across(relation):
        return remote(
            stage.at[relation - 1], landed.at[relation - 1],
            a2a_send.at[relation - 1], a2a_recv.at[relation - 1], at.peer(relation),
        )

    for slot in order:
        relation = RELATIONS[slot // 2][slot % 2]
        hop(slot, total - 2, True).wait_recv()
        value = arrived[slot, total - 2].astype(F32) + term[slot].astype(F32)
        if relation == 0:
            place(me, value)
        else:
            stage[relation - 1] = value.astype(BF16)
            sent_across(relation).start()
    vectors_end()
    for relation in (1, 2, 3):
        sent_across(relation).wait_recv()
        place(flip(me, relation), landed[relation - 1].astype(F32))
    for relation in (1, 2, 3):
        sent_across(relation).wait_send()
        near(relation).wait_send()
    for n in range(1, total):
        for kind in (0, 1):
            distant(kind, n).wait_send()
    for n in (0, 1):
        for kind in (0, 1, 2):
            row_copy(kind, n).wait_send()

    def sent(step, carry):
        for slot in order:
            hop(slot, step, True).wait_send()
        return carry

    lax.fori_loop(0, total - 1, sent, 0)


def final(
    total, d_project, full_in, turned, down, hidden, d_hidden, tok, gain_one, valid, sums_two, d_group
):
    rows, width = tok.shape
    count, wide = d_project.shape
    block = width // GROUP // total
    vmem, hbm = pl.BlockSpec(memory_space=pltpu.VMEM), pl.BlockSpec(memory_space=ANY)
    dma = pltpu.SemaphoreType.DMA
    group_width = d_group.shape[0] * d_group.shape[2]
    shapes = (
        ((block, wide * GROUP), F32),
        ((rows, width), BF16),
        ((rows, width), BF16),
        ((8, 128), F32),
        ((8, 128), F32),
    )
    return pl.pallas_call(
        functools.partial(final_kernel, total),
        out_shape=[jax.ShapeDtypeStruct(s, d) for s, d in shapes],
        in_specs=[hbm] * 4 + [vmem] * 7,
        out_specs=[vmem] * 5,
        scratch_shapes=[
            pltpu.VMEM((count, wide), BF16),
            pltpu.VMEM(turned.shape, BF16),
            pltpu.VMEM((4, block, wide), BF16),
            pltpu.VMEM((4, block, wide), BF16),
            pltpu.VMEM((4, total - 1, block, wide), BF16),
            pltpu.VMEM((2, 256, wide), BF16),
            pltpu.VMEM((count, width), BF16),
            pltpu.VMEM((2, rows, width), BF16),
            pltpu.VMEM((2, 2, rows, width), BF16),
            pltpu.VMEM((2, rows, width), BF16),
            pltpu.VMEM((2, rows, width), BF16),
            pltpu.VMEM((3, block, wide), BF16),
            pltpu.VMEM((3, block, wide), BF16),
            pltpu.VMEM((8, width), F32),
            pltpu.VMEM((8, group_width), F32),
            pltpu.VMEM((3, 8, width // GROUP), F32),
            pltpu.VMEM((8, width // GROUP), F32),
            pltpu.VMEM((total - 1, 8, 128), F32),
            pltpu.VMEM((total - 1, 8, 128), F32),
            dma((2,)), dma((2, 2)), dma((4, total - 1)), dma((4, total - 1)), dma((3,)), dma((3,)),
            dma((2, 3)), dma((2, 3)), dma((2,)), dma((3,)), dma((3,)), dma((2, total - 1)), dma((2, total - 1)),
        ],
        compiler_params=pltpu.CompilerParams(
            collective_id=3, has_side_effects=True, vmem_limit_bytes=63 * MIB
        ),
        name="final_sums",
    )(d_project, full_in, turned, down, hidden, d_hidden, tok, gain_one, valid, sums_two, d_group)


def mean(values):
    return jnp.mean(values, axis=-1, keepdims=True)


def local(
    total,
    tokens,
    cotangent,
    w_in,
    w_out,
    w_up,
    w_down,
    ln1_gain,
    ln1_bias,
    group_gain,
    ln2_gain,
    ln2_bias,
    seq_lens,
    seq_owner,
    seq_offset,
):
    rows, width = tokens.shape
    heads = HEADS // GROUP
    qk, vv = heads * QKH, heads * VH
    me, inner = lax.axis_index("dp"), lax.axis_index("fsdp")
    small, large = ln1_gain.shape[0], group_gain.shape[0]

    count = GROUP * rows
    vectors = jnp.stack([ln1_gain, ln1_bias, ln2_gain, ln2_bias]).astype(F32)
    pack = jnp.zeros((8, 128), F32)
    pack = lax.dynamic_update_slice(pack, vectors, (0, lax.rem(inner * small, 128)))
    pack = lax.dynamic_update_slice(pack, group_gain.astype(F32)[None], (4, lax.rem(inner * large, 128)))
    rates = jnp.log1p(-(2.0 ** (-5.0 - (me * heads + jnp.arange(heads)).astype(F32))))
    rates = jnp.broadcast_to(rates[:, None, None], (heads, 1, rows))
    entries = jnp.stack([seq_lens, seq_owner, seq_offset])
    (
        full_in, full_up, full_out, full_down, seed, turned, query, keys, values, gate, mixed, gated, hidden, two,
        own_seed, cosine, sine, growth, shrink, powers, ident_col, ident_row, gains, gain_group,
    ) = forward(
        total, w_in, w_up, w_out, w_down, tokens, cotangent, pack, rates, entries[:, :, None], entries[:, None, :]
    )
    tables = (cosine, sine, growth, shrink)
    full_up = full_up.reshape(width, -1)
    full_out = full_out.reshape(-1, width)
    full_down = full_down.reshape(-1, width)
    two = two.reshape(count, width)
    seed = seed.reshape(count, width)
    upper = dot(two, full_up)
    cdf = 0.5 * (1.0 + lax.erf(upper * (0.5**0.5)))
    active = (upper * cdf).astype(BF16)
    down = dot(active, full_down).astype(BF16).reshape(GROUP, rows, width)

    slope = cdf + upper * jnp.exp(-0.5 * upper * upper) * (2.0 * jnp.pi) ** -0.5
    d_upper = (dot_back(seed, full_down) * slope).astype(BF16)
    d_two = dot_back(d_upper, full_up).astype(BF16).reshape(GROUP, rows, width)
    g_down = dot_rows(active, seed).astype(BF16)
    grad_down, grad_up, grad_out, d_hidden, _, sums_two, d_group, d_project = backward(
        total, g_down, two, d_upper, d_two, own_seed, hidden, gains, gated, full_out, query, keys, values,
        gate, mixed, tables, powers, ident_col, ident_row, gain_group,
    )
    grad_in, output, d_tokens, vec_one, vec_two = final(
        total, d_project, full_in, turned, down, hidden, d_hidden, tokens, gains, ident_col, sums_two, d_group
    )
    grads = lax.dynamic_slice(vec_one, (0, lax.rem(inner * small, 128)), (4, small))
    grad_group = lax.dynamic_slice(vec_two, (0, lax.rem(inner * large, 128)), (1, large))[0]
    return (
        output,
        d_tokens,
        grad_in,
        grad_out,
        grad_up,
        grad_down,
        grads[0],
        grads[1],
        grad_group,
        grads[2],
        grads[3],
    )


def solution(mesh):
    flat = ("dp", "fsdp")
    matrix, vector = P(flat, None), P(flat)
    return jax.shard_map(
        functools.partial(local, mesh.shape["fsdp"]),
        mesh=mesh,
        in_specs=(matrix,) * 6 + (vector,) * 5 + (P(),) * 3,
        out_specs=(matrix,) * 6 + (vector,) * 5,
        check_vma=False,
    )
```

```python
import functools

import jax
import jax.numpy as jnp
import numpy as np
from jax import lax
from jax.experimental import pallas as pl
from jax.experimental.pallas import tpu as pltpu
from jax.sharding import PartitionSpec as P

HEADS = 8
QKH = 256
VH = 512
EPSILON = 1e-05
GROUP_EPSILON = 0.1
GROUP = 4
MESH = pl.DeviceIdType.MESH
ANY = pl.ANY
BF16 = jnp.bfloat16
F32 = jnp.float32
MIB = 1 << 20


def ring_place(index, total):
    half = index // 2
    return jnp.where(index % 2 == 0, half, total - 1 - half)


def ring_index(place, total):
    place = lax.rem(place + 2 * total, total)
    return jnp.where(place < total // 2, 2 * place, 2 * (total - 1 - place) + 1)


def flip(group_index, relation):
    low, high = group_index % 2, group_index // 2
    if relation % 2:
        low = 1 - low
    if relation // 2:
        high = 1 - high
    return 2 * high + low


class Place:
    def __init__(self, total):
        self.total = total
        self.group = lax.axis_index("dp")
        self.inner = lax.axis_index("fsdp")
        self.place = ring_place(self.inner, total)
        self.next = (
            ring_index(self.place + 1, total),
            ring_index(self.place - 1, total),
        )

    def peer(self, relation):
        return (flip(self.group, relation), self.inner)

    def neighbour(self, way):
        return (self.group, self.next[way])

    def behind(self, way, steps):
        return ring_index(self.place - steps if way == 0 else self.place + steps, self.total)


def greet(devices):
    barrier = pltpu.get_barrier_semaphore()
    for device in devices:
        pl.semaphore_signal(barrier, inc=1, device_id=device, device_id_type=MESH)
    pl.semaphore_wait(barrier, len(devices))


def remote(src, dst, send_sem, recv_sem, device):
    return pltpu.make_async_remote_copy(
        src_ref=src,
        dst_ref=dst,
        send_sem=send_sem,
        recv_sem=recv_sem,
        device_id=device,
        device_id_type=MESH,
    )


def column_pieces():
    heads = HEADS // GROUP
    table = []
    base, off = 0, 0
    for size in (QKH, QKH, VH, VH):
        for h in range(heads):
            table.append((base + h * size, heads * size, h, off, size))
        base += HEADS * size
        off += size
    return table


def dot(left, right):
    return jnp.dot(left, right, preferred_element_type=F32)


def dot_rows(left, right):
    return lax.dot_general(left, right, (((0,), (0,)), ((), ())), preferred_element_type=F32)


def dot_back(left, right):
    return lax.dot_general(left, right, (((1,), (1,)), ((), ())), preferred_element_type=F32)


def norm_parts(values, epsilon):
    center = values - jnp.mean(values, axis=-1, keepdims=True)
    spread = jnp.mean(center * center, axis=-1, keepdims=True)
    scale = lax.rsqrt(spread + epsilon)
    return center * scale, scale


RELATIONS = ((2, 0), (3, 1))


class Passing:
    def __init__(self, at, way, own, place, sends, recvs):
        self.at, self.way, self.own, self.place = at, way, own, place
        self.sends, self.recvs = sends, recvs

    def hop(self, step, first=False):
        which = self.at.inner if first else self.at.behind(self.way, step)
        dst = self.place(which)
        return remote(
            self.own if first else dst, dst, self.sends.at[step], self.recvs.at[step],
            self.at.neighbour(self.way),
        )

    def begin(self):
        self.hop(0, True).start()

    def onward(self, step):
        self.hop(step - 1).wait_recv()
        self.hop(step).start()

    def finish(self):
        self.hop(self.at.total - 2).wait_recv()


def wait_sent(rings, total):
    def body(step, carry):
        for ring in rings:
            ring.hop(step).wait_send()
        return carry

    lax.fori_loop(0, total - 1, body, 0)


def tick_plan(total, places):
    steps = total - 2
    cuts = [1 + (steps * n) // places for n in range(places + 1)]
    return list(zip(cuts[:-1], cuts[1:]))


def run_steps(rings, start, stop):
    def body(step, carry):
        for ring in rings:
            ring.onward(step)
        return carry

    lax.fori_loop(start, stop, body, 0)


def weight_rings(at, w_out, w_down, full_up, full_out, full_down, sends, recvs):
    me = at.group
    half = w_out.shape[0] // 2
    side = w_out.shape[1] // 2

    def halves(own, full, slot):
        return [
            Passing(
                at, way,
                own.at[pl.ds(way * half, half), pl.ds(c * side, side)],
                lambda which, way=way, c=c: full.at[which, pl.ds(way * half, half), pl.ds(c * side, side)],
                sends.at[slot + 2 * c + way], recvs.at[slot + 2 * c + way],
            )
            for c in (0, 1)
            for way in (0, 1)
        ]

    ups = []
    for order in (0, 1):
        for way in (0, 1):
            relation = RELATIONS[way][order]
            slot = 8 + 2 * order + way
            ups.append(
                Passing(
                    at, way, full_up.at[flip(me, relation), at.inner],
                    lambda which, relation=relation: full_up.at[flip(me, relation), which],
                    sends.at[slot], recvs.at[slot],
                )
            )
    return halves(w_out, full_out, 0), ups, halves(w_down, full_down, 4)


def rotated(value, cosine, sine, scale):
    half = QKH // 2
    first, second = value[:, :half], value[:, half:]
    return jnp.concatenate(
        [(first * cosine - second * sine) * scale, (second * cosine + first * sine) * scale], axis=1
    )


def forward_kernel(
    total, w_in, w_up, w_out, w_down, tok, cot, pack, rates, seq_cols, seq_rows, curves,
    full_in, full_up, full_out, full_down, full_seed, o_turned, o_query, o_keys, o_values, o_gate, o_mixed,
    o_gated, o_active, o_upper, o_g_down, hidden, full_two, own_seed, cosine, sine, growth, shrink, powers, ident_col, ident_row, gains,
    gain_group,
    win, part, x, query, keys, values, gate, mixed, gated, wo, core_in, out_x, in_x, low, full_vec,
    win_up, wd, ring_send, ring_recv, own_sem, load_sem, fetch_sem, store_sem, row_send, row_recv, row_own,
    swap_send, swap_recv, swap_own, vec_send, vec_recv,
):
    at = Place(total)
    me, inner = at.group, at.inner
    core, across = at.peer(1), at.peer(2)
    others = [(me, lax.rem(inner + n, total)) for n in range(1, total)]
    greet([core, across, at.peer(3)] + others)
    rows, width = tok.shape
    count = GROUP * rows
    heads = HEADS // GROUP
    r_in = w_in.shape[0]
    up_width = full_up.shape[-1]
    pieces = column_pieces()
    step_rows = 32

    def rows_in(group_index, which):
        return pl.ds(pl.multiple_of((group_index * total + which) * r_in, r_in), r_in)

    last = len(pieces)

    def swap(relation, slot):
        other = flip(me, relation)
        if slot < last:
            base, stride, h, off, size = pieces[slot]
            src = w_in.at[:, pl.ds(pl.multiple_of(base + other * stride, 128), size)]
            dst = win.at[h, rows_in(me, inner), pl.ds(off, size)]
        elif slot == last:
            src = w_up.at[:, pl.ds(pl.multiple_of(other * up_width, 128), up_width)]
            dst = full_up.at[me, inner]
        elif slot == last + 1:
            src, dst = pack, full_vec.at[inner, me]
        elif slot == last + 2:
            src, dst = tok, part.at[me]
        else:
            src, dst = own_seed, full_seed.at[me]
        if relation == 0:
            return pltpu.make_async_copy(src, dst, swap_own.at[slot])
        return remote(
            src, dst, swap_send.at[relation - 1, slot], swap_recv.at[relation - 1, slot], at.peer(relation)
        )

    def arrived(relation, slot):
        if relation == 0:
            swap(0, slot).wait()
        else:
            swap(relation, slot).wait_recv()

    for h in range(heads):
        for relation in (1, 0, 2, 3):
            for slot in range(last):
                if pieces[slot][2] == h:
                    swap(relation, slot).start()
        if h == 0:
            for relation in range(4):
                swap(relation, last + 1).start()
    for slot in (last + 2, last):
        for relation in (1, 0, 2, 3):
            swap(relation, slot).start()

    def in_ring(h, relation):
        def place(which):
            return win.at[h, rows_in(flip(me, relation), which), :]

        slot = 12 + 4 * h + relation
        return Passing(at, relation % 2, place(inner), place, ring_send.at[slot], ring_recv.at[slot])

    ins = [[in_ring(h, relation) for relation in range(4)] for h in range(heads)]
    near, far_in = ins[0][:2], ins[0][2:]

    def await_head(h, relation):
        for slot in range(last):
            if pieces[slot][2] == h:
                arrived(relation, slot)

    for relation in (0, 1):
        await_head(0, relation)
        near[relation].begin()

    def layout_of(b, down):
        shape = (rows, 1) if down else (1, rows)
        source = seq_rows if down else seq_cols
        lens, owner, offset = source[0], source[1], source[2]
        positions = lax.broadcasted_iota(jnp.int32, shape, 0 if down else 1)
        inside = (
            (owner == b * total + inner)
            & (lens > 0)
            & (positions >= offset)
            & (positions < offset + lens)
        )
        axis = 1 if down else 0
        number = lax.broadcasted_iota(jnp.int32, lens.shape, axis).astype(F32) + 1.0
        ident = jnp.sum(jnp.where(inside, number, 0.0), axis=axis, keepdims=True) - 1.0
        starts = jnp.sum(jnp.where(inside, offset.astype(F32), 0.0), axis=axis, keepdims=True)
        places = jnp.where(ident >= 0.0, positions.astype(F32) - starts, 0.0)
        return ident, places

    for b in range(GROUP):
        ident_col[b] = layout_of(b, True)[0]
        ident_row[b] = layout_of(b, False)[0]

    def seed_rows(n, carry):
        s = pl.ds(pl.multiple_of(n * step_rows, step_rows), step_rows)
        valid = jnp.where(ident_col[me, s, :] >= 0.0, 1.0, 0.0)
        own_seed[s, :] = (cot[s, :].astype(F32) * valid).astype(BF16)
        return carry

    lax.fori_loop(0, rows // step_rows, seed_rows, 0)

    for relation in range(4):
        arrived(relation, last + 1)

    def spread(n):
        target = lax.rem(inner + n, total)
        return remote(
            full_vec.at[inner], full_vec.at[inner], vec_send.at[n - 1], vec_recv.at[n - 1], (me, target)
        )

    for n in range(1, total):
        spread(n).start()
    for ring in near:
        ring.onward(1)
    for relation in (2, 3):
        await_head(0, relation)
        far_in[relation - 2].begin()
    for relation in (1, 0, 2, 3):
        swap(relation, last + 3).start()

    def both_in(step, carry):
        for ring in near:
            ring.onward(step)
        for ring in far_in:
            ring.onward(step - 1)
        return carry

    def take_vectors():
        for n in range(1, total):
            spread(n).wait_recv()
        quarter = width // GROUP
        small = quarter // total
        large = heads * VH // total
        for d in range(GROUP):
            tiles = {}
            for f in range(total):
                t = f * small // 128
                value = full_vec[f, d]
                tiles[t] = tiles[t] + value if t in tiles else value
            for t, value in tiles.items():
                gains[:, d * quarter + t * 128 : d * quarter + (t + 1) * 128] = value
        tiles = {}
        for f in range(total):
            t = f * large // 128
            value = full_vec[f, me, 4:5, :]
            tiles[t] = tiles[t] + value if t in tiles else value
        for t, value in tiles.items():
            h, off = t * 128 // VH, t * 128 % VH
            gain_group[h, :, off : off + 128] = value

    def make_tables():
        distance = lax.broadcasted_iota(jnp.int32, (rows, rows), 0) - lax.broadcasted_iota(
            jnp.int32, (rows, rows), 1
        )
        away = jnp.maximum(distance, 0).astype(F32)
        for h in range(heads):
            powers[h] = jnp.where(distance >= 0, jnp.exp(rates[h] * away), 0.0)
        for b in range(GROUP):
            places = layout_of(b, True)[1]
            angles = places * curves[0:1, :]
            r = slice(b * rows, (b + 1) * rows)
            cosine[r, :] = jnp.cos(angles)
            sine[r, :] = jnp.sin(angles)
            lift = places * (1.0 / 512.0) * curves[1:2, :]
            growth[r, :] = jnp.exp(lift)
            shrink[r, :] = jnp.exp(-lift)

    def norm_buffer(relation):
        b = flip(me, relation)
        arrived(relation, last + 2)

        def norm_rows(n, carry):
            r = pl.multiple_of(n * step_rows, step_rows)
            normal, _ = norm_parts(part[b, pl.ds(r, step_rows), :].astype(F32), EPSILON)
            at_rows = pl.ds(pl.multiple_of(b * rows + r, step_rows), step_rows)
            x[at_rows, :] = (normal * gains[0:1, :] + gains[1:2, :]).astype(BF16)
            return carry

        lax.fori_loop(0, rows // step_rows, norm_rows, 0)

    beside = [
        make_tables,
        take_vectors,
        lambda: (norm_buffer(0), norm_buffer(1)),
        lambda: norm_buffer(2),
        lambda: norm_buffer(3),
    ]
    cuts = [2 + (total - 3) * n // 5 for n in range(6)]
    for n in range(5):
        lax.fori_loop(cuts[n], cuts[n + 1], both_in, 0)
        beside[n]()
    for ring in far_in:
        ring.onward(total - 2)
    for h in range(1, heads):
        for relation in range(4):
            await_head(h, relation)
            ins[h][relation].begin()
    outs, ups, downs = weight_rings(
        at, w_out, w_down, full_up, full_out, full_down, ring_send, ring_recv
    )
    own_copies = [
        pltpu.make_async_copy(w_out, full_out.at[inner], own_sem.at[0]),
        pltpu.make_async_copy(w_down, full_down.at[inner], own_sem.at[1]),
    ]
    for copy in own_copies:
        copy.start()
    plan = tick_plan(total, 6)
    tile = 512

    def project(h, off, m):
        r = pl.ds(pl.multiple_of(m * tile, tile), tile)
        return r, dot(x[r, :], win[h, :, off : off + QKH])

    def turn_tile(h, m):
        r, value = project(h, 0, m)
        turned = rotated(value, cosine[r, :], sine[r, :], growth[r, :])
        query[h, r, :] = (turned * QKH ** (-0.5)).astype(BF16)
        r, value = project(h, QKH, m)
        keys[h, r, :] = rotated(value, cosine[r, :], sine[r, :], shrink[r, :]).astype(BF16)

    def plain_tile(h, c, m):
        off = c * QKH
        r, value = project(h, 2 * QKH + off, m)
        values[h, r, off : off + QKH] = value.astype(BF16)
        r, value = project(h, 2 * QKH + VH + off, m)
        gate[h, r, off : off + QKH] = value

    def retain(h, b):
        r = pl.ds(pl.multiple_of(b * rows, rows), rows)
        raw = dot_back(query[h, r, :], keys[h, r, :])
        linked = (ident_col[b] == ident_row[b]) & (ident_col[b] >= 0.0)
        masked = (raw * jnp.where(linked, powers[h], 0.0)).astype(BF16)
        mixed[h, r, :] = dot(masked, values[h, r, :])

        def some_rows(n, carry):
            s = pl.ds(pl.multiple_of(b * rows + n * step_rows, step_rows), step_rows)
            normal, _ = norm_parts(mixed[h, s, :], GROUP_EPSILON)
            z = gate[h, s, :]
            result = z / (1.0 + jnp.exp(-z)) * (normal * gain_group[h])
            gated[s, h * VH : (h + 1) * VH] = result.astype(BF16)
            return carry

        lax.fori_loop(0, rows // step_rows, some_rows, 0)

    def looped(count_of, body):
        def some(n, carry):
            body(n)
            return carry

        lax.fori_loop(0, count_of, some, 0)

    def head_units(h):
        return [
            lambda: looped(count // tile, lambda m: turn_tile(h, m)),
            lambda: looped(count // tile, lambda m: plain_tile(h, 0, m)),
            lambda: looped(count // tile, lambda m: plain_tile(h, 1, m)),
            lambda: looped(2, lambda b: retain(h, b)),
            lambda: looped(2, lambda b: retain(h, 2 + b)),
        ]

    stores = []

    def store_head(h):
        for n, (src, dst) in enumerate(
            ((win, full_in), (query, o_query), (keys, o_keys), (values, o_values), (gate, o_gate), (mixed, o_mixed))
        ):
            copy = pltpu.make_async_copy(src.at[h], dst.at[h], store_sem.at[h, n])
            copy.start()
            stores.append(copy)

    for h in range(heads):
        ring_set = ins[h + 1] if h + 1 < heads else outs
        if h + 1 == heads:
            for ring in outs:
                ring.begin()
        for ring in ins[h]:
            ring.finish()
        units = head_units(h)
        for number in range(6):
            if number < len(units):
                units[number]()
            run_steps(ring_set, *plan[number])
        store_head(h)
    for relation in range(4):
        arrived(relation, last)
    for ring in ups:
        ring.begin()
    for ring in outs:
        ring.finish()
    stores.append(pltpu.make_async_copy(gated, o_gated, store_sem.at[0, 6]))
    stores[-1].start()
    own_copies[0].wait()
    block = w_out.shape[0]
    fetch = pltpu.make_async_copy(full_out, wo, load_sem.at[0])
    fetch.start()
    fetch.wait()

    chunks = 4
    size = rows // chunks

    def branch(relation):
        b = flip(me, relation)

        def column(n, carry):
            wide = 512
            c = pl.ds(pl.multiple_of(n * wide, wide), wide)
            r = pl.ds(pl.multiple_of(b * rows, rows), rows)
            acc = jnp.zeros((rows, wide), F32)
            piece = gated[r, :]
            acc = dot(piece, wo[:, :, c].reshape(total * block, wide))
            part[b, :, c] = acc.astype(BF16)
            return carry

        lax.fori_loop(0, width // 512, column, 0)

    def rows_of(c):
        return pl.ds(c * size, size)

    far = flip(me, 2)

    def copy(kind, c):
        r = rows_of(c)
        if kind == 0:
            src, dst, dev = part.at[flip(me, 3), r], core_in.at[0, r], core
        elif kind == 1:
            src, dst, dev = part.at[flip(me, 1), r], core_in.at[1, r], core
        elif kind == 2:
            src, dst, dev = out_x.at[r], in_x.at[r], across
        elif kind == 3:
            src, dst, dev = low.at[r], full_two.at[me, r], across
        elif kind == 4:
            src, dst, dev = low.at[r], full_two.at[me, r], core
        else:
            src, dst, dev = full_two.at[far, r], full_two.at[far, r], core
        return remote(src, dst, row_send.at[kind, c], row_recv.at[kind, c], dev)

    def store(c):
        r = rows_of(c)
        return pltpu.make_async_copy(low.at[r], full_two.at[me, r], row_own.at[c])

    branch(3)
    for c in range(chunks):
        copy(0, c).start()
    branch(2)
    run_steps(ups, *plan[0])
    for c in range(chunks):
        r = rows_of(c)
        copy(0, c).wait_recv()
        out_x[r, :] = (part[far, r, :].astype(F32) + core_in[0, r, :].astype(F32)).astype(BF16)
        copy(2, c).start()
    branch(1)
    for c in range(chunks):
        copy(1, c).start()
    branch(0)
    run_steps(ups, *plan[1])
    for copy_out in stores:
        copy_out.wait()
    wait_sent([ring for rings in ins for ring in rings], total)

    def turn(n, carry):
        i, j = n // (count // 256), lax.rem(n, count // 256)
        i, j = (pl.ds(pl.multiple_of(k * 256, 256), 256) for k in (i, j))
        win[0, i, j] = x[j, i].T
        return carry

    blocks = (width // 256) * (count // 256)
    lax.fori_loop(0, blocks // 2, turn, 0)
    run_steps(ups, *plan[2])
    for c in range(chunks):
        r = rows_of(c)
        copy(1, c).wait_recv()
        copy(2, c).wait_recv()

        def finish_rows(n, carry, c=c):
            s = pl.ds(pl.multiple_of(c * size + n * step_rows, step_rows), step_rows)
            value = tok[s, :].astype(F32) + (
                part[me, s, :].astype(F32) + core_in[1, s, :].astype(F32) + in_x[s, :].astype(F32)
            )
            hidden[s, :] = value
            normal, _ = norm_parts(value, EPSILON)
            low[s, :] = (normal * gains[2:3, :] + gains[3:4, :]).astype(BF16)
            return carry

        lax.fori_loop(0, size // step_rows, finish_rows, 0)
        copy(3, c).start()
        copy(4, c).start()
        store(c).start()
        if c:
            run_steps(ups, *plan[2 + c])
    for ring in downs:
        ring.begin()
    lax.fori_loop(blocks // 2, blocks, turn, 0)
    store_turned = pltpu.make_async_copy(win.at[0, :, pl.ds(0, count)], o_turned, own_sem.at[0])
    store_turned.start()
    for relation in range(4):
        arrived(relation, last + 3)
    fetch_seed = [
        pltpu.make_async_copy(full_seed.at[b], x.at[pl.ds(b * rows, rows)], fetch_sem.at[b])
        for b in range(GROUP)
    ]
    for fetch in fetch_seed:
        fetch.start()
    for ring in ups:
        ring.finish()
    fetch_up = [
        pltpu.make_async_copy(full_up.at[b], win_up.at[b], fetch_sem.at[GROUP + b]) for b in range(GROUP)
    ]
    for fetch in fetch_up:
        fetch.start()
    for c in range(chunks):
        copy(3, c).wait_recv()
        copy(5, c).start()
        if c % 2:
            run_steps(downs, *plan[c // 2])
    for c in range(chunks):
        copy(4, c).wait_recv()
        copy(5, c).wait_recv()
        store(c).wait()
        for kind in range(6):
            copy(kind, c).wait_send()
    fetch_two = pltpu.make_async_copy(full_two, part, load_sem.at[1])
    fetch_two.start()
    for fetch in fetch_seed + fetch_up:
        fetch.wait()
    fetch_two.wait()

    quarters = heads * VH // 256

    def upper_tile(n, carry):
        b, j = n // quarters, lax.rem(n, quarters)
        c = pl.ds(pl.multiple_of(j * 256, 256), 256)
        r = pl.ds(pl.multiple_of(b * rows, rows), rows)
        upper = dot(part[b], win_up[:, :, :, c].reshape(width, 256))
        cdf = 0.5 * (1.0 + lax.erf(upper * (0.5**0.5)))
        gated[r, c] = (upper * cdf).astype(BF16)
        half = pl.ds(pl.multiple_of(lax.rem(j, 2) * 256, 256), 256)
        gate[j // 2, r, half] = cdf + upper * jnp.exp(-0.5 * upper * upper) * (2.0 * np.pi) ** -0.5
        return carry

    tiles = GROUP * quarters
    lax.fori_loop(0, tiles // 2, upper_tile, 0)
    run_steps(downs, *plan[2])
    lax.fori_loop(tiles // 2, tiles, upper_tile, 0)
    run_steps(downs, *plan[3])
    store_active = pltpu.make_async_copy(gated, o_active, store_sem.at[0, 0])
    store_active.start()
    per_tile = 256 // block
    wide = 512

    def down_tile(n, carry):
        i, j = n // (width // wide), lax.rem(n, width // wide)
        a = pl.ds(pl.multiple_of(i * 256, 256), 256)
        c = pl.ds(pl.multiple_of(j * wide, wide), wide)
        value = dot_rows(gated[:, a], x[:, c]).astype(BF16)
        wo[pl.ds(i * per_tile, per_tile), :, c] = value.reshape(per_tile, block, wide)
        return carry

    tiles = quarters * (width // wide)
    lax.fori_loop(0, tiles // 2, down_tile, 0)
    run_steps(downs, *plan[4])
    lax.fori_loop(tiles // 2, tiles, down_tile, 0)
    run_steps(downs, *plan[5])
    store_down = pltpu.make_async_copy(wo, o_g_down, store_sem.at[0, 1])
    store_down.start()
    own_copies[1].wait()
    for ring in downs:
        ring.finish()
    fetch = pltpu.make_async_copy(full_down, wd, load_sem.at[0])
    fetch.start()
    fetch.wait()

    def d_upper_tile(n, carry):
        h, j = n // 4, lax.rem(n, 4)
        m, side = j // 2, lax.rem(j, 2)
        r = pl.ds(pl.multiple_of(m * tile, tile), tile)
        c = pl.ds(pl.multiple_of(side * 256, 256), 256)
        piece = wd[pl.ds((2 * h + side) * per_tile, per_tile)].reshape(256, width)
        values[h, r, c] = (dot_back(x[r, :], piece) * gate[h, r, c]).astype(BF16)
        return carry

    lax.fori_loop(0, 4 * heads, d_upper_tile, 0)
    last_stores = [store_active, store_down] + [
        pltpu.make_async_copy(values.at[h], o_upper.at[:, pl.ds(h * VH, VH)], store_sem.at[0, 2 + h])
        for h in range(heads)
    ]
    for copy_out in last_stores[2:]:
        copy_out.start()
    wait_sent(outs + downs + ups, total)
    for relation in (1, 2, 3):
        for slot in range(last + 4):
            swap(relation, slot).wait_send()
    for n in range(1, total):
        spread(n).wait_send()
    store_turned.wait()
    for copy_out in last_stores:
        copy_out.wait()


def forward(total, w_in, w_up, w_out, w_down, tok, cot, pack, rates, seq_cols, seq_rows):
    rows, width = tok.shape
    count = GROUP * rows
    heads = HEADS // GROUP
    head_width = 2 * (QKH + VH)
    vmem, hbm = pl.BlockSpec(memory_space=pltpu.VMEM), pl.BlockSpec(memory_space=ANY)
    dma = pltpu.SemaphoreType.DMA
    pair = np.arange(QKH // 2) / (QKH // 2)
    curves = np.zeros((8, QKH // 2), np.float32)
    curves[0] = 10000.0**-pair
    curves[1] = np.log((pair + 0.4) / 1.4)
    kept = (
        ((heads, count, QKH), BF16),
        ((heads, count, QKH), BF16),
        ((heads, count, VH), BF16),
        ((heads, count, VH), F32),
        ((heads, count, VH), F32),
        ((count, heads * VH), BF16),
    )
    in_hbm = (
        ((heads, width, head_width), BF16),
        ((GROUP, total, w_up.shape[0], w_up.shape[1] // GROUP), BF16),
        ((total,) + w_out.shape, BF16),
        ((total,) + w_down.shape, BF16),
        ((GROUP, rows, width), BF16),
        ((width, count), BF16),
        *kept,
        kept[-1],
        kept[-1],
        ((total,) + w_out.shape, BF16),
    )
    in_vmem = (
        ((rows, width), BF16),
        ((count, QKH // 2), F32),
        ((count, QKH // 2), F32),
        ((count, QKH // 2), F32),
        ((count, QKH // 2), F32),
        ((heads, rows, rows), F32),
        ((GROUP, rows, 1), F32),
        ((GROUP, 1, rows), F32),
        ((8, width), F32),
        ((heads, 1, VH), F32),
    )
    shapes = (*in_hbm, ((rows, width), F32), ((GROUP, rows, width), BF16), *in_vmem)
    return pl.pallas_call(
        functools.partial(forward_kernel, total),
        out_shape=[jax.ShapeDtypeStruct(s, d) for s, d in shapes],
        in_specs=[hbm] * 4 + [vmem] * 7,
        out_specs=[hbm] * len(in_hbm) + [vmem, hbm] + [vmem] * len(in_vmem),
        scratch_shapes=[
            pltpu.VMEM((heads, width, head_width), BF16),
            pltpu.VMEM((GROUP, rows, width), BF16),
            pltpu.VMEM((count, width), BF16),
            *[pltpu.VMEM(s, d) for s, d in kept],
            pltpu.VMEM((total,) + w_out.shape, BF16),
            pltpu.VMEM((2, rows, width), BF16),
            pltpu.VMEM((rows, width), BF16),
            pltpu.VMEM((rows, width), BF16),
            pltpu.VMEM((rows, width), BF16),
            pltpu.VMEM((total, GROUP, 8, 128), F32),
            pltpu.VMEM((GROUP, total, w_up.shape[0], w_up.shape[1] // GROUP), BF16),
            pltpu.VMEM((total,) + w_down.shape, BF16),
            dma((20, total - 1)), dma((20, total - 1)), dma((2,)), dma((2,)), dma((2 * GROUP,)),
            dma((heads, 7)), dma((6, 4)), dma((6, 4)), dma((4,)),
            dma((3, 12)), dma((3, 12)), dma((12,)), dma((total - 1,)), dma((total - 1,)),
        ],
        compiler_params=pltpu.CompilerParams(
            collective_id=1, has_side_effects=True, vmem_limit_bytes=63 * MIB
        ),
        name="forward_retention",
    )(w_in, w_up, w_out, w_down, tok, cot, pack, rates, seq_cols, seq_rows, jnp.asarray(curves))


class Adding:
    def __init__(self, at, way, term, arrived, sends, recvs):
        self.at, self.way, self.term, self.arrived = at, way, term, arrived
        self.sends, self.recvs = sends, recvs

    def hop(self, step, first=False):
        src = self.term(self.at.behind(self.way, 1)) if first else self.arrived.at[step - 1]
        return remote(
            src, self.arrived.at[step], self.sends.at[step], self.recvs.at[step], self.at.neighbour(self.way)
        )

    def begin(self):
        self.hop(0, True).start()

    def sum_at(self, step, which):
        self.hop(step, True).wait_recv()
        return self.arrived[step].astype(F32) + self.term(which)[...].astype(F32)

    def onward(self, step):
        self.arrived[step - 1] = self.sum_at(step - 1, self.at.behind(self.way, step + 1)).astype(BF16)
        self.hop(step).start()

    def finish(self):
        return self.sum_at(self.at.total - 2, self.at.inner)


def wait_added(rings, total):
    def body(step, carry):
        for ring in rings:
            ring.hop(step, True).wait_send()
        return carry

    lax.fori_loop(0, total - 1, body, 0)


def backward_kernel(
    total, g_down, two, d_upper, h_up, seed, hidden, gains_all, h_gated, h_out, h_query, h_keys, h_values, h_gate,
    h_mixed, cosine, sine, growth, shrink, powers, ident_col, ident_row, gain_group,
    o_down, o_up, o_out, d_hidden, full_branch, sums, o_group, o_project,
    g_up, g_out, arrived, wide_buf, narrow_buf, wo, part, core_in, out_x, in_x, low,
    query, keys, values, gate, mixed, back, d_mixed, staged, stage, landed,
    ring_send, ring_recv, row_send, row_recv, row_own, load_sem, unit_sem, out_sem, a2a_send, a2a_recv,
):
    at = Place(total)
    me = at.group
    core, across = at.peer(1), at.peer(2)
    greet([core, across, at.peer(3), at.neighbour(0), at.neighbour(1)])
    rows, width = seed.shape
    count = GROUP * rows
    heads = HEADS // GROUP
    r_up, r_out = o_up.shape[0], o_out.shape[0]
    up_width = o_up.shape[1] // GROUP
    half, side = r_out // 2, width // 2

    def halves(source, base):
        return [
            Adding(
                at, way,
                lambda which, way=way, c=c: source.at[
                    pl.ds(pl.multiple_of(which * r_out + way * half, half), half), pl.ds(c * side, side)
                ],
                arrived.at[base + 2 * c + way], ring_send.at[base + 2 * c + way], ring_recv.at[base + 2 * c + way],
            )
            for c in (0, 1)
            for way in (0, 1)
        ]

    downs, outs, ups = halves(g_down, 0), halves(g_out, 8), []
    for order in (0, 1):
        for way in (0, 1):
            relation = RELATIONS[way][order]
            slot = 4 + 2 * order + way
            ups.append(
                Adding(
                    at, way,
                    lambda which, relation=relation: g_up.at[
                        pl.ds(pl.multiple_of((flip(me, relation) * total + which) * r_up, r_up), r_up), :
                    ],
                    arrived.at[slot], ring_send.at[slot], ring_recv.at[slot],
                )
            )

    chunks = 4
    size = rows // chunks
    step_rows = 32
    far = flip(me, 2)

    def rows_of(c):
        return pl.ds(c * size, size)

    def copy(kind, c):
        r = rows_of(c)
        if kind == 0:
            src, dst, dev = part.at[flip(me, 3), r], core_in.at[0, r], core
        elif kind == 1:
            src, dst, dev = part.at[flip(me, 1), r], core_in.at[1, r], core
        elif kind == 2:
            src, dst, dev = out_x.at[r], in_x.at[r], across
        elif kind == 3:
            src, dst, dev = low.at[r], full_branch.at[me, r], across
        elif kind == 4:
            src, dst, dev = low.at[r], full_branch.at[me, r], core
        else:
            src, dst, dev = full_branch.at[far, r], full_branch.at[far, r], core
        return remote(src, dst, row_send.at[kind, c], row_recv.at[kind, c], dev)

    def store(c):
        r = rows_of(c)
        return pltpu.make_async_copy(low.at[r], full_branch.at[me, r], row_own.at[c])

    for ring in downs:
        ring.begin()
    upper_columns = pl.ds(0, up_width)
    fetch_upper = pltpu.make_async_copy(d_upper, g_out.at[:, upper_columns], load_sem.at[1])
    fetch_up = pltpu.make_async_copy(h_up, g_up, load_sem.at[7])
    fetch_two = pltpu.make_async_copy(two, wide_buf, load_sem.at[0])
    fetch_gated = pltpu.make_async_copy(h_gated, narrow_buf, load_sem.at[8])
    fetch_out = pltpu.make_async_copy(h_out, wo, load_sem.at[2])
    for fetch in (fetch_upper, fetch_up, fetch_two, fetch_gated, fetch_out):
        fetch.start()

    def unit_loads(unit, slot):
        h, b = unit // GROUP, lax.rem(unit, GROUP)
        r = pl.ds(pl.multiple_of(b * rows, rows), rows)
        pairs = ((h_query, query), (h_keys, keys), (h_values, values), (h_gate, gate), (h_mixed, mixed))
        return [
            pltpu.make_async_copy(src.at[h, r], dst.at[slot], unit_sem.at[slot, n])
            for n, (src, dst) in enumerate(pairs)
        ]

    for unit in (0, 1):
        for fetch in unit_loads(jnp.int32(unit), unit):
            fetch.start()

    def send_sums(c):
        r = rows_of(c)
        copy(0, c).wait_recv()
        out_x[r, :] = (part[far, r, :].astype(F32) + core_in[0, r, :].astype(F32)).astype(BF16)
        copy(2, c).start()

    def norm_back(c):
        copy(1, c).wait_recv()
        copy(2, c).wait_recv()

        def some_rows(n, carry):
            s = pl.ds(pl.multiple_of(c * size + n * step_rows, step_rows), step_rows)
            e = part[me, s, :].astype(F32) + core_in[1, s, :].astype(F32) + in_x[s, :].astype(F32)
            normal, scale = norm_parts(hidden[s, :], EPSILON)
            with_gain = e * gains_all[2:3, :]
            sums[0:1, :] += jnp.sum(e * normal, axis=0, keepdims=True)
            sums[1:2, :] += jnp.sum(e, axis=0, keepdims=True)
            value = seed[s, :].astype(F32) + scale * (
                with_gain
                - jnp.mean(with_gain, axis=-1, keepdims=True)
                - normal * jnp.mean(with_gain * normal, axis=-1, keepdims=True)
            )
            d_hidden[s, :] = value
            low[s, :] = value.astype(BF16)
            return carry

        lax.fori_loop(0, size // step_rows, some_rows, 0)
        copy(3, c).start()
        copy(4, c).start()
        store(c).start()

    sums[...] = jnp.zeros_like(sums)
    o_group[...] = jnp.zeros_like(o_group)
    def d_two(relation):
        b = flip(me, relation)
        r = pl.ds(pl.multiple_of(b * rows, rows), rows)

        def column(n, carry):
            c = pl.ds(pl.multiple_of(n * 256, 256), 256)
            part[b, :, c] = dot_back(g_out[r, :up_width], g_up[c, :]).astype(BF16)
            return carry

        lax.fori_loop(0, width // 256, column, 0)

    plan = tick_plan(total, 6)
    fetch_upper.wait()
    fetch_up.wait()
    d_two(3)
    for c in range(chunks):
        copy(0, c).start()
    d_two(2)
    for c in range(chunks):
        send_sums(c)
    add_steps(downs, *plan[0])
    d_two(1)
    for c in range(chunks):
        copy(1, c).start()
    d_two(0)
    fetch_two.wait()

    def grad_tiles(left, right, span, out, start, stop):
        wide = 512

        def tile(n, carry):
            rows_n = span // wide
            i, j = n // rows_n, lax.rem(n, rows_n)
            a = pl.ds(pl.multiple_of(i * 256, 256), 256)
            c = pl.ds(pl.multiple_of(j * wide, wide), wide)
            out[a, c] = dot_rows(left[:, a], right[:, c]).astype(BF16)
            return carry

        lax.fori_loop(start, stop, tile, 0)

    tiles = (width // 256) * (up_width // 512)
    for quarter in range(4):
        grad_tiles(wide_buf, g_out, up_width, g_up, tiles * quarter // 4, tiles * (quarter + 1) // 4)
        if quarter:
            norm_back(quarter - 1)
        add_steps(downs, *plan[1 + quarter])
    norm_back(3)
    add_steps(downs, *plan[5])
    for ring in ups:
        ring.begin()
    for n, ring in enumerate(downs):
        c, way = n // 2, n % 2
        o_down[pl.ds(way * half, half), pl.ds(c * side, side)] = ring.finish()
    for c in range(chunks):
        copy(3, c).wait_recv()
        copy(5, c).start()
        if c % 2:
            add_steps(ups, *plan[c // 2])
    for c in range(chunks):
        copy(4, c).wait_recv()
        copy(5, c).wait_recv()
        store(c).wait()
    branch = wide_buf
    fetch_branch = [
        pltpu.make_async_copy(full_branch.at[b], branch.at[pl.ds(b * rows, rows)], load_sem.at[3 + b])
        for b in range(GROUP)
    ]
    for fetch in fetch_branch:
        fetch.start()
    for fetch in fetch_branch:
        fetch.wait()
    fetch_gated.wait()
    fetch_out.wait()
    tiles = (narrow_buf.shape[1] // 256) * (width // 512)
    for quarter in range(4):
        grad_tiles(narrow_buf, branch, width, g_out, tiles * quarter // 4, tiles * (quarter + 1) // 4)
        add_steps(ups, *plan[2 + quarter])
    for ring in outs:
        ring.begin()

    def sent_across(relation):
        return remote(
            stage.at[relation - 1], landed.at[relation - 1],
            a2a_send.at[relation - 1], a2a_recv.at[relation - 1], at.peer(relation),
        )

    for n, ring in enumerate(ups):
        relation = RELATIONS[n % 2][n // 2]
        value = ring.finish()
        if relation == 0:
            o_up[:, pl.ds(pl.multiple_of(me * up_width, 128), up_width)] = value
        else:
            stage[relation - 1] = value.astype(BF16)
            sent_across(relation).start()

    units = heads * GROUP

    def unit_stores(unit, slot):
        h, b = unit // GROUP, lax.rem(unit, GROUP)
        r = pl.ds(pl.multiple_of(b * rows, rows), rows)
        start = pl.multiple_of(h * staged.shape[2], 128)
        return pltpu.make_async_copy(
            staged.at[slot], o_project.at[r, pl.ds(start, staged.shape[2])], out_sem.at[slot]
        )

    def unrotated(value, r, scale):
        mid = QKH // 2
        first, second = value[:, :mid], value[:, mid:]
        c, s = cosine[r, :], sine[r, :]
        return jnp.concatenate(
            [(first * c + second * s) * scale, (second * c - first * s) * scale], axis=1
        )

    def unit_body(unit, carry):
        slot = lax.rem(unit, 2)
        h, b = unit // GROUP, lax.rem(unit, GROUP)
        r = pl.ds(pl.multiple_of(b * rows, rows), rows)
        back[...] = dot_back(branch[r, :], wo[pl.ds(pl.multiple_of(h * VH, VH), VH), :])
        for fetch in unit_loads(unit, slot):
            fetch.wait()

        @pl.when(unit >= 2)
        def _():
            unit_stores(unit - 2, slot).wait()

        gains = gain_group[h]

        def some_rows(n, carry):
            s = pl.ds(pl.multiple_of(n * step_rows, step_rows), step_rows)
            normal, scale = norm_parts(mixed[slot, s, :], GROUP_EPSILON)
            z = gate[slot, s, :]
            f = back[s, :]
            sigmoid = 1.0 / (1.0 + jnp.exp(-z))
            silu = z * sigmoid
            d_silu = f * (normal * gains)
            staged[slot, s, 2 * QKH + VH :] = (d_silu * (sigmoid + silu * (1.0 - sigmoid))).astype(BF16)
            d_scaled = f * silu
            o_group[h] += jnp.sum(d_scaled * normal, axis=0, keepdims=True)
            d_normal = d_scaled * gains
            d_mixed[s, :] = (
                scale
                * (
                    d_normal
                    - jnp.mean(d_normal, axis=-1, keepdims=True)
                    - normal * jnp.mean(d_normal * normal, axis=-1, keepdims=True)
                )
            ).astype(BF16)
            return carry

        lax.fori_loop(0, rows // step_rows, some_rows, 0)
        linked = (ident_col[b] == ident_row[b]) & (ident_col[b] >= 0.0)
        decay = jnp.where(linked, powers[h], 0.0)
        masked = (dot_back(query[slot], keys[slot]) * decay).astype(BF16)
        staged[slot, :, 2 * QKH : 2 * QKH + VH] = dot_rows(masked, d_mixed[...]).astype(BF16)
        d_raw = (dot_back(d_mixed[...], values[slot]) * decay).astype(BF16)
        d_query = dot(d_raw, keys[slot]) * QKH ** (-0.5)
        staged[slot, :, :QKH] = unrotated(d_query, r, growth[r, :]).astype(BF16)
        d_keys = dot_rows(d_raw, query[slot])
        staged[slot, :, QKH : 2 * QKH] = unrotated(d_keys, r, shrink[r, :]).astype(BF16)
        unit_stores(unit, slot).start()

        @pl.when(unit + 2 < units)
        def _():
            for fetch in unit_loads(unit + 2, slot):
                fetch.start()

        steps = total - 2
        add_steps(outs, 1 + (steps * unit) // units, 1 + (steps * (unit + 1)) // units)
        return carry

    lax.fori_loop(0, units, unit_body, 0)
    for relation in (1, 2, 3):
        sent_across(relation).wait_recv()
        o_up[:, pl.ds(pl.multiple_of(flip(me, relation) * up_width, 128), up_width)] = landed[
            relation - 1
        ].astype(F32)
        sent_across(relation).wait_send()
    for slot in (0, 1):
        unit_stores(jnp.int32(units - 2 + slot), slot).wait()
    for n, ring in enumerate(outs):
        c, way = n // 2, n % 2
        o_out[pl.ds(way * half, half), pl.ds(c * side, side)] = ring.finish()
    for c in range(chunks):
        for kind in range(6):
            copy(kind, c).wait_send()
    wait_added(downs + ups + outs, total)


def add_steps(rings, start, stop):
    def body(step, carry):
        for ring in rings:
            ring.onward(step)
        return carry

    lax.fori_loop(start, stop, body, 0)


def backward(
    total, g_down, two, d_upper, full_up, seed, hidden, gain_two, gated, full_out, query, keys, values, gate, mixed,
    tables, powers, ident_col, ident_row, gain_group,
):
    rows, width = seed.shape
    count = GROUP * rows
    heads = HEADS // GROUP
    up_width = d_upper.shape[1]
    r_out, r_up = g_down.shape[0] // total, width // GROUP // total
    half, side = r_out // 2, width // 2
    vmem, hbm = pl.BlockSpec(memory_space=pltpu.VMEM), pl.BlockSpec(memory_space=ANY)
    dma = pltpu.SemaphoreType.DMA
    shapes = (
        ((r_out, width), F32),
        ((r_up, up_width * GROUP), F32),
        ((r_out, width), F32),
        ((rows, width), F32),
        ((GROUP, rows, width), BF16),
        ((8, width), F32),
        ((heads, 1, VH), F32),
        ((count, 2 * heads * (QKH + VH)), BF16),
    )
    return pl.pallas_call(
        functools.partial(backward_kernel, total),
        out_shape=[jax.ShapeDtypeStruct(s, d) for s, d in shapes],
        in_specs=[vmem, hbm, hbm, hbm, vmem, vmem, vmem] + [hbm] * 7 + [vmem] * 8,
        out_specs=[vmem] * 4 + [hbm, vmem, vmem, hbm],
        scratch_shapes=[
            pltpu.VMEM((width, up_width), BF16),
            pltpu.VMEM(g_down.shape, BF16),
            pltpu.VMEM((12, total - 1, half, side), BF16),
            pltpu.VMEM((count, width), BF16),
            pltpu.VMEM((count, up_width), BF16),
            pltpu.VMEM(full_out.shape, BF16),
            pltpu.VMEM((GROUP, rows, width), BF16),
            pltpu.VMEM((2, rows, width), BF16),
            pltpu.VMEM((rows, width), BF16),
            pltpu.VMEM((rows, width), BF16),
            pltpu.VMEM((rows, width), BF16),
            pltpu.VMEM((2, rows, QKH), BF16),
            pltpu.VMEM((2, rows, QKH), BF16),
            pltpu.VMEM((2, rows, VH), BF16),
            pltpu.VMEM((2, rows, VH), F32),
            pltpu.VMEM((2, rows, VH), F32),
            pltpu.VMEM((rows, VH), F32),
            pltpu.VMEM((rows, VH), BF16),
            pltpu.VMEM((2, rows, 2 * (QKH + VH)), BF16),
            pltpu.VMEM((3, r_up, up_width), BF16),
            pltpu.VMEM((3, r_up, up_width), BF16),
            dma((12, total - 1)), dma((12, total - 1)), dma((6, 4)), dma((6, 4)), dma((4,)), dma((9,)),
            dma((2, 5)), dma((2,)), dma((3,)), dma((3,)),
        ],
        compiler_params=pltpu.CompilerParams(
            collective_id=2, has_side_effects=True, vmem_limit_bytes=63 * MIB
        ),
        name="backward_retention",
    )(
        g_down, two, d_upper, full_up, seed, hidden, gain_two, gated, full_out, query, keys, values, gate, mixed,
        *tables, powers, ident_col, ident_row, gain_group,
    )


def final_kernel(
    total, h_project, h_in, h_turned, h_active, h_down, hidden, d_hidden, tok, gains_all, ident_col, sums_two, d_group,
    o_in, output, d_tokens, o_vec, o_grp,
    project, turned, first_term, term, arrived, win, part, active, wd, rows_f32, core_in, out_x, in_x, stage, landed,
    vec, grp, near_in, mid, far_in, far_grp,
    load_sem, win_sem, ring_send, ring_recv, a2a_send, a2a_recv, row_send, row_recv,
    near_send, near_recv, far_send, far_recv,
):
    at = Place(total)
    me, inner = at.group, at.inner
    others = [(me, lax.rem(inner + n, total)) for n in range(1, total)]
    greet([at.peer(r) for r in (1, 2, 3)] + others)
    rows, width = tok.shape
    count = GROUP * rows
    block = o_in.shape[0]
    step_rows = 32

    fetch_turned = pltpu.make_async_copy(h_turned, turned, load_sem.at[0])
    fetch_project = pltpu.make_async_copy(h_project, project, load_sem.at[1])
    fetch_turned.start()
    fetch_project.start()

    def source(n, b):
        return part.at[pl.ds(pl.multiple_of(b * rows, rows), rows), :]

    def row_copy(kind, n):
        if kind < 2:
            return remote(
                source(n, flip(me, 3 - 2 * kind)), core_in.at[n, kind], row_send.at[n, kind], row_recv.at[n, kind],
                at.peer(1),
            )
        return remote(out_x.at[n], in_x.at[n], row_send.at[n, 2], row_recv.at[n, 2], at.peer(2))

    def own_rows(n, which, r):
        b = flip(me, 2) if which == 0 else me
        return part[pl.ds(pl.multiple_of(b * rows + r, step_rows), step_rows), :]

    def by_rows(body):
        def some(k, carry):
            body(pl.multiple_of(k * step_rows, step_rows))
            return carry

        lax.fori_loop(0, rows // step_rows, some, 0)

    def send_rows(n):
        row_copy(0, n).wait_recv()

        def some(r):
            s = pl.ds(r, step_rows)
            out_x[n, s, :] = (own_rows(n, 0, r).astype(F32) + core_in[n, 0, s, :].astype(F32)).astype(BF16)

        by_rows(some)
        row_copy(2, n).start()

    def summed_rows(n, r):
        s = pl.ds(r, step_rows)
        return own_rows(n, 1, r).astype(F32) + core_in[n, 1, s, :].astype(F32) + in_x[n, s, :].astype(F32)

    def take_down():
        fetch_hidden.wait()
        row_copy(1, 0).wait_recv()
        row_copy(2, 0).wait_recv()

        def some(r):
            s = pl.ds(r, step_rows)
            valid = jnp.where(ident_col[me, s, :] >= 0.0, 1.0, 0.0)
            output[s, :] = ((rows_f32[s, :] + summed_rows(0, r)) * valid).astype(BF16)

        by_rows(some)
        row_copy(0, 0).wait_send()
        row_copy(1, 0).wait_send()
        fetch_d_hidden.start()

    def take_rows():
        fetch_d_hidden.wait()
        row_copy(1, 1).wait_recv()
        row_copy(2, 1).wait_recv()
        vec[...] = jnp.zeros_like(vec)
        vec[2:4, :] = sums_two[0:2, :]

        def some(r):
            s = pl.ds(r, step_rows)
            e = summed_rows(1, r)
            normal, scale = norm_parts(tok[s, :].astype(F32), EPSILON)
            with_gain = e * gains_all[0:1, :]
            vec[0:1, :] += jnp.sum(e * normal, axis=0, keepdims=True)
            vec[1:2, :] += jnp.sum(e, axis=0, keepdims=True)
            value = rows_f32[s, :] + scale * (
                with_gain
                - jnp.mean(with_gain, axis=-1, keepdims=True)
                - normal * jnp.mean(with_gain * normal, axis=-1, keepdims=True)
            )
            d_tokens[s, :] = value.astype(BF16)

        by_rows(some)

    quarter = width // GROUP
    small = quarter // total
    large = grp.shape[1] // total

    def near(relation):
        start = pl.multiple_of(flip(me, relation) * quarter, 128)
        return remote(
            vec.at[:, pl.ds(start, quarter)], near_in.at[relation - 1], near_send.at[relation - 1],
            near_recv.at[relation - 1], at.peer(relation),
        )

    def tile_of(index, size):
        return pl.ds(pl.multiple_of((index * size) // 128 * 128, 128), 128)

    def distant(kind, n):
        target = lax.rem(inner + n, total)
        src = mid.at[:, tile_of(target, small)] if kind == 0 else grp.at[:, tile_of(target, large)]
        dst = far_in if kind == 0 else far_grp
        return remote(
            src, dst.at[n - 1], far_send.at[kind, n - 1], far_recv.at[kind, n - 1], (me, target)
        )

    def vectors_near():
        for relation in (1, 2, 3):
            near(relation).start()
        grp[...] = jnp.zeros_like(grp)
        for h in range(d_group.shape[0]):
            grp[0:1, h * VH : (h + 1) * VH] = d_group[h]

    def vectors_far():
        for relation in (1, 2, 3):
            near(relation).wait_recv()
        mid[...] = (
            vec[:, pl.ds(pl.multiple_of(me * quarter, 128), quarter)] + near_in[0] + near_in[1] + near_in[2]
        )
        for n in range(1, total):
            for kind in (0, 1):
                distant(kind, n).start()

    def vectors_end():
        for n in range(1, total):
            for kind in (0, 1):
                distant(kind, n).wait_recv()
        o_vec[...] = mid[:, tile_of(inner, small)] + jnp.sum(far_in[...], axis=0)
        o_grp[...] = grp[:, tile_of(inner, large)] + jnp.sum(far_grp[...], axis=0)

    wide = 512

    def terms(step, out):
        for way in (0, 1):
            which = at.behind(way, step + 1)
            left = jnp.concatenate(
                [
                    turned[
                        pl.ds(pl.multiple_of((flip(me, relation) * total + which) * block, block), block), :
                    ]
                    for relation in RELATIONS[way]
                ],
                axis=0,
            )

            def tile(n, carry, left=left, way=way):
                c = pl.ds(pl.multiple_of(n * wide, wide), wide)
                value = dot(left, project[:, c]).astype(BF16)
                out[2 * way, :, c] = value[:block]
                out[2 * way + 1, :, c] = value[block:]
                return carry

            lax.fori_loop(0, project.shape[1] // wide, tile, 0)

    def hop(slot, step, first=False):
        src = first_term.at[slot] if first else arrived.at[slot, step - 1]
        return remote(
            src, arrived.at[slot, step], ring_send.at[slot, step], ring_recv.at[slot, step],
            at.neighbour(slot // 2),
        )

    order = (0, 2, 1, 3)

    def onward(step, carry):
        terms(step, term)
        for slot in order:
            hop(slot, step - 1, True).wait_recv()
            arrived[slot, step - 1] = (
                arrived[slot, step - 1].astype(F32) + term[slot].astype(F32)
            ).astype(BF16)
            hop(slot, step).start()
        return carry

    parts = h_in.shape[0]
    part_width = h_in.shape[2]

    class fetch_win:
        def __init__(self, n):
            self.copies = [
                pltpu.make_async_copy(
                    h_in.at[h, pl.ds(n * 256, 256), :],
                    win.at[n % 2, :, pl.ds(h * part_width, part_width)],
                    win_sem.at[n % 2, h],
                )
                for h in range(parts)
            ]

        def start(self):
            for copy in self.copies:
                copy.start()

        def wait(self):
            for copy in self.copies:
                copy.wait()

    columns = width // 256

    def row_tiles(n):
        fetch_win(n).wait()

        def tile(m, carry):
            r = pl.ds(pl.multiple_of(m * 512, 512), 512)
            part[r, n * 256 : (n + 1) * 256] = dot_back(project[r, :], win[n % 2]).astype(BF16)
            return carry

        lax.fori_loop(0, count // 512, tile, 0)
        if n + 2 < columns:
            fetch_win(n + 2).start()

    def down_rows(relation):
        b = flip(me, relation)
        r = pl.ds(pl.multiple_of(b * rows, rows), rows)

        def column(n, carry):
            c = pl.ds(pl.multiple_of(n * wide, wide), wide)
            part[r, c] = dot(active[r, :], wd[:, c]).astype(BF16)
            return carry

        lax.fori_loop(0, width // wide, column, 0)

    fetch_active = pltpu.make_async_copy(h_active, active, load_sem.at[2])
    fetch_down = pltpu.make_async_copy(h_down, wd, load_sem.at[3])
    fetch_hidden = pltpu.make_async_copy(hidden, rows_f32, load_sem.at[4])
    fetch_d_hidden = pltpu.make_async_copy(d_hidden, rows_f32, load_sem.at[5])
    for fetch in (fetch_active, fetch_down, fetch_hidden):
        fetch.start()
    fetch_win(0).start()
    fetch_win(1).start()
    fetch_turned.wait()
    fetch_project.wait()
    terms(0, first_term)
    for slot in order:
        hop(slot, 0, True).start()
    fetch_active.wait()
    fetch_down.wait()
    down_rows(3)
    row_copy(0, 0).start()
    down_rows(2)
    down_rows(1)
    row_copy(1, 0).start()
    down_rows(0)
    send_rows(0)
    plan = tick_plan(total, 6)

    def extra(number):
        if number == 1:
            take_down()
        elif number in (2, 3):
            for n in range(columns * (number - 2) // 2, columns * (number - 1) // 2):
                row_tiles(n)
            if number == 3:
                row_copy(0, 1).start()
                row_copy(1, 1).start()
        elif number == 4:
            send_rows(1)
        elif number == 5:
            take_rows()
            vectors_near()

    for number in range(6):
        extra(number)
        lax.fori_loop(*plan[number], onward, 0)
    vectors_far()
    terms(total - 1, term)
    pieces = column_pieces()

    def place(other, value):
        for base, stride, h, off, size in pieces:
            start = pl.multiple_of(base + other * stride, 128)
            off = h * part_width + off
            o_in[:, pl.ds(start, size)] = value[:, off : off + size]

    def sent_across(relation):
        return remote(
            stage.at[relation - 1], landed.at[relation - 1],
            a2a_send.at[relation - 1], a2a_recv.at[relation - 1], at.peer(relation),
        )

    for slot in order:
        relation = RELATIONS[slot // 2][slot % 2]
        hop(slot, total - 2, True).wait_recv()
        value = arrived[slot, total - 2].astype(F32) + term[slot].astype(F32)
        if relation == 0:
            place(me, value)
        else:
            stage[relation - 1] = value.astype(BF16)
            sent_across(relation).start()
    vectors_end()
    for relation in (1, 2, 3):
        sent_across(relation).wait_recv()
        place(flip(me, relation), landed[relation - 1].astype(F32))
    for relation in (1, 2, 3):
        sent_across(relation).wait_send()
        near(relation).wait_send()
    for n in range(1, total):
        for kind in (0, 1):
            distant(kind, n).wait_send()
    row_copy(2, 0).wait_send()
    for kind in (0, 1, 2):
        row_copy(kind, 1).wait_send()

    def sent(step, carry):
        for slot in order:
            hop(slot, step, True).wait_send()
        return carry

    lax.fori_loop(0, total - 1, sent, 0)


def final(
    total, d_project, full_in, turned, active, full_down, hidden, d_hidden, tok, gains, ident_col, sums_two, d_group
):
    rows, width = tok.shape
    count, wide = d_project.shape
    block = width // GROUP // total
    vmem, hbm = pl.BlockSpec(memory_space=pltpu.VMEM), pl.BlockSpec(memory_space=ANY)
    dma = pltpu.SemaphoreType.DMA
    group_width = d_group.shape[0] * d_group.shape[2]
    shapes = (
        ((block, wide * GROUP), F32),
        ((rows, width), BF16),
        ((rows, width), BF16),
        ((8, 128), F32),
        ((8, 128), F32),
    )
    return pl.pallas_call(
        functools.partial(final_kernel, total),
        out_shape=[jax.ShapeDtypeStruct(s, d) for s, d in shapes],
        in_specs=[hbm] * 7 + [vmem] * 5,
        out_specs=[vmem] * 5,
        scratch_shapes=[
            pltpu.VMEM((count, wide), BF16),
            pltpu.VMEM(turned.shape, BF16),
            pltpu.VMEM((4, block, wide), BF16),
            pltpu.VMEM((4, block, wide), BF16),
            pltpu.VMEM((4, total - 1, block, wide), BF16),
            pltpu.VMEM((2, 256, wide), BF16),
            pltpu.VMEM((count, width), BF16),
            pltpu.VMEM(active.shape, BF16),
            pltpu.VMEM(full_down.shape, BF16),
            pltpu.VMEM((rows, width), F32),
            pltpu.VMEM((2, 2, rows, width), BF16),
            pltpu.VMEM((2, rows, width), BF16),
            pltpu.VMEM((2, rows, width), BF16),
            pltpu.VMEM((3, block, wide), BF16),
            pltpu.VMEM((3, block, wide), BF16),
            pltpu.VMEM((8, width), F32),
            pltpu.VMEM((8, group_width), F32),
            pltpu.VMEM((3, 8, width // GROUP), F32),
            pltpu.VMEM((8, width // GROUP), F32),
            pltpu.VMEM((total - 1, 8, 128), F32),
            pltpu.VMEM((total - 1, 8, 128), F32),
            dma((6,)), dma((2, 2)), dma((4, total - 1)), dma((4, total - 1)), dma((3,)), dma((3,)),
            dma((2, 3)), dma((2, 3)), dma((3,)), dma((3,)), dma((2, total - 1)), dma((2, total - 1)),
        ],
        compiler_params=pltpu.CompilerParams(
            collective_id=3, has_side_effects=True, vmem_limit_bytes=63 * MIB
        ),
        name="final_sums",
    )(d_project, full_in, turned, active, full_down, hidden, d_hidden, tok, gains, ident_col, sums_two, d_group)


def mean(values):
    return jnp.mean(values, axis=-1, keepdims=True)


def local(
    total,
    tokens,
    cotangent,
    w_in,
    w_out,
    w_up,
    w_down,
    ln1_gain,
    ln1_bias,
    group_gain,
    ln2_gain,
    ln2_bias,
    seq_lens,
    seq_owner,
    seq_offset,
):
    rows, width = tokens.shape
    heads = HEADS // GROUP
    qk, vv = heads * QKH, heads * VH
    me, inner = lax.axis_index("dp"), lax.axis_index("fsdp")
    small, large = ln1_gain.shape[0], group_gain.shape[0]

    count = GROUP * rows
    vectors = jnp.stack([ln1_gain, ln1_bias, ln2_gain, ln2_bias]).astype(F32)
    pack = jnp.zeros((8, 128), F32)
    pack = lax.dynamic_update_slice(pack, vectors, (0, lax.rem(inner * small, 128)))
    pack = lax.dynamic_update_slice(pack, group_gain.astype(F32)[None], (4, lax.rem(inner * large, 128)))
    rates = jnp.log1p(-(2.0 ** (-5.0 - (me * heads + jnp.arange(heads)).astype(F32))))
    rates = jnp.broadcast_to(rates[:, None, None], (heads, 1, rows))
    entries = jnp.stack([seq_lens, seq_owner, seq_offset])
    (
        full_in, full_up, full_out, full_down, _, turned, query, keys, values, gate, mixed, gated, active, d_upper,
        g_down, hidden, two,
        own_seed, cosine, sine, growth, shrink, powers, ident_col, ident_row, gains, gain_group,
    ) = forward(
        total, w_in, w_up, w_out, w_down, tokens, cotangent, pack, rates, entries[:, :, None], entries[:, None, :]
    )
    tables = (cosine, sine, growth, shrink)
    full_up = full_up.reshape(width, -1)
    full_out = full_out.reshape(-1, width)
    full_down = full_down.reshape(-1, width)
    two = two.reshape(count, width)
    grad_down, grad_up, grad_out, d_hidden, _, sums_two, d_group, d_project = backward(
        total, g_down.reshape(-1, width), two, d_upper, full_up, own_seed, hidden, gains, gated, full_out, query,
        keys, values, gate, mixed, tables, powers, ident_col, ident_row, gain_group,
    )
    grad_in, output, d_tokens, vec_one, vec_two = final(
        total, d_project, full_in, turned, active, full_down, hidden, d_hidden, tokens, gains, ident_col, sums_two,
        d_group,
    )
    grads = lax.dynamic_slice(vec_one, (0, lax.rem(inner * small, 128)), (4, small))
    grad_group = lax.dynamic_slice(vec_two, (0, lax.rem(inner * large, 128)), (1, large))[0]
    return (
        output,
        d_tokens,
        grad_in,
        grad_out,
        grad_up,
        grad_down,
        grads[0],
        grads[1],
        grad_group,
        grads[2],
        grads[3],
    )


def solution(mesh):
    flat = ("dp", "fsdp")
    matrix, vector = P(flat, None), P(flat)
    return jax.shard_map(
        functools.partial(local, mesh.shape["fsdp"]),
        mesh=mesh,
        in_specs=(matrix,) * 6 + (vector,) * 5 + (P(),) * 3,
        out_specs=(matrix,) * 6 + (vector,) * 5,
        check_vma=False,
    )
```

```python
import functools

import jax
import jax.numpy as jnp
import numpy as np
from jax import lax
from jax.experimental import pallas as pl
from jax.experimental.pallas import tpu as pltpu
from jax.sharding import PartitionSpec as P

HEADS = 8
QKH = 256
VH = 512
EPSILON = 1e-05
GROUP_EPSILON = 0.1
GROUP = 4
MESH = pl.DeviceIdType.MESH
ANY = pl.ANY
BF16 = jnp.bfloat16
F32 = jnp.float32
MIB = 1 << 20


def ring_place(index, total):
    half = index // 2
    return jnp.where(index % 2 == 0, half, total - 1 - half)


def ring_index(place, total):
    place = lax.rem(place + 2 * total, total)
    return jnp.where(place < total // 2, 2 * place, 2 * (total - 1 - place) + 1)


def flip(group_index, relation):
    low, high = group_index % 2, group_index // 2
    if relation % 2:
        low = 1 - low
    if relation // 2:
        high = 1 - high
    return 2 * high + low


class Place:
    def __init__(self, total):
        self.total = total
        self.group = lax.axis_index("dp")
        self.inner = lax.axis_index("fsdp")
        self.place = ring_place(self.inner, total)
        self.next = (
            ring_index(self.place + 1, total),
            ring_index(self.place - 1, total),
        )

    def peer(self, relation):
        return (flip(self.group, relation), self.inner)

    def neighbour(self, way):
        return (self.group, self.next[way])

    def behind(self, way, steps):
        return ring_index(self.place - steps if way == 0 else self.place + steps, self.total)


def greet(devices):
    barrier = pltpu.get_barrier_semaphore()
    for device in devices:
        pl.semaphore_signal(barrier, inc=1, device_id=device, device_id_type=MESH)
    pl.semaphore_wait(barrier, len(devices))


def remote(src, dst, send_sem, recv_sem, device):
    return pltpu.make_async_remote_copy(
        src_ref=src,
        dst_ref=dst,
        send_sem=send_sem,
        recv_sem=recv_sem,
        device_id=device,
        device_id_type=MESH,
    )


def column_pieces():
    heads = HEADS // GROUP
    table = []
    base, off = 0, 0
    for size in (QKH, QKH, VH, VH):
        for h in range(heads):
            table.append((base + h * size, heads * size, h, off, size))
        base += HEADS * size
        off += size
    return table


def dot(left, right):
    return jnp.dot(left, right, preferred_element_type=F32)


def dot_rows(left, right):
    return lax.dot_general(left, right, (((0,), (0,)), ((), ())), preferred_element_type=F32)


def dot_back(left, right):
    return lax.dot_general(left, right, (((1,), (1,)), ((), ())), preferred_element_type=F32)


def norm_parts(values, epsilon):
    center = values - jnp.mean(values, axis=-1, keepdims=True)
    spread = jnp.mean(center * center, axis=-1, keepdims=True)
    scale = lax.rsqrt(spread + epsilon)
    return center * scale, scale


RELATIONS = ((2, 0), (3, 1))


class Passing:
    def __init__(self, at, way, own, place, sends, recvs):
        self.at, self.way, self.own, self.place = at, way, own, place
        self.sends, self.recvs = sends, recvs

    def hop(self, step, first=False):
        which = self.at.inner if first else self.at.behind(self.way, step)
        dst = self.place(which)
        return remote(
            self.own if first else dst, dst, self.sends.at[step], self.recvs.at[step],
            self.at.neighbour(self.way),
        )

    def begin(self):
        self.hop(0, True).start()

    def onward(self, step):
        self.hop(step - 1).wait_recv()
        self.hop(step).start()

    def finish(self):
        self.hop(self.at.total - 2).wait_recv()


def wait_sent(rings, total):
    def body(step, carry):
        for ring in rings:
            ring.hop(step).wait_send()
        return carry

    lax.fori_loop(0, total - 1, body, 0)


def tick_plan(total, places):
    steps = total - 2
    cuts = [1 + (steps * n) // places for n in range(places + 1)]
    return list(zip(cuts[:-1], cuts[1:]))


def run_steps(rings, start, stop):
    def body(step, carry):
        for ring in rings:
            ring.onward(step)
        return carry

    lax.fori_loop(start, stop, body, 0)


def weight_rings(at, w_out, w_down, full_up, full_out, full_down, sends, recvs):
    me = at.group
    half = w_out.shape[0] // 2
    side = w_out.shape[1] // 2

    def halves(own, full, slot):
        return [
            Passing(
                at, way,
                own.at[pl.ds(way * half, half), pl.ds(c * side, side)],
                lambda which, way=way, c=c: full.at[which, pl.ds(way * half, half), pl.ds(c * side, side)],
                sends.at[slot + 2 * c + way], recvs.at[slot + 2 * c + way],
            )
            for c in (0, 1)
            for way in (0, 1)
        ]

    ups = []
    for order in (0, 1):
        for way in (0, 1):
            relation = RELATIONS[way][order]
            slot = 8 + 2 * order + way
            ups.append(
                Passing(
                    at, way, full_up.at[flip(me, relation), at.inner],
                    lambda which, relation=relation: full_up.at[flip(me, relation), which],
                    sends.at[slot], recvs.at[slot],
                )
            )
    return halves(w_out, full_out, 0), ups, halves(w_down, full_down, 4)


def rotated(value, cosine, sine, scale):
    half = QKH // 2
    first, second = value[:, :half], value[:, half:]
    return jnp.concatenate(
        [(first * cosine - second * sine) * scale, (second * cosine + first * sine) * scale], axis=1
    )


def forward_kernel(
    total, w_in, w_up, w_out, w_down, h_tok, h_cot, pack, rates, seq_cols, seq_rows, curves,
    full_in, full_up, full_out, full_down, full_seed, o_turned, o_query, o_keys, o_values, o_gate, o_mixed,
    o_gated, o_active, o_upper, o_g_down, to_hidden, full_two, to_seed, to_cosine, to_sine, to_growth, to_shrink,
    to_powers, ident_col, ident_row, gains, gain_group,
    hidden, own_seed, cosine, sine, growth, shrink, powers, tok, cot,
    win, part, x, query, keys, values, gate, mixed, gated, wo, core_in, out_x, in_x, low, full_vec,
    win_up, wd, ring_send, ring_recv, own_sem, load_sem, fetch_sem, store_sem, row_send, row_recv, row_own,
    swap_send, swap_recv, swap_own, vec_send, vec_recv, early_sem,
):
    at = Place(total)
    me, inner = at.group, at.inner
    core, across = at.peer(1), at.peer(2)
    others = [(me, lax.rem(inner + n, total)) for n in range(1, total)]
    greet([core, across, at.peer(3)] + others)
    rows, width = tok.shape
    count = GROUP * rows
    heads = HEADS // GROUP
    r_in = w_in.shape[0]
    up_width = full_up.shape[-1]
    pieces = column_pieces()
    step_rows = 32

    def rows_in(group_index, which):
        return pl.ds(pl.multiple_of((group_index * total + which) * r_in, r_in), r_in)

    last = len(pieces)

    def swap(relation, slot):
        other = flip(me, relation)
        if slot < last:
            base, stride, h, off, size = pieces[slot]
            src = w_in.at[:, pl.ds(pl.multiple_of(base + other * stride, 128), size)]
            dst = win.at[h, rows_in(me, inner), pl.ds(off, size)]
        elif slot == last:
            src = w_up.at[:, pl.ds(pl.multiple_of(other * up_width, 128), up_width)]
            dst = full_up.at[me, inner]
        elif slot == last + 1:
            src, dst = pack, full_vec.at[inner, me]
        elif slot == last + 2:
            src, dst = h_tok, part.at[me]
        else:
            src, dst = own_seed, full_seed.at[me]
        if relation == 0:
            return pltpu.make_async_copy(src, dst, swap_own.at[slot])
        return remote(
            src, dst, swap_send.at[relation - 1, slot], swap_recv.at[relation - 1, slot], at.peer(relation)
        )

    def arrived(relation, slot):
        if relation == 0:
            swap(0, slot).wait()
        else:
            swap(relation, slot).wait_recv()

    for h in range(heads):
        for relation in (1, 0, 2, 3):
            for slot in range(last):
                if pieces[slot][2] == h:
                    swap(relation, slot).start()
        if h == 0:
            for relation in range(4):
                swap(relation, last + 1).start()
    for slot in (last + 2, last):
        for relation in (1, 0, 2, 3):
            swap(relation, slot).start()

    fetch_cot = pltpu.make_async_copy(h_cot, cot, early_sem.at[0])
    fetch_tok = pltpu.make_async_copy(h_tok, tok, early_sem.at[1])
    fetch_cot.start()
    fetch_tok.start()
    early_stores = [
        pltpu.make_async_copy(src, dst, early_sem.at[2 + n])
        for n, (src, dst) in enumerate(
            (
                (own_seed, to_seed), (cosine, to_cosine), (sine, to_sine), (growth, to_growth),
                (shrink, to_shrink), (powers, to_powers), (hidden, to_hidden),
            )
        )
    ]

    def in_ring(h, relation):
        def place(which):
            return win.at[h, rows_in(flip(me, relation), which), :]

        slot = 12 + 4 * h + relation
        return Passing(at, relation % 2, place(inner), place, ring_send.at[slot], ring_recv.at[slot])

    ins = [[in_ring(h, relation) for relation in range(4)] for h in range(heads)]
    near, far_in = ins[0][:2], ins[0][2:]

    def await_head(h, relation):
        for slot in range(last):
            if pieces[slot][2] == h:
                arrived(relation, slot)

    for relation in (0, 1):
        await_head(0, relation)
        near[relation].begin()

    def layout_of(b, down):
        shape = (rows, 1) if down else (1, rows)
        source = seq_rows if down else seq_cols
        lens, owner, offset = source[0], source[1], source[2]
        positions = lax.broadcasted_iota(jnp.int32, shape, 0 if down else 1)
        inside = (
            (owner == b * total + inner)
            & (lens > 0)
            & (positions >= offset)
            & (positions < offset + lens)
        )
        axis = 1 if down else 0
        number = lax.broadcasted_iota(jnp.int32, lens.shape, axis).astype(F32) + 1.0
        ident = jnp.sum(jnp.where(inside, number, 0.0), axis=axis, keepdims=True) - 1.0
        starts = jnp.sum(jnp.where(inside, offset.astype(F32), 0.0), axis=axis, keepdims=True)
        places = jnp.where(ident >= 0.0, positions.astype(F32) - starts, 0.0)
        return ident, places

    for b in range(GROUP):
        ident_col[b] = layout_of(b, True)[0]
        ident_row[b] = layout_of(b, False)[0]

    def seed_rows(n, carry):
        s = pl.ds(pl.multiple_of(n * step_rows, step_rows), step_rows)
        valid = jnp.where(ident_col[me, s, :] >= 0.0, 1.0, 0.0)
        own_seed[s, :] = (cot[s, :].astype(F32) * valid).astype(BF16)
        return carry

    fetch_cot.wait()
    lax.fori_loop(0, rows // step_rows, seed_rows, 0)
    early_stores[0].start()

    for relation in range(4):
        arrived(relation, last + 1)

    def spread(n):
        target = lax.rem(inner + n, total)
        return remote(
            full_vec.at[inner], full_vec.at[inner], vec_send.at[n - 1], vec_recv.at[n - 1], (me, target)
        )

    for n in range(1, total):
        spread(n).start()
    for ring in near:
        ring.onward(1)
    for relation in (2, 3):
        await_head(0, relation)
        far_in[relation - 2].begin()
    for relation in (1, 0, 2, 3):
        swap(relation, last + 3).start()

    def both_in(step, carry):
        for ring in near:
            ring.onward(step)
        for ring in far_in:
            ring.onward(step - 1)
        return carry

    def take_vectors():
        for n in range(1, total):
            spread(n).wait_recv()
        quarter = width // GROUP
        small = quarter // total
        large = heads * VH // total
        for d in range(GROUP):
            tiles = {}
            for f in range(total):
                t = f * small // 128
                value = full_vec[f, d]
                tiles[t] = tiles[t] + value if t in tiles else value
            for t, value in tiles.items():
                gains[:, d * quarter + t * 128 : d * quarter + (t + 1) * 128] = value
        tiles = {}
        for f in range(total):
            t = f * large // 128
            value = full_vec[f, me, 4:5, :]
            tiles[t] = tiles[t] + value if t in tiles else value
        for t, value in tiles.items():
            h, off = t * 128 // VH, t * 128 % VH
            gain_group[h, :, off : off + 128] = value

    def make_tables():
        distance = lax.broadcasted_iota(jnp.int32, (rows, rows), 0) - lax.broadcasted_iota(
            jnp.int32, (rows, rows), 1
        )
        away = jnp.maximum(distance, 0).astype(F32)
        for h in range(heads):
            powers[h] = jnp.where(distance >= 0, jnp.exp(rates[h] * away), 0.0)
        for b in range(GROUP):
            places = layout_of(b, True)[1]
            angles = places * curves[0:1, :]
            r = slice(b * rows, (b + 1) * rows)
            cosine[r, :] = jnp.cos(angles)
            sine[r, :] = jnp.sin(angles)
            lift = places * (1.0 / 512.0) * curves[1:2, :]
            growth[r, :] = jnp.exp(lift)
            shrink[r, :] = jnp.exp(-lift)
        for store_one in early_stores[1:6]:
            store_one.start()

    def norm_buffer(relation):
        b = flip(me, relation)
        arrived(relation, last + 2)

        def norm_rows(n, carry):
            r = pl.multiple_of(n * step_rows, step_rows)
            normal, _ = norm_parts(part[b, pl.ds(r, step_rows), :].astype(F32), EPSILON)
            at_rows = pl.ds(pl.multiple_of(b * rows + r, step_rows), step_rows)
            x[at_rows, :] = (normal * gains[0:1, :] + gains[1:2, :]).astype(BF16)
            return carry

        lax.fori_loop(0, rows // step_rows, norm_rows, 0)

    beside = [
        make_tables,
        take_vectors,
        lambda: (norm_buffer(0), norm_buffer(1)),
        lambda: norm_buffer(2),
        lambda: norm_buffer(3),
    ]
    cuts = [2 + (total - 3) * n // 5 for n in range(6)]
    for n in range(5):
        lax.fori_loop(cuts[n], cuts[n + 1], both_in, 0)
        beside[n]()
    for ring in far_in:
        ring.onward(total - 2)
    for h in range(1, heads):
        for relation in range(4):
            await_head(h, relation)
            ins[h][relation].begin()
    outs, ups, downs = weight_rings(
        at, w_out, w_down, full_up, full_out, wd, ring_send, ring_recv
    )
    own_copies = [
        pltpu.make_async_copy(w_out, full_out.at[inner], own_sem.at[0]),
        pltpu.make_async_copy(w_down, wd.at[inner], own_sem.at[1]),
    ]
    for copy in own_copies:
        copy.start()
    plan = tick_plan(total, 6)
    tile = 512

    def project(h, off, m):
        r = pl.ds(pl.multiple_of(m * tile, tile), tile)
        return r, dot(x[r, :], win[h, :, off : off + QKH])

    def turn_tile(h, m):
        r, value = project(h, 0, m)
        turned = rotated(value, cosine[r, :], sine[r, :], growth[r, :])
        query[h, r, :] = (turned * QKH ** (-0.5)).astype(BF16)
        r, value = project(h, QKH, m)
        keys[h, r, :] = rotated(value, cosine[r, :], sine[r, :], shrink[r, :]).astype(BF16)

    def plain_tile(h, c, m):
        off = c * QKH
        r, value = project(h, 2 * QKH + off, m)
        values[h, r, off : off + QKH] = value.astype(BF16)
        r, value = project(h, 2 * QKH + VH + off, m)
        gate[h, r, off : off + QKH] = value

    def retain(h, b):
        r = pl.ds(pl.multiple_of(b * rows, rows), rows)
        raw = dot_back(query[h, r, :], keys[h, r, :])
        linked = (ident_col[b] == ident_row[b]) & (ident_col[b] >= 0.0)
        masked = (raw * jnp.where(linked, powers[h], 0.0)).astype(BF16)
        mixed[h, r, :] = dot(masked, values[h, r, :])

        def some_rows(n, carry):
            s = pl.ds(pl.multiple_of(b * rows + n * step_rows, step_rows), step_rows)
            normal, _ = norm_parts(mixed[h, s, :], GROUP_EPSILON)
            z = gate[h, s, :]
            result = z / (1.0 + jnp.exp(-z)) * (normal * gain_group[h])
            gated[s, h * VH : (h + 1) * VH] = result.astype(BF16)
            return carry

        lax.fori_loop(0, rows // step_rows, some_rows, 0)

    def looped(count_of, body):
        def some(n, carry):
            body(n)
            return carry

        lax.fori_loop(0, count_of, some, 0)

    def head_units(h):
        return [
            lambda: looped(count // tile, lambda m: turn_tile(h, m)),
            lambda: looped(count // tile, lambda m: plain_tile(h, 0, m)),
            lambda: looped(count // tile, lambda m: plain_tile(h, 1, m)),
            lambda: looped(2, lambda b: retain(h, b)),
            lambda: looped(2, lambda b: retain(h, 2 + b)),
        ]

    stores = []

    def store_head(h):
        for n, (src, dst) in enumerate(
            ((win, full_in), (query, o_query), (keys, o_keys), (values, o_values), (gate, o_gate), (mixed, o_mixed))
        ):
            copy = pltpu.make_async_copy(src.at[h], dst.at[h], store_sem.at[h, n])
            copy.start()
            stores.append(copy)

    for h in range(heads):
        ring_set = ins[h + 1] if h + 1 < heads else outs
        if h + 1 == heads:
            for ring in outs:
                ring.begin()
        for ring in ins[h]:
            ring.finish()
        units = head_units(h)
        for number in range(6):
            if number < len(units):
                units[number]()
            run_steps(ring_set, *plan[number])
        store_head(h)
    for relation in range(4):
        arrived(relation, last)
    for ring in ups:
        ring.begin()
    for ring in outs:
        ring.finish()
    stores.append(pltpu.make_async_copy(gated, o_gated, store_sem.at[0, 6]))
    stores[-1].start()
    own_copies[0].wait()
    block = w_out.shape[0]
    fetch = pltpu.make_async_copy(full_out, wo, load_sem.at[0])
    fetch.start()
    fetch.wait()

    chunks = 4
    size = rows // chunks

    def branch(relation):
        b = flip(me, relation)

        def column(n, carry):
            wide = 512
            c = pl.ds(pl.multiple_of(n * wide, wide), wide)
            r = pl.ds(pl.multiple_of(b * rows, rows), rows)
            acc = jnp.zeros((rows, wide), F32)
            piece = gated[r, :]
            acc = dot(piece, wo[:, :, c].reshape(total * block, wide))
            part[b, :, c] = acc.astype(BF16)
            return carry

        lax.fori_loop(0, width // 512, column, 0)

    def rows_of(c):
        return pl.ds(c * size, size)

    far = flip(me, 2)

    def copy(kind, c):
        r = rows_of(c)
        if kind == 0:
            src, dst, dev = part.at[flip(me, 3), r], core_in.at[0, r], core
        elif kind == 1:
            src, dst, dev = part.at[flip(me, 1), r], core_in.at[1, r], core
        elif kind == 2:
            src, dst, dev = out_x.at[r], in_x.at[r], across
        elif kind == 3:
            src, dst, dev = low.at[r], full_two.at[me, r], across
        elif kind == 4:
            src, dst, dev = low.at[r], full_two.at[me, r], core
        else:
            src, dst, dev = full_two.at[far, r], full_two.at[far, r], core
        return remote(src, dst, row_send.at[kind, c], row_recv.at[kind, c], dev)

    def store(c):
        r = rows_of(c)
        return pltpu.make_async_copy(low.at[r], full_two.at[me, r], row_own.at[c])

    branch(3)
    for c in range(chunks):
        copy(0, c).start()
    branch(2)
    run_steps(ups, *plan[0])
    for c in range(chunks):
        r = rows_of(c)
        copy(0, c).wait_recv()
        out_x[r, :] = (part[far, r, :].astype(F32) + core_in[0, r, :].astype(F32)).astype(BF16)
        copy(2, c).start()
    branch(1)
    for c in range(chunks):
        copy(1, c).start()
    branch(0)
    run_steps(ups, *plan[1])
    for copy_out in stores:
        copy_out.wait()
    fetch_tok.wait()
    wait_sent([ring for rings in ins for ring in rings], total)

    def turn(n, carry):
        i, j = n // (count // 256), lax.rem(n, count // 256)
        i, j = (pl.ds(pl.multiple_of(k * 256, 256), 256) for k in (i, j))
        win[0, i, j] = x[j, i].T
        return carry

    blocks = (width // 256) * (count // 256)
    lax.fori_loop(0, blocks // 2, turn, 0)
    run_steps(ups, *plan[2])
    for c in range(chunks):
        r = rows_of(c)
        copy(1, c).wait_recv()
        copy(2, c).wait_recv()

        def finish_rows(n, carry, c=c):
            s = pl.ds(pl.multiple_of(c * size + n * step_rows, step_rows), step_rows)
            value = tok[s, :].astype(F32) + (
                part[me, s, :].astype(F32) + core_in[1, s, :].astype(F32) + in_x[s, :].astype(F32)
            )
            hidden[s, :] = value
            normal, _ = norm_parts(value, EPSILON)
            low[s, :] = (normal * gains[2:3, :] + gains[3:4, :]).astype(BF16)
            return carry

        lax.fori_loop(0, size // step_rows, finish_rows, 0)
        copy(3, c).start()
        copy(4, c).start()
        store(c).start()
        if c:
            run_steps(ups, *plan[2 + c])
    early_stores[6].start()
    for ring in downs:
        ring.begin()
    lax.fori_loop(blocks // 2, blocks, turn, 0)
    store_turned = pltpu.make_async_copy(win.at[0, :, pl.ds(0, count)], o_turned, own_sem.at[0])
    store_turned.start()
    for relation in range(4):
        arrived(relation, last + 3)
    fetch_seed = [
        pltpu.make_async_copy(full_seed.at[b], x.at[pl.ds(b * rows, rows)], fetch_sem.at[b])
        for b in range(GROUP)
    ]
    for fetch in fetch_seed:
        fetch.start()
    for ring in ups:
        ring.finish()
    fetch_up = [
        pltpu.make_async_copy(full_up.at[b], win_up.at[b], fetch_sem.at[GROUP + b]) for b in range(GROUP)
    ]
    for fetch in fetch_up:
        fetch.start()
    for c in range(chunks):
        copy(3, c).wait_recv()
        copy(5, c).start()
        if c % 2:
            run_steps(downs, *plan[c // 2])
    for c in range(chunks):
        copy(4, c).wait_recv()
        copy(5, c).wait_recv()
        store(c).wait()
        for kind in range(6):
            copy(kind, c).wait_send()
    fetch_two = pltpu.make_async_copy(full_two, part, load_sem.at[1])
    fetch_two.start()
    for fetch in fetch_seed + fetch_up:
        fetch.wait()
    fetch_two.wait()

    quarters = heads * VH // 256

    def upper_tile(n, carry):
        b, j = n // quarters, lax.rem(n, quarters)
        c = pl.ds(pl.multiple_of(j * 256, 256), 256)
        r = pl.ds(pl.multiple_of(b * rows, rows), rows)
        upper = dot(part[b], win_up[:, :, :, c].reshape(width, 256))
        cdf = 0.5 * (1.0 + lax.erf(upper * (0.5**0.5)))
        gated[r, c] = (upper * cdf).astype(BF16)
        half = pl.ds(pl.multiple_of(lax.rem(j, 2) * 256, 256), 256)
        gate[j // 2, r, half] = cdf + upper * jnp.exp(-0.5 * upper * upper) * (2.0 * np.pi) ** -0.5
        return carry

    tiles = GROUP * quarters
    lax.fori_loop(0, tiles // 2, upper_tile, 0)
    run_steps(downs, *plan[2])
    lax.fori_loop(tiles // 2, tiles, upper_tile, 0)
    run_steps(downs, *plan[3])
    store_active = pltpu.make_async_copy(gated, o_active, store_sem.at[0, 0])
    store_active.start()
    per_tile = 256 // block
    wide = 512

    def down_tile(n, carry):
        i, j = n // (width // wide), lax.rem(n, width // wide)
        a = pl.ds(pl.multiple_of(i * 256, 256), 256)
        c = pl.ds(pl.multiple_of(j * wide, wide), wide)
        value = dot_rows(gated[:, a], x[:, c]).astype(BF16)
        wo[pl.ds(i * per_tile, per_tile), :, c] = value.reshape(per_tile, block, wide)
        return carry

    tiles = quarters * (width // wide)
    lax.fori_loop(0, tiles // 2, down_tile, 0)
    run_steps(downs, *plan[4])
    lax.fori_loop(tiles // 2, tiles, down_tile, 0)
    run_steps(downs, *plan[5])
    store_down = pltpu.make_async_copy(wo, o_g_down, store_sem.at[0, 1])
    store_down.start()
    own_copies[1].wait()
    for ring in downs:
        ring.finish()
    store_full = pltpu.make_async_copy(wd, full_down, load_sem.at[0])
    store_full.start()

    def d_upper_tile(n, carry):
        h, j = n // 4, lax.rem(n, 4)
        m, side = j // 2, lax.rem(j, 2)
        r = pl.ds(pl.multiple_of(m * tile, tile), tile)
        c = pl.ds(pl.multiple_of(side * 256, 256), 256)
        piece = wd[pl.ds((2 * h + side) * per_tile, per_tile)].reshape(256, width)
        values[h, r, c] = (dot_back(x[r, :], piece) * gate[h, r, c]).astype(BF16)
        return carry

    last_stores = [store_active, store_down, store_full]
    for h in range(heads):
        lax.fori_loop(4 * h, 4 * (h + 1), d_upper_tile, 0)
        last_stores.append(
            pltpu.make_async_copy(values.at[h], o_upper.at[:, pl.ds(h * VH, VH)], store_sem.at[0, 2 + h])
        )
        last_stores[-1].start()
    wait_sent(outs + downs + ups, total)
    for relation in (1, 2, 3):
        for slot in range(last + 4):
            swap(relation, slot).wait_send()
    for n in range(1, total):
        spread(n).wait_send()
    store_turned.wait()
    for copy_out in last_stores + early_stores:
        copy_out.wait()


def forward(total, w_in, w_up, w_out, w_down, tok, cot, pack, rates, seq_cols, seq_rows):
    rows, width = tok.shape
    count = GROUP * rows
    heads = HEADS // GROUP
    head_width = 2 * (QKH + VH)
    vmem, hbm = pl.BlockSpec(memory_space=pltpu.VMEM), pl.BlockSpec(memory_space=ANY)
    dma = pltpu.SemaphoreType.DMA
    pair = np.arange(QKH // 2) / (QKH // 2)
    curves = np.zeros((8, QKH // 2), np.float32)
    curves[0] = 10000.0**-pair
    curves[1] = np.log((pair + 0.4) / 1.4)
    kept = (
        ((heads, count, QKH), BF16),
        ((heads, count, QKH), BF16),
        ((heads, count, VH), BF16),
        ((heads, count, VH), F32),
        ((heads, count, VH), F32),
        ((count, heads * VH), BF16),
    )
    in_hbm = (
        ((heads, width, head_width), BF16),
        ((GROUP, total, w_up.shape[0], w_up.shape[1] // GROUP), BF16),
        ((total,) + w_out.shape, BF16),
        ((total,) + w_down.shape, BF16),
        ((GROUP, rows, width), BF16),
        ((width, count), BF16),
        *kept,
        kept[-1],
        kept[-1],
        ((total,) + w_out.shape, BF16),
    )
    in_vmem = (
        ((rows, width), BF16),
        ((count, QKH // 2), F32),
        ((count, QKH // 2), F32),
        ((count, QKH // 2), F32),
        ((count, QKH // 2), F32),
        ((heads, rows, rows), F32),
        ((GROUP, rows, 1), F32),
        ((GROUP, 1, rows), F32),
        ((8, width), F32),
        ((heads, 1, VH), F32),
    )
    shapes = (*in_hbm, ((rows, width), F32), ((GROUP, rows, width), BF16), *in_vmem)
    return pl.pallas_call(
        functools.partial(forward_kernel, total),
        out_shape=[jax.ShapeDtypeStruct(s, d) for s, d in shapes],
        in_specs=[hbm] * 6 + [vmem] * 5,
        out_specs=[hbm] * (len(in_hbm) + 8) + [vmem] * 4,
        scratch_shapes=[
            pltpu.VMEM((rows, width), F32),
            *[pltpu.VMEM(s, d) for s, d in in_vmem[:6]],
            pltpu.VMEM((rows, width), BF16),
            pltpu.VMEM((rows, width), BF16),
            pltpu.VMEM((heads, width, head_width), BF16),
            pltpu.VMEM((GROUP, rows, width), BF16),
            pltpu.VMEM((count, width), BF16),
            *[pltpu.VMEM(s, d) for s, d in kept],
            pltpu.VMEM((total,) + w_out.shape, BF16),
            pltpu.VMEM((2, rows, width), BF16),
            pltpu.VMEM((rows, width), BF16),
            pltpu.VMEM((rows, width), BF16),
            pltpu.VMEM((rows, width), BF16),
            pltpu.VMEM((total, GROUP, 8, 128), F32),
            pltpu.VMEM((GROUP, total, w_up.shape[0], w_up.shape[1] // GROUP), BF16),
            pltpu.VMEM((total,) + w_down.shape, BF16),
            dma((20, total - 1)), dma((20, total - 1)), dma((2,)), dma((2,)), dma((2 * GROUP,)),
            dma((heads, 7)), dma((6, 4)), dma((6, 4)), dma((4,)),
            dma((3, 12)), dma((3, 12)), dma((12,)), dma((total - 1,)), dma((total - 1,)), dma((9,)),
        ],
        compiler_params=pltpu.CompilerParams(
            collective_id=1, has_side_effects=True, vmem_limit_bytes=63 * MIB
        ),
        name="forward_retention",
    )(w_in, w_up, w_out, w_down, tok, cot, pack, rates, seq_cols, seq_rows, jnp.asarray(curves))


class Adding:
    def __init__(self, at, way, term, arrived, sends, recvs, origin=None):
        self.at, self.way, self.term, self.arrived = at, way, term, arrived
        self.origin = term if origin is None else origin
        self.sends, self.recvs = sends, recvs

    def hop(self, step, first=False):
        src = self.origin(self.at.behind(self.way, 1)) if first else self.arrived.at[step - 1]
        return remote(
            src, self.arrived.at[step], self.sends.at[step], self.recvs.at[step], self.at.neighbour(self.way)
        )

    def begin(self):
        self.hop(0, True).start()

    def sum_at(self, step, which):
        self.hop(step, True).wait_recv()
        return self.arrived[step].astype(F32) + self.term(which)[...].astype(F32)

    def onward(self, step):
        self.arrived[step - 1] = self.sum_at(step - 1, self.at.behind(self.way, step + 1)).astype(BF16)
        self.hop(step).start()

    def finish(self):
        return self.sum_at(self.at.total - 2, self.at.inner)


def wait_added(rings, total):
    def body(step, carry):
        for ring in rings:
            ring.hop(step, True).wait_send()
        return carry

    lax.fori_loop(0, total - 1, body, 0)


def backward_kernel(
    total, h_g_down, two, d_upper, h_up, h_seed, h_hidden, gains_all, h_gated, h_out, h_query, h_keys, h_values,
    h_gate, h_mixed, h_cosine, h_sine, h_growth, h_shrink, h_powers, ident_col, ident_row, gain_group,
    to_down, to_up, to_out, to_hidden, full_branch, sums, o_group, o_project,
    g_down, seed, hidden, cosine, sine, growth, shrink, powers, o_down, o_up, o_out, d_hidden, g_up, g_out, arrived, wide_buf, narrow_buf, wo, part, core_in, out_x, in_x, low,
    query, keys, values, gate, mixed, back, d_mixed, staged, stage, landed,
    ring_send, ring_recv, row_send, row_recv, row_own, load_sem, late_sem, unit_sem, out_sem, a2a_send, a2a_recv,
):
    at = Place(total)
    me = at.group
    core, across = at.peer(1), at.peer(2)
    greet([core, across, at.peer(3), at.neighbour(0), at.neighbour(1)])
    rows, width = seed.shape
    count = GROUP * rows
    heads = HEADS // GROUP
    r_up, r_out = o_up.shape[0], o_out.shape[0]
    up_width = o_up.shape[1] // GROUP
    half, side = r_out // 2, width // 2

    def halves(source, base, origin=None):
        def chunk_of(ref, way, c):
            return lambda which: ref.at[
                pl.ds(pl.multiple_of(which * r_out + way * half, half), half), pl.ds(c * side, side)
            ]

        return [
            Adding(
                at, way,
                chunk_of(source, way, c),
                arrived.at[base + 2 * c + way], ring_send.at[base + 2 * c + way], ring_recv.at[base + 2 * c + way],
                None if origin is None else chunk_of(origin, way, c),
            )
            for c in (0, 1)
            for way in (0, 1)
        ]

    downs, outs, ups = halves(g_down, 0, h_g_down), halves(g_out, 8), []
    for order in (0, 1):
        for way in (0, 1):
            relation = RELATIONS[way][order]
            slot = 4 + 2 * order + way
            ups.append(
                Adding(
                    at, way,
                    lambda which, relation=relation: g_up.at[
                        pl.ds(pl.multiple_of((flip(me, relation) * total + which) * r_up, r_up), r_up), :
                    ],
                    arrived.at[slot], ring_send.at[slot], ring_recv.at[slot],
                )
            )

    chunks = 4
    size = rows // chunks
    step_rows = 32
    far = flip(me, 2)

    def rows_of(c):
        return pl.ds(c * size, size)

    def copy(kind, c):
        r = rows_of(c)
        if kind == 0:
            src, dst, dev = part.at[flip(me, 3), r], core_in.at[0, r], core
        elif kind == 1:
            src, dst, dev = part.at[flip(me, 1), r], core_in.at[1, r], core
        elif kind == 2:
            src, dst, dev = out_x.at[r], in_x.at[r], across
        elif kind == 3:
            src, dst, dev = low.at[r], full_branch.at[me, r], across
        elif kind == 4:
            src, dst, dev = low.at[r], full_branch.at[me, r], core
        else:
            src, dst, dev = full_branch.at[far, r], full_branch.at[far, r], core
        return remote(src, dst, row_send.at[kind, c], row_recv.at[kind, c], dev)

    def store(c):
        r = rows_of(c)
        return pltpu.make_async_copy(low.at[r], full_branch.at[me, r], row_own.at[c])

    for ring in downs:
        ring.begin()
    upper_columns = pl.ds(0, up_width)
    fetch_upper = pltpu.make_async_copy(d_upper, g_out.at[:, upper_columns], load_sem.at[1])
    fetch_up = pltpu.make_async_copy(h_up, g_up, load_sem.at[7])
    fetch_two = pltpu.make_async_copy(two, wide_buf, load_sem.at[0])
    fetch_gated = pltpu.make_async_copy(h_gated, narrow_buf, load_sem.at[8])
    fetch_out = pltpu.make_async_copy(h_out, wo, load_sem.at[2])
    fetch_rows = [
        pltpu.make_async_copy(src, dst, late_sem.at[n])
        for n, (src, dst) in enumerate(((h_g_down, g_down), (h_seed, seed), (h_hidden, hidden)))
    ]
    fetch_tables = [
        pltpu.make_async_copy(src, dst, late_sem.at[3 + n])
        for n, (src, dst) in enumerate(
            ((h_cosine, cosine), (h_sine, sine), (h_growth, growth), (h_shrink, shrink), (h_powers, powers))
        )
    ]
    stores = [
        pltpu.make_async_copy(src, dst, late_sem.at[8 + n])
        for n, (src, dst) in enumerate(((o_down, to_down), (o_up, to_up), (o_out, to_out), (d_hidden, to_hidden)))
    ]
    for fetch in (fetch_upper, fetch_up, *fetch_rows, fetch_two, fetch_gated, fetch_out, *fetch_tables):
        fetch.start()

    def unit_loads(unit, slot):
        h, b = unit // GROUP, lax.rem(unit, GROUP)
        r = pl.ds(pl.multiple_of(b * rows, rows), rows)
        pairs = ((h_query, query), (h_keys, keys), (h_values, values), (h_gate, gate), (h_mixed, mixed))
        return [
            pltpu.make_async_copy(src.at[h, r], dst.at[slot], unit_sem.at[slot, n])
            for n, (src, dst) in enumerate(pairs)
        ]

    for unit in (0, 1):
        for fetch in unit_loads(jnp.int32(unit), unit):
            fetch.start()

    def send_sums(c):
        r = rows_of(c)
        copy(0, c).wait_recv()
        out_x[r, :] = (part[far, r, :].astype(F32) + core_in[0, r, :].astype(F32)).astype(BF16)
        copy(2, c).start()

    def norm_back(c):
        copy(1, c).wait_recv()
        copy(2, c).wait_recv()

        def some_rows(n, carry):
            s = pl.ds(pl.multiple_of(c * size + n * step_rows, step_rows), step_rows)
            e = part[me, s, :].astype(F32) + core_in[1, s, :].astype(F32) + in_x[s, :].astype(F32)
            normal, scale = norm_parts(hidden[s, :], EPSILON)
            with_gain = e * gains_all[2:3, :]
            sums[0:1, :] += jnp.sum(e * normal, axis=0, keepdims=True)
            sums[1:2, :] += jnp.sum(e, axis=0, keepdims=True)
            value = seed[s, :].astype(F32) + scale * (
                with_gain
                - jnp.mean(with_gain, axis=-1, keepdims=True)
                - normal * jnp.mean(with_gain * normal, axis=-1, keepdims=True)
            )
            d_hidden[s, :] = value
            low[s, :] = value.astype(BF16)
            return carry

        lax.fori_loop(0, size // step_rows, some_rows, 0)
        copy(3, c).start()
        copy(4, c).start()
        store(c).start()

    sums[...] = jnp.zeros_like(sums)
    o_group[...] = jnp.zeros_like(o_group)
    def d_two(relation):
        b = flip(me, relation)
        r = pl.ds(pl.multiple_of(b * rows, rows), rows)

        def column(n, carry):
            c = pl.ds(pl.multiple_of(n * 256, 256), 256)
            part[b, :, c] = dot_back(g_out[r, :up_width], g_up[c, :]).astype(BF16)
            return carry

        lax.fori_loop(0, width // 256, column, 0)

    plan = tick_plan(total, 6)
    fetch_upper.wait()
    fetch_up.wait()
    d_two(3)
    for c in range(chunks):
        copy(0, c).start()
    d_two(2)
    for c in range(chunks):
        send_sums(c)
    for fetch in fetch_rows:
        fetch.wait()
    add_steps(downs, *plan[0])
    d_two(1)
    for c in range(chunks):
        copy(1, c).start()
    d_two(0)
    fetch_two.wait()

    def grad_tiles(left, right, span, out, start, stop):
        wide = 512

        def tile(n, carry):
            rows_n = span // wide
            i, j = n // rows_n, lax.rem(n, rows_n)
            a = pl.ds(pl.multiple_of(i * 256, 256), 256)
            c = pl.ds(pl.multiple_of(j * wide, wide), wide)
            out[a, c] = dot_rows(left[:, a], right[:, c]).astype(BF16)
            return carry

        lax.fori_loop(start, stop, tile, 0)

    tiles = (width // 256) * (up_width // 512)
    for quarter in range(4):
        grad_tiles(wide_buf, g_out, up_width, g_up, tiles * quarter // 4, tiles * (quarter + 1) // 4)
        if quarter:
            norm_back(quarter - 1)
        add_steps(downs, *plan[1 + quarter])
    norm_back(3)
    add_steps(downs, *plan[5])
    for ring in ups:
        ring.begin()
    for n, ring in enumerate(downs):
        c, way = n // 2, n % 2
        o_down[pl.ds(way * half, half), pl.ds(c * side, side)] = ring.finish()
    stores[0].start()
    stores[3].start()
    for c in range(chunks):
        copy(3, c).wait_recv()
        copy(5, c).start()
        if c % 2:
            add_steps(ups, *plan[c // 2])
    for c in range(chunks):
        copy(4, c).wait_recv()
        copy(5, c).wait_recv()
        store(c).wait()
    branch = wide_buf
    fetch_branch = [
        pltpu.make_async_copy(full_branch.at[b], branch.at[pl.ds(b * rows, rows)], load_sem.at[3 + b])
        for b in range(GROUP)
    ]
    for fetch in fetch_branch:
        fetch.start()
    for fetch in fetch_branch:
        fetch.wait()
    fetch_gated.wait()
    fetch_out.wait()
    tiles = (narrow_buf.shape[1] // 256) * (width // 512)
    for part_of in range(2):
        grad_tiles(narrow_buf, branch, width, g_out, tiles * part_of // 2, tiles * (part_of + 1) // 2)
        add_steps(ups, *plan[2 + part_of])
    for fetch in fetch_tables:
        fetch.wait()

    units = heads * GROUP

    def unit_stores(unit, slot):
        h, b = unit // GROUP, lax.rem(unit, GROUP)
        r = pl.ds(pl.multiple_of(b * rows, rows), rows)
        start = pl.multiple_of(h * staged.shape[2], 128)
        return pltpu.make_async_copy(
            staged.at[slot], o_project.at[r, pl.ds(start, staged.shape[2])], out_sem.at[slot]
        )

    def unrotated(value, r, scale):
        mid = QKH // 2
        first, second = value[:, :mid], value[:, mid:]
        c, s = cosine[r, :], sine[r, :]
        return jnp.concatenate(
            [(first * c + second * s) * scale, (second * c - first * s) * scale], axis=1
        )

    def unit_body(unit):
        slot = lax.rem(unit, 2)
        h, b = unit // GROUP, lax.rem(unit, GROUP)
        r = pl.ds(pl.multiple_of(b * rows, rows), rows)
        back[...] = dot_back(branch[r, :], wo[pl.ds(pl.multiple_of(h * VH, VH), VH), :])
        for fetch in unit_loads(unit, slot):
            fetch.wait()

        @pl.when(unit >= 2)
        def _():
            unit_stores(unit - 2, slot).wait()

        gains = gain_group[h]

        def some_rows(n, carry):
            s = pl.ds(pl.multiple_of(n * step_rows, step_rows), step_rows)
            normal, scale = norm_parts(mixed[slot, s, :], GROUP_EPSILON)
            z = gate[slot, s, :]
            f = back[s, :]
            sigmoid = 1.0 / (1.0 + jnp.exp(-z))
            silu = z * sigmoid
            d_silu = f * (normal * gains)
            staged[slot, s, 2 * QKH + VH :] = (d_silu * (sigmoid + silu * (1.0 - sigmoid))).astype(BF16)
            d_scaled = f * silu
            o_group[h] += jnp.sum(d_scaled * normal, axis=0, keepdims=True)
            d_normal = d_scaled * gains
            d_mixed[s, :] = (
                scale
                * (
                    d_normal
                    - jnp.mean(d_normal, axis=-1, keepdims=True)
                    - normal * jnp.mean(d_normal * normal, axis=-1, keepdims=True)
                )
            ).astype(BF16)
            return carry

        lax.fori_loop(0, rows // step_rows, some_rows, 0)
        linked = (ident_col[b] == ident_row[b]) & (ident_col[b] >= 0.0)
        decay = jnp.where(linked, powers[h], 0.0)
        masked = (dot_back(query[slot], keys[slot]) * decay).astype(BF16)
        staged[slot, :, 2 * QKH : 2 * QKH + VH] = dot_rows(masked, d_mixed[...]).astype(BF16)
        d_raw = (dot_back(d_mixed[...], values[slot]) * decay).astype(BF16)
        d_query = dot(d_raw, keys[slot]) * QKH ** (-0.5)
        staged[slot, :, :QKH] = unrotated(d_query, r, growth[r, :]).astype(BF16)
        d_keys = dot_rows(d_raw, query[slot])
        staged[slot, :, QKH : 2 * QKH] = unrotated(d_keys, r, shrink[r, :]).astype(BF16)
        unit_stores(unit, slot).start()

        @pl.when(unit + 2 < units)
        def _():
            for fetch in unit_loads(unit + 2, slot):
                fetch.start()

    early = 2

    def with_ups(unit, carry):
        unit_body(unit)
        (low_a, high_a), (low_b, high_b) = plan[4], plan[5]
        add_steps(ups, low_a + unit * (low_b - low_a), high_a + unit * (high_b - high_a))
        return carry

    def with_outs(unit, carry):
        unit_body(unit)
        steps, number = total - 2, unit - early
        add_steps(outs, 1 + (steps * number) // (units - early), 1 + (steps * (number + 1)) // (units - early))
        return carry

    lax.fori_loop(0, early, with_ups, 0)
    for ring in outs:
        ring.begin()

    def sent_across(relation):
        return remote(
            stage.at[relation - 1], landed.at[relation - 1],
            a2a_send.at[relation - 1], a2a_recv.at[relation - 1], at.peer(relation),
        )

    for n, ring in enumerate(ups):
        relation = RELATIONS[n % 2][n // 2]
        value = ring.finish()
        if relation == 0:
            o_up[:, pl.ds(pl.multiple_of(me * up_width, 128), up_width)] = value
        else:
            stage[relation - 1] = value.astype(BF16)
            sent_across(relation).start()
    lax.fori_loop(early, units, with_outs, 0)
    for relation in (1, 2, 3):
        sent_across(relation).wait_recv()
        o_up[:, pl.ds(pl.multiple_of(flip(me, relation) * up_width, 128), up_width)] = landed[
            relation - 1
        ].astype(F32)
        sent_across(relation).wait_send()
    stores[1].start()
    for slot in (0, 1):
        unit_stores(jnp.int32(units - 2 + slot), slot).wait()
    for n, ring in enumerate(outs):
        c, way = n // 2, n % 2
        o_out[pl.ds(way * half, half), pl.ds(c * side, side)] = ring.finish()
    stores[2].start()
    for c in range(chunks):
        for kind in range(6):
            copy(kind, c).wait_send()
    wait_added(downs + ups + outs, total)
    for store_one in stores:
        store_one.wait()


def add_steps(rings, start, stop):
    def body(step, carry):
        for ring in rings:
            ring.onward(step)
        return carry

    lax.fori_loop(start, stop, body, 0)


def backward(
    total, g_down, two, d_upper, full_up, seed, hidden, gain_two, gated, full_out, query, keys, values, gate, mixed,
    tables, powers, ident_col, ident_row, gain_group,
):
    rows, width = seed.shape
    count = GROUP * rows
    heads = HEADS // GROUP
    up_width = d_upper.shape[1]
    r_out, r_up = g_down.shape[0] // total, width // GROUP // total
    half, side = r_out // 2, width // 2
    vmem, hbm = pl.BlockSpec(memory_space=pltpu.VMEM), pl.BlockSpec(memory_space=ANY)
    dma = pltpu.SemaphoreType.DMA
    shapes = (
        ((r_out, width), F32),
        ((r_up, up_width * GROUP), F32),
        ((r_out, width), F32),
        ((rows, width), F32),
        ((GROUP, rows, width), BF16),
        ((8, width), F32),
        ((heads, 1, VH), F32),
        ((count, 2 * heads * (QKH + VH)), BF16),
    )
    return pl.pallas_call(
        functools.partial(backward_kernel, total),
        out_shape=[jax.ShapeDtypeStruct(s, d) for s, d in shapes],
        in_specs=[hbm] * 6 + [vmem] + [hbm] * 12 + [vmem] * 3,
        out_specs=[hbm] * 5 + [vmem, vmem, hbm],
        scratch_shapes=[
            pltpu.VMEM(g_down.shape, BF16),
            pltpu.VMEM(seed.shape, BF16),
            pltpu.VMEM(hidden.shape, F32),
            *[pltpu.VMEM(v.shape, F32) for v in (*tables, powers)],
            *[pltpu.VMEM(s, d) for s, d in shapes[:4]],
            pltpu.VMEM((width, up_width), BF16),
            pltpu.VMEM(g_down.shape, BF16),
            pltpu.VMEM((12, total - 1, half, side), BF16),
            pltpu.VMEM((count, width), BF16),
            pltpu.VMEM((count, up_width), BF16),
            pltpu.VMEM(full_out.shape, BF16),
            pltpu.VMEM((GROUP, rows, width), BF16),
            pltpu.VMEM((2, rows, width), BF16),
            pltpu.VMEM((rows, width), BF16),
            pltpu.VMEM((rows, width), BF16),
            pltpu.VMEM((rows, width), BF16),
            pltpu.VMEM((2, rows, QKH), BF16),
            pltpu.VMEM((2, rows, QKH), BF16),
            pltpu.VMEM((2, rows, VH), BF16),
            pltpu.VMEM((2, rows, VH), F32),
            pltpu.VMEM((2, rows, VH), F32),
            pltpu.VMEM((rows, VH), F32),
            pltpu.VMEM((rows, VH), BF16),
            pltpu.VMEM((2, rows, 2 * (QKH + VH)), BF16),
            pltpu.VMEM((3, r_up, up_width), BF16),
            pltpu.VMEM((3, r_up, up_width), BF16),
            dma((12, total - 1)), dma((12, total - 1)), dma((6, 4)), dma((6, 4)), dma((4,)), dma((9,)), dma((12,)),
            dma((2, 5)), dma((2,)), dma((3,)), dma((3,)),
        ],
        compiler_params=pltpu.CompilerParams(
            collective_id=2, has_side_effects=True, vmem_limit_bytes=63 * MIB
        ),
        name="backward_retention",
    )(
        g_down, two, d_upper, full_up, seed, hidden, gain_two, gated, full_out, query, keys, values, gate, mixed,
        *tables, powers, ident_col, ident_row, gain_group,
    )


def final_kernel(
    total, h_project, h_in, h_turned, h_active, h_down, hidden, d_hidden, tok, gains_all, ident_col, sums_two, d_group,
    o_in, o_output, o_tokens, o_vec, o_grp,
    output, d_tokens, full_rows, project, turned, term, arrived, win, part, active, wd, rows_f32, core_in, out_x, in_x, stage, landed,
    vec, grp, near_in, mid, far_in, far_grp,
    load_sem, win_sem, ring_send, ring_recv, a2a_send, a2a_recv, row_send, row_recv, in_sem, piece_sem,
    near_send, near_recv, far_send, far_recv,
):
    at = Place(total)
    me, inner = at.group, at.inner
    others = [(me, lax.rem(inner + n, total)) for n in range(1, total)]
    greet([at.peer(r) for r in (1, 2, 3)] + others)
    rows, width = tok.shape
    count = GROUP * rows
    block = o_in.shape[0]
    step_rows = 32

    store_output = pltpu.make_async_copy(output, o_output, load_sem.at[6])
    store_tokens = pltpu.make_async_copy(d_tokens, o_tokens, load_sem.at[7])
    fetch_turned = pltpu.make_async_copy(h_turned, turned, load_sem.at[0])
    wide = 512
    fetch_project = [
        pltpu.make_async_copy(
            h_project.at[:, pl.ds(n * wide, wide)], project.at[:, pl.ds(n * wide, wide)], piece_sem.at[n]
        )
        for n in range(project.shape[1] // wide)
    ]
    fetch_turned.start()
    for fetch in fetch_project:
        fetch.start()

    def source(n, b):
        return part.at[pl.ds(pl.multiple_of(b * rows, rows), rows), :]

    def row_copy(kind, n):
        if kind < 2:
            return remote(
                source(n, flip(me, 3 - 2 * kind)), core_in.at[n, kind], row_send.at[n, kind], row_recv.at[n, kind],
                at.peer(1),
            )
        return remote(out_x.at[n], in_x.at[n], row_send.at[n, 2], row_recv.at[n, 2], at.peer(2))

    def own_rows(n, which, r):
        b = flip(me, 2) if which == 0 else me
        return part[pl.ds(pl.multiple_of(b * rows + r, step_rows), step_rows), :]

    def by_rows(body):
        def some(k, carry):
            body(pl.multiple_of(k * step_rows, step_rows))
            return carry

        lax.fori_loop(0, rows // step_rows, some, 0)

    def send_rows(n):
        row_copy(0, n).wait_recv()

        def some(r):
            s = pl.ds(r, step_rows)
            out_x[n, s, :] = (own_rows(n, 0, r).astype(F32) + core_in[n, 0, s, :].astype(F32)).astype(BF16)

        by_rows(some)
        row_copy(2, n).start()

    def hold_down():
        fetch_hidden.wait()
        row_copy(1, 0).wait_recv()

        def some(r):
            s = pl.ds(r, step_rows)
            rows_f32[s, :] += own_rows(0, 1, r).astype(F32) + core_in[0, 1, s, :].astype(F32)

        by_rows(some)
        row_copy(0, 0).wait_send()
        row_copy(1, 0).wait_send()

    def summed_rows(n, r):
        s = pl.ds(r, step_rows)
        return own_rows(n, 1, r).astype(F32) + core_in[n, 1, s, :].astype(F32) + in_x[n, s, :].astype(F32)

    def take_down():
        row_copy(2, 0).wait_recv()

        def some(r):
            s = pl.ds(r, step_rows)
            valid = jnp.where(ident_col[me, s, :] >= 0.0, 1.0, 0.0)
            output[s, :] = ((rows_f32[s, :] + in_x[0, s, :].astype(F32)) * valid).astype(BF16)

        by_rows(some)
        fetch_d_hidden.start()
        store_output.start()

    def take_rows():
        fetch_d_hidden.wait()
        row_copy(1, 1).wait_recv()
        row_copy(2, 1).wait_recv()
        vec[...] = jnp.zeros_like(vec)
        vec[2:4, :] = sums_two[0:2, :]

        def some(r):
            s = pl.ds(r, step_rows)
            e = summed_rows(1, r)
            normal, scale = norm_parts(tok[s, :].astype(F32), EPSILON)
            with_gain = e * gains_all[0:1, :]
            vec[0:1, :] += jnp.sum(e * normal, axis=0, keepdims=True)
            vec[1:2, :] += jnp.sum(e, axis=0, keepdims=True)
            value = rows_f32[s, :] + scale * (
                with_gain
                - jnp.mean(with_gain, axis=-1, keepdims=True)
                - normal * jnp.mean(with_gain * normal, axis=-1, keepdims=True)
            )
            d_tokens[s, :] = value.astype(BF16)

        by_rows(some)
        store_tokens.start()

    quarter = width // GROUP
    small = quarter // total
    large = grp.shape[1] // total

    def near(relation):
        start = pl.multiple_of(flip(me, relation) * quarter, 128)
        return remote(
            vec.at[:, pl.ds(start, quarter)], near_in.at[relation - 1], near_send.at[relation - 1],
            near_recv.at[relation - 1], at.peer(relation),
        )

    def tile_of(index, size):
        return pl.ds(pl.multiple_of((index * size) // 128 * 128, 128), 128)

    def distant(kind, n):
        target = lax.rem(inner + n, total)
        src = mid.at[:, tile_of(target, small)] if kind == 0 else grp.at[:, tile_of(target, large)]
        dst = far_in if kind == 0 else far_grp
        return remote(
            src, dst.at[n - 1], far_send.at[kind, n - 1], far_recv.at[kind, n - 1], (me, target)
        )

    def vectors_near():
        for relation in (1, 2, 3):
            near(relation).start()
        grp[...] = jnp.zeros_like(grp)
        for h in range(d_group.shape[0]):
            grp[0:1, h * VH : (h + 1) * VH] = d_group[h]

    def vectors_far():
        for relation in (1, 2, 3):
            near(relation).wait_recv()
        mid[...] = (
            vec[:, pl.ds(pl.multiple_of(me * quarter, 128), quarter)] + near_in[0] + near_in[1] + near_in[2]
        )
        for n in range(1, total):
            for kind in (0, 1):
                distant(kind, n).start()

    def vectors_end():
        for n in range(1, total):
            for kind in (0, 1):
                distant(kind, n).wait_recv()
        o_vec[...] = mid[:, tile_of(inner, small)] + jnp.sum(far_in[...], axis=0)
        o_grp[...] = grp[:, tile_of(inner, large)] + jnp.sum(far_grp[...], axis=0)


    def terms(step, far_at, near_at, arriving=False):
        lefts = []
        for way in (0, 1):
            which = at.behind(way, step + 1)
            lefts.append(
                jnp.concatenate(
                    [
                        turned[
                            pl.ds(pl.multiple_of((flip(me, relation) * total + which) * block, block), block), :
                        ]
                        for relation in RELATIONS[way]
                    ],
                    axis=0,
                )
            )

        def tile(n, way):
            c = pl.ds(pl.multiple_of(n * wide, wide), wide)
            value = dot(lefts[way], project[:, c]).astype(BF16)
            term[far_at + way, :, c] = value[:block]
            term[near_at + way, :, c] = value[block:]

        if arriving:
            for n, fetch in enumerate(fetch_project):
                fetch.wait()
                tile(n, 0)
                tile(n, 1)
            return
        for way in (0, 1):

            def some(n, carry, way=way):
                tile(n, way)
                return carry

            lax.fori_loop(0, project.shape[1] // wide, some, 0)

    far_slots, near_slots = (0, 2), (1, 3)

    def near_place(step):
        return 6 + 2 * lax.rem(step, 2)

    def hop(slot, step, first=False):
        src = term.at[2 * (slot % 2) + slot // 2] if first else arrived.at[slot, step - 1]
        return remote(
            src, arrived.at[slot, step], ring_send.at[slot, step], ring_recv.at[slot, step],
            at.neighbour(slot // 2),
        )

    def sum_into(out, slot, step, base):
        hop(slot, step, True).wait_recv()

        def some(n, carry):
            c = pl.ds(pl.multiple_of(n * wide, wide), wide)
            value = arrived[slot, step, :, c].astype(F32) + term[base + slot // 2, :, c].astype(F32)
            out[:, c] = value.astype(BF16)
            return carry

        lax.fori_loop(0, project.shape[1] // wide, some, 0)

    def send_on(slots, step, base):
        for slot in slots:
            sum_into(arrived.at[slot, step - 1], slot, step - 1, base)
            hop(slot, step).start()

    def onward(step, carry):
        terms(step, 4, near_place(step))
        send_on(far_slots, step, 4)
        send_on(near_slots, step - 1, near_place(step - 1))
        return carry

    parts = h_in.shape[0]
    part_width = h_in.shape[2]

    class fetch_win:
        def __init__(self, n):
            self.copies = [
                pltpu.make_async_copy(
                    h_in.at[h, pl.ds(n * 256, 256), :],
                    win.at[n % 2, :, pl.ds(h * part_width, part_width)],
                    win_sem.at[n % 2, h],
                )
                for h in range(parts)
            ]

        def start(self):
            for copy in self.copies:
                copy.start()

        def wait(self):
            for copy in self.copies:
                copy.wait()

    columns = width // 256

    def row_tiles(n):
        fetch_win(n).wait()

        def tile(m, carry):
            r = pl.ds(pl.multiple_of(m * 512, 512), 512)
            part[r, n * 256 : (n + 1) * 256] = dot_back(project[r, :], win[n % 2]).astype(BF16)
            return carry

        lax.fori_loop(0, count // 512, tile, 0)
        if n + 2 < columns:
            fetch_win(n + 2).start()

    def down_rows(relation):
        b = flip(me, relation)
        r = pl.ds(pl.multiple_of(b * rows, rows), rows)

        def column(n, carry):
            c = pl.ds(pl.multiple_of(n * wide, wide), wide)
            part[r, c] = dot(active[r, :], wd[:, c]).astype(BF16)
            return carry

        lax.fori_loop(0, width // wide, column, 0)

    fetch_active = pltpu.make_async_copy(h_active, active, load_sem.at[2])
    fetch_down = pltpu.make_async_copy(h_down, wd, load_sem.at[3])
    fetch_hidden = pltpu.make_async_copy(hidden, rows_f32, load_sem.at[4])
    fetch_d_hidden = pltpu.make_async_copy(d_hidden, rows_f32, load_sem.at[5])
    for fetch in (fetch_active, fetch_down, fetch_hidden):
        fetch.start()
    fetch_win(0).start()
    fetch_win(1).start()
    fetch_turned.wait()
    terms(0, 0, 2, True)
    for slot in far_slots:
        hop(slot, 0, True).start()
    fetch_active.wait()
    fetch_down.wait()
    down_rows(3)
    row_copy(0, 0).start()
    for slot in near_slots:
        hop(slot, 0, True).start()
    down_rows(2)
    down_rows(1)
    row_copy(1, 0).start()
    down_rows(0)
    send_rows(0)
    hold_down()
    plan = tick_plan(total, 6)

    def extra(number):
        if number < 3:
            for n in range(columns * number // 3, columns * (number + 1) // 3):
                row_tiles(n)
            if number == 2:
                row_copy(0, 1).start()
                row_copy(1, 1).start()
        elif number == 3:
            send_rows(1)
            take_down()
        elif number == 5:
            take_rows()
            vectors_near()

    terms(1, 4, near_place(1))
    send_on(far_slots, 1, 4)
    for number in range(6):
        extra(number)
        lax.fori_loop(max(plan[number][0], 2), plan[number][1], onward, 0)
    terms(total - 1, 4, near_place(total - 1))
    pieces = column_pieces()

    def place(relation, columns_of):
        other = flip(me, relation)
        for base, stride, h, off, size in pieces:
            start = pl.multiple_of(base + other * stride, 128)
            off = h * part_width + off
            full_rows[:, pl.ds(start, size)] = columns_of(off, size)
        for copy in stored(relation):
            copy.start()

    def stored(relation):
        other = flip(me, relation)
        return [
            pltpu.make_async_copy(
                full_rows.at[:, pl.ds(pl.multiple_of(base + other * stride, 128), size)],
                o_in.at[:, pl.ds(pl.multiple_of(base + other * stride, 128), size)],
                in_sem.at[relation, n],
            )
            for n, (base, stride, h, off, size) in enumerate(pieces)
        ]

    def sent_across(relation):
        return remote(
            stage.at[relation - 1], landed.at[relation - 1],
            a2a_send.at[relation - 1], a2a_recv.at[relation - 1], at.peer(relation),
        )

    for slot in far_slots:
        relation = RELATIONS[slot // 2][0]
        sum_into(stage.at[relation - 1], slot, total - 2, 4)
        sent_across(relation).start()
    send_on(near_slots, total - 2, near_place(total - 2))
    vectors_far()
    for slot in reversed(near_slots):
        relation = RELATIONS[slot // 2][1]
        base = near_place(total - 1)
        if relation == 0:
            hop(slot, total - 2, True).wait_recv()
            place(
                0,
                lambda off, size: arrived[slot, total - 2, :, off : off + size].astype(F32)
                + term[base + slot // 2, :, off : off + size].astype(F32),
            )
        else:
            sum_into(stage.at[relation - 1], slot, total - 2, base)
            sent_across(relation).start()
    for relation in (2, 3, 1):
        sent_across(relation).wait_recv()
        place(relation, lambda off, size: landed[relation - 1, :, off : off + size].astype(F32))
    vectors_end()
    for relation in range(4):
        for copy in stored(relation):
            copy.wait()
    for copy in (store_output, store_tokens):
        copy.wait()
    for relation in (1, 2, 3):
        sent_across(relation).wait_send()
        near(relation).wait_send()
    for n in range(1, total):
        for kind in (0, 1):
            distant(kind, n).wait_send()
    row_copy(2, 0).wait_send()
    for kind in (0, 1, 2):
        row_copy(kind, 1).wait_send()

    def sent(step, carry):
        for slot in range(4):
            hop(slot, step, True).wait_send()
        return carry

    lax.fori_loop(0, total - 1, sent, 0)


def final(
    total, d_project, full_in, turned, active, full_down, hidden, d_hidden, tok, gains, ident_col, sums_two, d_group
):
    rows, width = tok.shape
    count, wide = d_project.shape
    block = width // GROUP // total
    vmem, hbm = pl.BlockSpec(memory_space=pltpu.VMEM), pl.BlockSpec(memory_space=ANY)
    dma = pltpu.SemaphoreType.DMA
    group_width = d_group.shape[0] * d_group.shape[2]
    shapes = (
        ((block, wide * GROUP), F32),
        ((rows, width), BF16),
        ((rows, width), BF16),
        ((8, 128), F32),
        ((8, 128), F32),
    )
    return pl.pallas_call(
        functools.partial(final_kernel, total),
        out_shape=[jax.ShapeDtypeStruct(s, d) for s, d in shapes],
        in_specs=[hbm] * 7 + [vmem] * 5,
        out_specs=[hbm] * 3 + [vmem] * 2,
        scratch_shapes=[
            pltpu.VMEM((rows, width), BF16),
            pltpu.VMEM((rows, width), BF16),
            pltpu.VMEM((block, wide * GROUP), F32),
            pltpu.VMEM((count, wide), BF16),
            pltpu.VMEM(turned.shape, BF16),
            pltpu.VMEM((10, block, wide), BF16),
            pltpu.VMEM((4, total - 1, block, wide), BF16),
            pltpu.VMEM((2, 256, wide), BF16),
            pltpu.VMEM((count, width), BF16),
            pltpu.VMEM(active.shape, BF16),
            pltpu.VMEM(full_down.shape, BF16),
            pltpu.VMEM((rows, width), F32),
            pltpu.VMEM((2, 2, rows, width), BF16),
            pltpu.VMEM((2, rows, width), BF16),
            pltpu.VMEM((2, rows, width), BF16),
            pltpu.VMEM((3, block, wide), BF16),
            pltpu.VMEM((3, block, wide), BF16),
            pltpu.VMEM((8, width), F32),
            pltpu.VMEM((8, group_width), F32),
            pltpu.VMEM((3, 8, width // GROUP), F32),
            pltpu.VMEM((8, width // GROUP), F32),
            pltpu.VMEM((total - 1, 8, 128), F32),
            pltpu.VMEM((total - 1, 8, 128), F32),
            dma((8,)), dma((2, 2)), dma((4, total - 1)), dma((4, total - 1)), dma((3,)), dma((3,)),
            dma((2, 3)), dma((2, 3)), dma((GROUP, 8)), dma((6,)), dma((3,)), dma((3,)), dma((2, total - 1)), dma((2, total - 1)),
        ],
        compiler_params=pltpu.CompilerParams(
            collective_id=3, has_side_effects=True, vmem_limit_bytes=63 * MIB
        ),
        name="final_sums",
    )(d_project, full_in, turned, active, full_down, hidden, d_hidden, tok, gains, ident_col, sums_two, d_group)


def mean(values):
    return jnp.mean(values, axis=-1, keepdims=True)


def local(
    total,
    tokens,
    cotangent,
    w_in,
    w_out,
    w_up,
    w_down,
    ln1_gain,
    ln1_bias,
    group_gain,
    ln2_gain,
    ln2_bias,
    seq_lens,
    seq_owner,
    seq_offset,
):
    rows, width = tokens.shape
    heads = HEADS // GROUP
    qk, vv = heads * QKH, heads * VH
    me, inner = lax.axis_index("dp"), lax.axis_index("fsdp")
    small, large = ln1_gain.shape[0], group_gain.shape[0]

    count = GROUP * rows
    vectors = jnp.stack([ln1_gain, ln1_bias, ln2_gain, ln2_bias]).astype(F32)
    pack = jnp.zeros((8, 128), F32)
    pack = lax.dynamic_update_slice(pack, vectors, (0, lax.rem(inner * small, 128)))
    pack = lax.dynamic_update_slice(pack, group_gain.astype(F32)[None], (4, lax.rem(inner * large, 128)))
    rates = jnp.log1p(-(2.0 ** (-5.0 - (me * heads + jnp.arange(heads)).astype(F32))))
    rates = jnp.broadcast_to(rates[:, None, None], (heads, 1, rows))
    entries = jnp.stack([seq_lens, seq_owner, seq_offset])
    (
        full_in, full_up, full_out, full_down, _, turned, query, keys, values, gate, mixed, gated, active, d_upper,
        g_down, hidden, two,
        own_seed, cosine, sine, growth, shrink, powers, ident_col, ident_row, gains, gain_group,
    ) = forward(
        total, w_in, w_up, w_out, w_down, tokens, cotangent, pack, rates, entries[:, :, None], entries[:, None, :]
    )
    tables = (cosine, sine, growth, shrink)
    full_up = full_up.reshape(width, -1)
    full_out = full_out.reshape(-1, width)
    full_down = full_down.reshape(-1, width)
    two = two.reshape(count, width)
    grad_down, grad_up, grad_out, d_hidden, _, sums_two, d_group, d_project = backward(
        total, g_down.reshape(-1, width), two, d_upper, full_up, own_seed, hidden, gains, gated, full_out, query,
        keys, values, gate, mixed, tables, powers, ident_col, ident_row, gain_group,
    )
    grad_in, output, d_tokens, vec_one, vec_two = final(
        total, d_project, full_in, turned, active, full_down, hidden, d_hidden, tokens, gains, ident_col, sums_two,
        d_group,
    )
    grads = lax.dynamic_slice(vec_one, (0, lax.rem(inner * small, 128)), (4, small))
    grad_group = lax.dynamic_slice(vec_two, (0, lax.rem(inner * large, 128)), (1, large))[0]
    return (
        output,
        d_tokens,
        grad_in,
        grad_out,
        grad_up,
        grad_down,
        grads[0],
        grads[1],
        grad_group,
        grads[2],
        grads[3],
    )


def solution(mesh):
    flat = ("dp", "fsdp")
    matrix, vector = P(flat, None), P(flat)
    return jax.shard_map(
        functools.partial(local, mesh.shape["fsdp"]),
        mesh=mesh,
        in_specs=(matrix,) * 6 + (vector,) * 5 + (P(),) * 3,
        out_specs=(matrix,) * 6 + (vector,) * 5,
        check_vma=False,
    )
```

```python
import functools

import jax
import jax.numpy as jnp
import numpy as np
from jax import lax
from jax.experimental import pallas as pl
from jax.experimental.pallas import tpu as pltpu
from jax.sharding import PartitionSpec as P

HEADS = 8
QKH = 256
VH = 512
EPSILON = 1e-05
GROUP_EPSILON = 0.1
GROUP = 4
MESH = pl.DeviceIdType.MESH
ANY = pl.ANY
BF16 = jnp.bfloat16
F32 = jnp.float32
MIB = 1 << 20


def ring_place(index, total):
    half = index // 2
    return jnp.where(index % 2 == 0, half, total - 1 - half)


def ring_index(place, total):
    place = lax.rem(place + 2 * total, total)
    return jnp.where(place < total // 2, 2 * place, 2 * (total - 1 - place) + 1)


def flip(group_index, relation):
    low, high = group_index % 2, group_index // 2
    if relation % 2:
        low = 1 - low
    if relation // 2:
        high = 1 - high
    return 2 * high + low


class Place:
    def __init__(self, total):
        self.total = total
        self.group = lax.axis_index("dp")
        self.inner = lax.axis_index("fsdp")
        self.place = ring_place(self.inner, total)
        self.next = (
            ring_index(self.place + 1, total),
            ring_index(self.place - 1, total),
        )

    def peer(self, relation):
        return (flip(self.group, relation), self.inner)

    def neighbour(self, way):
        return (self.group, self.next[way])

    def behind(self, way, steps):
        return ring_index(self.place - steps if way == 0 else self.place + steps, self.total)


def greet(devices):
    barrier = pltpu.get_barrier_semaphore()
    for device in devices:
        pl.semaphore_signal(barrier, inc=1, device_id=device, device_id_type=MESH)
    pl.semaphore_wait(barrier, len(devices))


def remote(src, dst, send_sem, recv_sem, device):
    return pltpu.make_async_remote_copy(
        src_ref=src,
        dst_ref=dst,
        send_sem=send_sem,
        recv_sem=recv_sem,
        device_id=device,
        device_id_type=MESH,
    )


def column_pieces():
    heads = HEADS // GROUP
    table = []
    base, off = 0, 0
    for size in (QKH, QKH, VH, VH):
        for h in range(heads):
            table.append((base + h * size, heads * size, h, off, size))
        base += HEADS * size
        off += size
    return table


def dot(left, right):
    return jnp.dot(left, right, preferred_element_type=F32)


def dot_rows(left, right):
    return lax.dot_general(left, right, (((0,), (0,)), ((), ())), preferred_element_type=F32)


def dot_back(left, right):
    return lax.dot_general(left, right, (((1,), (1,)), ((), ())), preferred_element_type=F32)


def norm_parts(values, epsilon):
    center = values - jnp.mean(values, axis=-1, keepdims=True)
    spread = jnp.mean(center * center, axis=-1, keepdims=True)
    scale = lax.rsqrt(spread + epsilon)
    return center * scale, scale


RELATIONS = ((2, 0), (3, 1))


class Passing:
    def __init__(self, at, way, own, place, sends, recvs):
        self.at, self.way, self.own, self.place = at, way, own, place
        self.sends, self.recvs = sends, recvs

    def hop(self, step, first=False):
        which = self.at.inner if first else self.at.behind(self.way, step)
        dst = self.place(which)
        return remote(
            self.own if first else dst, dst, self.sends.at[step], self.recvs.at[step],
            self.at.neighbour(self.way),
        )

    def begin(self):
        self.hop(0, True).start()

    def onward(self, step):
        self.hop(step - 1).wait_recv()
        self.hop(step).start()

    def finish(self):
        self.hop(self.at.total - 2).wait_recv()


def wait_sent(rings, total):
    def body(step, carry):
        for ring in rings:
            ring.hop(step).wait_send()
        return carry

    lax.fori_loop(0, total - 1, body, 0)


def tick_plan(total, places):
    steps = total - 2
    cuts = [1 + (steps * n) // places for n in range(places + 1)]
    return list(zip(cuts[:-1], cuts[1:]))


def run_steps(rings, start, stop):
    def body(step, carry):
        for ring in rings:
            ring.onward(step)
        return carry

    lax.fori_loop(start, stop, body, 0)


def weight_rings(at, w_out, w_down, full_up, full_out, full_down, sends, recvs):
    me = at.group
    half = w_out.shape[0] // 2
    side = w_out.shape[1] // 2

    def halves(own, full, slot):
        return [
            Passing(
                at, way,
                own.at[pl.ds(way * half, half), pl.ds(c * side, side)],
                lambda which, way=way, c=c: full.at[which, pl.ds(way * half, half), pl.ds(c * side, side)],
                sends.at[slot + 2 * c + way], recvs.at[slot + 2 * c + way],
            )
            for c in (0, 1)
            for way in (0, 1)
        ]

    ups = []
    for order in (0, 1):
        for way in (0, 1):
            relation = RELATIONS[way][order]
            slot = 8 + 2 * order + way
            ups.append(
                Passing(
                    at, way, full_up.at[flip(me, relation), at.inner],
                    lambda which, relation=relation: full_up.at[flip(me, relation), which],
                    sends.at[slot], recvs.at[slot],
                )
            )
    return halves(w_out, full_out, 0), ups, halves(w_down, full_down, 4)


def rotated(value, cosine, sine, scale):
    half = QKH // 2
    first, second = value[:, :half], value[:, half:]
    return jnp.concatenate(
        [(first * cosine - second * sine) * scale, (second * cosine + first * sine) * scale], axis=1
    )


def forward_kernel(
    total, w_in, w_up, w_out, w_down, h_tok, h_cot, pack, rates, seq_cols, seq_rows, curves,
    full_in, full_up, full_out, full_down, full_seed, o_turned, o_query, o_keys, o_values, o_gate, o_mixed,
    o_gated, o_active, o_upper, o_g_down, to_hidden, full_two, to_seed, to_cosine, to_sine, to_growth, to_shrink,
    to_powers, ident_col, ident_row, gains, gain_group,
    hidden, own_seed, cosine, sine, growth, shrink, powers, tok, cot,
    win, part, x, query, keys, values, gate, mixed, gated, wo, core_in, out_x, in_x, low, full_vec,
    win_up, wd, ring_send, ring_recv, own_sem, load_sem, fetch_sem, store_sem, row_send, row_recv, row_own,
    swap_send, swap_recv, swap_own, vec_send, vec_recv, early_sem,
):
    at = Place(total)
    me, inner = at.group, at.inner
    core, across = at.peer(1), at.peer(2)
    others = [(me, lax.rem(inner + n, total)) for n in range(1, total)]
    greet([core, across, at.peer(3)] + others)
    rows, width = tok.shape
    count = GROUP * rows
    heads = HEADS // GROUP
    r_in = w_in.shape[0]
    up_width = full_up.shape[-1]
    pieces = column_pieces()
    step_rows = 32

    def rows_in(group_index, which):
        return pl.ds(pl.multiple_of((group_index * total + which) * r_in, r_in), r_in)

    last = len(pieces)

    def swap(relation, slot):
        other = flip(me, relation)
        if slot < last:
            base, stride, h, off, size = pieces[slot]
            src = w_in.at[:, pl.ds(pl.multiple_of(base + other * stride, 128), size)]
            dst = win.at[h, rows_in(me, inner), pl.ds(off, size)]
        elif slot == last:
            src = w_up.at[:, pl.ds(pl.multiple_of(other * up_width, 128), up_width)]
            dst = full_up.at[me, inner]
        elif slot == last + 1:
            src, dst = pack, full_vec.at[inner, me]
        elif slot == last + 2:
            src, dst = h_tok, part.at[me]
        else:
            src, dst = own_seed, full_seed.at[me]
        if relation == 0:
            return pltpu.make_async_copy(src, dst, swap_own.at[slot])
        return remote(
            src, dst, swap_send.at[relation - 1, slot], swap_recv.at[relation - 1, slot], at.peer(relation)
        )

    def arrived(relation, slot):
        if relation == 0:
            swap(0, slot).wait()
        else:
            swap(relation, slot).wait_recv()

    def start_head(h):
        for relation in (0, 1, 2, 3):
            for slot in range(last):
                if pieces[slot][2] == h:
                    swap(relation, slot).start()

    start_head(0)

    fetch_cot = pltpu.make_async_copy(h_cot, cot, early_sem.at[0])
    fetch_tok = pltpu.make_async_copy(h_tok, tok, early_sem.at[1])
    early_stores = [
        pltpu.make_async_copy(src, dst, early_sem.at[2 + n])
        for n, (src, dst) in enumerate(
            (
                (own_seed, to_seed), (cosine, to_cosine), (sine, to_sine), (growth, to_growth),
                (shrink, to_shrink), (powers, to_powers), (hidden, to_hidden),
            )
        )
    ]

    def in_ring(h, relation):
        def place(which):
            return win.at[h, rows_in(flip(me, relation), which), :]

        slot = 12 + 4 * h + relation
        return Passing(at, relation % 2, place(inner), place, ring_send.at[slot], ring_recv.at[slot])

    ins = [[in_ring(h, relation) for relation in range(4)] for h in range(heads)]
    near, far_in = ins[0][:2], ins[0][2:]

    def await_head(h, relation):
        for slot in range(last):
            if pieces[slot][2] == h:
                arrived(relation, slot)

    for relation in (0, 1):
        await_head(0, relation)
        near[relation].begin()
    fetch_cot.start()
    fetch_tok.start()
    for relation in (2, 3, 1, 0):
        swap(relation, last + 1).start()
    for slot in (last + 2, last):
        for relation in (2, 3, 1, 0):
            swap(relation, slot).start()
    for h in range(1, heads):
        start_head(h)

    def layout_of(b, down):
        shape = (rows, 1) if down else (1, rows)
        source = seq_rows if down else seq_cols
        lens, owner, offset = source[0], source[1], source[2]
        positions = lax.broadcasted_iota(jnp.int32, shape, 0 if down else 1)
        inside = (
            (owner == b * total + inner)
            & (lens > 0)
            & (positions >= offset)
            & (positions < offset + lens)
        )
        axis = 1 if down else 0
        number = lax.broadcasted_iota(jnp.int32, lens.shape, axis).astype(F32) + 1.0
        ident = jnp.sum(jnp.where(inside, number, 0.0), axis=axis, keepdims=True) - 1.0
        starts = jnp.sum(jnp.where(inside, offset.astype(F32), 0.0), axis=axis, keepdims=True)
        places = jnp.where(ident >= 0.0, positions.astype(F32) - starts, 0.0)
        return ident, places

    for b in range(GROUP):
        ident_col[b] = layout_of(b, True)[0]
        ident_row[b] = layout_of(b, False)[0]

    def seed_rows(n, carry):
        s = pl.ds(pl.multiple_of(n * step_rows, step_rows), step_rows)
        valid = jnp.where(ident_col[me, s, :] >= 0.0, 1.0, 0.0)
        own_seed[s, :] = (cot[s, :].astype(F32) * valid).astype(BF16)
        return carry

    fetch_cot.wait()
    lax.fori_loop(0, rows // step_rows, seed_rows, 0)
    early_stores[0].start()

    for relation in range(4):
        arrived(relation, last + 1)

    def spread(n):
        target = lax.rem(inner + n, total)
        return remote(
            full_vec.at[inner], full_vec.at[inner], vec_send.at[n - 1], vec_recv.at[n - 1], (me, target)
        )

    for n in range(1, total):
        spread(n).start()
    for ring in near:
        ring.onward(1)
    for relation in (2, 3):
        await_head(0, relation)
        far_in[relation - 2].begin()
    for relation in (1, 0, 2, 3):
        swap(relation, last + 3).start()

    def both_in(step, carry):
        for ring in near:
            ring.onward(step)
        for ring in far_in:
            ring.onward(step - 1)
        return carry

    def take_vectors():
        for n in range(1, total):
            spread(n).wait_recv()
        quarter = width // GROUP
        small = quarter // total
        large = heads * VH // total
        for d in range(GROUP):
            tiles = {}
            for f in range(total):
                t = f * small // 128
                value = full_vec[f, d]
                tiles[t] = tiles[t] + value if t in tiles else value
            for t, value in tiles.items():
                gains[:, d * quarter + t * 128 : d * quarter + (t + 1) * 128] = value
        tiles = {}
        for f in range(total):
            t = f * large // 128
            value = full_vec[f, me, 4:5, :]
            tiles[t] = tiles[t] + value if t in tiles else value
        for t, value in tiles.items():
            h, off = t * 128 // VH, t * 128 % VH
            gain_group[h, :, off : off + 128] = value

    def make_tables():
        distance = lax.broadcasted_iota(jnp.int32, (rows, rows), 0) - lax.broadcasted_iota(
            jnp.int32, (rows, rows), 1
        )
        away = jnp.maximum(distance, 0).astype(F32)
        for h in range(heads):
            powers[h] = jnp.where(distance >= 0, jnp.exp(rates[h] * away), 0.0)
        for b in range(GROUP):
            places = layout_of(b, True)[1]
            angles = places * curves[0:1, :]
            r = slice(b * rows, (b + 1) * rows)
            cosine[r, :] = jnp.cos(angles)
            sine[r, :] = jnp.sin(angles)
            lift = places * (1.0 / 512.0) * curves[1:2, :]
            growth[r, :] = jnp.exp(lift)
            shrink[r, :] = jnp.exp(-lift)
        for store_one in early_stores[1:6]:
            store_one.start()

    def norm_buffer(relation):
        b = flip(me, relation)
        arrived(relation, last + 2)

        def norm_rows(n, carry):
            r = pl.multiple_of(n * step_rows, step_rows)
            normal, _ = norm_parts(part[b, pl.ds(r, step_rows), :].astype(F32), EPSILON)
            at_rows = pl.ds(pl.multiple_of(b * rows + r, step_rows), step_rows)
            x[at_rows, :] = (normal * gains[0:1, :] + gains[1:2, :]).astype(BF16)
            return carry

        lax.fori_loop(0, rows // step_rows, norm_rows, 0)

    beside = [
        make_tables,
        take_vectors,
        lambda: (norm_buffer(0), norm_buffer(1)),
        lambda: norm_buffer(2),
        lambda: norm_buffer(3),
    ]
    cuts = [2 + (total - 3) * n // 5 for n in range(6)]
    for n in range(5):
        lax.fori_loop(cuts[n], cuts[n + 1], both_in, 0)
        beside[n]()
    for ring in far_in:
        ring.onward(total - 2)
    for h in range(1, heads):
        for relation in range(4):
            await_head(h, relation)
            ins[h][relation].begin()
    outs, ups, downs = weight_rings(
        at, w_out, w_down, full_up, full_out, wd, ring_send, ring_recv
    )
    own_copies = [
        pltpu.make_async_copy(w_out, full_out.at[inner], own_sem.at[0]),
        pltpu.make_async_copy(w_down, wd.at[inner], own_sem.at[1]),
    ]
    for copy in own_copies:
        copy.start()
    plan = tick_plan(total, 6)
    tile = 512

    def project(h, off, m):
        r = pl.ds(pl.multiple_of(m * tile, tile), tile)
        return r, dot(x[r, :], win[h, :, off : off + QKH])

    def turn_tile(h, m):
        r, value = project(h, 0, m)
        turned = rotated(value, cosine[r, :], sine[r, :], growth[r, :])
        query[h, r, :] = (turned * QKH ** (-0.5)).astype(BF16)
        r, value = project(h, QKH, m)
        keys[h, r, :] = rotated(value, cosine[r, :], sine[r, :], shrink[r, :]).astype(BF16)

    def plain_tile(h, c, m):
        off = c * QKH
        r, value = project(h, 2 * QKH + off, m)
        values[h, r, off : off + QKH] = value.astype(BF16)
        r, value = project(h, 2 * QKH + VH + off, m)
        gate[h, r, off : off + QKH] = value

    def retain(h, b):
        r = pl.ds(pl.multiple_of(b * rows, rows), rows)
        raw = dot_back(query[h, r, :], keys[h, r, :])
        linked = (ident_col[b] == ident_row[b]) & (ident_col[b] >= 0.0)
        masked = (raw * jnp.where(linked, powers[h], 0.0)).astype(BF16)
        mixed[h, r, :] = dot(masked, values[h, r, :])

        def some_rows(n, carry):
            s = pl.ds(pl.multiple_of(b * rows + n * step_rows, step_rows), step_rows)
            normal, _ = norm_parts(mixed[h, s, :], GROUP_EPSILON)
            z = gate[h, s, :]
            result = z / (1.0 + jnp.exp(-z)) * (normal * gain_group[h])
            gated[s, h * VH : (h + 1) * VH] = result.astype(BF16)
            return carry

        lax.fori_loop(0, rows // step_rows, some_rows, 0)

    def looped(count_of, body):
        def some(n, carry):
            body(n)
            return carry

        lax.fori_loop(0, count_of, some, 0)

    def head_units(h):
        return [
            lambda: looped(count // tile, lambda m: turn_tile(h, m)),
            lambda: looped(count // tile, lambda m: plain_tile(h, 0, m)),
            lambda: looped(count // tile, lambda m: plain_tile(h, 1, m)),
            lambda: looped(2, lambda b: retain(h, b)),
            lambda: looped(2, lambda b: retain(h, 2 + b)),
        ]

    stores = []

    def store_head(h):
        for n, (src, dst) in enumerate(
            ((win, full_in), (query, o_query), (keys, o_keys), (values, o_values), (gate, o_gate), (mixed, o_mixed))
        ):
            copy = pltpu.make_async_copy(src.at[h], dst.at[h], store_sem.at[h, n])
            copy.start()
            stores.append(copy)

    for h in range(heads):
        ring_set = ins[h + 1] if h + 1 < heads else outs
        if h + 1 == heads:
            for ring in outs:
                ring.begin()
        for ring in ins[h]:
            ring.finish()
        units = head_units(h)
        for number in range(6):
            if number < len(units):
                units[number]()
            run_steps(ring_set, *plan[number])
        store_head(h)
    for relation in range(4):
        arrived(relation, last)
    for ring in ups:
        ring.begin()
    for ring in outs:
        ring.finish()
    stores.append(pltpu.make_async_copy(gated, o_gated, store_sem.at[0, 6]))
    stores[-1].start()
    own_copies[0].wait()
    block = w_out.shape[0]
    fetch = pltpu.make_async_copy(full_out, wo, load_sem.at[0])
    fetch.start()
    fetch.wait()

    chunks = 4
    size = rows // chunks

    def branch(relation):
        b = flip(me, relation)

        def column(n, carry):
            wide = 512
            c = pl.ds(pl.multiple_of(n * wide, wide), wide)
            r = pl.ds(pl.multiple_of(b * rows, rows), rows)
            acc = jnp.zeros((rows, wide), F32)
            piece = gated[r, :]
            acc = dot(piece, wo[:, :, c].reshape(total * block, wide))
            part[b, :, c] = acc.astype(BF16)
            return carry

        lax.fori_loop(0, width // 512, column, 0)

    def rows_of(c):
        return pl.ds(c * size, size)

    far = flip(me, 2)

    def copy(kind, c):
        r = rows_of(c)
        if kind == 0:
            src, dst, dev = part.at[flip(me, 3), r], core_in.at[0, r], core
        elif kind == 1:
            src, dst, dev = part.at[flip(me, 1), r], core_in.at[1, r], core
        elif kind == 2:
            src, dst, dev = out_x.at[r], in_x.at[r], across
        elif kind == 3:
            src, dst, dev = low.at[r], full_two.at[me, r], across
        elif kind == 4:
            src, dst, dev = low.at[r], full_two.at[me, r], core
        else:
            src, dst, dev = full_two.at[far, r], full_two.at[far, r], core
        return remote(src, dst, row_send.at[kind, c], row_recv.at[kind, c], dev)

    def store(c):
        r = rows_of(c)
        return pltpu.make_async_copy(low.at[r], full_two.at[me, r], row_own.at[c])

    branch(3)
    for c in range(chunks):
        copy(0, c).start()
    branch(2)
    run_steps(ups, *plan[0])
    for c in range(chunks):
        r = rows_of(c)
        copy(0, c).wait_recv()
        out_x[r, :] = (part[far, r, :].astype(F32) + core_in[0, r, :].astype(F32)).astype(BF16)
        copy(2, c).start()
    branch(1)
    for c in range(chunks):
        copy(1, c).start()
    branch(0)
    run_steps(ups, *plan[1])
    for copy_out in stores:
        copy_out.wait()
    fetch_tok.wait()
    wait_sent([ring for rings in ins for ring in rings], total)

    def turn(n, carry):
        i, j = n // (count // 256), lax.rem(n, count // 256)
        i, j = (pl.ds(pl.multiple_of(k * 256, 256), 256) for k in (i, j))
        win[0, i, j] = x[j, i].T
        return carry

    blocks = (width // 256) * (count // 256)
    lax.fori_loop(0, blocks // 2, turn, 0)
    run_steps(ups, *plan[2])
    for c in range(chunks):
        r = rows_of(c)
        copy(1, c).wait_recv()
        copy(2, c).wait_recv()

        def finish_rows(n, carry, c=c):
            s = pl.ds(pl.multiple_of(c * size + n * step_rows, step_rows), step_rows)
            value = tok[s, :].astype(F32) + (
                part[me, s, :].astype(F32) + core_in[1, s, :].astype(F32) + in_x[s, :].astype(F32)
            )
            hidden[s, :] = value
            normal, _ = norm_parts(value, EPSILON)
            low[s, :] = (normal * gains[2:3, :] + gains[3:4, :]).astype(BF16)
            return carry

        lax.fori_loop(0, size // step_rows, finish_rows, 0)
        copy(3, c).start()
        copy(4, c).start()
        store(c).start()
        if c:
            run_steps(ups, *plan[2 + c])
    early_stores[6].start()
    for ring in downs:
        ring.begin()
    lax.fori_loop(blocks // 2, blocks, turn, 0)
    store_turned = pltpu.make_async_copy(win.at[0, :, pl.ds(0, count)], o_turned, own_sem.at[0])
    store_turned.start()
    for relation in range(4):
        arrived(relation, last + 3)
    fetch_seed = [
        pltpu.make_async_copy(full_seed.at[b], x.at[pl.ds(b * rows, rows)], fetch_sem.at[b])
        for b in range(GROUP)
    ]
    for fetch in fetch_seed:
        fetch.start()
    for ring in ups:
        ring.finish()
    fetch_up = [
        pltpu.make_async_copy(full_up.at[b], win_up.at[b], fetch_sem.at[GROUP + b]) for b in range(GROUP)
    ]
    for fetch in fetch_up:
        fetch.start()
    for c in range(chunks):
        copy(3, c).wait_recv()
        copy(5, c).start()
        if c % 2:
            run_steps(downs, *plan[c // 2])
    for c in range(chunks):
        copy(4, c).wait_recv()
        copy(5, c).wait_recv()
        store(c).wait()
        for kind in range(6):
            copy(kind, c).wait_send()
    fetch_two = pltpu.make_async_copy(full_two, part, load_sem.at[1])
    fetch_two.start()
    for fetch in fetch_seed + fetch_up:
        fetch.wait()
    fetch_two.wait()

    quarters = heads * VH // 256

    def upper_tile(n, carry):
        b, j = n // quarters, lax.rem(n, quarters)
        c = pl.ds(pl.multiple_of(j * 256, 256), 256)
        r = pl.ds(pl.multiple_of(b * rows, rows), rows)
        upper = dot(part[b], win_up[:, :, :, c].reshape(width, 256))
        cdf = 0.5 * (1.0 + lax.erf(upper * (0.5**0.5)))
        gated[r, c] = (upper * cdf).astype(BF16)
        half = pl.ds(pl.multiple_of(lax.rem(j, 2) * 256, 256), 256)
        gate[j // 2, r, half] = cdf + upper * jnp.exp(-0.5 * upper * upper) * (2.0 * np.pi) ** -0.5
        return carry

    tiles = GROUP * quarters
    lax.fori_loop(0, tiles // 2, upper_tile, 0)
    run_steps(downs, *plan[2])
    lax.fori_loop(tiles // 2, tiles, upper_tile, 0)
    run_steps(downs, *plan[3])
    store_active = pltpu.make_async_copy(gated, o_active, store_sem.at[0, 0])
    store_active.start()
    per_tile = 256 // block
    wide = 512

    def down_tile(n, carry):
        i, j = n // (width // wide), lax.rem(n, width // wide)
        a = pl.ds(pl.multiple_of(i * 256, 256), 256)
        c = pl.ds(pl.multiple_of(j * wide, wide), wide)
        value = dot_rows(gated[:, a], x[:, c]).astype(BF16)
        wo[pl.ds(i * per_tile, per_tile), :, c] = value.reshape(per_tile, block, wide)
        return carry

    tiles = quarters * (width // wide)
    lax.fori_loop(0, tiles // 2, down_tile, 0)
    run_steps(downs, *plan[4])
    lax.fori_loop(tiles // 2, tiles, down_tile, 0)
    run_steps(downs, *plan[5])
    store_down = pltpu.make_async_copy(wo, o_g_down, store_sem.at[0, 1])
    store_down.start()
    own_copies[1].wait()
    for ring in downs:
        ring.finish()
    store_full = pltpu.make_async_copy(wd, full_down, load_sem.at[0])
    store_full.start()

    def d_upper_tile(n, carry):
        h, j = n // 4, lax.rem(n, 4)
        m, side = j // 2, lax.rem(j, 2)
        r = pl.ds(pl.multiple_of(m * tile, tile), tile)
        c = pl.ds(pl.multiple_of(side * 256, 256), 256)
        piece = wd[pl.ds((2 * h + side) * per_tile, per_tile)].reshape(256, width)
        values[h, r, c] = (dot_back(x[r, :], piece) * gate[h, r, c]).astype(BF16)
        return carry

    last_stores = [store_active, store_down, store_full]
    for h in range(heads):
        lax.fori_loop(4 * h, 4 * (h + 1), d_upper_tile, 0)
        last_stores.append(
            pltpu.make_async_copy(values.at[h], o_upper.at[:, pl.ds(h * VH, VH)], store_sem.at[0, 2 + h])
        )
        last_stores[-1].start()
    wait_sent(outs + downs + ups, total)
    for relation in (1, 2, 3):
        for slot in range(last + 4):
            swap(relation, slot).wait_send()
    for n in range(1, total):
        spread(n).wait_send()
    store_turned.wait()
    for copy_out in last_stores + early_stores:
        copy_out.wait()


def forward(total, w_in, w_up, w_out, w_down, tok, cot, pack, rates, seq_cols, seq_rows):
    rows, width = tok.shape
    count = GROUP * rows
    heads = HEADS // GROUP
    head_width = 2 * (QKH + VH)
    vmem, hbm = pl.BlockSpec(memory_space=pltpu.VMEM), pl.BlockSpec(memory_space=ANY)
    dma = pltpu.SemaphoreType.DMA
    pair = np.arange(QKH // 2) / (QKH // 2)
    curves = np.zeros((8, QKH // 2), np.float32)
    curves[0] = 10000.0**-pair
    curves[1] = np.log((pair + 0.4) / 1.4)
    kept = (
        ((heads, count, QKH), BF16),
        ((heads, count, QKH), BF16),
        ((heads, count, VH), BF16),
        ((heads, count, VH), F32),
        ((heads, count, VH), F32),
        ((count, heads * VH), BF16),
    )
    in_hbm = (
        ((heads, width, head_width), BF16),
        ((GROUP, total, w_up.shape[0], w_up.shape[1] // GROUP), BF16),
        ((total,) + w_out.shape, BF16),
        ((total,) + w_down.shape, BF16),
        ((GROUP, rows, width), BF16),
        ((width, count), BF16),
        *kept,
        kept[-1],
        kept[-1],
        ((total,) + w_out.shape, BF16),
    )
    in_vmem = (
        ((rows, width), BF16),
        ((count, QKH // 2), F32),
        ((count, QKH // 2), F32),
        ((count, QKH // 2), F32),
        ((count, QKH // 2), F32),
        ((heads, rows, rows), F32),
        ((GROUP, rows, 1), F32),
        ((GROUP, 1, rows), F32),
        ((8, width), F32),
        ((heads, 1, VH), F32),
    )
    shapes = (*in_hbm, ((rows, width), F32), ((GROUP, rows, width), BF16), *in_vmem)
    return pl.pallas_call(
        functools.partial(forward_kernel, total),
        out_shape=[jax.ShapeDtypeStruct(s, d) for s, d in shapes],
        in_specs=[hbm] * 6 + [vmem] * 5,
        out_specs=[hbm] * (len(in_hbm) + 8) + [vmem] * 4,
        scratch_shapes=[
            pltpu.VMEM((rows, width), F32),
            *[pltpu.VMEM(s, d) for s, d in in_vmem[:6]],
            pltpu.VMEM((rows, width), BF16),
            pltpu.VMEM((rows, width), BF16),
            pltpu.VMEM((heads, width, head_width), BF16),
            pltpu.VMEM((GROUP, rows, width), BF16),
            pltpu.VMEM((count, width), BF16),
            *[pltpu.VMEM(s, d) for s, d in kept],
            pltpu.VMEM((total,) + w_out.shape, BF16),
            pltpu.VMEM((2, rows, width), BF16),
            pltpu.VMEM((rows, width), BF16),
            pltpu.VMEM((rows, width), BF16),
            pltpu.VMEM((rows, width), BF16),
            pltpu.VMEM((total, GROUP, 8, 128), F32),
            pltpu.VMEM((GROUP, total, w_up.shape[0], w_up.shape[1] // GROUP), BF16),
            pltpu.VMEM((total,) + w_down.shape, BF16),
            dma((20, total - 1)), dma((20, total - 1)), dma((2,)), dma((2,)), dma((2 * GROUP,)),
            dma((heads, 7)), dma((6, 4)), dma((6, 4)), dma((4,)),
            dma((3, 12)), dma((3, 12)), dma((12,)), dma((total - 1,)), dma((total - 1,)), dma((9,)),
        ],
        compiler_params=pltpu.CompilerParams(
            collective_id=1, has_side_effects=True, vmem_limit_bytes=63 * MIB
        ),
        name="forward_retention",
    )(w_in, w_up, w_out, w_down, tok, cot, pack, rates, seq_cols, seq_rows, jnp.asarray(curves))


class Adding:
    def __init__(self, at, way, term, arrived, sends, recvs, origin=None):
        self.at, self.way, self.term, self.arrived = at, way, term, arrived
        self.origin = term if origin is None else origin
        self.sends, self.recvs = sends, recvs

    def hop(self, step, first=False):
        src = self.origin(self.at.behind(self.way, 1)) if first else self.arrived.at[step - 1]
        return remote(
            src, self.arrived.at[step], self.sends.at[step], self.recvs.at[step], self.at.neighbour(self.way)
        )

    def begin(self):
        self.hop(0, True).start()

    def sum_at(self, step, which):
        self.hop(step, True).wait_recv()
        return self.arrived[step].astype(F32) + self.term(which)[...].astype(F32)

    def onward(self, step):
        self.arrived[step - 1] = self.sum_at(step - 1, self.at.behind(self.way, step + 1)).astype(BF16)
        self.hop(step).start()

    def finish(self):
        return self.sum_at(self.at.total - 2, self.at.inner)


def wait_added(rings, total):
    def body(step, carry):
        for ring in rings:
            ring.hop(step, True).wait_send()
        return carry

    lax.fori_loop(0, total - 1, body, 0)


def backward_kernel(
    total, h_g_down, two, d_upper, h_up, h_seed, h_hidden, gains_all, h_gated, h_out, h_query, h_keys, h_values,
    h_gate, h_mixed, h_cosine, h_sine, h_growth, h_shrink, h_powers, ident_col, ident_row, gain_group,
    to_down, to_up, to_out, to_hidden, full_branch, sums, o_group, o_project,
    g_down, seed, hidden, cosine, sine, growth, shrink, powers, o_down, o_up, o_out, d_hidden, g_up, g_out, arrived, wide_buf, narrow_buf, wo, part, core_in, out_x, in_x, low,
    query, keys, values, gate, mixed, back, d_mixed, staged, stage, landed,
    ring_send, ring_recv, row_send, row_recv, row_own, load_sem, late_sem, unit_sem, out_sem, a2a_send, a2a_recv,
):
    at = Place(total)
    me = at.group
    core, across = at.peer(1), at.peer(2)
    greet([core, across, at.peer(3), at.neighbour(0), at.neighbour(1)])
    rows, width = seed.shape
    count = GROUP * rows
    heads = HEADS // GROUP
    r_up, r_out = o_up.shape[0], o_out.shape[0]
    up_width = o_up.shape[1] // GROUP
    half, side = r_out // 2, width // 2

    def halves(source, base, origin=None):
        def chunk_of(ref, way, c):
            return lambda which: ref.at[
                pl.ds(pl.multiple_of(which * r_out + way * half, half), half), pl.ds(c * side, side)
            ]

        return [
            Adding(
                at, way,
                chunk_of(source, way, c),
                arrived.at[base + 2 * c + way], ring_send.at[base + 2 * c + way], ring_recv.at[base + 2 * c + way],
                None if origin is None else chunk_of(origin, way, c),
            )
            for c in (0, 1)
            for way in (0, 1)
        ]

    downs, outs, ups = halves(g_down, 0, h_g_down), halves(g_out, 8), []
    for order in (0, 1):
        for way in (0, 1):
            relation = RELATIONS[way][order]
            slot = 4 + 2 * order + way
            ups.append(
                Adding(
                    at, way,
                    lambda which, relation=relation: g_up.at[
                        pl.ds(pl.multiple_of((flip(me, relation) * total + which) * r_up, r_up), r_up), :
                    ],
                    arrived.at[slot], ring_send.at[slot], ring_recv.at[slot],
                )
            )

    chunks = 4
    size = rows // chunks
    step_rows = 32
    far = flip(me, 2)

    def rows_of(c):
        return pl.ds(c * size, size)

    def copy(kind, c):
        r = rows_of(c)
        if kind == 0:
            src, dst, dev = part.at[flip(me, 3), r], core_in.at[0, r], core
        elif kind == 1:
            src, dst, dev = part.at[flip(me, 1), r], core_in.at[1, r], core
        elif kind == 2:
            src, dst, dev = out_x.at[r], in_x.at[r], across
        elif kind == 3:
            src, dst, dev = low.at[r], full_branch.at[me, r], across
        elif kind == 4:
            src, dst, dev = low.at[r], full_branch.at[me, r], core
        else:
            src, dst, dev = full_branch.at[far, r], full_branch.at[far, r], core
        return remote(src, dst, row_send.at[kind, c], row_recv.at[kind, c], dev)

    def store(c):
        r = rows_of(c)
        return pltpu.make_async_copy(low.at[r], full_branch.at[me, r], row_own.at[c])

    for ring in downs:
        ring.begin()
    upper_columns = pl.ds(0, up_width)
    fetch_upper = pltpu.make_async_copy(d_upper, g_out.at[:, upper_columns], load_sem.at[1])
    fetch_up = pltpu.make_async_copy(h_up, g_up, load_sem.at[7])
    fetch_two = pltpu.make_async_copy(two, wide_buf, load_sem.at[0])
    fetch_gated = pltpu.make_async_copy(h_gated, narrow_buf, load_sem.at[8])
    fetch_out = pltpu.make_async_copy(h_out, wo, load_sem.at[2])
    fetch_rows = [
        pltpu.make_async_copy(src, dst, late_sem.at[n])
        for n, (src, dst) in enumerate(((h_g_down, g_down), (h_seed, seed), (h_hidden, hidden)))
    ]
    fetch_tables = [
        pltpu.make_async_copy(src, dst, late_sem.at[3 + n])
        for n, (src, dst) in enumerate(
            ((h_cosine, cosine), (h_sine, sine), (h_growth, growth), (h_shrink, shrink), (h_powers, powers))
        )
    ]
    stores = [
        pltpu.make_async_copy(src, dst, late_sem.at[8 + n])
        for n, (src, dst) in enumerate(((o_down, to_down), (o_up, to_up), (o_out, to_out), (d_hidden, to_hidden)))
    ]
    for fetch in (fetch_upper, fetch_up, *fetch_rows, fetch_two, fetch_gated, fetch_out, *fetch_tables):
        fetch.start()

    def unit_loads(unit, slot):
        h, b = unit // GROUP, lax.rem(unit, GROUP)
        r = pl.ds(pl.multiple_of(b * rows, rows), rows)
        pairs = ((h_query, query), (h_keys, keys), (h_values, values), (h_gate, gate), (h_mixed, mixed))
        return [
            pltpu.make_async_copy(src.at[h, r], dst.at[slot], unit_sem.at[slot, n])
            for n, (src, dst) in enumerate(pairs)
        ]

    for unit in (0, 1):
        for fetch in unit_loads(jnp.int32(unit), unit):
            fetch.start()

    def send_sums(c):
        r = rows_of(c)
        copy(0, c).wait_recv()
        out_x[r, :] = (part[far, r, :].astype(F32) + core_in[0, r, :].astype(F32)).astype(BF16)
        copy(2, c).start()

    def norm_back(c):
        copy(1, c).wait_recv()
        copy(2, c).wait_recv()

        def some_rows(n, carry):
            s = pl.ds(pl.multiple_of(c * size + n * step_rows, step_rows), step_rows)
            e = part[me, s, :].astype(F32) + core_in[1, s, :].astype(F32) + in_x[s, :].astype(F32)
            normal, scale = norm_parts(hidden[s, :], EPSILON)
            with_gain = e * gains_all[2:3, :]
            sums[0:1, :] += jnp.sum(e * normal, axis=0, keepdims=True)
            sums[1:2, :] += jnp.sum(e, axis=0, keepdims=True)
            value = seed[s, :].astype(F32) + scale * (
                with_gain
                - jnp.mean(with_gain, axis=-1, keepdims=True)
                - normal * jnp.mean(with_gain * normal, axis=-1, keepdims=True)
            )
            d_hidden[s, :] = value
            low[s, :] = value.astype(BF16)
            return carry

        lax.fori_loop(0, size // step_rows, some_rows, 0)
        copy(3, c).start()
        copy(4, c).start()
        store(c).start()

    sums[...] = jnp.zeros_like(sums)
    o_group[...] = jnp.zeros_like(o_group)
    def d_two(relation):
        b = flip(me, relation)
        r = pl.ds(pl.multiple_of(b * rows, rows), rows)

        def column(n, carry):
            c = pl.ds(pl.multiple_of(n * 256, 256), 256)
            part[b, :, c] = dot_back(g_out[r, :up_width], g_up[c, :]).astype(BF16)
            return carry

        lax.fori_loop(0, width // 256, column, 0)

    plan = tick_plan(total, 6)
    fetch_upper.wait()
    fetch_up.wait()
    d_two(3)
    for c in range(chunks):
        copy(0, c).start()
    d_two(2)
    for c in range(chunks):
        send_sums(c)
    for fetch in fetch_rows:
        fetch.wait()
    add_steps(downs, *plan[0])
    d_two(1)
    for c in range(chunks):
        copy(1, c).start()
    d_two(0)
    fetch_two.wait()

    def grad_tiles(left, right, span, out, start, stop):
        wide = 512

        def tile(n, carry):
            rows_n = span // wide
            i, j = n // rows_n, lax.rem(n, rows_n)
            a = pl.ds(pl.multiple_of(i * 256, 256), 256)
            c = pl.ds(pl.multiple_of(j * wide, wide), wide)
            out[a, c] = dot_rows(left[:, a], right[:, c]).astype(BF16)
            return carry

        lax.fori_loop(start, stop, tile, 0)

    tiles = (width // 256) * (up_width // 512)
    for quarter in range(4):
        grad_tiles(wide_buf, g_out, up_width, g_up, tiles * quarter // 4, tiles * (quarter + 1) // 4)
        if quarter:
            norm_back(quarter - 1)
        add_steps(downs, *plan[1 + quarter])
    norm_back(3)
    add_steps(downs, *plan[5])
    for ring in ups:
        ring.begin()
    for n, ring in enumerate(downs):
        c, way = n // 2, n % 2
        o_down[pl.ds(way * half, half), pl.ds(c * side, side)] = ring.finish()
    stores[0].start()
    stores[3].start()
    for c in range(chunks):
        copy(3, c).wait_recv()
        copy(5, c).start()
        if c % 2:
            add_steps(ups, *plan[c // 2])
    for c in range(chunks):
        copy(4, c).wait_recv()
        copy(5, c).wait_recv()
        store(c).wait()
    branch = wide_buf
    fetch_branch = [
        pltpu.make_async_copy(full_branch.at[b], branch.at[pl.ds(b * rows, rows)], load_sem.at[3 + b])
        for b in range(GROUP)
    ]
    for fetch in fetch_branch:
        fetch.start()
    for fetch in fetch_branch:
        fetch.wait()
    fetch_gated.wait()
    fetch_out.wait()
    tiles = (narrow_buf.shape[1] // 256) * (width // 512)
    for part_of in range(2):
        grad_tiles(narrow_buf, branch, width, g_out, tiles * part_of // 2, tiles * (part_of + 1) // 2)
        add_steps(ups, *plan[2 + part_of])
    for fetch in fetch_tables:
        fetch.wait()

    units = heads * GROUP

    def unit_stores(unit, slot):
        h, b = unit // GROUP, lax.rem(unit, GROUP)
        r = pl.ds(pl.multiple_of(b * rows, rows), rows)
        start = pl.multiple_of(h * staged.shape[2], 128)
        return pltpu.make_async_copy(
            staged.at[slot], o_project.at[r, pl.ds(start, staged.shape[2])], out_sem.at[slot]
        )

    def unrotated(value, r, scale):
        mid = QKH // 2
        first, second = value[:, :mid], value[:, mid:]
        c, s = cosine[r, :], sine[r, :]
        return jnp.concatenate(
            [(first * c + second * s) * scale, (second * c - first * s) * scale], axis=1
        )

    def unit_body(unit):
        slot = lax.rem(unit, 2)
        h, b = unit // GROUP, lax.rem(unit, GROUP)
        r = pl.ds(pl.multiple_of(b * rows, rows), rows)
        back[...] = dot_back(branch[r, :], wo[pl.ds(pl.multiple_of(h * VH, VH), VH), :])
        for fetch in unit_loads(unit, slot):
            fetch.wait()

        @pl.when(unit >= 2)
        def _():
            unit_stores(unit - 2, slot).wait()

        gains = gain_group[h]

        def some_rows(n, carry):
            s = pl.ds(pl.multiple_of(n * step_rows, step_rows), step_rows)
            normal, scale = norm_parts(mixed[slot, s, :], GROUP_EPSILON)
            z = gate[slot, s, :]
            f = back[s, :]
            sigmoid = 1.0 / (1.0 + jnp.exp(-z))
            silu = z * sigmoid
            d_silu = f * (normal * gains)
            staged[slot, s, 2 * QKH + VH :] = (d_silu * (sigmoid + silu * (1.0 - sigmoid))).astype(BF16)
            d_scaled = f * silu
            o_group[h] += jnp.sum(d_scaled * normal, axis=0, keepdims=True)
            d_normal = d_scaled * gains
            d_mixed[s, :] = (
                scale
                * (
                    d_normal
                    - jnp.mean(d_normal, axis=-1, keepdims=True)
                    - normal * jnp.mean(d_normal * normal, axis=-1, keepdims=True)
                )
            ).astype(BF16)
            return carry

        lax.fori_loop(0, rows // step_rows, some_rows, 0)
        linked = (ident_col[b] == ident_row[b]) & (ident_col[b] >= 0.0)
        decay = jnp.where(linked, powers[h], 0.0)
        masked = (dot_back(query[slot], keys[slot]) * decay).astype(BF16)
        staged[slot, :, 2 * QKH : 2 * QKH + VH] = dot_rows(masked, d_mixed[...]).astype(BF16)
        d_raw = (dot_back(d_mixed[...], values[slot]) * decay).astype(BF16)
        d_query = dot(d_raw, keys[slot]) * QKH ** (-0.5)
        staged[slot, :, :QKH] = unrotated(d_query, r, growth[r, :]).astype(BF16)
        d_keys = dot_rows(d_raw, query[slot])
        staged[slot, :, QKH : 2 * QKH] = unrotated(d_keys, r, shrink[r, :]).astype(BF16)
        unit_stores(unit, slot).start()

        @pl.when(unit + 2 < units)
        def _():
            for fetch in unit_loads(unit + 2, slot):
                fetch.start()

    early = 2

    def with_ups(unit, carry):
        unit_body(unit)
        (low_a, high_a), (low_b, high_b) = plan[4], plan[5]
        add_steps(ups, low_a + unit * (low_b - low_a), high_a + unit * (high_b - high_a))
        return carry

    def with_outs(unit, carry):
        unit_body(unit)
        steps, number = total - 2, unit - early
        add_steps(outs, 1 + (steps * number) // (units - early), 1 + (steps * (number + 1)) // (units - early))
        return carry

    lax.fori_loop(0, early, with_ups, 0)
    for ring in outs:
        ring.begin()

    def sent_across(relation):
        return remote(
            stage.at[relation - 1], landed.at[relation - 1],
            a2a_send.at[relation - 1], a2a_recv.at[relation - 1], at.peer(relation),
        )

    for n, ring in enumerate(ups):
        relation = RELATIONS[n % 2][n // 2]
        value = ring.finish()
        if relation == 0:
            o_up[:, pl.ds(pl.multiple_of(me * up_width, 128), up_width)] = value
        else:
            stage[relation - 1] = value.astype(BF16)
            sent_across(relation).start()
    lax.fori_loop(early, units, with_outs, 0)
    for relation in (1, 2, 3):
        sent_across(relation).wait_recv()
        o_up[:, pl.ds(pl.multiple_of(flip(me, relation) * up_width, 128), up_width)] = landed[
            relation - 1
        ].astype(F32)
        sent_across(relation).wait_send()
    stores[1].start()
    for slot in (0, 1):
        unit_stores(jnp.int32(units - 2 + slot), slot).wait()
    for n, ring in enumerate(outs):
        c, way = n // 2, n % 2
        o_out[pl.ds(way * half, half), pl.ds(c * side, side)] = ring.finish()
    stores[2].start()
    for c in range(chunks):
        for kind in range(6):
            copy(kind, c).wait_send()
    wait_added(downs + ups + outs, total)
    for store_one in stores:
        store_one.wait()


def add_steps(rings, start, stop):
    def body(step, carry):
        for ring in rings:
            ring.onward(step)
        return carry

    lax.fori_loop(start, stop, body, 0)


def backward(
    total, g_down, two, d_upper, full_up, seed, hidden, gain_two, gated, full_out, query, keys, values, gate, mixed,
    tables, powers, ident_col, ident_row, gain_group,
):
    rows, width = seed.shape
    count = GROUP * rows
    heads = HEADS // GROUP
    up_width = d_upper.shape[1]
    r_out, r_up = g_down.shape[0] // total, width // GROUP // total
    half, side = r_out // 2, width // 2
    vmem, hbm = pl.BlockSpec(memory_space=pltpu.VMEM), pl.BlockSpec(memory_space=ANY)
    dma = pltpu.SemaphoreType.DMA
    shapes = (
        ((r_out, width), F32),
        ((r_up, up_width * GROUP), F32),
        ((r_out, width), F32),
        ((rows, width), F32),
        ((GROUP, rows, width), BF16),
        ((8, width), F32),
        ((heads, 1, VH), F32),
        ((count, 2 * heads * (QKH + VH)), BF16),
    )
    return pl.pallas_call(
        functools.partial(backward_kernel, total),
        out_shape=[jax.ShapeDtypeStruct(s, d) for s, d in shapes],
        in_specs=[hbm] * 6 + [vmem] + [hbm] * 12 + [vmem] * 3,
        out_specs=[hbm] * 5 + [vmem, vmem, hbm],
        scratch_shapes=[
            pltpu.VMEM(g_down.shape, BF16),
            pltpu.VMEM(seed.shape, BF16),
            pltpu.VMEM(hidden.shape, F32),
            *[pltpu.VMEM(v.shape, F32) for v in (*tables, powers)],
            *[pltpu.VMEM(s, d) for s, d in shapes[:4]],
            pltpu.VMEM((width, up_width), BF16),
            pltpu.VMEM(g_down.shape, BF16),
            pltpu.VMEM((12, total - 1, half, side), BF16),
            pltpu.VMEM((count, width), BF16),
            pltpu.VMEM((count, up_width), BF16),
            pltpu.VMEM(full_out.shape, BF16),
            pltpu.VMEM((GROUP, rows, width), BF16),
            pltpu.VMEM((2, rows, width), BF16),
            pltpu.VMEM((rows, width), BF16),
            pltpu.VMEM((rows, width), BF16),
            pltpu.VMEM((rows, width), BF16),
            pltpu.VMEM((2, rows, QKH), BF16),
            pltpu.VMEM((2, rows, QKH), BF16),
            pltpu.VMEM((2, rows, VH), BF16),
            pltpu.VMEM((2, rows, VH), F32),
            pltpu.VMEM((2, rows, VH), F32),
            pltpu.VMEM((rows, VH), F32),
            pltpu.VMEM((rows, VH), BF16),
            pltpu.VMEM((2, rows, 2 * (QKH + VH)), BF16),
            pltpu.VMEM((3, r_up, up_width), BF16),
            pltpu.VMEM((3, r_up, up_width), BF16),
            dma((12, total - 1)), dma((12, total - 1)), dma((6, 4)), dma((6, 4)), dma((4,)), dma((9,)), dma((12,)),
            dma((2, 5)), dma((2,)), dma((3,)), dma((3,)),
        ],
        compiler_params=pltpu.CompilerParams(
            collective_id=2, has_side_effects=True, vmem_limit_bytes=63 * MIB
        ),
        name="backward_retention",
    )(
        g_down, two, d_upper, full_up, seed, hidden, gain_two, gated, full_out, query, keys, values, gate, mixed,
        *tables, powers, ident_col, ident_row, gain_group,
    )


def final_kernel(
    total, h_project, h_in, h_turned, h_active, h_down, hidden, d_hidden, tok, gains_all, ident_col, sums_two, d_group,
    o_in, o_output, o_tokens, o_vec, o_grp,
    output, d_tokens, full_rows, project, turned, term, arrived, win, part, active, wd, rows_f32, core_in, out_x, in_x, stage, landed,
    vec, grp, near_in, mid, far_in, far_grp,
    load_sem, win_sem, ring_send, ring_recv, a2a_send, a2a_recv, row_send, row_recv, in_sem, piece_sem,
    near_send, near_recv, far_send, far_recv,
):
    at = Place(total)
    me, inner = at.group, at.inner
    others = [(me, lax.rem(inner + n, total)) for n in range(1, total)]
    greet([at.peer(r) for r in (1, 2, 3)] + others)
    rows, width = tok.shape
    count = GROUP * rows
    block = o_in.shape[0]
    step_rows = 32

    store_output = pltpu.make_async_copy(output, o_output, load_sem.at[6])
    store_tokens = pltpu.make_async_copy(d_tokens, o_tokens, load_sem.at[7])
    fetch_turned = pltpu.make_async_copy(h_turned, turned, load_sem.at[0])
    wide = 512
    fetch_project = [
        pltpu.make_async_copy(
            h_project.at[:, pl.ds(n * wide, wide)], project.at[:, pl.ds(n * wide, wide)], piece_sem.at[n]
        )
        for n in range(project.shape[1] // wide)
    ]
    fetch_turned.start()
    for fetch in fetch_project:
        fetch.start()

    def source(n, b):
        return part.at[pl.ds(pl.multiple_of(b * rows, rows), rows), :]

    def row_copy(kind, n):
        if kind < 2:
            return remote(
                source(n, flip(me, 3 - 2 * kind)), core_in.at[n, kind], row_send.at[n, kind], row_recv.at[n, kind],
                at.peer(1),
            )
        return remote(out_x.at[n], in_x.at[n], row_send.at[n, 2], row_recv.at[n, 2], at.peer(2))

    def own_rows(n, which, r):
        b = flip(me, 2) if which == 0 else me
        return part[pl.ds(pl.multiple_of(b * rows + r, step_rows), step_rows), :]

    def by_rows(body):
        def some(k, carry):
            body(pl.multiple_of(k * step_rows, step_rows))
            return carry

        lax.fori_loop(0, rows // step_rows, some, 0)

    def send_rows(n):
        row_copy(0, n).wait_recv()

        def some(r):
            s = pl.ds(r, step_rows)
            out_x[n, s, :] = (own_rows(n, 0, r).astype(F32) + core_in[n, 0, s, :].astype(F32)).astype(BF16)

        by_rows(some)
        row_copy(2, n).start()

    def hold_down():
        fetch_hidden.wait()
        row_copy(1, 0).wait_recv()

        def some(r):
            s = pl.ds(r, step_rows)
            rows_f32[s, :] += own_rows(0, 1, r).astype(F32) + core_in[0, 1, s, :].astype(F32)

        by_rows(some)
        row_copy(0, 0).wait_send()
        row_copy(1, 0).wait_send()

    def summed_rows(n, r):
        s = pl.ds(r, step_rows)
        return own_rows(n, 1, r).astype(F32) + core_in[n, 1, s, :].astype(F32) + in_x[n, s, :].astype(F32)

    def take_down():
        row_copy(2, 0).wait_recv()

        def some(r):
            s = pl.ds(r, step_rows)
            valid = jnp.where(ident_col[me, s, :] >= 0.0, 1.0, 0.0)
            output[s, :] = ((rows_f32[s, :] + in_x[0, s, :].astype(F32)) * valid).astype(BF16)

        by_rows(some)
        fetch_d_hidden.start()
        store_output.start()

    def take_rows():
        fetch_d_hidden.wait()
        row_copy(1, 1).wait_recv()
        row_copy(2, 1).wait_recv()
        vec[...] = jnp.zeros_like(vec)
        vec[2:4, :] = sums_two[0:2, :]

        def some(r):
            s = pl.ds(r, step_rows)
            e = summed_rows(1, r)
            normal, scale = norm_parts(tok[s, :].astype(F32), EPSILON)
            with_gain = e * gains_all[0:1, :]
            vec[0:1, :] += jnp.sum(e * normal, axis=0, keepdims=True)
            vec[1:2, :] += jnp.sum(e, axis=0, keepdims=True)
            value = rows_f32[s, :] + scale * (
                with_gain
                - jnp.mean(with_gain, axis=-1, keepdims=True)
                - normal * jnp.mean(with_gain * normal, axis=-1, keepdims=True)
            )
            d_tokens[s, :] = value.astype(BF16)

        by_rows(some)
        store_tokens.start()

    quarter = width // GROUP
    small = quarter // total
    large = grp.shape[1] // total

    def near(relation):
        start = pl.multiple_of(flip(me, relation) * quarter, 128)
        return remote(
            vec.at[:, pl.ds(start, quarter)], near_in.at[relation - 1], near_send.at[relation - 1],
            near_recv.at[relation - 1], at.peer(relation),
        )

    def tile_of(index, size):
        return pl.ds(pl.multiple_of((index * size) // 128 * 128, 128), 128)

    def distant(kind, n):
        target = lax.rem(inner + n, total)
        src = mid.at[:, tile_of(target, small)] if kind == 0 else grp.at[:, tile_of(target, large)]
        dst = far_in if kind == 0 else far_grp
        return remote(
            src, dst.at[n - 1], far_send.at[kind, n - 1], far_recv.at[kind, n - 1], (me, target)
        )

    def vectors_near():
        for relation in (1, 2, 3):
            near(relation).start()
        grp[...] = jnp.zeros_like(grp)
        for h in range(d_group.shape[0]):
            grp[0:1, h * VH : (h + 1) * VH] = d_group[h]

    def vectors_far():
        for relation in (1, 2, 3):
            near(relation).wait_recv()
        mid[...] = (
            vec[:, pl.ds(pl.multiple_of(me * quarter, 128), quarter)] + near_in[0] + near_in[1] + near_in[2]
        )
        for n in range(1, total):
            for kind in (0, 1):
                distant(kind, n).start()

    def vectors_end():
        for n in range(1, total):
            for kind in (0, 1):
                distant(kind, n).wait_recv()
        o_vec[...] = mid[:, tile_of(inner, small)] + jnp.sum(far_in[...], axis=0)
        o_grp[...] = grp[:, tile_of(inner, large)] + jnp.sum(far_grp[...], axis=0)


    def terms(step, far_at, near_at, arriving=False):
        left = jnp.concatenate(
            [
                turned[
                    pl.ds(
                        pl.multiple_of((flip(me, relation) * total + at.behind(way, step + 1)) * block, block), block
                    ),
                    :,
                ]
                for way in (0, 1)
                for relation in RELATIONS[way]
            ],
            axis=0,
        )

        def tile(n, carry):
            c = pl.ds(pl.multiple_of(n * wide, wide), wide)
            value = dot(left, project[:, c]).astype(BF16)
            for way in (0, 1):
                first = 2 * way * block
                term[far_at + way, :, c] = value[first : first + block]
                term[near_at + way, :, c] = value[first + block : first + 2 * block]
            return carry

        if arriving:
            for n, fetch in enumerate(fetch_project):
                fetch.wait()
                tile(n, 0)
        else:
            lax.fori_loop(0, project.shape[1] // wide, tile, 0)

    far_slots, near_slots = (0, 2), (1, 3)

    def near_place(step):
        return 6 + 2 * lax.rem(step, 2)

    def hop(slot, step, first=False):
        src = term.at[2 * (slot % 2) + slot // 2] if first else arrived.at[slot, step - 1]
        return remote(
            src, arrived.at[slot, step], ring_send.at[slot, step], ring_recv.at[slot, step],
            at.neighbour(slot // 2),
        )

    def sum_into(out, slot, step, base):
        hop(slot, step, True).wait_recv()

        def some(n, carry):
            c = pl.ds(pl.multiple_of(n * wide, wide), wide)
            value = arrived[slot, step, :, c].astype(F32) + term[base + slot // 2, :, c].astype(F32)
            out[:, c] = value.astype(BF16)
            return carry

        lax.fori_loop(0, project.shape[1] // wide, some, 0)

    def send_on(slots, step, base):
        for slot in slots:
            sum_into(arrived.at[slot, step - 1], slot, step - 1, base)
            hop(slot, step).start()

    def onward(step, carry):
        terms(step, 4, near_place(step))
        send_on(far_slots, step, 4)
        send_on(near_slots, step - 1, near_place(step - 1))
        return carry

    parts = h_in.shape[0]
    part_width = h_in.shape[2]

    class fetch_win:
        def __init__(self, n):
            self.copies = [
                pltpu.make_async_copy(
                    h_in.at[h, pl.ds(n * 256, 256), :],
                    win.at[n % 2, :, pl.ds(h * part_width, part_width)],
                    win_sem.at[n % 2, h],
                )
                for h in range(parts)
            ]

        def start(self):
            for copy in self.copies:
                copy.start()

        def wait(self):
            for copy in self.copies:
                copy.wait()

    columns = width // 256

    def row_tiles(n):
        fetch_win(n).wait()

        def tile(m, carry):
            r = pl.ds(pl.multiple_of(m * 512, 512), 512)
            part[r, n * 256 : (n + 1) * 256] = dot_back(project[r, :], win[n % 2]).astype(BF16)
            return carry

        lax.fori_loop(0, count // 512, tile, 0)
        if n + 2 < columns:
            fetch_win(n + 2).start()

    def down_rows(relation):
        b = flip(me, relation)
        r = pl.ds(pl.multiple_of(b * rows, rows), rows)

        def column(n, carry):
            c = pl.ds(pl.multiple_of(n * wide, wide), wide)
            part[r, c] = dot(active[r, :], wd[:, c]).astype(BF16)
            return carry

        lax.fori_loop(0, width // wide, column, 0)

    fetch_active = pltpu.make_async_copy(h_active, active, load_sem.at[2])
    fetch_down = pltpu.make_async_copy(h_down, wd, load_sem.at[3])
    fetch_hidden = pltpu.make_async_copy(hidden, rows_f32, load_sem.at[4])
    fetch_d_hidden = pltpu.make_async_copy(d_hidden, rows_f32, load_sem.at[5])
    for fetch in (fetch_active, fetch_down, fetch_hidden):
        fetch.start()
    fetch_win(0).start()
    fetch_win(1).start()
    fetch_turned.wait()
    terms(0, 0, 2, True)
    for slot in far_slots:
        hop(slot, 0, True).start()
    fetch_active.wait()
    fetch_down.wait()
    down_rows(3)
    row_copy(0, 0).start()
    for slot in near_slots:
        hop(slot, 0, True).start()
    down_rows(2)
    down_rows(1)
    row_copy(1, 0).start()
    down_rows(0)
    send_rows(0)
    hold_down()
    plan = tick_plan(total, 6)

    def extra(number):
        if number < 3:
            for n in range(columns * number // 3, columns * (number + 1) // 3):
                row_tiles(n)
            if number == 2:
                row_copy(0, 1).start()
                row_copy(1, 1).start()
        elif number == 3:
            send_rows(1)
            take_down()
        elif number == 5:
            take_rows()
            vectors_near()

    terms(1, 4, near_place(1))
    send_on(far_slots, 1, 4)
    for number in range(6):
        extra(number)
        lax.fori_loop(max(plan[number][0], 2), plan[number][1], onward, 0)
    terms(total - 1, 4, near_place(total - 1))
    pieces = column_pieces()

    def place(relation, columns_of):
        other = flip(me, relation)
        for base, stride, h, off, size in pieces:
            start = pl.multiple_of(base + other * stride, 128)
            off = h * part_width + off
            full_rows[:, pl.ds(start, size)] = columns_of(off, size)
        for copy in stored(relation):
            copy.start()

    def stored(relation):
        other = flip(me, relation)
        return [
            pltpu.make_async_copy(
                full_rows.at[:, pl.ds(pl.multiple_of(base + other * stride, 128), size)],
                o_in.at[:, pl.ds(pl.multiple_of(base + other * stride, 128), size)],
                in_sem.at[relation, n],
            )
            for n, (base, stride, h, off, size) in enumerate(pieces)
        ]

    def sent_across(relation):
        return remote(
            stage.at[relation - 1], landed.at[relation - 1],
            a2a_send.at[relation - 1], a2a_recv.at[relation - 1], at.peer(relation),
        )

    for slot in far_slots:
        relation = RELATIONS[slot // 2][0]
        sum_into(stage.at[relation - 1], slot, total - 2, 4)
        sent_across(relation).start()
    send_on(near_slots, total - 2, near_place(total - 2))
    vectors_far()
    for slot in reversed(near_slots):
        relation = RELATIONS[slot // 2][1]
        base = near_place(total - 1)
        if relation == 0:
            hop(slot, total - 2, True).wait_recv()
            place(
                0,
                lambda off, size: arrived[slot, total - 2, :, off : off + size].astype(F32)
                + term[base + slot // 2, :, off : off + size].astype(F32),
            )
        else:
            sum_into(stage.at[relation - 1], slot, total - 2, base)
            sent_across(relation).start()
    for relation in (2, 3, 1):
        sent_across(relation).wait_recv()
        place(relation, lambda off, size: landed[relation - 1, :, off : off + size].astype(F32))
    vectors_end()
    for relation in range(4):
        for copy in stored(relation):
            copy.wait()
    for copy in (store_output, store_tokens):
        copy.wait()
    for relation in (1, 2, 3):
        sent_across(relation).wait_send()
        near(relation).wait_send()
    for n in range(1, total):
        for kind in (0, 1):
            distant(kind, n).wait_send()
    row_copy(2, 0).wait_send()
    for kind in (0, 1, 2):
        row_copy(kind, 1).wait_send()

    def sent(step, carry):
        for slot in range(4):
            hop(slot, step, True).wait_send()
        return carry

    lax.fori_loop(0, total - 1, sent, 0)


def final(
    total, d_project, full_in, turned, active, full_down, hidden, d_hidden, tok, gains, ident_col, sums_two, d_group
):
    rows, width = tok.shape
    count, wide = d_project.shape
    block = width // GROUP // total
    vmem, hbm = pl.BlockSpec(memory_space=pltpu.VMEM), pl.BlockSpec(memory_space=ANY)
    dma = pltpu.SemaphoreType.DMA
    group_width = d_group.shape[0] * d_group.shape[2]
    shapes = (
        ((block, wide * GROUP), F32),
        ((rows, width), BF16),
        ((rows, width), BF16),
        ((8, 128), F32),
        ((8, 128), F32),
    )
    return pl.pallas_call(
        functools.partial(final_kernel, total),
        out_shape=[jax.ShapeDtypeStruct(s, d) for s, d in shapes],
        in_specs=[hbm] * 7 + [vmem] * 5,
        out_specs=[hbm] * 3 + [vmem] * 2,
        scratch_shapes=[
            pltpu.VMEM((rows, width), BF16),
            pltpu.VMEM((rows, width), BF16),
            pltpu.VMEM((block, wide * GROUP), F32),
            pltpu.VMEM((count, wide), BF16),
            pltpu.VMEM(turned.shape, BF16),
            pltpu.VMEM((10, block, wide), BF16),
            pltpu.VMEM((4, total - 1, block, wide), BF16),
            pltpu.VMEM((2, 256, wide), BF16),
            pltpu.VMEM((count, width), BF16),
            pltpu.VMEM(active.shape, BF16),
            pltpu.VMEM(full_down.shape, BF16),
            pltpu.VMEM((rows, width), F32),
            pltpu.VMEM((2, 2, rows, width), BF16),
            pltpu.VMEM((2, rows, width), BF16),
            pltpu.VMEM((2, rows, width), BF16),
            pltpu.VMEM((3, block, wide), BF16),
            pltpu.VMEM((3, block, wide), BF16),
            pltpu.VMEM((8, width), F32),
            pltpu.VMEM((8, group_width), F32),
            pltpu.VMEM((3, 8, width // GROUP), F32),
            pltpu.VMEM((8, width // GROUP), F32),
            pltpu.VMEM((total - 1, 8, 128), F32),
            pltpu.VMEM((total - 1, 8, 128), F32),
            dma((8,)), dma((2, 2)), dma((4, total - 1)), dma((4, total - 1)), dma((3,)), dma((3,)),
            dma((2, 3)), dma((2, 3)), dma((GROUP, 8)), dma((6,)), dma((3,)), dma((3,)), dma((2, total - 1)), dma((2, total - 1)),
        ],
        compiler_params=pltpu.CompilerParams(
            collective_id=3, has_side_effects=True, vmem_limit_bytes=63 * MIB
        ),
        name="final_sums",
    )(d_project, full_in, turned, active, full_down, hidden, d_hidden, tok, gains, ident_col, sums_two, d_group)


def mean(values):
    return jnp.mean(values, axis=-1, keepdims=True)


def local(
    total,
    tokens,
    cotangent,
    w_in,
    w_out,
    w_up,
    w_down,
    ln1_gain,
    ln1_bias,
    group_gain,
    ln2_gain,
    ln2_bias,
    seq_lens,
    seq_owner,
    seq_offset,
):
    rows, width = tokens.shape
    heads = HEADS // GROUP
    qk, vv = heads * QKH, heads * VH
    me, inner = lax.axis_index("dp"), lax.axis_index("fsdp")
    small, large = ln1_gain.shape[0], group_gain.shape[0]

    count = GROUP * rows
    vectors = jnp.stack([ln1_gain, ln1_bias, ln2_gain, ln2_bias]).astype(F32)
    pack = jnp.zeros((8, 128), F32)
    pack = lax.dynamic_update_slice(pack, vectors, (0, lax.rem(inner * small, 128)))
    pack = lax.dynamic_update_slice(pack, group_gain.astype(F32)[None], (4, lax.rem(inner * large, 128)))
    rates = jnp.log1p(-(2.0 ** (-5.0 - (me * heads + jnp.arange(heads)).astype(F32))))
    rates = jnp.broadcast_to(rates[:, None, None], (heads, 1, rows))
    entries = jnp.stack([seq_lens, seq_owner, seq_offset])
    (
        full_in, full_up, full_out, full_down, _, turned, query, keys, values, gate, mixed, gated, active, d_upper,
        g_down, hidden, two,
        own_seed, cosine, sine, growth, shrink, powers, ident_col, ident_row, gains, gain_group,
    ) = forward(
        total, w_in, w_up, w_out, w_down, tokens, cotangent, pack, rates, entries[:, :, None], entries[:, None, :]
    )
    tables = (cosine, sine, growth, shrink)
    full_up = full_up.reshape(width, -1)
    full_out = full_out.reshape(-1, width)
    full_down = full_down.reshape(-1, width)
    two = two.reshape(count, width)
    grad_down, grad_up, grad_out, d_hidden, _, sums_two, d_group, d_project = backward(
        total, g_down.reshape(-1, width), two, d_upper, full_up, own_seed, hidden, gains, gated, full_out, query,
        keys, values, gate, mixed, tables, powers, ident_col, ident_row, gain_group,
    )
    grad_in, output, d_tokens, vec_one, vec_two = final(
        total, d_project, full_in, turned, active, full_down, hidden, d_hidden, tokens, gains, ident_col, sums_two,
        d_group,
    )
    grads = lax.dynamic_slice(vec_one, (0, lax.rem(inner * small, 128)), (4, small))
    grad_group = lax.dynamic_slice(vec_two, (0, lax.rem(inner * large, 128)), (1, large))[0]
    return (
        output,
        d_tokens,
        grad_in,
        grad_out,
        grad_up,
        grad_down,
        grads[0],
        grads[1],
        grad_group,
        grads[2],
        grads[3],
    )


def solution(mesh):
    flat = ("dp", "fsdp")
    matrix, vector = P(flat, None), P(flat)
    return jax.shard_map(
        functools.partial(local, mesh.shape["fsdp"]),
        mesh=mesh,
        in_specs=(matrix,) * 6 + (vector,) * 5 + (P(),) * 3,
        out_specs=(matrix,) * 6 + (vector,) * 5,
        check_vma=False,
    )
```

```python
import functools

import jax
import jax.numpy as jnp
import numpy as np
from jax import lax
from jax.experimental import pallas as pl
from jax.experimental.pallas import tpu as pltpu
from jax.sharding import PartitionSpec as P

HEADS = 8
QKH = 256
VH = 512
EPSILON = 1e-05
GROUP_EPSILON = 0.1
GROUP = 4
MESH = pl.DeviceIdType.MESH
ANY = pl.ANY
BF16 = jnp.bfloat16
F32 = jnp.float32
MIB = 1 << 20


def ring_place(index, total):
    half = index // 2
    return jnp.where(index % 2 == 0, half, total - 1 - half)


def ring_index(place, total):
    place = lax.rem(place + 2 * total, total)
    return jnp.where(place < total // 2, 2 * place, 2 * (total - 1 - place) + 1)


def flip(group_index, relation):
    low, high = group_index % 2, group_index // 2
    if relation % 2:
        low = 1 - low
    if relation // 2:
        high = 1 - high
    return 2 * high + low


class Place:
    def __init__(self, total):
        self.total = total
        self.group = lax.axis_index("dp")
        self.inner = lax.axis_index("fsdp")
        self.place = ring_place(self.inner, total)
        self.next = (
            ring_index(self.place + 1, total),
            ring_index(self.place - 1, total),
        )

    def peer(self, relation):
        return (flip(self.group, relation), self.inner)

    def neighbour(self, way):
        return (self.group, self.next[way])

    def behind(self, way, steps):
        return ring_index(self.place - steps if way == 0 else self.place + steps, self.total)


def greet(devices):
    barrier = pltpu.get_barrier_semaphore()
    for device in devices:
        pl.semaphore_signal(barrier, inc=1, device_id=device, device_id_type=MESH)
    pl.semaphore_wait(barrier, len(devices))


def remote(src, dst, send_sem, recv_sem, device):
    return pltpu.make_async_remote_copy(
        src_ref=src,
        dst_ref=dst,
        send_sem=send_sem,
        recv_sem=recv_sem,
        device_id=device,
        device_id_type=MESH,
    )


def column_pieces():
    heads = HEADS // GROUP
    table = []
    base, off = 0, 0
    for size in (QKH, QKH, VH, VH):
        for h in range(heads):
            table.append((base + h * size, heads * size, h, off, size))
        base += HEADS * size
        off += size
    return table


def dot(left, right):
    return jnp.dot(left, right, preferred_element_type=F32)


def dot_rows(left, right):
    return lax.dot_general(left, right, (((0,), (0,)), ((), ())), preferred_element_type=F32)


def dot_back(left, right):
    return lax.dot_general(left, right, (((1,), (1,)), ((), ())), preferred_element_type=F32)


def norm_parts(values, epsilon):
    center = values - jnp.mean(values, axis=-1, keepdims=True)
    spread = jnp.mean(center * center, axis=-1, keepdims=True)
    scale = lax.rsqrt(spread + epsilon)
    return center * scale, scale


RELATIONS = ((2, 0), (3, 1))


class Passing:
    def __init__(self, at, way, own, place, sends, recvs):
        self.at, self.way, self.own, self.place = at, way, own, place
        self.sends, self.recvs = sends, recvs

    def hop(self, step, first=False):
        which = self.at.inner if first else self.at.behind(self.way, step)
        dst = self.place(which)
        return remote(
            self.own if first else dst, dst, self.sends.at[step], self.recvs.at[step],
            self.at.neighbour(self.way),
        )

    def begin(self):
        self.hop(0, True).start()

    def onward(self, step):
        self.hop(step - 1).wait_recv()
        self.hop(step).start()

    def finish(self):
        self.hop(self.at.total - 2).wait_recv()


def wait_sent(rings, total):
    def body(step, carry):
        for ring in rings:
            ring.hop(step).wait_send()
        return carry

    lax.fori_loop(0, total - 1, body, 0)


def tick_plan(total, places):
    steps = total - 2
    cuts = [1 + (steps * n) // places for n in range(places + 1)]
    return list(zip(cuts[:-1], cuts[1:]))


def run_steps(rings, start, stop):
    def body(step, carry):
        for ring in rings:
            ring.onward(step)
        return carry

    lax.fori_loop(start, stop, body, 0)


def weight_rings(at, w_out, w_down, full_up, full_out, full_down, sends, recvs):
    me = at.group
    half = w_out.shape[0] // 2
    side = w_out.shape[1] // 2

    def halves(own, full, slot):
        return [
            Passing(
                at, way,
                own.at[pl.ds(way * half, half), pl.ds(c * side, side)],
                lambda which, way=way, c=c: full.at[which, pl.ds(way * half, half), pl.ds(c * side, side)],
                sends.at[slot + 2 * c + way], recvs.at[slot + 2 * c + way],
            )
            for c in (0, 1)
            for way in (0, 1)
        ]

    ups = []
    for order in (0, 1):
        for way in (0, 1):
            relation = RELATIONS[way][order]
            slot = 8 + 2 * order + way
            ups.append(
                Passing(
                    at, way, full_up.at[flip(me, relation), at.inner],
                    lambda which, relation=relation: full_up.at[flip(me, relation), which],
                    sends.at[slot], recvs.at[slot],
                )
            )
    return halves(w_out, full_out, 0), ups, halves(w_down, full_down, 4)


def rotated(value, cosine, sine, scale):
    half = QKH // 2
    first, second = value[:, :half], value[:, half:]
    return jnp.concatenate(
        [(first * cosine - second * sine) * scale, (second * cosine + first * sine) * scale], axis=1
    )


def forward_kernel(
    total, w_in, w_up, w_out, w_down, h_tok, h_cot, pack, rates, seq_cols, seq_rows, curves,
    full_in, full_up, full_out, full_down, full_seed, o_turned, o_query, o_keys, o_values, o_gate, o_mixed,
    o_gated, o_active, o_upper, o_g_down, to_hidden, full_two, to_seed, to_cosine, to_sine, to_growth, to_shrink,
    to_powers, ident_col, ident_row, gains, gain_group,
    hidden, own_seed, cosine, sine, growth, shrink, powers, tok, cot,
    win, part, x, query, keys, values, gate, mixed, gated, wo, core_in, out_x, in_x, low, full_vec,
    win_up, wd, ring_send, ring_recv, own_sem, load_sem, fetch_sem, store_sem, row_send, row_recv, row_own,
    swap_send, swap_recv, swap_own, vec_send, vec_recv, early_sem,
):
    at = Place(total)
    me, inner = at.group, at.inner
    core, across = at.peer(1), at.peer(2)
    others = [(me, lax.rem(inner + n, total)) for n in range(1, total)]
    greet([core, across, at.peer(3)] + others)
    rows, width = tok.shape
    count = GROUP * rows
    heads = HEADS // GROUP
    r_in = w_in.shape[0]
    up_width = full_up.shape[-1]
    pieces = column_pieces()
    step_rows = 32

    def rows_in(group_index, which):
        return pl.ds(pl.multiple_of((group_index * total + which) * r_in, r_in), r_in)

    last = len(pieces)

    def swap(relation, slot):
        other = flip(me, relation)
        if slot < last:
            base, stride, h, off, size = pieces[slot]
            src = w_in.at[:, pl.ds(pl.multiple_of(base + other * stride, 128), size)]
            dst = win.at[h, rows_in(me, inner), pl.ds(off, size)]
        elif slot == last:
            src = w_up.at[:, pl.ds(pl.multiple_of(other * up_width, 128), up_width)]
            dst = full_up.at[me, inner]
        elif slot == last + 1:
            src, dst = pack, full_vec.at[inner, me]
        elif slot == last + 2:
            src, dst = h_tok, part.at[me]
        else:
            src, dst = own_seed, full_seed.at[me]
        if relation == 0:
            return pltpu.make_async_copy(src, dst, swap_own.at[slot])
        return remote(
            src, dst, swap_send.at[relation - 1, slot], swap_recv.at[relation - 1, slot], at.peer(relation)
        )

    def arrived(relation, slot):
        if relation == 0:
            swap(0, slot).wait()
        else:
            swap(relation, slot).wait_recv()

    def start_head(h):
        for relation in (0, 1, 2, 3):
            for slot in range(last):
                if pieces[slot][2] == h:
                    swap(relation, slot).start()

    start_head(0)

    fetch_cot = pltpu.make_async_copy(h_cot, cot, early_sem.at[0])
    fetch_tok = pltpu.make_async_copy(h_tok, tok, early_sem.at[1])
    early_stores = [
        pltpu.make_async_copy(src, dst, early_sem.at[2 + n])
        for n, (src, dst) in enumerate(
            (
                (own_seed, to_seed), (cosine, to_cosine), (sine, to_sine), (growth, to_growth),
                (shrink, to_shrink), (powers, to_powers), (hidden, to_hidden),
            )
        )
    ]

    def in_ring(h, relation):
        def place(which):
            return win.at[h, rows_in(flip(me, relation), which), :]

        slot = 12 + 4 * h + relation
        return Passing(at, relation % 2, place(inner), place, ring_send.at[slot], ring_recv.at[slot])

    ins = [[in_ring(h, relation) for relation in range(4)] for h in range(heads)]
    near, far_in = ins[0][:2], ins[0][2:]

    def await_head(h, relation):
        for slot in range(last):
            if pieces[slot][2] == h:
                arrived(relation, slot)

    for relation in (0, 1):
        await_head(0, relation)
        near[relation].begin()
    fetch_cot.start()
    fetch_tok.start()
    for relation in (2, 3, 1, 0):
        swap(relation, last + 1).start()
    for slot in (last + 2, last):
        for relation in (2, 3, 1, 0):
            swap(relation, slot).start()
    for h in range(1, heads):
        start_head(h)

    def layout_of(b, down):
        shape = (rows, 1) if down else (1, rows)
        source = seq_rows if down else seq_cols
        lens, owner, offset = source[0], source[1], source[2]
        positions = lax.broadcasted_iota(jnp.int32, shape, 0 if down else 1)
        inside = (
            (owner == b * total + inner)
            & (lens > 0)
            & (positions >= offset)
            & (positions < offset + lens)
        )
        axis = 1 if down else 0
        number = lax.broadcasted_iota(jnp.int32, lens.shape, axis).astype(F32) + 1.0
        ident = jnp.sum(jnp.where(inside, number, 0.0), axis=axis, keepdims=True) - 1.0
        starts = jnp.sum(jnp.where(inside, offset.astype(F32), 0.0), axis=axis, keepdims=True)
        places = jnp.where(ident >= 0.0, positions.astype(F32) - starts, 0.0)
        return ident, places

    for b in range(GROUP):
        ident_col[b] = layout_of(b, True)[0]
        ident_row[b] = layout_of(b, False)[0]

    def seed_rows(n, carry):
        s = pl.ds(pl.multiple_of(n * step_rows, step_rows), step_rows)
        valid = jnp.where(ident_col[me, s, :] >= 0.0, 1.0, 0.0)
        own_seed[s, :] = (cot[s, :].astype(F32) * valid).astype(BF16)
        return carry

    fetch_cot.wait()
    lax.fori_loop(0, rows // step_rows, seed_rows, 0)
    early_stores[0].start()

    for relation in range(4):
        arrived(relation, last + 1)

    def spread(n):
        target = lax.rem(inner + n, total)
        return remote(
            full_vec.at[inner], full_vec.at[inner], vec_send.at[n - 1], vec_recv.at[n - 1], (me, target)
        )

    for n in range(1, total):
        spread(n).start()
    for ring in near:
        ring.onward(1)
    for relation in (2, 3):
        await_head(0, relation)
        far_in[relation - 2].begin()
    for relation in (1, 0, 2, 3):
        swap(relation, last + 3).start()

    def both_in(step, carry):
        for ring in near:
            ring.onward(step)
        for ring in far_in:
            ring.onward(step - 1)
        return carry

    def take_vectors():
        for n in range(1, total):
            spread(n).wait_recv()
        quarter = width // GROUP
        small = quarter // total
        large = heads * VH // total
        for d in range(GROUP):
            tiles = {}
            for f in range(total):
                t = f * small // 128
                value = full_vec[f, d]
                tiles[t] = tiles[t] + value if t in tiles else value
            for t, value in tiles.items():
                gains[:, d * quarter + t * 128 : d * quarter + (t + 1) * 128] = value
        tiles = {}
        for f in range(total):
            t = f * large // 128
            value = full_vec[f, me, 4:5, :]
            tiles[t] = tiles[t] + value if t in tiles else value
        for t, value in tiles.items():
            h, off = t * 128 // VH, t * 128 % VH
            gain_group[h, :, off : off + 128] = value

    def make_tables():
        distance = lax.broadcasted_iota(jnp.int32, (rows, rows), 0) - lax.broadcasted_iota(
            jnp.int32, (rows, rows), 1
        )
        away = jnp.maximum(distance, 0).astype(F32)
        for h in range(heads):
            powers[h] = jnp.where(distance >= 0, jnp.exp(rates[h] * away), 0.0)
        for b in range(GROUP):
            places = layout_of(b, True)[1]
            angles = places * curves[0:1, :]
            r = slice(b * rows, (b + 1) * rows)
            cosine[r, :] = jnp.cos(angles)
            sine[r, :] = jnp.sin(angles)
            lift = places * (1.0 / 512.0) * curves[1:2, :]
            growth[r, :] = jnp.exp(lift)
            shrink[r, :] = jnp.exp(-lift)
        for store_one in early_stores[1:6]:
            store_one.start()

    def norm_buffer(relation):
        b = flip(me, relation)
        arrived(relation, last + 2)

        def norm_rows(n, carry):
            r = pl.multiple_of(n * step_rows, step_rows)
            normal, _ = norm_parts(part[b, pl.ds(r, step_rows), :].astype(F32), EPSILON)
            at_rows = pl.ds(pl.multiple_of(b * rows + r, step_rows), step_rows)
            x[at_rows, :] = (normal * gains[0:1, :] + gains[1:2, :]).astype(BF16)
            return carry

        lax.fori_loop(0, rows // step_rows, norm_rows, 0)

    beside = [
        make_tables,
        take_vectors,
        lambda: (norm_buffer(0), norm_buffer(1)),
        lambda: norm_buffer(2),
        lambda: norm_buffer(3),
    ]
    cuts = [2 + (total - 3) * n // 5 for n in range(6)]
    for n in range(5):
        lax.fori_loop(cuts[n], cuts[n + 1], both_in, 0)
        beside[n]()
    for ring in far_in:
        ring.onward(total - 2)
    for h in range(1, heads):
        for relation in range(4):
            await_head(h, relation)
            ins[h][relation].begin()
    outs, ups, downs = weight_rings(
        at, w_out, w_down, full_up, full_out, wd, ring_send, ring_recv
    )
    own_copies = [
        pltpu.make_async_copy(w_out, full_out.at[inner], own_sem.at[0]),
        pltpu.make_async_copy(w_down, wd.at[inner], own_sem.at[1]),
    ]
    for copy in own_copies:
        copy.start()
    plan = tick_plan(total, 6)
    tile = 512

    def project(h, off, m):
        r = pl.ds(pl.multiple_of(m * tile, tile), tile)
        return r, dot(x[r, :], win[h, :, off : off + QKH])

    def turn_tile(h, m):
        r, value = project(h, 0, m)
        turned = rotated(value, cosine[r, :], sine[r, :], growth[r, :])
        query[h, r, :] = (turned * QKH ** (-0.5)).astype(BF16)
        r, value = project(h, QKH, m)
        keys[h, r, :] = rotated(value, cosine[r, :], sine[r, :], shrink[r, :]).astype(BF16)

    def plain_tile(h, c, m):
        off = c * QKH
        r, value = project(h, 2 * QKH + off, m)
        values[h, r, off : off + QKH] = value.astype(BF16)
        r, value = project(h, 2 * QKH + VH + off, m)
        gate[h, r, off : off + QKH] = value

    def retain(h, b):
        r = pl.ds(pl.multiple_of(b * rows, rows), rows)
        raw = dot_back(query[h, r, :], keys[h, r, :])
        linked = (ident_col[b] == ident_row[b]) & (ident_col[b] >= 0.0)
        masked = (raw * jnp.where(linked, powers[h], 0.0)).astype(BF16)
        mixed[h, r, :] = dot(masked, values[h, r, :])

        def some_rows(n, carry):
            s = pl.ds(pl.multiple_of(b * rows + n * step_rows, step_rows), step_rows)
            normal, _ = norm_parts(mixed[h, s, :], GROUP_EPSILON)
            z = gate[h, s, :]
            result = z / (1.0 + jnp.exp(-z)) * (normal * gain_group[h])
            gated[s, h * VH : (h + 1) * VH] = result.astype(BF16)
            return carry

        lax.fori_loop(0, rows // step_rows, some_rows, 0)

    def looped(count_of, body):
        def some(n, carry):
            body(n)
            return carry

        lax.fori_loop(0, count_of, some, 0)

    def head_units(h):
        return [
            lambda: looped(count // tile, lambda m: turn_tile(h, m)),
            lambda: looped(count // tile, lambda m: plain_tile(h, 0, m)),
            lambda: looped(count // tile, lambda m: plain_tile(h, 1, m)),
            lambda: looped(2, lambda b: retain(h, b)),
            lambda: looped(2, lambda b: retain(h, 2 + b)),
        ]

    stores = []

    def store_head(h):
        for n, (src, dst) in enumerate(
            ((win, full_in), (query, o_query), (keys, o_keys), (values, o_values), (gate, o_gate), (mixed, o_mixed))
        ):
            copy = pltpu.make_async_copy(src.at[h], dst.at[h], store_sem.at[h, n])
            copy.start()
            stores.append(copy)

    for h in range(heads):
        ring_set = ins[h + 1] if h + 1 < heads else outs
        if h + 1 == heads:
            for ring in outs:
                ring.begin()
        for ring in ins[h]:
            ring.finish()
        units = head_units(h)
        for number in range(6):
            if number < len(units):
                units[number]()
            run_steps(ring_set, *plan[number])
        store_head(h)
    for relation in range(4):
        arrived(relation, last)
    for ring in ups:
        ring.begin()
    for ring in outs:
        ring.finish()
    stores.append(pltpu.make_async_copy(gated, o_gated, store_sem.at[0, 6]))
    stores[-1].start()
    own_copies[0].wait()
    block = w_out.shape[0]
    fetch = pltpu.make_async_copy(full_out, wo, load_sem.at[0])
    fetch.start()
    fetch.wait()

    chunks = 4
    size = rows // chunks

    def branch(relation):
        b = flip(me, relation)

        def column(n, carry):
            wide = 512
            c = pl.ds(pl.multiple_of(n * wide, wide), wide)
            r = pl.ds(pl.multiple_of(b * rows, rows), rows)
            acc = jnp.zeros((rows, wide), F32)
            piece = gated[r, :]
            acc = dot(piece, wo[:, :, c].reshape(total * block, wide))
            part[b, :, c] = acc.astype(BF16)
            return carry

        lax.fori_loop(0, width // 512, column, 0)

    def rows_of(c):
        return pl.ds(c * size, size)

    far = flip(me, 2)

    def copy(kind, c):
        r = rows_of(c)
        if kind == 0:
            src, dst, dev = part.at[flip(me, 3), r], core_in.at[0, r], core
        elif kind == 1:
            src, dst, dev = part.at[flip(me, 1), r], core_in.at[1, r], core
        elif kind == 2:
            src, dst, dev = out_x.at[r], in_x.at[r], across
        elif kind == 3:
            src, dst, dev = low.at[r], full_two.at[me, r], across
        elif kind == 4:
            src, dst, dev = low.at[r], full_two.at[me, r], core
        else:
            src, dst, dev = full_two.at[far, r], full_two.at[far, r], core
        return remote(src, dst, row_send.at[kind, c], row_recv.at[kind, c], dev)

    def store(c):
        r = rows_of(c)
        return pltpu.make_async_copy(low.at[r], full_two.at[me, r], row_own.at[c])

    branch(3)
    for c in range(chunks):
        copy(0, c).start()
    branch(2)
    run_steps(ups, *plan[0])
    for c in range(chunks):
        r = rows_of(c)
        copy(0, c).wait_recv()
        out_x[r, :] = (part[far, r, :].astype(F32) + core_in[0, r, :].astype(F32)).astype(BF16)
        copy(2, c).start()
    branch(1)
    for c in range(chunks):
        copy(1, c).start()
    branch(0)
    run_steps(ups, *plan[1])
    for copy_out in stores:
        copy_out.wait()
    fetch_tok.wait()
    wait_sent([ring for rings in ins for ring in rings], total)

    def turn(n, carry):
        i, j = n // (count // 256), lax.rem(n, count // 256)
        i, j = (pl.ds(pl.multiple_of(k * 256, 256), 256) for k in (i, j))
        win[0, i, j] = x[j, i].T
        return carry

    blocks = (width // 256) * (count // 256)
    lax.fori_loop(0, blocks // 2, turn, 0)
    run_steps(ups, *plan[2])
    for c in range(chunks):
        r = rows_of(c)
        copy(1, c).wait_recv()
        copy(2, c).wait_recv()

        def finish_rows(n, carry, c=c):
            s = pl.ds(pl.multiple_of(c * size + n * step_rows, step_rows), step_rows)
            value = tok[s, :].astype(F32) + (
                part[me, s, :].astype(F32) + core_in[1, s, :].astype(F32) + in_x[s, :].astype(F32)
            )
            hidden[s, :] = value
            normal, _ = norm_parts(value, EPSILON)
            low[s, :] = (normal * gains[2:3, :] + gains[3:4, :]).astype(BF16)
            return carry

        lax.fori_loop(0, size // step_rows, finish_rows, 0)
        copy(3, c).start()
        copy(4, c).start()
        store(c).start()
        if c:
            run_steps(ups, *plan[2 + c])
    early_stores[6].start()
    for ring in downs:
        ring.begin()
    lax.fori_loop(blocks // 2, blocks, turn, 0)
    store_turned = pltpu.make_async_copy(win.at[0, :, pl.ds(0, count)], o_turned, own_sem.at[0])
    store_turned.start()
    for relation in range(4):
        arrived(relation, last + 3)
    fetch_seed = [
        pltpu.make_async_copy(full_seed.at[b], x.at[pl.ds(b * rows, rows)], fetch_sem.at[b])
        for b in range(GROUP)
    ]
    for fetch in fetch_seed:
        fetch.start()
    for ring in ups:
        ring.finish()
    fetch_up = [
        pltpu.make_async_copy(full_up.at[b], win_up.at[b], fetch_sem.at[GROUP + b]) for b in range(GROUP)
    ]
    for fetch in fetch_up:
        fetch.start()
    for c in range(chunks):
        copy(3, c).wait_recv()
        copy(5, c).start()
        if c % 2:
            run_steps(downs, *plan[c // 2])
    for c in range(chunks):
        copy(4, c).wait_recv()
        copy(5, c).wait_recv()
        store(c).wait()
        for kind in range(6):
            copy(kind, c).wait_send()
    fetch_two = pltpu.make_async_copy(full_two, part, load_sem.at[1])
    fetch_two.start()
    for fetch in fetch_seed + fetch_up:
        fetch.wait()
    fetch_two.wait()

    quarters = heads * VH // 256

    def upper_tile(n, carry):
        b, j = n // quarters, lax.rem(n, quarters)
        c = pl.ds(pl.multiple_of(j * 256, 256), 256)
        r = pl.ds(pl.multiple_of(b * rows, rows), rows)
        upper = dot(part[b], win_up[:, :, :, c].reshape(width, 256))
        cdf = 0.5 * (1.0 + lax.erf(upper * (0.5**0.5)))
        gated[r, c] = (upper * cdf).astype(BF16)
        half = pl.ds(pl.multiple_of(lax.rem(j, 2) * 256, 256), 256)
        gate[j // 2, r, half] = cdf + upper * jnp.exp(-0.5 * upper * upper) * (2.0 * np.pi) ** -0.5
        return carry

    tiles = GROUP * quarters
    lax.fori_loop(0, tiles // 2, upper_tile, 0)
    run_steps(downs, *plan[2])
    lax.fori_loop(tiles // 2, tiles, upper_tile, 0)
    run_steps(downs, *plan[3])
    store_active = pltpu.make_async_copy(gated, o_active, store_sem.at[0, 0])
    store_active.start()
    per_tile = 256 // block
    wide = 512

    def down_tile(n, carry):
        i, j = n // (width // wide), lax.rem(n, width // wide)
        a = pl.ds(pl.multiple_of(i * 256, 256), 256)
        c = pl.ds(pl.multiple_of(j * wide, wide), wide)
        value = dot_rows(gated[:, a], x[:, c]).astype(BF16)
        wo[pl.ds(i * per_tile, per_tile), :, c] = value.reshape(per_tile, block, wide)
        return carry

    tiles = quarters * (width // wide)
    lax.fori_loop(0, tiles // 2, down_tile, 0)
    run_steps(downs, *plan[4])
    lax.fori_loop(tiles // 2, tiles, down_tile, 0)
    run_steps(downs, *plan[5])
    store_down = pltpu.make_async_copy(wo, o_g_down, store_sem.at[0, 1])
    store_down.start()
    own_copies[1].wait()
    for ring in downs:
        ring.finish()
    store_full = pltpu.make_async_copy(wd, full_down, load_sem.at[0])
    store_full.start()

    def d_upper_tile(n, carry):
        h, j = n // 4, lax.rem(n, 4)
        m, side = j // 2, lax.rem(j, 2)
        r = pl.ds(pl.multiple_of(m * tile, tile), tile)
        c = pl.ds(pl.multiple_of(side * 256, 256), 256)
        piece = wd[pl.ds((2 * h + side) * per_tile, per_tile)].reshape(256, width)
        values[h, r, c] = (dot_back(x[r, :], piece) * gate[h, r, c]).astype(BF16)
        return carry

    last_stores = [store_active, store_down, store_full]
    for h in range(heads):
        lax.fori_loop(4 * h, 4 * (h + 1), d_upper_tile, 0)
        last_stores.append(
            pltpu.make_async_copy(values.at[h], o_upper.at[:, pl.ds(h * VH, VH)], store_sem.at[0, 2 + h])
        )
        last_stores[-1].start()
    wait_sent(outs + downs + ups, total)
    for relation in (1, 2, 3):
        for slot in range(last + 4):
            swap(relation, slot).wait_send()
    for n in range(1, total):
        spread(n).wait_send()
    store_turned.wait()
    for copy_out in last_stores + early_stores:
        copy_out.wait()


def forward(total, w_in, w_up, w_out, w_down, tok, cot, pack, rates, seq_cols, seq_rows):
    rows, width = tok.shape
    count = GROUP * rows
    heads = HEADS // GROUP
    head_width = 2 * (QKH + VH)
    vmem, hbm = pl.BlockSpec(memory_space=pltpu.VMEM), pl.BlockSpec(memory_space=ANY)
    dma = pltpu.SemaphoreType.DMA
    pair = np.arange(QKH // 2) / (QKH // 2)
    curves = np.zeros((8, QKH // 2), np.float32)
    curves[0] = 10000.0**-pair
    curves[1] = np.log((pair + 0.4) / 1.4)
    kept = (
        ((heads, count, QKH), BF16),
        ((heads, count, QKH), BF16),
        ((heads, count, VH), BF16),
        ((heads, count, VH), F32),
        ((heads, count, VH), F32),
        ((count, heads * VH), BF16),
    )
    in_hbm = (
        ((heads, width, head_width), BF16),
        ((GROUP, total, w_up.shape[0], w_up.shape[1] // GROUP), BF16),
        ((total,) + w_out.shape, BF16),
        ((total,) + w_down.shape, BF16),
        ((GROUP, rows, width), BF16),
        ((width, count), BF16),
        *kept,
        kept[-1],
        kept[-1],
        ((total,) + w_out.shape, BF16),
    )
    in_vmem = (
        ((rows, width), BF16),
        ((count, QKH // 2), F32),
        ((count, QKH // 2), F32),
        ((count, QKH // 2), F32),
        ((count, QKH // 2), F32),
        ((heads, rows, rows), F32),
        ((GROUP, rows, 1), F32),
        ((GROUP, 1, rows), F32),
        ((8, width), F32),
        ((heads, 1, VH), F32),
    )
    shapes = (*in_hbm, ((rows, width), F32), ((GROUP, rows, width), BF16), *in_vmem)
    return pl.pallas_call(
        functools.partial(forward_kernel, total),
        out_shape=[jax.ShapeDtypeStruct(s, d) for s, d in shapes],
        in_specs=[hbm] * 6 + [vmem] * 5,
        out_specs=[hbm] * (len(in_hbm) + 8) + [vmem] * 4,
        scratch_shapes=[
            pltpu.VMEM((rows, width), F32),
            *[pltpu.VMEM(s, d) for s, d in in_vmem[:6]],
            pltpu.VMEM((rows, width), BF16),
            pltpu.VMEM((rows, width), BF16),
            pltpu.VMEM((heads, width, head_width), BF16),
            pltpu.VMEM((GROUP, rows, width), BF16),
            pltpu.VMEM((count, width), BF16),
            *[pltpu.VMEM(s, d) for s, d in kept],
            pltpu.VMEM((total,) + w_out.shape, BF16),
            pltpu.VMEM((2, rows, width), BF16),
            pltpu.VMEM((rows, width), BF16),
            pltpu.VMEM((rows, width), BF16),
            pltpu.VMEM((rows, width), BF16),
            pltpu.VMEM((total, GROUP, 8, 128), F32),
            pltpu.VMEM((GROUP, total, w_up.shape[0], w_up.shape[1] // GROUP), BF16),
            pltpu.VMEM((total,) + w_down.shape, BF16),
            dma((20, total - 1)), dma((20, total - 1)), dma((2,)), dma((2,)), dma((2 * GROUP,)),
            dma((heads, 7)), dma((6, 4)), dma((6, 4)), dma((4,)),
            dma((3, 12)), dma((3, 12)), dma((12,)), dma((total - 1,)), dma((total - 1,)), dma((9,)),
        ],
        compiler_params=pltpu.CompilerParams(
            collective_id=1, has_side_effects=True, vmem_limit_bytes=63 * MIB
        ),
        name="forward_retention",
    )(w_in, w_up, w_out, w_down, tok, cot, pack, rates, seq_cols, seq_rows, jnp.asarray(curves))


class Adding:
    def __init__(self, at, way, term, arrived, sends, recvs, origin=None):
        self.at, self.way, self.term, self.arrived = at, way, term, arrived
        self.origin = term if origin is None else origin
        self.sends, self.recvs = sends, recvs

    def hop(self, step, first=False):
        src = self.origin(self.at.behind(self.way, 1)) if first else self.arrived.at[step - 1]
        return remote(
            src, self.arrived.at[step], self.sends.at[step], self.recvs.at[step], self.at.neighbour(self.way)
        )

    def begin(self):
        self.hop(0, True).start()

    def sum_at(self, step, which):
        self.hop(step, True).wait_recv()
        return self.arrived[step].astype(F32) + self.term(which)[...].astype(F32)

    def onward(self, step):
        self.arrived[step - 1] = self.sum_at(step - 1, self.at.behind(self.way, step + 1)).astype(BF16)
        self.hop(step).start()

    def finish(self):
        return self.sum_at(self.at.total - 2, self.at.inner)


def wait_added(rings, total):
    def body(step, carry):
        for ring in rings:
            ring.hop(step, True).wait_send()
        return carry

    lax.fori_loop(0, total - 1, body, 0)


def backward_kernel(
    total, h_g_down, two, d_upper, h_up, h_seed, h_hidden, gains_all, h_gated, h_out, h_query, h_keys, h_values,
    h_gate, h_mixed, h_cosine, h_sine, h_growth, h_shrink, h_powers, ident_col, ident_row, gain_group,
    to_down, to_up, to_out, to_hidden, full_branch, sums, o_group, o_project,
    g_down, seed, hidden, cosine, sine, growth, shrink, powers, o_down, o_up, o_out, d_hidden, g_up, g_out, arrived, wide_buf, narrow_buf, wo, part, core_in, out_x, in_x, low,
    query, keys, values, gate, mixed, back, d_mixed, staged, stage, landed,
    ring_send, ring_recv, row_send, row_recv, row_own, load_sem, late_sem, unit_sem, out_sem, a2a_send, a2a_recv,
):
    at = Place(total)
    me = at.group
    core, across = at.peer(1), at.peer(2)
    greet([core, across, at.peer(3), at.neighbour(0), at.neighbour(1)])
    rows, width = seed.shape
    count = GROUP * rows
    heads = HEADS // GROUP
    r_up, r_out = o_up.shape[0], o_out.shape[0]
    up_width = o_up.shape[1] // GROUP
    half, side = r_out // 2, width // 2

    def halves(source, base, origin=None):
        def chunk_of(ref, way, c):
            return lambda which: ref.at[
                pl.ds(pl.multiple_of(which * r_out + way * half, half), half), pl.ds(c * side, side)
            ]

        return [
            Adding(
                at, way,
                chunk_of(source, way, c),
                arrived.at[base + 2 * c + way], ring_send.at[base + 2 * c + way], ring_recv.at[base + 2 * c + way],
                None if origin is None else chunk_of(origin, way, c),
            )
            for c in (0, 1)
            for way in (0, 1)
        ]

    downs, outs, ups = halves(g_down, 0, h_g_down), halves(g_out, 8), []
    for order in (0, 1):
        for way in (0, 1):
            relation = RELATIONS[way][order]
            slot = 4 + 2 * order + way
            ups.append(
                Adding(
                    at, way,
                    lambda which, relation=relation: g_up.at[
                        pl.ds(pl.multiple_of((flip(me, relation) * total + which) * r_up, r_up), r_up), :
                    ],
                    arrived.at[slot], ring_send.at[slot], ring_recv.at[slot],
                )
            )

    chunks = 4
    size = rows // chunks
    step_rows = 32
    far = flip(me, 2)

    def rows_of(c):
        return pl.ds(c * size, size)

    def copy(kind, c):
        r = rows_of(c)
        if kind == 0:
            src, dst, dev = part.at[flip(me, 3), r], core_in.at[0, r], core
        elif kind == 1:
            src, dst, dev = part.at[flip(me, 1), r], core_in.at[1, r], core
        elif kind == 2:
            src, dst, dev = out_x.at[r], in_x.at[r], across
        elif kind == 3:
            src, dst, dev = low.at[r], full_branch.at[me, r], across
        elif kind == 4:
            src, dst, dev = low.at[r], full_branch.at[me, r], core
        else:
            src, dst, dev = full_branch.at[far, r], full_branch.at[far, r], core
        return remote(src, dst, row_send.at[kind, c], row_recv.at[kind, c], dev)

    def store(c):
        r = rows_of(c)
        return pltpu.make_async_copy(low.at[r], full_branch.at[me, r], row_own.at[c])

    for ring in downs:
        ring.begin()
    upper_columns = pl.ds(0, up_width)
    fetch_upper = pltpu.make_async_copy(d_upper, g_out.at[:, upper_columns], load_sem.at[1])
    fetch_up = pltpu.make_async_copy(h_up, g_up, load_sem.at[7])
    fetch_two = pltpu.make_async_copy(two, wide_buf, load_sem.at[0])
    fetch_gated = pltpu.make_async_copy(h_gated, narrow_buf, load_sem.at[8])
    fetch_out = pltpu.make_async_copy(h_out, wo, load_sem.at[2])
    fetch_rows = [
        pltpu.make_async_copy(src, dst, late_sem.at[n])
        for n, (src, dst) in enumerate(((h_g_down, g_down), (h_seed, seed), (h_hidden, hidden)))
    ]
    fetch_tables = [
        pltpu.make_async_copy(src, dst, late_sem.at[3 + n])
        for n, (src, dst) in enumerate(
            ((h_cosine, cosine), (h_sine, sine), (h_growth, growth), (h_shrink, shrink), (h_powers, powers))
        )
    ]
    stores = [
        pltpu.make_async_copy(src, dst, late_sem.at[8 + n])
        for n, (src, dst) in enumerate(((o_down, to_down), (o_up, to_up), (o_out, to_out), (d_hidden, to_hidden)))
    ]
    for fetch in (fetch_upper, fetch_up, *fetch_rows, fetch_two, fetch_gated, fetch_out, *fetch_tables):
        fetch.start()

    def unit_loads(unit, slot):
        h, b = unit // GROUP, lax.rem(unit, GROUP)
        r = pl.ds(pl.multiple_of(b * rows, rows), rows)
        pairs = ((h_query, query), (h_keys, keys), (h_values, values), (h_gate, gate), (h_mixed, mixed))
        return [
            pltpu.make_async_copy(src.at[h, r], dst.at[slot], unit_sem.at[slot, n])
            for n, (src, dst) in enumerate(pairs)
        ]

    for unit in (0, 1):
        for fetch in unit_loads(jnp.int32(unit), unit):
            fetch.start()

    def send_sums(c):
        r = rows_of(c)
        copy(0, c).wait_recv()
        out_x[r, :] = (part[far, r, :].astype(F32) + core_in[0, r, :].astype(F32)).astype(BF16)
        copy(2, c).start()

    def norm_back(c):
        copy(1, c).wait_recv()
        copy(2, c).wait_recv()

        def some_rows(n, carry):
            s = pl.ds(pl.multiple_of(c * size + n * step_rows, step_rows), step_rows)
            e = part[me, s, :].astype(F32) + core_in[1, s, :].astype(F32) + in_x[s, :].astype(F32)
            normal, scale = norm_parts(hidden[s, :], EPSILON)
            with_gain = e * gains_all[2:3, :]
            sums[0:1, :] += jnp.sum(e * normal, axis=0, keepdims=True)
            sums[1:2, :] += jnp.sum(e, axis=0, keepdims=True)
            value = seed[s, :].astype(F32) + scale * (
                with_gain
                - jnp.mean(with_gain, axis=-1, keepdims=True)
                - normal * jnp.mean(with_gain * normal, axis=-1, keepdims=True)
            )
            d_hidden[s, :] = value
            low[s, :] = value.astype(BF16)
            return carry

        lax.fori_loop(0, size // step_rows, some_rows, 0)
        copy(3, c).start()
        copy(4, c).start()
        store(c).start()

    sums[...] = jnp.zeros_like(sums)
    o_group[...] = jnp.zeros_like(o_group)
    def d_two(relation):
        b = flip(me, relation)
        r = pl.ds(pl.multiple_of(b * rows, rows), rows)

        def column(n, carry):
            c = pl.ds(pl.multiple_of(n * 256, 256), 256)
            part[b, :, c] = dot_back(g_out[r, :up_width], g_up[c, :]).astype(BF16)
            return carry

        lax.fori_loop(0, width // 256, column, 0)

    plan = tick_plan(total, 6)
    fetch_upper.wait()
    fetch_up.wait()
    d_two(3)
    for c in range(chunks):
        copy(0, c).start()
    d_two(2)
    for c in range(chunks):
        send_sums(c)
    for fetch in fetch_rows:
        fetch.wait()
    add_steps(downs, *plan[0])
    d_two(1)
    for c in range(chunks):
        copy(1, c).start()
    d_two(0)
    fetch_two.wait()

    def grad_tiles(left, right, span, out, start, stop):
        wide = 512

        def tile(n, carry):
            rows_n = span // wide
            i, j = n // rows_n, lax.rem(n, rows_n)
            a = pl.ds(pl.multiple_of(i * 256, 256), 256)
            c = pl.ds(pl.multiple_of(j * wide, wide), wide)
            out[a, c] = dot_rows(left[:, a], right[:, c]).astype(BF16)
            return carry

        lax.fori_loop(start, stop, tile, 0)

    tiles = (width // 256) * (up_width // 512)
    for quarter in range(4):
        grad_tiles(wide_buf, g_out, up_width, g_up, tiles * quarter // 4, tiles * (quarter + 1) // 4)
        if quarter:
            norm_back(quarter - 1)
        add_steps(downs, *plan[1 + quarter])
    norm_back(3)
    add_steps(downs, *plan[5])
    for ring in ups:
        ring.begin()
    for n, ring in enumerate(downs):
        c, way = n // 2, n % 2
        o_down[pl.ds(way * half, half), pl.ds(c * side, side)] = ring.finish()
    stores[0].start()
    stores[3].start()
    for c in range(chunks):
        copy(3, c).wait_recv()
        copy(5, c).start()
        if c % 2:
            add_steps(ups, *plan[c // 2])
    for c in range(chunks):
        copy(4, c).wait_recv()
        copy(5, c).wait_recv()
        store(c).wait()
    branch = wide_buf
    fetch_branch = [
        pltpu.make_async_copy(full_branch.at[b], branch.at[pl.ds(b * rows, rows)], load_sem.at[3 + b])
        for b in range(GROUP)
    ]
    for fetch in fetch_branch:
        fetch.start()
    for fetch in fetch_branch:
        fetch.wait()
    fetch_gated.wait()
    fetch_out.wait()
    tiles = (narrow_buf.shape[1] // 256) * (width // 512)
    for part_of in range(2):
        grad_tiles(narrow_buf, branch, width, g_out, tiles * part_of // 2, tiles * (part_of + 1) // 2)
        add_steps(ups, *plan[2 + part_of])
    for fetch in fetch_tables:
        fetch.wait()

    units = heads * GROUP

    def unit_stores(unit, slot):
        h, b = unit // GROUP, lax.rem(unit, GROUP)
        r = pl.ds(pl.multiple_of(b * rows, rows), rows)
        start = pl.multiple_of(h * staged.shape[2], 128)
        return pltpu.make_async_copy(
            staged.at[slot], o_project.at[r, pl.ds(start, staged.shape[2])], out_sem.at[slot]
        )

    def unrotated(value, r, scale):
        mid = QKH // 2
        first, second = value[:, :mid], value[:, mid:]
        c, s = cosine[r, :], sine[r, :]
        return jnp.concatenate(
            [(first * c + second * s) * scale, (second * c - first * s) * scale], axis=1
        )

    def unit_body(unit):
        slot = lax.rem(unit, 2)
        h, b = unit // GROUP, lax.rem(unit, GROUP)
        r = pl.ds(pl.multiple_of(b * rows, rows), rows)
        back[...] = dot_back(branch[r, :], wo[pl.ds(pl.multiple_of(h * VH, VH), VH), :])
        for fetch in unit_loads(unit, slot):
            fetch.wait()

        @pl.when(unit >= 2)
        def _():
            unit_stores(unit - 2, slot).wait()

        gains = gain_group[h]

        def some_rows(n, carry):
            s = pl.ds(pl.multiple_of(n * step_rows, step_rows), step_rows)
            normal, scale = norm_parts(mixed[slot, s, :], GROUP_EPSILON)
            z = gate[slot, s, :]
            f = back[s, :]
            sigmoid = 1.0 / (1.0 + jnp.exp(-z))
            silu = z * sigmoid
            d_silu = f * (normal * gains)
            staged[slot, s, 2 * QKH + VH :] = (d_silu * (sigmoid + silu * (1.0 - sigmoid))).astype(BF16)
            d_scaled = f * silu
            o_group[h] += jnp.sum(d_scaled * normal, axis=0, keepdims=True)
            d_normal = d_scaled * gains
            d_mixed[s, :] = (
                scale
                * (
                    d_normal
                    - jnp.mean(d_normal, axis=-1, keepdims=True)
                    - normal * jnp.mean(d_normal * normal, axis=-1, keepdims=True)
                )
            ).astype(BF16)
            return carry

        lax.fori_loop(0, rows // step_rows, some_rows, 0)
        linked = (ident_col[b] == ident_row[b]) & (ident_col[b] >= 0.0)
        decay = jnp.where(linked, powers[h], 0.0)
        masked = (dot_back(query[slot], keys[slot]) * decay).astype(BF16)
        staged[slot, :, 2 * QKH : 2 * QKH + VH] = dot_rows(masked, d_mixed[...]).astype(BF16)
        d_raw = (dot_back(d_mixed[...], values[slot]) * decay).astype(BF16)
        d_query = dot(d_raw, keys[slot]) * QKH ** (-0.5)
        staged[slot, :, :QKH] = unrotated(d_query, r, growth[r, :]).astype(BF16)
        d_keys = dot_rows(d_raw, query[slot])
        staged[slot, :, QKH : 2 * QKH] = unrotated(d_keys, r, shrink[r, :]).astype(BF16)
        unit_stores(unit, slot).start()

        @pl.when(unit + 2 < units)
        def _():
            for fetch in unit_loads(unit + 2, slot):
                fetch.start()

    early = 2

    def with_ups(unit, carry):
        unit_body(unit)
        (low_a, high_a), (low_b, high_b) = plan[4], plan[5]
        add_steps(ups, low_a + unit * (low_b - low_a), high_a + unit * (high_b - high_a))
        return carry

    def with_outs(unit, carry):
        unit_body(unit)
        steps, number = total - 2, unit - early
        add_steps(outs, 1 + (steps * number) // (units - early), 1 + (steps * (number + 1)) // (units - early))
        return carry

    lax.fori_loop(0, early, with_ups, 0)
    for ring in outs:
        ring.begin()

    def sent_across(relation):
        return remote(
            stage.at[relation - 1], landed.at[relation - 1],
            a2a_send.at[relation - 1], a2a_recv.at[relation - 1], at.peer(relation),
        )

    for n, ring in enumerate(ups):
        relation = RELATIONS[n % 2][n // 2]
        value = ring.finish()
        if relation == 0:
            o_up[:, pl.ds(pl.multiple_of(me * up_width, 128), up_width)] = value
        else:
            stage[relation - 1] = value.astype(BF16)
            sent_across(relation).start()
    lax.fori_loop(early, units, with_outs, 0)
    for relation in (1, 2, 3):
        sent_across(relation).wait_recv()
        o_up[:, pl.ds(pl.multiple_of(flip(me, relation) * up_width, 128), up_width)] = landed[
            relation - 1
        ].astype(F32)
        sent_across(relation).wait_send()
    stores[1].start()
    for slot in (0, 1):
        unit_stores(jnp.int32(units - 2 + slot), slot).wait()
    for n, ring in enumerate(outs):
        c, way = n // 2, n % 2
        o_out[pl.ds(way * half, half), pl.ds(c * side, side)] = ring.finish()
    stores[2].start()
    for c in range(chunks):
        for kind in range(6):
            copy(kind, c).wait_send()
    wait_added(downs + ups + outs, total)
    for store_one in stores:
        store_one.wait()


def add_steps(rings, start, stop):
    def body(step, carry):
        for ring in rings:
            ring.onward(step)
        return carry

    lax.fori_loop(start, stop, body, 0)


def backward(
    total, g_down, two, d_upper, full_up, seed, hidden, gain_two, gated, full_out, query, keys, values, gate, mixed,
    tables, powers, ident_col, ident_row, gain_group,
):
    rows, width = seed.shape
    count = GROUP * rows
    heads = HEADS // GROUP
    up_width = d_upper.shape[1]
    r_out, r_up = g_down.shape[0] // total, width // GROUP // total
    half, side = r_out // 2, width // 2
    vmem, hbm = pl.BlockSpec(memory_space=pltpu.VMEM), pl.BlockSpec(memory_space=ANY)
    dma = pltpu.SemaphoreType.DMA
    shapes = (
        ((r_out, width), F32),
        ((r_up, up_width * GROUP), F32),
        ((r_out, width), F32),
        ((rows, width), F32),
        ((GROUP, rows, width), BF16),
        ((8, width), F32),
        ((heads, 1, VH), F32),
        ((count, 2 * heads * (QKH + VH)), BF16),
    )
    return pl.pallas_call(
        functools.partial(backward_kernel, total),
        out_shape=[jax.ShapeDtypeStruct(s, d) for s, d in shapes],
        in_specs=[hbm] * 6 + [vmem] + [hbm] * 12 + [vmem] * 3,
        out_specs=[hbm] * 5 + [vmem, vmem, hbm],
        scratch_shapes=[
            pltpu.VMEM(g_down.shape, BF16),
            pltpu.VMEM(seed.shape, BF16),
            pltpu.VMEM(hidden.shape, F32),
            *[pltpu.VMEM(v.shape, F32) for v in (*tables, powers)],
            *[pltpu.VMEM(s, d) for s, d in shapes[:4]],
            pltpu.VMEM((width, up_width), BF16),
            pltpu.VMEM(g_down.shape, BF16),
            pltpu.VMEM((12, total - 1, half, side), BF16),
            pltpu.VMEM((count, width), BF16),
            pltpu.VMEM((count, up_width), BF16),
            pltpu.VMEM(full_out.shape, BF16),
            pltpu.VMEM((GROUP, rows, width), BF16),
            pltpu.VMEM((2, rows, width), BF16),
            pltpu.VMEM((rows, width), BF16),
            pltpu.VMEM((rows, width), BF16),
            pltpu.VMEM((rows, width), BF16),
            pltpu.VMEM((2, rows, QKH), BF16),
            pltpu.VMEM((2, rows, QKH), BF16),
            pltpu.VMEM((2, rows, VH), BF16),
            pltpu.VMEM((2, rows, VH), F32),
            pltpu.VMEM((2, rows, VH), F32),
            pltpu.VMEM((rows, VH), F32),
            pltpu.VMEM((rows, VH), BF16),
            pltpu.VMEM((2, rows, 2 * (QKH + VH)), BF16),
            pltpu.VMEM((3, r_up, up_width), BF16),
            pltpu.VMEM((3, r_up, up_width), BF16),
            dma((12, total - 1)), dma((12, total - 1)), dma((6, 4)), dma((6, 4)), dma((4,)), dma((9,)), dma((12,)),
            dma((2, 5)), dma((2,)), dma((3,)), dma((3,)),
        ],
        compiler_params=pltpu.CompilerParams(
            collective_id=2, has_side_effects=True, vmem_limit_bytes=63 * MIB
        ),
        name="backward_retention",
    )(
        g_down, two, d_upper, full_up, seed, hidden, gain_two, gated, full_out, query, keys, values, gate, mixed,
        *tables, powers, ident_col, ident_row, gain_group,
    )


def final_kernel(
    total, h_project, h_in, h_turned, h_active, h_down, hidden, d_hidden, tok, gains_all, ident_col, sums_two, d_group,
    o_in, o_output, o_tokens, o_vec, o_grp,
    output, d_tokens, full_rows, project, turned, term, arrived, win, part, active, wd, rows_f32, core_in, out_x, in_x, stage, landed,
    vec, grp, near_in, mid, far_in, far_grp,
    load_sem, win_sem, ring_send, ring_recv, a2a_send, a2a_recv, row_send, row_recv, in_sem, piece_sem,
    near_send, near_recv, far_send, far_recv,
):
    at = Place(total)
    me, inner = at.group, at.inner
    others = [(me, lax.rem(inner + n, total)) for n in range(1, total)]
    greet([at.peer(r) for r in (1, 2, 3)] + others)
    rows, width = tok.shape
    count = GROUP * rows
    block = o_in.shape[0]
    step_rows = 32

    store_output = pltpu.make_async_copy(output, o_output, load_sem.at[6])
    store_tokens = pltpu.make_async_copy(d_tokens, o_tokens, load_sem.at[7])
    fetch_turned = pltpu.make_async_copy(h_turned, turned, load_sem.at[0])
    wide = 512
    fetch_project = [
        pltpu.make_async_copy(
            h_project.at[:, pl.ds(n * wide, wide)], project.at[:, pl.ds(n * wide, wide)], piece_sem.at[n]
        )
        for n in range(project.shape[1] // wide)
    ]
    fetch_turned.start()
    for fetch in fetch_project:
        fetch.start()

    def source(n, b):
        return part.at[pl.ds(pl.multiple_of(b * rows, rows), rows), :]

    def row_copy(kind, n):
        if kind < 2:
            return remote(
                source(n, flip(me, 3 - 2 * kind)), core_in.at[n, kind], row_send.at[n, kind], row_recv.at[n, kind],
                at.peer(1),
            )
        return remote(out_x.at[n], in_x.at[n], row_send.at[n, 2], row_recv.at[n, 2], at.peer(2))

    def own_rows(n, which, r):
        b = flip(me, 2) if which == 0 else me
        return part[pl.ds(pl.multiple_of(b * rows + r, step_rows), step_rows), :]

    def by_rows(body):
        def some(k, carry):
            body(pl.multiple_of(k * step_rows, step_rows))
            return carry

        lax.fori_loop(0, rows // step_rows, some, 0)

    def send_rows(n):
        row_copy(0, n).wait_recv()

        def some(r):
            s = pl.ds(r, step_rows)
            out_x[n, s, :] = (own_rows(n, 0, r).astype(F32) + core_in[n, 0, s, :].astype(F32)).astype(BF16)

        by_rows(some)
        row_copy(2, n).start()

    def hold_down():
        fetch_hidden.wait()
        row_copy(1, 0).wait_recv()

        def some(r):
            s = pl.ds(r, step_rows)
            rows_f32[s, :] += own_rows(0, 1, r).astype(F32) + core_in[0, 1, s, :].astype(F32)

        by_rows(some)
        row_copy(0, 0).wait_send()
        row_copy(1, 0).wait_send()

    def summed_rows(n, r):
        s = pl.ds(r, step_rows)
        return own_rows(n, 1, r).astype(F32) + core_in[n, 1, s, :].astype(F32) + in_x[n, s, :].astype(F32)

    def take_down():
        row_copy(2, 0).wait_recv()

        def some(r):
            s = pl.ds(r, step_rows)
            valid = jnp.where(ident_col[me, s, :] >= 0.0, 1.0, 0.0)
            output[s, :] = ((rows_f32[s, :] + in_x[0, s, :].astype(F32)) * valid).astype(BF16)

        by_rows(some)
        fetch_d_hidden.start()
        store_output.start()

    def take_rows():
        fetch_d_hidden.wait()
        row_copy(1, 1).wait_recv()
        row_copy(2, 1).wait_recv()
        vec[...] = jnp.zeros_like(vec)
        vec[2:4, :] = sums_two[0:2, :]

        def some(r):
            s = pl.ds(r, step_rows)
            e = summed_rows(1, r)
            normal, scale = norm_parts(tok[s, :].astype(F32), EPSILON)
            with_gain = e * gains_all[0:1, :]
            vec[0:1, :] += jnp.sum(e * normal, axis=0, keepdims=True)
            vec[1:2, :] += jnp.sum(e, axis=0, keepdims=True)
            value = rows_f32[s, :] + scale * (
                with_gain
                - jnp.mean(with_gain, axis=-1, keepdims=True)
                - normal * jnp.mean(with_gain * normal, axis=-1, keepdims=True)
            )
            d_tokens[s, :] = value.astype(BF16)

        by_rows(some)
        store_tokens.start()

    quarter = width // GROUP
    small = quarter // total
    large = grp.shape[1] // total

    def near(relation):
        start = pl.multiple_of(flip(me, relation) * quarter, 128)
        return remote(
            vec.at[:, pl.ds(start, quarter)], near_in.at[relation - 1], near_send.at[relation - 1],
            near_recv.at[relation - 1], at.peer(relation),
        )

    def tile_of(index, size):
        return pl.ds(pl.multiple_of((index * size) // 128 * 128, 128), 128)

    def distant(kind, n):
        target = lax.rem(inner + n, total)
        src = mid.at[:, tile_of(target, small)] if kind == 0 else grp.at[:, tile_of(target, large)]
        dst = far_in if kind == 0 else far_grp
        return remote(
            src, dst.at[n - 1], far_send.at[kind, n - 1], far_recv.at[kind, n - 1], (me, target)
        )

    def vectors_near():
        for relation in (1, 2, 3):
            near(relation).start()
        grp[...] = jnp.zeros_like(grp)
        for h in range(d_group.shape[0]):
            grp[0:1, h * VH : (h + 1) * VH] = d_group[h]

    def vectors_far():
        for relation in (1, 2, 3):
            near(relation).wait_recv()
        mid[...] = (
            vec[:, pl.ds(pl.multiple_of(me * quarter, 128), quarter)] + near_in[0] + near_in[1] + near_in[2]
        )
        for n in range(1, total):
            for kind in (0, 1):
                distant(kind, n).start()

    def vectors_end():
        for n in range(1, total):
            for kind in (0, 1):
                distant(kind, n).wait_recv()
        o_vec[...] = mid[:, tile_of(inner, small)] + jnp.sum(far_in[...], axis=0)
        o_grp[...] = grp[:, tile_of(inner, large)] + jnp.sum(far_grp[...], axis=0)


    def terms(step, far_at, near_at, arriving=False):
        left = jnp.concatenate(
            [
                turned[
                    pl.ds(
                        pl.multiple_of((flip(me, relation) * total + at.behind(way, step + 1)) * block, block), block
                    ),
                    :,
                ]
                for way in (0, 1)
                for relation in RELATIONS[way]
            ],
            axis=0,
        )

        def tile(n, carry):
            c = pl.ds(pl.multiple_of(n * wide, wide), wide)
            value = dot(left, project[:, c]).astype(BF16)
            for way in (0, 1):
                first = 2 * way * block
                term[far_at + way, :, c] = value[first : first + block]
                term[near_at + way, :, c] = value[first + block : first + 2 * block]
            return carry

        if arriving:
            for n, fetch in enumerate(fetch_project):
                fetch.wait()
                tile(n, 0)
        else:
            lax.fori_loop(0, project.shape[1] // wide, tile, 0)

    far_slots, near_slots = (0, 2), (1, 3)

    def near_place(step):
        return 6 + 2 * lax.rem(step, 2)

    def hop(slot, step, first=False):
        src = term.at[2 * (slot % 2) + slot // 2] if first else arrived.at[slot, step - 1]
        return remote(
            src, arrived.at[slot, step], ring_send.at[slot, step], ring_recv.at[slot, step],
            at.neighbour(slot // 2),
        )

    def sum_into(out, slot, step, base):
        hop(slot, step, True).wait_recv()

        def some(n, carry):
            c = pl.ds(pl.multiple_of(n * wide, wide), wide)
            value = arrived[slot, step, :, c].astype(F32) + term[base + slot // 2, :, c].astype(F32)
            out[:, c] = value.astype(BF16)
            return carry

        lax.fori_loop(0, project.shape[1] // wide, some, 0)

    def send_on(slots, step, base):
        for slot in slots:
            sum_into(arrived.at[slot, step - 1], slot, step - 1, base)
            hop(slot, step).start()

    def onward(step, carry):
        terms(step, 4, near_place(step))
        send_on(far_slots, step, 4)
        send_on(near_slots, step - 1, near_place(step - 1))
        return carry

    parts = h_in.shape[0]
    part_width = h_in.shape[2]

    class fetch_win:
        def __init__(self, n):
            self.copies = [
                pltpu.make_async_copy(
                    h_in.at[h, pl.ds(n * 256, 256), :],
                    win.at[n % 2, :, pl.ds(h * part_width, part_width)],
                    win_sem.at[n % 2, h],
                )
                for h in range(parts)
            ]

        def start(self):
            for copy in self.copies:
                copy.start()

        def wait(self):
            for copy in self.copies:
                copy.wait()

    columns = width // 256

    def row_tiles(n):
        fetch_win(n).wait()

        def tile(m, carry):
            r = pl.ds(pl.multiple_of(m * 512, 512), 512)
            part[r, n * 256 : (n + 1) * 256] = dot_back(project[r, :], win[n % 2]).astype(BF16)
            return carry

        lax.fori_loop(0, count // 512, tile, 0)
        if n + 2 < columns:
            fetch_win(n + 2).start()

    def down_rows(relation):
        b = flip(me, relation)
        r = pl.ds(pl.multiple_of(b * rows, rows), rows)

        def column(n, carry):
            c = pl.ds(pl.multiple_of(n * wide, wide), wide)
            part[r, c] = dot(active[r, :], wd[:, c]).astype(BF16)
            return carry

        lax.fori_loop(0, width // wide, column, 0)

    fetch_active = pltpu.make_async_copy(h_active, active, load_sem.at[2])
    fetch_down = pltpu.make_async_copy(h_down, wd, load_sem.at[3])
    fetch_hidden = pltpu.make_async_copy(hidden, rows_f32, load_sem.at[4])
    fetch_d_hidden = pltpu.make_async_copy(d_hidden, rows_f32, load_sem.at[5])
    for fetch in (fetch_active, fetch_down, fetch_hidden):
        fetch.start()
    fetch_win(0).start()
    fetch_win(1).start()
    fetch_turned.wait()
    terms(0, 0, 2, True)
    for slot in far_slots:
        hop(slot, 0, True).start()
    fetch_active.wait()
    fetch_down.wait()
    down_rows(3)
    row_copy(0, 0).start()
    for slot in near_slots:
        hop(slot, 0, True).start()
    down_rows(2)
    down_rows(1)
    row_copy(1, 0).start()
    down_rows(0)
    send_rows(0)
    hold_down()
    plan = tick_plan(total, 6)

    def extra(number):
        if number < 3:
            for n in range(columns * number // 3, columns * (number + 1) // 3):
                row_tiles(n)
            if number == 2:
                row_copy(0, 1).start()
                row_copy(1, 1).start()
        elif number == 3:
            send_rows(1)
            take_down()
        elif number == 5:
            take_rows()
            vectors_near()

    terms(1, 4, near_place(1))
    send_on(far_slots, 1, 4)
    for number in range(6):
        extra(number)
        lax.fori_loop(max(plan[number][0], 2), plan[number][1], onward, 0)
    terms(total - 1, 4, near_place(total - 1))
    pieces = column_pieces()

    def place(relation, columns_of):
        other = flip(me, relation)
        for base, stride, h, off, size in pieces:
            start = pl.multiple_of(base + other * stride, 128)
            off = h * part_width + off
            full_rows[:, pl.ds(start, size)] = columns_of(off, size).astype(BF16)
        for copy in stored(relation):
            copy.start()

    def stored(relation):
        other = flip(me, relation)
        return [
            pltpu.make_async_copy(
                full_rows.at[:, pl.ds(pl.multiple_of(base + other * stride, 128), size)],
                o_in.at[:, pl.ds(pl.multiple_of(base + other * stride, 128), size)],
                in_sem.at[relation, n],
            )
            for n, (base, stride, h, off, size) in enumerate(pieces)
        ]

    def sent_across(relation):
        return remote(
            stage.at[relation - 1], landed.at[relation - 1],
            a2a_send.at[relation - 1], a2a_recv.at[relation - 1], at.peer(relation),
        )

    for slot in far_slots:
        relation = RELATIONS[slot // 2][0]
        sum_into(stage.at[relation - 1], slot, total - 2, 4)
        sent_across(relation).start()
    send_on(near_slots, total - 2, near_place(total - 2))
    vectors_far()
    for slot in reversed(near_slots):
        relation = RELATIONS[slot // 2][1]
        base = near_place(total - 1)
        if relation == 0:
            hop(slot, total - 2, True).wait_recv()
            place(
                0,
                lambda off, size: arrived[slot, total - 2, :, off : off + size].astype(F32)
                + term[base + slot // 2, :, off : off + size].astype(F32),
            )
        else:
            sum_into(stage.at[relation - 1], slot, total - 2, base)
            sent_across(relation).start()
    for relation in (2, 3, 1):
        sent_across(relation).wait_recv()
        place(relation, lambda off, size: landed[relation - 1, :, off : off + size])
    vectors_end()
    for relation in range(4):
        for copy in stored(relation):
            copy.wait()
    for copy in (store_output, store_tokens):
        copy.wait()
    for relation in (1, 2, 3):
        sent_across(relation).wait_send()
        near(relation).wait_send()
    for n in range(1, total):
        for kind in (0, 1):
            distant(kind, n).wait_send()
    row_copy(2, 0).wait_send()
    for kind in (0, 1, 2):
        row_copy(kind, 1).wait_send()

    def sent(step, carry):
        for slot in range(4):
            hop(slot, step, True).wait_send()
        return carry

    lax.fori_loop(0, total - 1, sent, 0)


def final(
    total, d_project, full_in, turned, active, full_down, hidden, d_hidden, tok, gains, ident_col, sums_two, d_group
):
    rows, width = tok.shape
    count, wide = d_project.shape
    block = width // GROUP // total
    vmem, hbm = pl.BlockSpec(memory_space=pltpu.VMEM), pl.BlockSpec(memory_space=ANY)
    dma = pltpu.SemaphoreType.DMA
    group_width = d_group.shape[0] * d_group.shape[2]
    shapes = (
        ((block, wide * GROUP), BF16),
        ((rows, width), BF16),
        ((rows, width), BF16),
        ((8, 128), F32),
        ((8, 128), F32),
    )
    return pl.pallas_call(
        functools.partial(final_kernel, total),
        out_shape=[jax.ShapeDtypeStruct(s, d) for s, d in shapes],
        in_specs=[hbm] * 7 + [vmem] * 5,
        out_specs=[hbm] * 3 + [vmem] * 2,
        scratch_shapes=[
            pltpu.VMEM((rows, width), BF16),
            pltpu.VMEM((rows, width), BF16),
            pltpu.VMEM((block, wide * GROUP), BF16),
            pltpu.VMEM((count, wide), BF16),
            pltpu.VMEM(turned.shape, BF16),
            pltpu.VMEM((10, block, wide), BF16),
            pltpu.VMEM((4, total - 1, block, wide), BF16),
            pltpu.VMEM((2, 256, wide), BF16),
            pltpu.VMEM((count, width), BF16),
            pltpu.VMEM(active.shape, BF16),
            pltpu.VMEM(full_down.shape, BF16),
            pltpu.VMEM((rows, width), F32),
            pltpu.VMEM((2, 2, rows, width), BF16),
            pltpu.VMEM((2, rows, width), BF16),
            pltpu.VMEM((2, rows, width), BF16),
            pltpu.VMEM((3, block, wide), BF16),
            pltpu.VMEM((3, block, wide), BF16),
            pltpu.VMEM((8, width), F32),
            pltpu.VMEM((8, group_width), F32),
            pltpu.VMEM((3, 8, width // GROUP), F32),
            pltpu.VMEM((8, width // GROUP), F32),
            pltpu.VMEM((total - 1, 8, 128), F32),
            pltpu.VMEM((total - 1, 8, 128), F32),
            dma((8,)), dma((2, 2)), dma((4, total - 1)), dma((4, total - 1)), dma((3,)), dma((3,)),
            dma((2, 3)), dma((2, 3)), dma((GROUP, 8)), dma((6,)), dma((3,)), dma((3,)), dma((2, total - 1)), dma((2, total - 1)),
        ],
        compiler_params=pltpu.CompilerParams(
            collective_id=3, has_side_effects=True, vmem_limit_bytes=63 * MIB
        ),
        name="final_sums",
    )(d_project, full_in, turned, active, full_down, hidden, d_hidden, tok, gains, ident_col, sums_two, d_group)


def mean(values):
    return jnp.mean(values, axis=-1, keepdims=True)


def local(
    total,
    tokens,
    cotangent,
    w_in,
    w_out,
    w_up,
    w_down,
    ln1_gain,
    ln1_bias,
    group_gain,
    ln2_gain,
    ln2_bias,
    seq_lens,
    seq_owner,
    seq_offset,
):
    rows, width = tokens.shape
    heads = HEADS // GROUP
    qk, vv = heads * QKH, heads * VH
    me, inner = lax.axis_index("dp"), lax.axis_index("fsdp")
    small, large = ln1_gain.shape[0], group_gain.shape[0]

    count = GROUP * rows
    vectors = jnp.stack([ln1_gain, ln1_bias, ln2_gain, ln2_bias]).astype(F32)
    pack = jnp.zeros((8, 128), F32)
    pack = lax.dynamic_update_slice(pack, vectors, (0, lax.rem(inner * small, 128)))
    pack = lax.dynamic_update_slice(pack, group_gain.astype(F32)[None], (4, lax.rem(inner * large, 128)))
    rates = jnp.log1p(-(2.0 ** (-5.0 - (me * heads + jnp.arange(heads)).astype(F32))))
    rates = jnp.broadcast_to(rates[:, None, None], (heads, 1, rows))
    entries = jnp.stack([seq_lens, seq_owner, seq_offset])
    (
        full_in, full_up, full_out, full_down, _, turned, query, keys, values, gate, mixed, gated, active, d_upper,
        g_down, hidden, two,
        own_seed, cosine, sine, growth, shrink, powers, ident_col, ident_row, gains, gain_group,
    ) = forward(
        total, w_in, w_up, w_out, w_down, tokens, cotangent, pack, rates, entries[:, :, None], entries[:, None, :]
    )
    tables = (cosine, sine, growth, shrink)
    full_up = full_up.reshape(width, -1)
    full_out = full_out.reshape(-1, width)
    full_down = full_down.reshape(-1, width)
    two = two.reshape(count, width)
    grad_down, grad_up, grad_out, d_hidden, _, sums_two, d_group, d_project = backward(
        total, g_down.reshape(-1, width), two, d_upper, full_up, own_seed, hidden, gains, gated, full_out, query,
        keys, values, gate, mixed, tables, powers, ident_col, ident_row, gain_group,
    )
    grad_in, output, d_tokens, vec_one, vec_two = final(
        total, d_project, full_in, turned, active, full_down, hidden, d_hidden, tokens, gains, ident_col, sums_two,
        d_group,
    )
    grads = lax.dynamic_slice(vec_one, (0, lax.rem(inner * small, 128)), (4, small))
    grad_group = lax.dynamic_slice(vec_two, (0, lax.rem(inner * large, 128)), (1, large))[0]
    return (
        output,
        d_tokens,
        grad_in.astype(F32),
        grad_out,
        grad_up,
        grad_down,
        grads[0],
        grads[1],
        grad_group,
        grads[2],
        grads[3],
    )


def solution(mesh):
    flat = ("dp", "fsdp")
    matrix, vector = P(flat, None), P(flat)
    return jax.shard_map(
        functools.partial(local, mesh.shape["fsdp"]),
        mesh=mesh,
        in_specs=(matrix,) * 6 + (vector,) * 5 + (P(),) * 3,
        out_specs=(matrix,) * 6 + (vector,) * 5,
        check_vma=False,
    )
```
